32 devices in a mesh: dp: 8 (over y, x, core), seq: 4 (over z).
Axes of the slice: x: 2, y: 2, z: 4, core: 2. Of those that a mesh axis runs over, the one named last changes fastest.
Arguments:
- patches: bfloat16 [32, 1024, 768], P('dp', 'seq'), may hold values from -6 to 6
- captions: bfloat16 [32, 64, 768], P('dp', 'seq'), may hold values from -6 to 6
- pairs: int32 [32, 32], replicated, may hold values from 0 to 1, as said below
- image_attend_in: bfloat16 [768, 2304], P(('dp', 'seq')), may hold values from -0.21875 to 0.21875
- image_attend_out: bfloat16 [768, 768], P(('dp', 'seq')), may hold values from -0.875 to 0.875
- image_up_weight: bfloat16 [768, 3072], P(('dp', 'seq')), may hold values from -0.21875 to 0.21875
- image_up_bias: bfloat16 [3072], P(('dp', 'seq')), may hold values from -3 to 3
- image_down_weight: bfloat16 [3072, 768], P(('dp', 'seq')), may hold values from -0.109375 to 0.109375
- image_vectors: bfloat16 [11, 768], P(None, ('dp', 'seq')), may hold values from -3.5 to 3.5, as said below
- probe_query_weight: bfloat16 [768, 768], P(('dp', 'seq')), may hold values from -0.21875 to 0.21875
- probe_pair_weight: bfloat16 [768, 1536], P(('dp', 'seq')), may hold values from -0.21875 to 0.21875
- probe_out_weight: bfloat16 [768, 768], P(('dp', 'seq')), may hold values from -0.21875 to 0.21875
- probe_up_weight: bfloat16 [768, 3072], P(('dp', 'seq')), may hold values from -0.21875 to 0.21875
- probe_up_bias: bfloat16 [3072], P(('dp', 'seq')), may hold values from -3 to 3
- probe_down_weight: bfloat16 [3072, 768], P(('dp', 'seq')), may hold values from -0.109375 to 0.109375
- text_attend_in: bfloat16 [768, 2304], P(('dp', 'seq')), may hold values from -0.21875 to 0.21875
- text_attend_out: bfloat16 [768, 768], P(('dp', 'seq')), may hold values from -0.4375 to 0.4375
- text_up_weight: bfloat16 [768, 3072], P(('dp', 'seq')), may hold values from -0.21875 to 0.21875
- text_up_bias: bfloat16 [3072], P(('dp', 'seq')), may hold values from -3 to 3
- text_down_weight: bfloat16 [3072, 768], P(('dp', 'seq')), may hold values from -0.109375 to 0.109375
- text_vectors: bfloat16 [7, 768], P(None, ('dp', 'seq')), may hold values from -1 to 1.6, as said below
- text_head_weight: bfloat16 [768, 768], P(('dp', 'seq')), may hold values from -0.21875 to 0.21875
- temp_bias: float32 [2], replicated, may hold values from -3 to 2.5, as said below
Outputs:
- loss: float32 [], replicated
- grad_patches: float32 [32, 1024, 768], P('dp', 'seq')
- grad_captions: float32 [32, 64, 768], P('dp', 'seq')
- grad_image_attend_in: float32 [768, 2304], P(('dp', 'seq'))
- grad_image_attend_out: float32 [768, 768], P(('dp', 'seq'))
- grad_image_up_weight: float32 [768, 3072], P(('dp', 'seq'))
- grad_image_up_bias: float32 [3072], P(('dp', 'seq'))
- grad_image_down_weight: float32 [3072, 768], P(('dp', 'seq'))
- grad_image_vectors: float32 [11, 768], P(None, ('dp', 'seq'))
- grad_probe_query_weight: float32 [768, 768], P(('dp', 'seq'))
- grad_probe_pair_weight: float32 [768, 1536], P(('dp', 'seq'))
- grad_probe_out_weight: float32 [768, 768], P(('dp', 'seq'))
- grad_probe_up_weight: float32 [768, 3072], P(('dp', 'seq'))
- grad_probe_up_bias: float32 [3072], P(('dp', 'seq'))
- grad_probe_down_weight: float32 [3072, 768], P(('dp', 'seq'))
- grad_text_attend_in: float32 [768, 2304], P(('dp', 'seq'))
- grad_text_attend_out: float32 [768, 768], P(('dp', 'seq'))
- grad_text_up_weight: float32 [768, 3072], P(('dp', 'seq'))
- grad_text_up_bias: float32 [3072], P(('dp', 'seq'))
- grad_text_down_weight: float32 [3072, 768], P(('dp', 'seq'))
- grad_text_vectors: float32 [7, 768], P(None, ('dp', 'seq'))
- grad_text_head_weight: float32 [768, 768], P(('dp', 'seq'))
- grad_temp_bias: float32 [2], replicated
The draws below stay inside these ranges and needn't reach their ends.
Inputs may be any that keep to these rules, and one draw needn't show every extreme that they name: `pairs`: each image has between 2 and 5 positive captions; some image has exactly 2 and some exactly 5. `image_vectors`: gain rows lie near 1, shift and bias rows near 0, the probe row is of order one. `text_vectors`: gain rows lie near 1, shift and bias rows near 0. `temp_bias`: t between 1.5 and 2.5, bias between -3 and -1.
All inputs are finite; a program needn't handle non-finite values.
Results may differ from the reference program's by a relative error of at most 0.014.
Values may be sent and summed in bfloat16 or wider, within the bound.
A program may use at most 320 MiB of HBM per device.

```python
import jax
import jax.numpy as jnp
from jax import lax

D = 768
FF = 3072
HEADS = 12
HEAD_DIM = 64
PATCHES = 1024
TXT = 64
IMAGES = 32


def vector_table(noise, gain_scale, shift_scale, probe_scale):
    rows = jnp.arange(noise.shape[0])[:, None]
    is_gain = (rows == 0) | (rows == 2) | (rows == 5) | (rows == 8)
    is_probe = rows == 7
    return jnp.where(is_gain, 1.0 + gain_scale * noise, jnp.where(is_probe, probe_scale * noise, shift_scale * noise))


def draw_image_vectors(key, part):
    key = jax.random.fold_in(key, 11)
    noise = jnp.clip(jax.random.normal(key, (11, D), jnp.float32), -2.0, 2.0)
    return vector_table(noise, 0.25, 0.4, 1.5).astype(jnp.bfloat16)


def draw_text_vectors(key, part):
    key = jax.random.fold_in(key, 13)
    noise = jnp.clip(jax.random.normal(key, (7, D), jnp.float32), -2.0, 2.0)
    return vector_table(noise, 0.25, 0.4, 1.5).astype(jnp.bfloat16)


def draw_temp_bias(key, part):
    key = jax.random.fold_in(key, 17)
    first, second = jax.random.split(key)
    temper = jax.random.uniform(first, (1,), jnp.float32, 1.5, 2.5)
    offset = jax.random.uniform(second, (1,), jnp.float32, -3.0, -1.0)
    return jnp.concatenate([temper, offset]).astype(jnp.float32)


def draw_pairs(key, part):
    key = jax.random.fold_in(key, 5)
    key_count, key_order = jax.random.split(key)
    counts = jax.random.randint(key_count, (IMAGES,), 2, 6)
    counts = counts.at[0].set(5).at[IMAGES - 1].set(2)
    row_keys = jax.random.split(key_order, IMAGES)
    orders = jax.vmap(lambda single: jax.random.permutation(single, IMAGES))(row_keys)
    ranks = jnp.argsort(orders, axis=1, stable=True)
    return (ranks < counts[:, None]).astype(jnp.int32)


def block_scale(key, dims, cuts, smallest, top_value):
    loudness = 1.0
    for dim, shards_of in cuts:
        draws = jax.random.uniform(jax.random.fold_in(jax.random.fold_in(key, 6), dim), (shards_of,), jnp.float32, smallest / len(cuts), top_value / len(cuts))
        loudness = loudness * jnp.repeat(jnp.exp(draws), dims[dim] // shards_of).reshape((-1,) + (1,) * (len(dims) - 1 - dim))
    return loudness


def normal_values(own_key, dims, deviation, most, cuts=(), dtype=jnp.bfloat16):
    level = block_scale(own_key, dims, cuts, -0.22, 0.18) if cuts else 1.0
    drawn = jax.random.normal(own_key, dims, jnp.float32) * deviation * level
    return jnp.minimum(jnp.maximum(drawn, -most), most).astype(dtype)


def setup_inputs(seed: int = 0) -> dict:
    seeds = jax.random.split(jax.random.key(seed), 24)
    patches = normal_values(seeds[0], (IMAGES, PATCHES, D), 1.0, 6.0, ((0, 8), (1, 4)))
    captions = normal_values(seeds[1], (IMAGES, TXT, D), 1.0, 6.0, ((0, 8), (1, 4)))
    pairs = draw_pairs(jax.random.fold_in(seeds[23], 71), 0)
    image_attend_in = normal_values(seeds[3], (D, 3 * D), D ** -0.5, 0.21875, ((0, 32),))
    image_attend_out = normal_values(seeds[4], (D, D), (D // 16) ** -0.5, 0.875, ((0, 32),))
    image_up_weight = normal_values(seeds[5], (D, FF), D ** -0.5, 0.21875, ((0, 32),))
    image_up_bias = normal_values(seeds[6], (FF,), 0.5, 3.0, ((0, 32),))
    image_down_weight = normal_values(seeds[7], (FF, D), FF ** -0.5, 0.109375, ((0, 32),))
    image_vectors = draw_image_vectors(jax.random.fold_in(seeds[23], 71), 0)
    probe_query_weight = normal_values(seeds[9], (D, D), D ** -0.5, 0.21875, ((0, 32),))
    probe_pair_weight = normal_values(seeds[10], (D, 2 * D), D ** -0.5, 0.21875, ((0, 32),))
    probe_out_weight = normal_values(seeds[11], (D, D), D ** -0.5, 0.21875, ((0, 32),))
    probe_up_weight = normal_values(seeds[12], (D, FF), D ** -0.5, 0.21875, ((0, 32),))
    probe_up_bias = normal_values(seeds[13], (FF,), 0.5, 3.0, ((0, 32),))
    probe_down_weight = normal_values(seeds[14], (FF, D), FF ** -0.5, 0.109375, ((0, 32),))
    text_attend_in = normal_values(seeds[15], (D, 3 * D), D ** -0.5, 0.21875, ((0, 32),))
    text_attend_out = normal_values(seeds[16], (D, D), (D // 4) ** -0.5, 0.4375, ((0, 32),))
    text_up_weight = normal_values(seeds[17], (D, FF), D ** -0.5, 0.21875, ((0, 32),))
    text_up_bias = normal_values(seeds[18], (FF,), 0.5, 3.0, ((0, 32),))
    text_down_weight = normal_values(seeds[19], (FF, D), FF ** -0.5, 0.109375, ((0, 32),))
    text_vectors = draw_text_vectors(jax.random.fold_in(seeds[23], 71), 0)
    text_head_weight = normal_values(seeds[21], (D, D), D ** -0.5, 0.21875, ((0, 32),))
    temp_bias = draw_temp_bias(jax.random.fold_in(seeds[23], 71), 0)
    return dict(patches=patches, captions=captions, pairs=pairs, image_attend_in=image_attend_in, image_attend_out=image_attend_out, image_up_weight=image_up_weight, image_up_bias=image_up_bias, image_down_weight=image_down_weight, image_vectors=image_vectors, probe_query_weight=probe_query_weight, probe_pair_weight=probe_pair_weight, probe_out_weight=probe_out_weight, probe_up_weight=probe_up_weight, probe_up_bias=probe_up_bias, probe_down_weight=probe_down_weight, text_attend_in=text_attend_in, text_attend_out=text_attend_out, text_up_weight=text_up_weight, text_up_bias=text_up_bias, text_down_weight=text_down_weight, text_vectors=text_vectors, text_head_weight=text_head_weight, temp_bias=temp_bias)


@jax.custom_vjp
def low(v):
    return lax.optimization_barrier(v.astype(jnp.bfloat16)).astype(jnp.float32)

@jax.custom_vjp
def low_back(v):
    return v

def low_keep(v):
    return (low(v), None)

def low_pass(kept, grad):
    return (grad,)

def back_keep(v):
    return (v, None)

def back_low(kept, grad):
    return (low(grad),)
low.defvjp(low_keep, low_pass)
low_back.defvjp(back_keep, back_low)
exact_mode = lax.Precision.HIGHEST
epsilon = 1e-06

def both_ways(values):
    return low(low_back(values))

def matmul(left, right):
    return jnp.einsum('...d,de->...e', left, right, precision=exact_mode)

def layer_norm(inputs, gain, shift):
    center = inputs - lax.optimization_barrier(jnp.mean(inputs, -1, keepdims=True))
    spread = lax.optimization_barrier(jnp.mean(center * center, -1, keepdims=True))
    return center * lax.rsqrt(spread + epsilon) * gain + shift

def residual_block(inputs, attend_in, attend_out, up_weight, up_bias, down_weight, vectors):
    length = inputs.shape[0]
    normed = low(layer_norm(inputs, vectors[0], vectors[1]))
    projected = both_ways(matmul(normed, attend_in))
    queries = projected[:, :D].reshape(length, HEADS, HEAD_DIM)
    keys = projected[:, D:2 * D].reshape(length, HEADS, HEAD_DIM)
    values = projected[:, 2 * D:].reshape(length, HEADS, HEAD_DIM)
    scores = low_back(jnp.einsum('thd,shd->hts', queries, keys, precision=exact_mode) * HEAD_DIM ** (-0.5))
    probs = low(jax.nn.softmax(scores, axis=-1))
    mixed = both_ways(jnp.einsum('hts,shd->thd', probs, values, precision=exact_mode).reshape(length, D))
    hidden = inputs + low_back(matmul(mixed, attend_out))
    second = low(layer_norm(hidden, vectors[2], vectors[3]))
    upper = low_back(matmul(second, up_weight) + up_bias)
    active = low(jax.nn.gelu(upper, approximate=True))
    return hidden + low_back(matmul(active, down_weight) + vectors[4])

def image_path(inputs, attend_in, attend_out, up_weight, up_bias, down_weight, vectors, query_weight, pair_weight, out_weight, head_up, head_bias, head_down):
    length = inputs.shape[0]
    block_out = residual_block(inputs, attend_in, attend_out, up_weight, up_bias, down_weight, vectors)
    final = low(layer_norm(block_out, vectors[5], vectors[6]))
    pool_pair = both_ways(matmul(final, pair_weight))
    keys = pool_pair[:, :D].reshape(length, HEADS, HEAD_DIM)
    values = pool_pair[:, D:].reshape(length, HEADS, HEAD_DIM)
    probe_query = matmul(vectors[7], query_weight).reshape(HEADS, HEAD_DIM)
    scores = jnp.einsum('hd,thd->ht', probe_query, keys, precision=exact_mode) * HEAD_DIM ** (-0.5)
    probs = jax.nn.softmax(scores, axis=-1)
    pooled = jnp.einsum('ht,thd->hd', probs, values, precision=exact_mode).reshape(D)
    head_start = matmul(pooled, out_weight)
    head_normed = low(layer_norm(head_start, vectors[8], vectors[9]))
    head_active = low(jax.nn.gelu(matmul(head_normed, head_up) + head_bias, approximate=True))
    return head_start + (matmul(head_active, head_down) + vectors[10])

def text_path(inputs, attend_in, attend_out, up_weight, up_bias, down_weight, vectors, head_weight):
    block_out = residual_block(inputs, attend_in, attend_out, up_weight, up_bias, down_weight, vectors)
    text_final = low(layer_norm(block_out[-1], vectors[5], vectors[6]))
    return matmul(text_final, head_weight)

def normalize(rows):
    return rows * lax.rsqrt(lax.optimization_barrier(jnp.sum(rows * rows, -1, keepdims=True)) + epsilon)

def sigmoid_loss(image_rows, text_rows, temp_bias, labels):
    logits = jnp.dot(normalize(image_rows), normalize(text_rows).T, precision=exact_mode) * jnp.exp(temp_bias[0]) + temp_bias[1]
    return -jnp.sum(jax.nn.log_sigmoid(labels * logits)) / image_rows.shape[0]

def reference(patches, captions, pairs, image_attend_in, image_attend_out, image_up_weight, image_up_bias, image_down_weight, image_vectors, probe_query_weight, probe_pair_weight, probe_out_weight, probe_up_weight, probe_up_bias, probe_down_weight, text_attend_in, text_attend_out, text_up_weight, text_up_bias, text_down_weight, text_vectors, text_head_weight, temp_bias):
    labels = (2 * pairs - 1).astype(jnp.float32)
    floats = [patches, captions, image_attend_in, image_attend_out, image_up_weight, image_up_bias, image_down_weight, image_vectors, probe_query_weight, probe_pair_weight, probe_out_weight, probe_up_weight, probe_up_bias, probe_down_weight, text_attend_in, text_attend_out, text_up_weight, text_up_bias, text_down_weight, text_vectors, text_head_weight]
    floats = [item.astype(jnp.float32) for item in floats] + [temp_bias.astype(jnp.float32)]

    def forward(image_in, text_in, *weights):
        image_weights = weights[0:12]
        text_weights = weights[12:19]
        image_rows = lax.map(jax.checkpoint(lambda single: image_path(single, *image_weights)), image_in)
        text_rows = jax.vmap(lambda single: text_path(single, *text_weights))(text_in)
        return sigmoid_loss(image_rows, text_rows, weights[19], labels)
    loss, pullback = jax.vjp(forward, *floats)
    grads = pullback(jnp.ones_like(loss))
    return (loss, grads[0], grads[1], grads[2], grads[3], grads[4], grads[5], grads[6], grads[7], grads[8], grads[9], grads[10], grads[11], grads[12], grads[13], grads[14], grads[15], grads[16], grads[17], grads[18], grads[19], grads[20], grads[21])
```

```python
from functools import partial

import jax
import jax.numpy as jnp
from jax import lax
from jax.experimental import pallas as pl
from jax.experimental.pallas import tpu as pltpu
from jax.sharding import PartitionSpec as P

HEADS = 12
ALL = ("dp", "seq")
F32, BF = jnp.float32, jnp.bfloat16
HIGH = lax.Precision.HIGHEST
EPS = 1e-06


def mm(a, b, ca=1, cb=0):
    return lax.dot_general(a, b, (((ca,), (cb,)), ((), ())), preferred_element_type=F32)


def mm_exact(a, b, ca=1, cb=0):
    return lax.dot_general(a, b, (((ca,), (cb,)), ((), ())), precision=HIGH, preferred_element_type=F32)


def split_two(a):
    high = a.astype(BF)
    return high, (a - high.astype(F32)).astype(BF)


def layer_norm(x, gain, shift):
    center = x - jnp.mean(x, -1, keepdims=True)
    spread = jnp.mean(center * center, -1, keepdims=True)
    return center * lax.rsqrt(spread + EPS) * gain + shift


def norm_back(x, gain, upstream):
    center = x - jnp.mean(x, -1, keepdims=True)
    inverse = lax.rsqrt(jnp.mean(center * center, -1, keepdims=True) + EPS)
    unit = center * inverse
    scaled = upstream * gain
    d_x = inverse * (
        scaled
        - jnp.mean(scaled, -1, keepdims=True)
        - unit * jnp.mean(scaled * unit, -1, keepdims=True)
    )
    return d_x, jnp.sum(upstream * unit, 0), jnp.sum(upstream, 0)


def norm_back_rows(x, gain, upstream):
    d_x, d_gain, d_shift = norm_back(x, gain, upstream)
    return d_x, d_gain[None], d_shift[None]


def mm_two(a, b, cb=0):
    high, low = split_two(a)
    return mm(high, b, 1, cb) + mm(low, b, 1, cb)


def gelu_pair(u):
    c = 0.7978845608028654
    t = jnp.tanh(c * (u + 0.044715 * u * u * u))
    value = 0.5 * u * (1.0 + t)
    slope = 0.5 * (1.0 + t) + 0.5 * u * (1.0 - t * t) * c * (1.0 + 3 * 0.044715 * u * u)
    return value, slope


def attend_fwd_kernel(q_ref, k_ref, v_ref, o_ref, lse_ref):
    q = q_ref[...] * 0.125
    k = k_ref[...]
    lane = lax.broadcasted_iota(jnp.int32, k.shape, 1)
    v_turned = jnp.transpose(v_ref[...])
    outs = []
    for h in range(2):
        keep = (lane < 64) if h == 0 else (lane >= 64)
        own_k = jnp.where(keep, k, jnp.zeros_like(k))
        s = mm(own_k, q, 1, 1)
        top = jnp.max(s, 0, keepdims=True)
        p = jnp.exp(s - top)
        total = jnp.sum(p, 0, keepdims=True)
        outs.append(mm(v_turned[64 * h : 64 * h + 64], p.astype(BF)) / total)
        lse_ref[0, h : h + 1, :] = top + jnp.log(total)
    o_ref[...] = jnp.transpose(jnp.concatenate(outs, 0)).astype(BF)


def attend_fwd(proj, length):
    rows, width = proj.shape[0], proj.shape[1] // 3
    pairs = width // 128
    block = lambda part: pl.BlockSpec((length, 128), lambda b, h: (b, part * pairs + h))
    return pl.pallas_call(
        attend_fwd_kernel,
        grid=(rows // length, pairs),
        in_specs=[block(0), block(1), block(2)],
        out_specs=[block(0), pl.BlockSpec((1, 2, length), lambda b, h: (h, 0, b))],
        out_shape=[
            jax.ShapeDtypeStruct((rows, width), BF),
            jax.ShapeDtypeStruct((pairs, 2, rows), F32),
        ],
        compiler_params=pltpu.CompilerParams(vmem_limit_bytes=48 << 20),
        cost_estimate=pl.CostEstimate(
            flops=rows * length * width * 8,
            bytes_accessed=rows * width * 8,
            transcendentals=rows * length * HEADS,
        ),
    )(proj, proj, proj)


def attend_bwd_kernel(q_ref, k_ref, v_ref, do_ref, lse_ref, d_ref, dq_ref, dk_ref, dv_ref):
    q = q_ref[...] * 0.125
    k, v, do = k_ref[...], v_ref[...], do_ref[...]
    lane = lax.broadcasted_iota(jnp.int32, k.shape, 1)
    dqs, dks, dvs = [], [], []
    for h in range(2):
        keep = (lane < 64) if h == 0 else (lane >= 64)
        s = mm(jnp.where(keep, k, jnp.zeros_like(k)), q, 1, 1)
        p = jnp.exp(s - lse_ref[0, h : h + 1, :])
        dp = mm(jnp.where(keep, v, jnp.zeros_like(v)), do, 1, 1)
        ds = (p * (dp - d_ref[0, h : h + 1, :])).astype(BF)
        dvs.append(mm(p.astype(BF), do))
        dks.append(mm(ds, q))
        dqs.append(mm(ds, k, 0, 0))
    low = lane < 64
    dq_ref[...] = (jnp.where(low, dqs[0], dqs[1]) * 0.125).astype(BF)
    dk_ref[...] = jnp.where(low, dks[0], dks[1]).astype(BF)
    dv_ref[...] = jnp.where(low, dvs[0], dvs[1]).astype(BF)


def attend_bwd(proj, d_out, lse, inner, length):
    rows, width = proj.shape[0], proj.shape[1] // 3
    pairs = width // 128
    block = lambda part: pl.BlockSpec((length, 128), lambda b, h: (b, part * pairs + h))
    row = pl.BlockSpec((1, 2, length), lambda b, h: (h, 0, b))
    result = jax.ShapeDtypeStruct((rows, width), BF)
    return pl.pallas_call(
        attend_bwd_kernel,
        grid=(rows // length, pairs),
        in_specs=[block(0), block(1), block(2), block(0), row, row],
        out_specs=[block(0)] * 3,
        out_shape=[result] * 3,
        compiler_params=pltpu.CompilerParams(vmem_limit_bytes=56 << 20),
        cost_estimate=pl.CostEstimate(
            flops=rows * length * width * 20,
            bytes_accessed=rows * width * 16,
            transcendentals=rows * length * HEADS,
        ),
    )(proj, proj, proj, d_out, lse, inner)


def head_blocks(width):
    own = jnp.arange(width)[None, :] // (width // HEADS) == jnp.arange(HEADS)[:, None]
    return own.astype(F32)


def spread_heads(rows):
    n, width = rows.shape
    return (rows[:, None, :] * head_blocks(width)[None]).reshape(n * HEADS, width)


def fold_heads(rows):
    total, width = rows.shape
    return jnp.sum(rows.reshape(total // HEADS, HEADS, width) * head_blocks(width)[None], 1)


def device_program(
    patches, captions, pairs,
    image_attend_in, image_attend_out, image_up_weight, image_up_bias, image_down_weight,
    image_vectors, probe_query_weight, probe_pair_weight, probe_out_weight, probe_up_weight,
    probe_up_bias, probe_down_weight, text_attend_in, text_attend_out, text_up_weight,
    text_up_bias, text_down_weight, text_vectors, text_head_weight, temp_bias,
):
    seq = lax.axis_size("seq")
    world = seq * lax.axis_size("dp")
    me = lax.axis_index("dp") * seq + lax.axis_index("seq")
    width = patches.shape[-1]
    head_width = width // HEADS
    factor = head_width ** (-0.5)
    hidden_width = image_up_weight.shape[1]
    part = width // world
    wide_part = hidden_width // world

    def gather(*weights):
        flat = jnp.concatenate([w.reshape(-1, width) for w in weights], 0)
        full = lax.all_gather(flat, ALL, axis=0)
        out, at = [], 0
        for w in weights:
            count = w.size // width
            piece = full[:, at : at + count]
            out.append(piece.reshape(world * w.shape[0], w.shape[1]))
            at += count
        return out

    small = jnp.concatenate(
        [image_vectors.reshape(-1), text_vectors.reshape(-1), image_up_bias, probe_up_bias, text_up_bias]
    )
    small_all = lax.all_gather(small, ALL, axis=0)
    sizes = [image_vectors.size, text_vectors.size, image_up_bias.size, probe_up_bias.size, text_up_bias.size]
    cuts = [sum(sizes[:i]) for i in range(len(sizes) + 1)]
    pieces = [small_all[:, cuts[i] : cuts[i + 1]].astype(F32) for i in range(len(sizes))]
    ivec = pieces[0].reshape(world, -1, part).transpose(1, 0, 2).reshape(-1, width)
    tvec = pieces[1].reshape(world, -1, part).transpose(1, 0, 2).reshape(-1, width)
    i_bias, p_bias, t_bias = (p.reshape(-1) for p in pieces[2:])

    (w_in,) = gather(image_attend_in)
    w_out, w_up, w_down = gather(image_attend_out, image_up_weight, image_down_weight)
    tw_in, tw_out, tw_up, tw_down, tw_head, pw_query, pw_pair, pw_out, pw_up, pw_down = gather(
        text_attend_in, text_attend_out, text_up_weight, text_down_weight, text_head_weight,
        probe_query_weight, probe_pair_weight, probe_out_weight, probe_up_weight, probe_down_weight,
    )

    def to_owner(x):
        return lax.all_to_all(x, "seq", 0, 1, tiled=True)

    x = to_owner(patches)
    own, length = x.shape[0], x.shape[1]
    x = x.reshape(own * length, width).astype(F32)
    captions_own = to_owner(captions)
    text_length = captions_own.shape[1]

    normed = layer_norm(x, ivec[0], ivec[1]).astype(BF)
    proj = mm(normed, w_in).astype(BF)
    mixed, lse = attend_fwd(proj, length)
    hidden = x + mm(mixed, w_out)
    second = layer_norm(hidden, ivec[2], ivec[3]).astype(BF)
    value, slope = gelu_pair(mm(second, w_up) + i_bias)
    active, slope = value.astype(BF), slope.astype(BF)
    block_out = hidden + mm(active, w_down) + ivec[4]
    final = layer_norm(block_out, ivec[5], ivec[6]).astype(BF)

    t_x = captions_own.astype(F32)
    t_normed = layer_norm(t_x, tvec[0], tvec[1]).astype(BF)
    t_last = t_normed[:, -1]
    tw_q, tw_k, tw_v = tw_in[:, :width], tw_in[:, width : 2 * width], tw_in[:, 2 * width :]
    t_q = mm(t_last, tw_q).astype(BF)
    t_keys = mm(spread_heads(t_q.astype(F32)).astype(BF), tw_k, 1, 1) * factor
    t_keys = t_keys.reshape(own, HEADS, width)
    k_high, k_low = split_two(t_keys)
    scores = jnp.einsum("bsd,bhd->bsh", t_normed, k_high, preferred_element_type=F32)
    scores += jnp.einsum("bsd,bhd->bsh", t_normed, k_low, preferred_element_type=F32)
    t_probs = jax.nn.softmax(scores, axis=1)
    t_used = jnp.einsum("bsh,bsd->bhd", t_probs, t_normed.astype(F32), precision=HIGH)
    t_mixed = fold_heads(mm(t_used.reshape(own * HEADS, width).astype(BF), tw_v)).astype(BF)
    t_hidden = t_x[:, -1] + mm(t_mixed, tw_out)
    t_second = layer_norm(t_hidden, tvec[2], tvec[3]).astype(BF)
    t_value, t_slope = gelu_pair(mm(t_second, tw_up) + t_bias)
    t_active = t_value.astype(BF)
    t_out = t_hidden + mm(t_active, tw_down) + tvec[4]
    t_final = layer_norm(t_out, tvec[5], tvec[6]).astype(BF)
    text_embed = mm(t_final, tw_head)

    pw_k, pw_v = pw_pair[:, :width], pw_pair[:, width:]
    probe_query = mm_exact(ivec[7:8], pw_query.astype(F32))
    p_keys = mm_exact(spread_heads(probe_query), pw_k.astype(F32), 1, 1) * factor
    k_high, k_low = split_two(p_keys)
    pool_scores = mm(k_high, final, 1, 1) + mm(k_low, final, 1, 1)
    pool_scores = pool_scores.reshape(HEADS, own, length)
    pool_probs = jax.nn.softmax(pool_scores, axis=-1)
    final_own = final.reshape(own, length, width)
    p_high, p_low = split_two(pool_probs)
    used = jnp.einsum("hbt,btd->bhd", p_high, final_own, preferred_element_type=F32)
    used += jnp.einsum("hbt,btd->bhd", p_low, final_own, preferred_element_type=F32)
    pooled = fold_heads(mm_exact(used.reshape(own * HEADS, width), pw_v.astype(F32)))
    head_start = mm_exact(pooled, pw_out.astype(F32))
    head_normed = layer_norm(head_start, ivec[8], ivec[9]).astype(BF)
    h_value, h_slope = gelu_pair(mm(head_normed, pw_up) + p_bias)
    head_active = h_value.astype(BF)
    image_embed = head_start + mm(head_active, pw_down) + ivec[10]

    embeds = lax.all_gather(jnp.stack([image_embed, text_embed], 1), ALL, axis=0, tiled=True)
    every_image, every_text = embeds[:, 0], embeds[:, 1]
    labels = (2 * pairs - 1).astype(F32)
    total = every_image.shape[0]
    i_scale = lax.rsqrt(jnp.sum(every_image * every_image, -1, keepdims=True) + EPS)
    t_scale = lax.rsqrt(jnp.sum(every_text * every_text, -1, keepdims=True) + EPS)
    z_i, z_t = every_image * i_scale, every_text * t_scale
    cosine = mm_exact(z_i, z_t, 1, 1)
    temper = jnp.exp(temp_bias[0])
    logits = cosine * temper + temp_bias[1]
    loss = -jnp.sum(jax.nn.log_sigmoid(labels * logits)) / total
    g = -labels * jax.nn.sigmoid(-labels * logits) / total
    grad_temp = jnp.stack([temper * jnp.sum(g * cosine), jnp.sum(g)])
    dz_i = temper * mm_exact(g, z_t)
    dz_t = temper * mm_exact(g, z_i, 0, 0)
    all_d_image = (dz_i - z_i * jnp.sum(z_i * dz_i, -1, keepdims=True)) * i_scale
    all_d_text = (dz_t - z_t * jnp.sum(z_t * dz_t, -1, keepdims=True)) * t_scale
    d_image = lax.dynamic_slice_in_dim(all_d_image, me * own, own, 0)
    d_text = lax.dynamic_slice_in_dim(all_d_text, me * own, own, 0)

    h_upper = mm_exact(d_image, pw_down.astype(F32), 1, 1) * h_slope
    h_norm = mm_exact(h_upper, pw_up.astype(F32), 1, 1)
    d_start, dv8, dv9 = norm_back(head_start, ivec[8], h_norm)
    d_start = d_image + d_start
    dv10 = jnp.sum(d_image, 0)
    d_pooled = mm_exact(d_start, pw_out.astype(F32), 1, 1)
    p_values = mm_exact(spread_heads(d_pooled), pw_v.astype(F32), 1, 1).reshape(own, HEADS, width)
    v_high, v_low = split_two(p_values)
    d_probs = jnp.einsum("bhd,btd->hbt", v_high, final_own, preferred_element_type=F32)
    d_probs += jnp.einsum("bhd,btd->hbt", v_low, final_own, preferred_element_type=F32)
    d_scores = pool_probs * (d_probs - jnp.sum(pool_probs * d_probs, -1, keepdims=True))
    s_high, s_low = split_two(d_scores)
    p_used = jnp.einsum("hbt,btd->bhd", s_high, final_own, preferred_element_type=F32)
    p_used += jnp.einsum("hbt,btd->bhd", s_low, final_own, preferred_element_type=F32)
    d_query = jnp.sum(fold_heads(mm_exact(p_used.reshape(own * HEADS, width), pw_k.astype(F32))), 0) * factor
    d_final = jnp.einsum(
        "hbt,bhd->btd",
        jnp.concatenate([s_high, p_high], 0),
        jnp.concatenate([jnp.broadcast_to(k_high[None], (own, HEADS, width)), v_high], 1),
        preferred_element_type=F32,
    ).reshape(own * length, width)
    dy, dv5, dv6 = norm_back(block_out, ivec[5], d_final)

    d_branch = dy.astype(BF)
    g_down = mm(active, d_branch, 0, 0)
    dv4 = jnp.sum(dy, 0)
    d_upper_f = mm(d_branch, w_down, 1, 1) * slope.astype(F32)
    d_upper = d_upper_f.astype(BF)
    g_bias = jnp.sum(d_upper_f, 0)
    g_up = mm(second, d_upper, 0, 0)
    d_hidden, dv2, dv3 = norm_back(hidden, ivec[2], mm(d_upper, w_up, 1, 1))
    d_hidden = dy + d_hidden
    d_attend = d_hidden.astype(BF)
    g_out = mm(mixed, d_attend, 0, 0)
    d_mixed = mm(d_attend, w_out, 1, 1).astype(BF)

    def scatter(*grads):
        flat = jnp.concatenate([g.astype(BF).reshape(world, -1, width) for g in grads], 1)
        mine = lax.psum_scatter(flat, ALL, scatter_dimension=0, tiled=False).astype(F32)
        out, at = [], 0
        for g in grads:
            count = g.size // world // width
            out.append(mine[at : at + count].reshape(g.shape[0] // world, g.shape[1]))
            at += count
        return out

    own_up, own_down, own_out = scatter(g_up, g_down, g_out)
    inner_rows = jnp.sum(
        (d_mixed.astype(F32) * mixed.astype(F32)).reshape(own * length, HEADS, head_width), -1
    ).T.reshape(HEADS // 2, 2, own * length)
    d_q, d_k, d_v = attend_bwd(proj, d_mixed, lse, inner_rows, length)
    g_in = jnp.concatenate([mm(normed, d, 0, 0) for d in (d_q, d_k, d_v)], 1)
    (own_in,) = scatter(g_in)
    d_normed = (
        mm(d_q, w_in[:, :width], 1, 1)
        + mm(d_k, w_in[:, width : 2 * width], 1, 1)
        + mm(d_v, w_in[:, 2 * width :], 1, 1)
    )
    d_x, dv0, dv1 = norm_back(x, ivec[0], d_normed)
    d_x = (d_hidden + d_x).reshape(own, length, width)

    def to_tokens(v):
        return lax.all_to_all(v.astype(BF), "seq", 1, 0, tiled=True).astype(F32)

    grad_patches = to_tokens(d_x)

    dt_final = mm_exact(d_text, tw_head.astype(F32), 1, 1)
    dt_out, tv5, tv6 = norm_back(t_out, tvec[5], dt_final)
    dt_branch = dt_out.astype(BF)
    tv4 = jnp.sum(dt_out, 0)
    dt_upper = (mm(dt_branch, tw_down, 1, 1) * t_slope).astype(BF)
    dt_hidden, tv2, tv3 = norm_back(t_hidden, tvec[2], mm(dt_upper, tw_up, 1, 1))
    dt_hidden = dt_out + dt_hidden
    dt_attend = dt_hidden.astype(BF)
    dt_mixed = mm(dt_attend, tw_out, 1, 1).astype(BF)
    t_values = mm(spread_heads(dt_mixed.astype(F32)).astype(BF), tw_v, 1, 1).reshape(own, HEADS, width)
    tv_high, tv_low = split_two(t_values)
    dt_probs = jnp.einsum("bsd,bhd->bsh", t_normed, tv_high, preferred_element_type=F32)
    dt_probs += jnp.einsum("bsd,bhd->bsh", t_normed, tv_low, preferred_element_type=F32)
    dt_scores = t_probs * (dt_probs - jnp.sum(t_probs * dt_probs, 1, keepdims=True))
    tk_used = jnp.einsum("bsh,bsd->bhd", dt_scores, t_normed.astype(F32), precision=HIGH)
    dt_q = fold_heads(mm(tk_used.reshape(own * HEADS, width).astype(BF), tw_k)) * factor
    dt_q = dt_q.astype(BF)
    dt_normed = jnp.einsum("bsh,bhd->bsd", dt_scores, t_keys, precision=HIGH)
    dt_normed += jnp.einsum("bsh,bhd->bsd", t_probs, t_values, precision=HIGH)
    dt_normed = dt_normed.at[:, -1].add(mm(dt_q, tw_q, 1, 1))
    flat_x = t_x.reshape(own * text_length, width)
    dt_x, tv0, tv1 = norm_back(flat_x, tvec[0], dt_normed.reshape(own * text_length, width))
    dt_x = dt_x.reshape(own, text_length, width).at[:, -1].add(dt_hidden)
    grad_captions = to_tokens(dt_x)

    whole = jnp.concatenate(
        [v.astype(F32) for v in (h_upper, d_start, d_pooled, dt_branch, dt_upper, dt_attend, dt_q, t_q, dt_mixed)], 1
    )
    whole = lax.all_gather(whole, ALL, axis=0, tiled=True)
    at = [0]

    def take(count):
        at[0] += count
        return whole[:, at[0] - count : at[0]]

    a_h_upper, a_start, a_pooled, a_branch, a_upper, a_attend, a_q, a_query, a_mixed = (
        take(c) for c in (hidden_width, width, width, width, hidden_width, width, width, width, width)
    )
    columns = [pooled, head_normed, t_last, t_mixed, t_second, t_final]
    columns += [used, t_used, tk_used * factor]
    columns += [head_active, t_active]
    columns = jnp.concatenate(
        [v.astype(F32).reshape(own, -1, width) for v in columns], 1
    )
    wide = 2 * (hidden_width // width)
    narrow = columns.shape[1] - wide
    cut = jnp.concatenate(
        [
            columns[:, :narrow].reshape(own, narrow, world, part).transpose(2, 0, 1, 3).reshape(world, own, -1),
            columns[:, narrow:].reshape(own, 2, world, wide_part).transpose(2, 0, 1, 3).reshape(world, own, -1),
        ],
        2,
    )
    cut = lax.all_to_all(cut, ALL, 0, 0, tiled=True).reshape(total, -1)
    slim = cut[:, : narrow * part].reshape(total, narrow, part)
    broad = cut[:, narrow * part :].reshape(total, 2, wide_part)

    def outer(rows, cols):
        return mm_exact(rows, cols, 0, 0)

    def outer_heads(rows, cols):
        cols = cols.reshape(total, HEADS, head_width)
        return jnp.einsum("chm,che->mhe", rows, cols, precision=HIGH).reshape(part, width)

    c_pooled, c_head, c_last, c_mixed, c_second, c_final = (slim[:, i] for i in range(6))
    c_used, ct_used, ctk_used = (slim[:, 6 + i * HEADS : 6 + (i + 1) * HEADS] for i in range(3))
    own_t_in = jnp.concatenate(
        [outer(c_last, a_q), outer_heads(ctk_used, a_query), outer_heads(ct_used, a_mixed)], 1
    )
    own_t_out = outer(c_mixed, a_attend)
    own_t_up = outer(c_second, a_upper)
    own_t_down = outer(broad[:, 1], a_branch)
    own_t_head = outer(c_final, all_d_text)
    own_p_out = outer(c_pooled, a_start)
    own_p_up = outer(c_head, a_h_upper)
    own_p_down = outer(broad[:, 0], all_d_image)
    own_p_values = outer_heads(c_used, a_pooled)

    summed = jnp.concatenate(
        [
            jnp.stack([dv0, dv1, dv2, dv3, dv4, dv5, dv6, dv8, dv9, dv10]),
            jnp.stack([tv0, tv1, tv2, tv3, tv4, tv5, tv6]),
            d_query[None],
            jnp.sum(p_used, 0),
            g_bias.reshape(-1, width),
        ],
        0,
    )
    summed = lax.psum(summed, ALL)
    total_query = summed[17]
    mine = lambda v, n: lax.dynamic_slice_in_dim(v, me * n, n, -1)
    own_probe = mine(ivec[7], part)
    own_p_query = own_probe[:, None] * total_query[None, :]
    dv7 = jnp.sum(probe_query_weight.astype(F32) * total_query[None, :], 1)
    pk_used = mine(summed[18 : 18 + HEADS], part)
    own_p_keys = jnp.einsum(
        "hm,he->mhe", pk_used, probe_query.reshape(HEADS, head_width) * factor
    ).reshape(part, width)
    own_p_pair = jnp.concatenate([own_p_keys, own_p_values], 1)
    ten = mine(summed[:10], part)
    own_ivec = jnp.concatenate([ten[:7], dv7[None], ten[7:]], 0)
    own_tvec = mine(summed[10:17], part)
    own_bias = mine(summed[18 + HEADS :].reshape(-1), wide_part)
    own_p_bias = mine(jnp.sum(a_h_upper, 0), wide_part)
    own_t_bias = mine(jnp.sum(a_upper, 0), wide_part)
    return (
        loss, grad_patches, grad_captions,
        own_in, own_out, own_up, own_bias, own_down, own_ivec,
        own_p_query, own_p_pair, own_p_out, own_p_up, own_p_bias, own_p_down,
        own_t_in, own_t_out, own_t_up, own_t_bias, own_t_down, own_tvec, own_t_head,
        grad_temp,
    )


MESH = pl.DeviceIdType.MESH

class Place:
    def __init__(self):
        i = lax.axis_index("dp")
        self.i, self.z = i, lax.axis_index("seq")
        self.y, self.x, self.c = i // 4, (i // 2) % 2, i % 2
        self.at_y = (i + 4 - 8 * self.y, self.z)
        self.at_x = (i + 2 - 4 * self.x, self.z)
        self.at_c = (i + 1 - 2 * self.c, self.z)

    def at_z(self, k):
        return (self.i, (self.z + k) % 4)

def greet(peers):
    barrier = pltpu.get_barrier_semaphore()
    for p in peers:
        pl.semaphore_signal(barrier, inc=1, device_id=p, device_id_type=MESH)
    pl.semaphore_wait(barrier, len(peers))

def gather_kernel(kinds, *refs):
    n = len(kinds)
    srcs, outs = refs[:n], refs[n:2 * n]
    send, recv, local = refs[2 * n:]
    me = Place()
    y, x, c, z = me.y, me.x, me.c, me.z
    greet([me.at_z(1), me.at_z(2), me.at_z(3), me.at_x, me.at_y, me.at_c])
    started = []
    pending = {}

    def push(a, slot, src, dst, dev, arriving):
        copy = pltpu.make_async_remote_copy(src, dst, send.at[a, slot], recv.at[a, slot], device_id=dev, device_id_type=MESH)
        copy.start()
        started.append(copy)
        return pltpu.make_async_remote_copy(arriving, arriving, send.at[a, slot], recv.at[a, slot], device_id=dev, device_id_type=MESH)

    def stage(a, s):
        kind, order = kinds[a]
        src, out = srcs[a], outs[a]
        for w in pending.pop((a, s - 1), []):
            w()
        waits = []
        if s == 0:
            if kind in ("full", "zg"):
                own = src
            elif kind in ("cols", "za"):
                own = src.at[z]
            else:
                own = src
            home = out.at[y, x, c, z] if kind in ("full", "cols") else out.at[z] if kind in ("zg", "za") else out.at[y, x, c]
            cp = pltpu.make_async_copy(own, home, local.at[a])
            cp.start()
            waits.append(cp.wait)
            if kind != "plane":
                for k in (1, 2, 3):
                    to, fro = (z + k) % 4, (z + 4 - k) % 4
                    s_ref = src.at[to] if kind in ("cols", "za") else src
                    if kind in ("full", "cols"):
                        dst, arr = out.at[y, x, c, z], out.at[y, x, c, fro]
                    else:
                        dst, arr = out.at[z], out.at[fro]
                    waits.append(push(a, k - 1, s_ref, dst, me.at_z(k), arr).wait_recv)
        elif kind in ("zg", "za"):
            return
        elif s == 1:
            if order in ("C", "S"):
                cut = (lambda r: r) if order == "C" else (lambda r: r.at[..., 0:r.shape[-1] // 2])
                waits.append(push(a, 3, cut(out.at[y, x, c]), cut(out.at[y, x, c]), me.at_x, cut(out.at[y, 1 - x, c])).wait_recv)
            if order in ("D", "S"):
                cut = (lambda r: r) if order == "D" else (lambda r: r.at[..., r.shape[-1] // 2:])
                waits.append(push(a, 4, cut(out.at[y, x, c]), cut(out.at[y, x, c]), me.at_y, cut(out.at[1 - y, x, c])).wait_recv)
        elif s == 2:
            if order in ("C", "S"):
                cut = (lambda r: r) if order == "C" else (lambda r: r.at[..., 0:r.shape[-1] // 2])
                waits.append(push(a, 5, cut(out.at[y, :, c]), cut(out.at[y, :, c]), me.at_y, cut(out.at[1 - y, :, c])).wait_recv)
            if order in ("D", "S"):
                cut = (lambda r: r) if order == "D" else (lambda r: r.at[..., r.shape[-1] // 2:])
                waits.append(push(a, 6, cut(out.at[:, x, c]), cut(out.at[:, x, c]), me.at_x, cut(out.at[:, 1 - x, c])).wait_recv)
        elif s == 3:
            waits.append(push(a, 7, out.at[:, :, c], out.at[:, :, c], me.at_c, out.at[:, :, 1 - c]).wait_recv)
        pending[(a, s)] = waits

    for t in range(n + 4):
        for a in range(max(0, t - 4), min(n, t + 1)):
            stage(a, t - a)
    for key in list(pending):
        for w in pending.pop(key):
            w()
    for copy in started:
        copy.wait_send()

def gather(ops, kinds, cid):
    shapes = []
    for o, (kind, _) in zip(ops, kinds):
        if kind == "full":
            s = (2, 2, 2, 4) + o.shape
        elif kind == "cols":
            s = (2, 2, 2, 4) + o.shape[1:]
        elif kind == "plane":
            s = (2, 2, 2) + o.shape
        elif kind == "zg":
            s = (4,) + o.shape
        else:
            s = o.shape
        shapes.append(jax.ShapeDtypeStruct(s, o.dtype))
    n = len(ops)
    return pl.pallas_call(
        partial(gather_kernel, kinds),
        out_shape=shapes,
        in_specs=[pl.BlockSpec(memory_space=pl.ANY)] * n,
        out_specs=[pl.BlockSpec(memory_space=pl.ANY)] * n,
        scratch_shapes=[pltpu.SemaphoreType.DMA((n, 8)), pltpu.SemaphoreType.DMA((n, 8)), pltpu.SemaphoreType.DMA((n,))],
        compiler_params=pltpu.CompilerParams(collective_id=cid, has_side_effects=True),
    )(*ops)

def reduce_kernel(g_ref, dx_ref, own_ref, moved_ref, from_c, acc_c, from_1, acc_1, from_2, acc_2, from_z, send, recv, local):
    me = Place()
    y, x, c, z = me.y, me.x, me.c, me.z
    greet([me.at_z(1), me.at_z(2), me.at_z(3), me.at_x, me.at_y, me.at_c])
    half = g_ref.shape[-1] // 2
    started = []

    def push(slot, src, dst, dev, arriving):
        copy = pltpu.make_async_remote_copy(src, dst, send.at[slot], recv.at[slot], device_id=dev, device_id_type=MESH)
        copy.start()
        started.append(copy)
        return pltpu.make_async_remote_copy(src, arriving, send.at[slot], recv.at[slot], device_id=dev, device_id_type=MESH)

    a_c = push(0, g_ref.at[:, :, 1 - c], from_c, me.at_c, from_c)
    home = pltpu.make_async_copy(g_ref.at[:, :, c], acc_c, local.at[0])
    home.start()
    rest = []
    for k in (1, 2, 3):
        to, fro = (z + k) % 4, (z + 4 - k) % 4
        rest.append(push(k, dx_ref.at[to], moved_ref.at[z], me.at_z(k), moved_ref.at[fro]))
    keep = pltpu.make_async_copy(dx_ref.at[z], moved_ref.at[z], local.at[1])
    keep.start()
    home.wait()
    a_c.wait_recv()
    f32 = lambda v: v.astype(jnp.float32)
    for a in range(2):
        for b in range(2):
            for q in range(4):
                acc_c[a, b, q] = (f32(acc_c[a, b, q]) + f32(from_c[a, b, q])).astype(acc_c.dtype)
    left, right = slice(0, half), slice(half, 2 * half)
    a_y = push(4, acc_c.at[1 - y, :, :, :, left], from_1.at[0], me.at_y, from_1.at[0])
    a_x = push(5, acc_c.at[:, 1 - x, :, :, right], from_1.at[1], me.at_x, from_1.at[1])
    a_y.wait_recv()
    for b in range(2):
        for q in range(4):
            acc_1[0, b, q] = (f32(acc_c[y, b, q, :, left]) + f32(from_1[0, b, q])).astype(acc_1.dtype)
    b_x = push(6, acc_1.at[0, 1 - x], from_2.at[0], me.at_x, from_2.at[0])
    a_x.wait_recv()
    for b in range(2):
        for q in range(4):
            acc_1[1, b, q] = (f32(acc_c[b, x, q, :, right]) + f32(from_1[1, b, q])).astype(acc_1.dtype)
    b_y = push(7, acc_1.at[1, 1 - y], from_2.at[1], me.at_y, from_2.at[1])
    b_x.wait_recv()
    for q in range(4):
        acc_2[q, :, left] = (f32(acc_1[0, x, q]) + f32(from_2[0, q])).astype(acc_2.dtype)
    b_y.wait_recv()
    for q in range(4):
        acc_2[q, :, right] = (f32(acc_1[1, y, q]) + f32(from_2[1, q])).astype(acc_2.dtype)
    last = []
    for k in (1, 2, 3):
        to, fro = (z + k) % 4, (z + 4 - k) % 4
        last.append(push(7 + k, acc_2.at[to], from_z.at[k - 1], me.at_z(k), from_z.at[k - 1]))
    total = f32(acc_2[z])
    for k in (1, 2, 3):
        last[k - 1].wait_recv()
        total += f32(from_z[k - 1])
    own_ref[...] = total
    keep.wait()
    for r in rest:
        r.wait_recv()
    for copy in started:
        copy.wait_send()

def reduce_and_move(g, dx, cid):
    rows, n = g.shape[0] // 32, g.shape[1]
    g = g.reshape(2, 2, 2, 4, rows, n)
    dx = dx.reshape(4, dx.shape[0] // 4, dx.shape[1])
    hbm = pl.BlockSpec(memory_space=pl.ANY)
    v = lambda *s: pltpu.VMEM(s, g.dtype)
    return pl.pallas_call(
        reduce_kernel,
        in_specs=[hbm, hbm],
        out_specs=[pl.BlockSpec(memory_space=pltpu.VMEM), hbm],
        out_shape=[jax.ShapeDtypeStruct((rows, n), jnp.float32), jax.ShapeDtypeStruct(dx.shape, dx.dtype)],
        scratch_shapes=[
            v(2, 2, 4, rows, n), v(2, 2, 4, rows, n), v(2, 2, 4, rows, n // 2), v(2, 2, 4, rows, n // 2),
            v(2, 4, rows, n // 2), v(4, rows, n), v(3, rows, n),
            pltpu.SemaphoreType.DMA((11,)), pltpu.SemaphoreType.DMA((11,)), pltpu.SemaphoreType.DMA((2,)),
        ],
        compiler_params=pltpu.CompilerParams(collective_id=cid, has_side_effects=True, vmem_limit_bytes=40 << 20),
    )(g, dx)

ROWS = 80

def middle_kernel(final_ref, block_ref, tokens_ref, tp_ref, outs_ref, ivec_ref, tvec_ref, pbias_ref, tbias_ref,
                  label_ref, temp_ref,
                  dy_ref, branch_ref, rows_ref, sums_ref, dcap_ref, loss_ref, dz_ref,
                  tn_ref, dn_ref, send_a, recv_a, send_l, recv_l, send_t, recv_t, send_sem, recv_sem):
    me = Place()
    z, i = me.z, me.i
    n_dp = recv_l.shape[0]
    plane = [((i + k) % n_dp, z) for k in range(1, n_dp)]
    greet([me.at_z(1), me.at_z(2), me.at_z(3)] + plane)
    width = final_ref.shape[1]
    part = width // 4
    started = []

    def exchange(n, values_for):
        for q in range(4):
            send_a[n, q] = values_for(q)
        recv_a[n, z] = send_a[n, z]
        arrive = []
        for k in (1, 2, 3):
            to, fro = (z + k) % 4, (z + 4 - k) % 4
            copy = pltpu.make_async_remote_copy(send_a.at[n, to], recv_a.at[n, z], send_sem.at[n, k - 1],
                                                recv_sem.at[n, k - 1], device_id=me.at_z(k), device_id_type=MESH)
            copy.start()
            started.append(copy)
            arrive.append(pltpu.make_async_remote_copy(send_a.at[n, to], recv_a.at[n, fro], send_sem.at[n, k - 1],
                                                       recv_sem.at[n, k - 1], device_id=me.at_z(k), device_id_type=MESH))

        def done():
            for a in arrive:
                a.wait_recv()
            return [recv_a[n, q] for q in range(4)]

        return done

    pad4 = jnp.zeros((4, width), F32)
    pad1 = jnp.zeros((1, width), F32)
    ivec, tvec = ivec_ref[...], tvec_ref[...]
    iv = lambda k: ivec[k:k + 1]
    tv = lambda k: tvec[k:k + 1]
    names = ["tq", "tk", "tv", "thead", "pq", "pk", "pv"]
    col = {n: 2 * width + 256 * k for k, n in enumerate(names)}
    small = lambda n: tp_ref[:, col[n]:col[n] + 256]
    p_up = lambda: tp_ref[:, 0:width]
    t_up = lambda: tp_ref[:, width:2 * width]
    base = 2 * width + 256 * 7
    t_down = lambda: tp_ref[:, base:base + width]
    p_down = lambda: tp_ref[:, base + width:base + 2 * width]
    t_out_w = lambda: outs_ref[0:part, 0:width]
    p_out_w = lambda: outs_ref[0:part, width:2 * width]
    lane = lax.broadcasted_iota(jnp.int32, (1, 256), 1)
    own = [((lane >= 64 * h) & (lane < 64 * h + 64)).astype(F32) for h in range(3)]

    def spread(a):
        return jnp.concatenate([a * own[h] for h in range(3)], 0)

    def fold(a):
        n = a.shape[0] // 3
        return sum(a[h * n:(h + 1) * n] * own[h] for h in range(3))

    t_x = tokens_ref[...].astype(F32)
    tn = layer_norm(t_x, tv(0), tv(1)).astype(BF)
    tn_ref[...] = tn.astype(F32)
    last_at = [3 * 64 + 16 * c + 15 for c in range(4)]
    t_last = jnp.concatenate([tn_ref[r:r + 1, :] for r in last_at], 0)
    x_last = jnp.concatenate([tokens_ref[3 * 64 + 16 * c:3 * 64 + 16 * c + 16, :].astype(F32)[15:16] for c in range(4)], 0)
    t_q = mm(t_last.astype(BF), small("tq")).astype(BF).astype(F32)
    t_keys = mm(spread(t_q).astype(BF), small("tk"), 1, 1) * 0.125
    scores = mm_two(t_keys, tn, 1)
    col_id = (lax.broadcasted_iota(jnp.int32, scores.shape, 1) // 16) % 4
    row_id = lax.broadcasted_iota(jnp.int32, scores.shape, 0) % 4
    mine = col_id == row_id
    top = jnp.max(jnp.where(mine, scores, -1e30), -1, keepdims=True)
    e = jnp.where(mine, jnp.exp(jnp.where(mine, scores - top, 0.0)), 0.0)
    t_probs = e / jnp.sum(e, -1, keepdims=True)
    t_used = mm_two(t_probs, tn)
    t_mixed = fold(mm(t_used.astype(BF), small("tv"))).astype(BF)
    t_part = mm(t_mixed[:, 0:part], t_out_w())

    p_q = mm(iv(7).astype(BF), small("pq"))
    p_keys_my = mm_two(spread(p_q), small("pk"), 1) * 0.125
    block = jnp.concatenate([t_part, p_keys_my, pad1], 0)
    x0 = exchange(0, lambda q: block)()
    t_hidden = x_last + (x0[0] + x0[1] + x0[2] + x0[3])[0:4]
    p_keys = jnp.concatenate([x0[q][4:7] for q in range(4)], 0)
    t_second = layer_norm(t_hidden, tv(2), tv(3)).astype(BF)
    t_value, t_slope = gelu_pair(mm(t_second, t_up()) + tbias_ref[...])
    t_active = t_value.astype(BF)
    t_part = mm(t_active, t_down())
    final = final_ref[...]
    p_scores = mm_two(p_keys, final, 1)
    e = jnp.exp(p_scores - jnp.max(p_scores, -1, keepdims=True))
    p_probs = e / jnp.sum(e, -1, keepdims=True)
    used = mm_two(p_probs, final)
    x1 = exchange(1, lambda q: jnp.concatenate([t_part, used[3 * q:3 * q + 3], pad1], 0))()
    t_out = t_hidden + (x1[0] + x1[1] + x1[2] + x1[3])[0:4] + tv(4)
    t_final = layer_norm(t_out, tv(5), tv(6)).astype(BF)
    t_piece = mm(t_final, small("thead"))
    got = jnp.concatenate([x1[q][4 + h:5 + h] for h in range(3) for q in range(4)], 0)
    pooled = fold(mm_two(got, small("pv")))
    h_part = mm_two(pooled[:, 0:part], p_out_w())
    block = jnp.concatenate([h_part, jnp.concatenate([t_piece[:, 0:part], jnp.zeros((4, width - part), F32)], 1)], 0)
    x2 = exchange(2, lambda q: block)()
    h_start = (x2[0] + x2[1] + x2[2] + x2[3])[0:4]
    text_embed = jnp.concatenate([x2[q][4:8, 0:part] for q in range(4)], 1)
    h_normed = layer_norm(h_start, iv(8), iv(9)).astype(BF)
    h_value, h_slope = gelu_pair(mm(h_normed, p_up()) + pbias_ref[...])
    h_active = h_value.astype(BF)
    h_part = mm(h_active, p_down())
    block = jnp.concatenate([h_part, pad4], 0)
    x3 = exchange(3, lambda q: block)()
    image_embed = h_start + ((x3[0] + x3[1] + x3[2] + x3[3])[0:4] + iv(10))
    send_l[...] = jnp.concatenate([image_embed, text_embed], 0)
    recv_l[i] = send_l[...]
    arrive = []
    for k in range(1, n_dp):
        copy = pltpu.make_async_remote_copy(send_l, recv_l.at[i], send_sem.at[8, k], recv_sem.at[8, k],
                                            device_id=plane[k - 1], device_id_type=MESH)
        copy.start()
        started.append(copy)
        arrive.append(pltpu.make_async_remote_copy(send_l, recv_l.at[(i + n_dp - k) % n_dp], send_sem.at[8, k], recv_sem.at[8, k],
                                                   device_id=plane[k - 1], device_id_type=MESH))
    for a in arrive:
        a.wait_recv()
    every = jnp.concatenate([recv_l[k] for k in range(n_dp)], 0)
    scale = lax.rsqrt(jnp.sum(every * every, -1, keepdims=True) + EPS)
    unit = every * scale
    cosine = mm_exact(unit, unit, 1, 1)
    temper = jnp.exp(jnp.full((1, 1), temp_ref[0], F32))
    logits = cosine * temper + temp_ref[1]
    label = label_ref[...]
    valid = label != 0.0
    signed = label * logits
    total = n_dp * 4
    nll = jnp.maximum(-signed, 0.0) + jnp.log(1.0 + jnp.exp(-jnp.abs(signed)))
    add_all = lambda a: jnp.sum(jnp.sum(a, -1, keepdims=True), 0, keepdims=True)
    loss = add_all(jnp.where(valid, nll, 0.0)) / total
    g = jnp.where(valid, -label / (1.0 + jnp.exp(signed)), 0.0) / total
    gt0 = temper * add_all(g * cosine)
    gt1 = add_all(g)
    at = lax.broadcasted_iota(jnp.int32, (8, 128), 1)
    loss_ref[...] = jnp.where(at == 0, loss, jnp.where(at == 1, gt0, gt1))
    dz = temper * mm_exact(g + jnp.transpose(g), unit)
    dz_ref[...] = (dz - unit * jnp.sum(unit * dz, -1, keepdims=True)) * scale
    d_both = dz_ref[pl.ds(pl.multiple_of(8 * i, 8), 8), :]
    d_image, d_text = d_both[0:4], d_both[4:8]

    dh_upper = mm_two(d_image, p_down(), 1) * h_slope
    h_part = mm_two(dh_upper, p_up(), 1)
    d_text_my = sum(jnp.where(z == q, d_text[:, part * q:part * q + part], 0.0) for q in range(4))
    t_part = mm_two(d_text_my, small("thead")[:, 0:part], 1)
    block = jnp.concatenate([h_part, t_part], 0)
    x4 = exchange(4, lambda q: block)()
    both = x4[0] + x4[1] + x4[2] + x4[3]
    d_start, dv8, dv9 = norm_back_rows(h_start, iv(8), both[0:4])
    d_start = d_image + d_start
    dv10 = jnp.sum(d_image, 0, keepdims=True)
    d_pooled = mm_two(d_start, p_out_w(), 1)
    d_pooled = jnp.concatenate([d_pooled, jnp.zeros((4, 256 - part), F32)], 1)
    p_values_my = mm_two(spread(d_pooled), small("pv"), 1)
    dt_out, tv5, tv6 = norm_back_rows(t_out, tv(5), both[4:8])
    tv4 = jnp.sum(dt_out, 0, keepdims=True)
    dt_branch = dt_out.astype(BF)
    dt_upper = (mm(dt_branch, t_down(), 1, 1) * t_slope).astype(BF)
    t_part = mm(dt_upper, t_up(), 1, 1)
    x5 = exchange(5, lambda q: jnp.concatenate(
        [t_part] + [p_values_my[4 * h + q:4 * h + q + 1] for h in range(3)] + [pad1], 0))()
    dt_hidden, tv2, tv3 = norm_back_rows(t_hidden, tv(2), (x5[0] + x5[1] + x5[2] + x5[3])[0:4])
    dt_hidden = dt_out + dt_hidden
    dt_attend = dt_hidden.astype(BF)
    dt_mixed = mm(dt_attend, t_out_w(), 1, 1).astype(BF).astype(F32)
    dt_mixed = jnp.concatenate([dt_mixed, jnp.zeros((4, 256 - part), F32)], 1)
    t_values = mm(spread(dt_mixed).astype(BF), small("tv"), 1, 1)
    dt_probs = mm_two(t_values, tn, 1)
    dt_scores = t_probs * (dt_probs - jnp.sum(t_probs * dt_probs, -1, keepdims=True))
    tk_used = mm_two(dt_scores, tn) * 0.125
    dt_q = fold(mm(tk_used.astype(BF), small("tk"))).astype(BF)
    dn = mm(dt_scores.astype(BF), t_keys.astype(BF), 0, 0) + mm(t_probs.astype(BF), t_values.astype(BF), 0, 0)
    row_at = lax.broadcasted_iota(jnp.int32, dn.shape, 0)
    dq_back = mm(dt_q, small("tq"), 1, 1)
    for c in range(4):
        dn = dn + jnp.where(row_at == last_at[c], dq_back[c:c + 1], 0.0)
    dn_ref[...] = dn.astype(BF)
    p_values = jnp.concatenate([x5[q][4:7] for q in range(4)], 0)
    d_probs = mm_two(p_values, final, 1)
    d_scores = p_probs * (d_probs - jnp.sum(p_probs * d_probs, -1, keepdims=True))
    p_used = mm_two(d_scores, final) * 0.125
    x6 = exchange(6, lambda q: jnp.concatenate([p_used[3 * q:3 * q + 3], pad1, pad4], 0))
    arrive = []
    for k in (1, 2, 3):
        to, fro = (z + k) % 4, (z + 4 - k) % 4
        rows_to = dn_ref.at[pl.ds(pl.multiple_of(64 * to, 64), 64), :]
        copy = pltpu.make_async_remote_copy(rows_to, recv_t.at[z], send_sem.at[7, k], recv_sem.at[7, k],
                                            device_id=me.at_z(k), device_id_type=MESH)
        copy.start()
        started.append(copy)
        arrive.append(pltpu.make_async_remote_copy(rows_to, recv_t.at[fro], send_sem.at[7, k], recv_sem.at[7, k],
                                                   device_id=me.at_z(k), device_id_type=MESH))
    s_high, s_low = split_two(d_scores)
    q_high, q_low = split_two(p_probs)
    k_high, k_low = split_two(p_keys)
    v_high, v_low = split_two(p_values)
    left = jnp.concatenate([s_high.astype(F32), q_high.astype(F32)], 0)
    right = jnp.concatenate([k_high.astype(F32), v_high.astype(F32)], 0).astype(BF)
    send_t[...] = jnp.transpose(jnp.concatenate([left, jnp.zeros((104, left.shape[1]), F32)], 0))
    right = jnp.concatenate([right, jnp.zeros((104, width), BF)], 0)
    sums_ref[...] = jnp.zeros_like(sums_ref)
    tile = 128

    def step(n, carry):
        at_rows = pl.ds(pl.multiple_of(n * tile, tile), tile)
        d_final = mm(send_t[at_rows, :].astype(BF), right)
        d_y, gain, shift = norm_back_rows(block_ref[at_rows, :], iv(5), d_final)
        dy_ref[at_rows, :] = d_y
        branch_ref[at_rows, :] = d_y.astype(BF)
        sums_ref[5:6] += gain
        sums_ref[6:7] += shift
        sums_ref[4:5] += jnp.sum(d_y, 0, keepdims=True)
        return carry

    lax.fori_loop(0, final_ref.shape[0] // tile, step, 0)
    got6 = x6()
    w_got = jnp.concatenate([got6[q][h:h + 1] for h in range(3) for q in range(4)], 0)
    dq_rows = fold(mm_two(w_got, small("pk")))
    dq_my = jnp.sum(dq_rows, 0, keepdims=True)
    recv_t[z] = dn_ref[pl.ds(pl.multiple_of(64 * z, 64), 64), :]
    for a in arrive:
        a.wait_recv()
    dt_normed = sum(recv_t[q].astype(F32) for q in range(4))
    x_mine = tokens_ref[pl.ds(pl.multiple_of(64 * z, 64), 64), :].astype(F32)
    d_cap, tv0, tv1 = norm_back_rows(x_mine, tv(0), dt_normed)
    row_c = lax.broadcasted_iota(jnp.int32, d_cap.shape, 0)
    for c in range(4):
        d_cap = d_cap + jnp.where((row_c == 16 * c + 15) & (z == 3), dt_hidden[c:c + 1], 0.0)
    dcap_ref[...] = d_cap
    first = (z == 0).astype(F32)
    sums_ref[8:9] = dv8 * first
    sums_ref[9:10] = dv9 * first
    sums_ref[10:11] = dv10 * first
    sums_ref[11:12] = tv0
    sums_ref[12:13] = tv1
    sums_ref[13:14] = tv2 * first
    sums_ref[14:15] = tv3 * first
    sums_ref[15:16] = tv4 * first
    sums_ref[16:17] = tv5 * first
    sums_ref[17:18] = tv6 * first
    own_row = lambda a: sum(jnp.where(z == q, a[q:q + 1].astype(F32), 0.0) for q in range(4))
    pick = lambda a: a[:, 0:part].astype(F32)
    wide = jnp.concatenate
    pieces = [
        dh_upper, dt_upper.astype(F32), h_active.astype(F32), t_active.astype(F32),
        wide([pick(d_pooled), pick(pooled), pick(dt_q), pick(t_q)], 1),
        wide([pick(dt_mixed), pick(t_mixed), jnp.broadcast_to(pick(dq_my), (4, part)), jnp.broadcast_to(pick(p_q), (4, part))], 1),
        own_row(h_normed), own_row(d_start), own_row(t_last), own_row(t_second),
        own_row(dt_attend), own_row(dt_branch), own_row(t_final), pad1,
        used, t_used, tk_used, p_used,
    ]
    rows_ref[...] = jnp.concatenate(pieces, 0)
    for copy in started:
        copy.wait_send()

def middle(final, block_out, tokens, tp, outs, ivec, tvec, pbias, tbias, label, temp, cid, n_dp):
    length, width = final.shape
    v = pl.BlockSpec(memory_space=pltpu.VMEM)
    f = lambda *s: jax.ShapeDtypeStruct(s, F32)
    return pl.pallas_call(
        middle_kernel,
        in_specs=[v] * 10 + [pl.BlockSpec(memory_space=pltpu.SMEM)],
        out_specs=[v] * 7,
        out_shape=[f(length, width), jax.ShapeDtypeStruct((length, width), BF), f(ROWS, width), f(24, width), f(64, width), f(8, 128), f(8 * n_dp, width)],
        scratch_shapes=[
            pltpu.VMEM((256, width), F32), pltpu.VMEM((256, width), BF),
            pltpu.VMEM((7, 4, 8, width), F32), pltpu.VMEM((7, 4, 8, width), F32),
            pltpu.VMEM((8, width), F32), pltpu.VMEM((n_dp, 8, width), F32),
            pltpu.VMEM((length, 128), F32), pltpu.VMEM((4, 64, width), BF),
            pltpu.SemaphoreType.DMA((9, 8)), pltpu.SemaphoreType.DMA((9, 8)),
        ],
        compiler_params=pltpu.CompilerParams(collective_id=cid, has_side_effects=True, vmem_limit_bytes=50 << 20),
    )(final, block_out, tokens, tp, outs, ivec, tvec, pbias, tbias, label, temp)


def fast_program(
    patches, captions, pairs,
    image_attend_in, image_attend_out, image_up_weight, image_up_bias, image_down_weight,
    image_vectors, probe_query_weight, probe_pair_weight, probe_out_weight, probe_up_weight,
    probe_up_bias, probe_down_weight, text_attend_in, text_attend_out, text_up_weight,
    text_up_bias, text_down_weight, text_vectors, text_head_weight, temp_bias,
):
    n_dp, n_z = lax.axis_size("dp"), lax.axis_size("seq")
    world = n_dp * n_z
    at_dp, at_z = lax.axis_index("dp"), lax.axis_index("seq")
    me = at_dp * n_z + at_z
    width = patches.shape[-1]
    head_width = width // HEADS
    hidden_width = image_up_weight.shape[1]
    part, quarter = width // world, width // n_z
    wide_part = hidden_width // world
    fold = hidden_width // width
    length = patches.shape[1] * n_z

    small = jnp.concatenate(
        [image_vectors.reshape(-1), text_vectors.reshape(-1), image_up_bias, probe_up_bias, text_up_bias]
    )
    sizes = [image_vectors.size, text_vectors.size, image_up_bias.size, probe_up_bias.size, text_up_bias.size]
    small = jnp.pad(small, (0, 2048 - small.shape[0])).reshape(16, 128)

    def by_units(w):
        return w.reshape(part, n_dp, n_z, wide_part).transpose(2, 0, 1, 3).reshape(n_z, part, width)

    def by_heads(w):
        cut = w.reshape(part, n_z, quarter).transpose(1, 0, 2)
        return jnp.pad(cut, ((0, 0), (0, 0), (0, 256 - quarter)))

    split = [by_units(probe_up_weight), by_units(text_up_weight)]
    split += [by_heads(text_attend_in[:, k * width : (k + 1) * width]) for k in range(3)]
    split += [by_heads(text_head_weight), by_heads(probe_query_weight)]
    split += [by_heads(probe_pair_weight[:, k * width : (k + 1) * width]) for k in range(2)]
    split = jnp.concatenate(split, 2)
    w_in, x, split, tokens, small_all = gather(
        [image_attend_in, patches, split, captions, small],
        [("full", "S"), ("za", None), ("za", None), ("zg", None), ("full", "C")],
        1,
    )
    w_in = w_in.reshape(width, 3 * width)
    x = x.reshape(length, width).astype(F32)
    main = jnp.concatenate(
        [
            image_attend_out,
            image_up_weight.reshape(part, width, fold).transpose(0, 2, 1).reshape(part, hidden_width),
            image_down_weight.reshape(part, hidden_width),
            text_attend_out,
            probe_out_weight,
        ],
        1,
    )
    main = lax.all_gather(main, ALL, axis=0, tiled=True)
    tp = jnp.concatenate(
        [split.reshape(n_z * part, -1), text_down_weight, probe_down_weight], 1
    )
    tp = lax.all_gather(tp, "dp", axis=0, tiled=True)
    w_out = main[:, :width]
    w_up = main[:, width : width + hidden_width]
    w_down = main[:, width + hidden_width : width + 2 * hidden_width]
    w_down = w_down.reshape(width, fold, width).transpose(1, 0, 2).reshape(hidden_width, width)
    outs = lax.dynamic_slice_in_dim(main[:, width + 2 * hidden_width :], at_z * quarter, quarter, 0)

    small_all = small_all.reshape(world, -1)
    cuts = [sum(sizes[:i]) for i in range(len(sizes) + 1)]
    pieces = [small_all[:, cuts[i] : cuts[i + 1]].astype(F32) for i in range(len(sizes))]
    ivec = pieces[0].reshape(world, -1, part).transpose(1, 0, 2).reshape(-1, width)
    tvec = pieces[1].reshape(world, -1, part).transpose(1, 0, 2).reshape(-1, width)
    i_bias = pieces[2].reshape(width, fold).T.reshape(1, hidden_width)

    def own_units(p):
        p = p.reshape(n_dp, n_z, wide_part)
        return lax.dynamic_index_in_dim(p, at_z, 1, False).reshape(1, width)

    p_bias, t_bias = own_units(pieces[3]), own_units(pieces[4])

    normed = layer_norm(x, ivec[0], ivec[1]).astype(BF)
    proj = mm(normed, w_in).astype(BF)
    mixed, lse = attend_fwd(proj, length)
    hidden = x + mm(mixed, w_out)
    second = layer_norm(hidden, ivec[2], ivec[3]).astype(BF)
    value, slope = gelu_pair(mm(second, w_up) + i_bias)
    active, slope = value.astype(BF), slope.astype(BF)
    block_out = hidden + mm(active, w_down) + ivec[4]
    final = layer_norm(block_out, ivec[5], ivec[6]).astype(BF)

    labels = (2 * pairs - 1).astype(F32).reshape(n_dp, n_z, n_dp, n_z)
    labels = jnp.pad(labels, ((0, 0), (0, n_z), (0, 0), (n_z, 0))).reshape(2 * world, 2 * world)
    dy, d_branch, rows, sums, d_captions, loss_row, d_embeds = middle(
        final, block_out, tokens.reshape(-1, width), tp, outs, ivec, tvec, p_bias, t_bias, labels, temp_bias, 2, n_dp
    )
    loss, grad_temp = loss_row[0, 0], loss_row[0, 1:3]
    grad_captions = d_captions.reshape(captions.shape)
    rows = lax.all_gather(rows.astype(BF), ALL, axis=0, tiled=False)

    g_down = mm(active, d_branch, 0, 0)
    d_upper_f = mm(d_branch, w_down, 1, 1) * slope.astype(F32)
    d_upper = d_upper_f.astype(BF)
    g_bias = jnp.sum(d_upper_f, 0)
    g_up = mm(second, d_upper, 0, 0)
    d_hidden, dv2, dv3 = norm_back(hidden, ivec[2], mm(d_upper, w_up, 1, 1))
    d_hidden = dy + d_hidden
    d_attend = d_hidden.astype(BF)
    g_out = mm(mixed, d_attend, 0, 0)
    d_mixed = mm(d_attend, w_out, 1, 1).astype(BF)
    g_main = jnp.concatenate(
        [
            g_out.astype(BF),
            g_up.astype(BF),
            g_down.astype(BF).reshape(fold, width, width).transpose(1, 0, 2).reshape(width, hidden_width),
        ],
        1,
    )
    g_main = lax.psum_scatter(g_main, ALL, scatter_dimension=0, tiled=True).astype(F32)
    own_out = g_main[:, :width]
    own_up = g_main[:, width : width + hidden_width].reshape(part, fold, width)
    own_up = own_up.transpose(0, 2, 1).reshape(part, hidden_width)
    own_down = g_main[:, width + hidden_width :].reshape(wide_part, width)
    inner_rows = jnp.sum(
        (d_mixed.astype(F32) * mixed.astype(F32)).reshape(length, HEADS, head_width), -1
    ).T.reshape(HEADS // 2, 2, length)
    d_q, d_k, d_v = attend_bwd(proj, d_mixed, lse, inner_rows, length)
    d_normed = (
        mm(d_q, w_in[:, :width], 1, 1)
        + mm(d_k, w_in[:, width : 2 * width], 1, 1)
        + mm(d_v, w_in[:, 2 * width :], 1, 1)
    )
    d_x, dv0, dv1 = norm_back(x, ivec[0], d_normed)
    d_x = (d_hidden + d_x).astype(BF)
    sums = jnp.concatenate([jnp.stack([dv0, dv1, dv2, dv3]), sums[4:], g_bias.reshape(fold, width)], 0)
    sums = jnp.pad(sums, ((0, 128 - sums.shape[0]), (0, 0))).T
    g_in = jnp.concatenate(
        [mm(normed, d, 0, 0).astype(BF) for d in (d_q, d_k, d_v)]
        + [sums.astype(BF), jnp.zeros((width, 128), BF)],
        1,
    )
    own_in, moved = reduce_and_move(g_in, d_x, 3)
    grad_patches = moved.astype(F32)
    own_sums = own_in[:, 3 * width : 3 * width + 128].T
    own_in = own_in[:, : 3 * width]

    rows = rows.reshape(n_dp, n_z, ROWS, width)
    column = lax.dynamic_slice_in_dim(rows, me * part, part, 3)
    one = lambda r: column[:, :, r]
    units = lax.dynamic_slice(rows, (0, at_z, 8, at_dp * wide_part), (n_dp, 1, 8, wide_part))[:, 0]
    each = quarter // part
    pooled = lax.dynamic_slice(rows, (0, me // each, 16, quarter + part * (me % each)), (n_dp, 1, 4, part))[:, 0]
    t_mixed = lax.dynamic_slice(rows, (0, me // each, 20, quarter + part * (me % each)), (n_dp, 1, 4, part))[:, 0]

    def ein(spec, a, b):
        return jnp.einsum(spec, a, b, preferred_element_type=F32)

    def wide(g):
        return g.reshape(part, n_z, n_dp, wide_part).transpose(0, 2, 1, 3).reshape(part, hidden_width)

    d_embeds = d_embeds.reshape(n_dp, 2, n_z, width).astype(BF)
    cut = lambda r, k: rows[:, :, r : r + 4, k * quarter : (k + 1) * quarter]
    heads = lambda v: v.reshape(v.shape[:-1] + (HEADS // n_z, head_width))
    per_head = lambda r: column[:, :, r : r + HEADS].reshape(n_dp, n_z, HEADS // n_z, n_z, part)
    own_p_up = wide(ein("icm,izcl->mzl", one(24), rows[:, :, 0:4]))
    own_t_up = wide(ein("icm,izcl->mzl", one(27), rows[:, :, 4:8]))
    own_p_down = ein("icm,icl->ml", units[:, 0:4], d_embeds[:, 0])
    own_t_down = ein("icm,icl->ml", units[:, 4:8], rows[:, :, 29])
    own_p_out = ein("icm,icl->ml", pooled, rows[:, :, 25])
    own_t_out = ein("icm,icl->ml", t_mixed, rows[:, :, 28])
    own_t_head = ein("icm,icl->ml", one(30), d_embeds[:, 1])
    own_t_q = ein("icm,izcl->mzl", one(26), cut(16, 2)).reshape(part, width)
    own_t_k = ein("izhcm,izche->mzhe", per_head(56), heads(cut(16, 3))).reshape(part, width)
    own_t_v = ein("izhcm,izche->mzhe", per_head(44), heads(cut(20, 0))).reshape(part, width)
    own_t_in = jnp.concatenate([own_t_q, own_t_k, own_t_v], 1)
    d_pooled = cut(16, 0).transpose(0, 2, 1, 3).reshape(n_dp, n_z, HEADS, head_width)
    own_p_v = ein("ichm,iche->mhe", column[:, :, 32:44], d_pooled).reshape(part, width)
    p_used = jnp.sum(column[:, :, 68:80].astype(F32), (0, 1))
    probe_query = cut(20, 3)[0, :, 0].reshape(HEADS, head_width).astype(F32)
    own_p_k = (p_used.T[:, :, None] * probe_query[None]).reshape(part, width)
    own_p_pair = jnp.concatenate([own_p_k, own_p_v], 1)
    d_query = jnp.sum(cut(20, 2)[:, :, 0].astype(F32), 0).reshape(width)
    mine = lambda v, n: lax.dynamic_slice_in_dim(v, me * n, n, -1)
    own_p_query = mine(ivec[7], part)[:, None] * d_query[None, :]
    dv7 = jnp.sum(probe_query_weight.astype(F32) * d_query[None, :], 1)
    bias_of = lambda r: jnp.sum(
        lax.dynamic_slice(rows, (0, at_z, r, at_dp * wide_part), (n_dp, 1, 4, wide_part)).astype(F32), (0, 1, 2)
    )
    own_ivec = jnp.concatenate([own_sums[0:7], dv7[None], own_sums[8:11]], 0)
    own_tvec = own_sums[11:18]
    own_bias = own_sums[24 : 24 + fold].T.reshape(wide_part)
    return (
        loss, grad_patches, grad_captions,
        own_in, own_out, own_up, own_bias, own_down, own_ivec,
        own_p_query, own_p_pair, own_p_out, own_p_up, bias_of(0), own_p_down,
        own_t_in, own_t_out, own_t_up, bias_of(4), own_t_down, own_tvec, own_t_head,
        grad_temp,
    )


def solution(mesh):
    tokens, matrix, vector, table = P("dp", "seq", None), P(ALL, None), P(ALL), P(None, ALL)
    weights = (
        (matrix, matrix, matrix, vector, matrix, table, matrix, matrix, matrix, matrix, vector, matrix)
        + (matrix, matrix, matrix, vector, matrix, table, matrix)
    )
    return jax.shard_map(
        fast_program if mesh.shape["dp"] == 8 and mesh.shape["seq"] == 4 else device_program,
        mesh=mesh,
        in_specs=(tokens, tokens, P()) + weights + (P(),),
        out_specs=(P(), tokens, tokens) + weights + (P(),),
        check_vma=False,
    )
```

```python
from functools import partial

import jax
import jax.numpy as jnp
from jax import lax
from jax.experimental import pallas as pl
from jax.experimental.pallas import tpu as pltpu
from jax.sharding import PartitionSpec as P

HEADS = 12
ALL = ("dp", "seq")
F32, BF = jnp.float32, jnp.bfloat16
HIGH = lax.Precision.HIGHEST
EPS = 1e-06


def mm(a, b, ca=1, cb=0):
    return lax.dot_general(a, b, (((ca,), (cb,)), ((), ())), preferred_element_type=F32)


def mm_exact(a, b, ca=1, cb=0):
    return lax.dot_general(a, b, (((ca,), (cb,)), ((), ())), precision=HIGH, preferred_element_type=F32)


def split_two(a):
    high = a.astype(BF)
    return high, (a - high.astype(F32)).astype(BF)


def layer_norm(x, gain, shift):
    center = x - jnp.mean(x, -1, keepdims=True)
    spread = jnp.mean(center * center, -1, keepdims=True)
    return center * lax.rsqrt(spread + EPS) * gain + shift


def norm_back(x, gain, upstream):
    center = x - jnp.mean(x, -1, keepdims=True)
    inverse = lax.rsqrt(jnp.mean(center * center, -1, keepdims=True) + EPS)
    unit = center * inverse
    scaled = upstream * gain
    d_x = inverse * (
        scaled
        - jnp.mean(scaled, -1, keepdims=True)
        - unit * jnp.mean(scaled * unit, -1, keepdims=True)
    )
    return d_x, jnp.sum(upstream * unit, 0), jnp.sum(upstream, 0)


def norm_back_rows(x, gain, upstream):
    d_x, d_gain, d_shift = norm_back(x, gain, upstream)
    return d_x, d_gain[None], d_shift[None]


def mm_two(a, b, cb=0):
    high, low = split_two(a)
    return mm(high, b, 1, cb) + mm(low, b, 1, cb)


def gelu_pair(u):
    c = 0.7978845608028654
    t = jnp.tanh(c * (u + 0.044715 * u * u * u))
    value = 0.5 * u * (1.0 + t)
    slope = 0.5 * (1.0 + t) + 0.5 * u * (1.0 - t * t) * c * (1.0 + 3 * 0.044715 * u * u)
    return value, slope


def attend_fwd_kernel(q_ref, k_ref, v_ref, o_ref, lse_ref):
    q = q_ref[...] * 0.125
    k = k_ref[...]
    lane = lax.broadcasted_iota(jnp.int32, k.shape, 1)
    v_turned = jnp.transpose(v_ref[...])
    outs = []
    for h in range(2):
        keep = (lane < 64) if h == 0 else (lane >= 64)
        own_k = jnp.where(keep, k, jnp.zeros_like(k))
        s = mm(own_k, q, 1, 1)
        top = jnp.max(s, 0, keepdims=True)
        p = jnp.exp(s - top)
        total = jnp.sum(p, 0, keepdims=True)
        outs.append(mm(v_turned[64 * h : 64 * h + 64], p.astype(BF)) / total)
        lse_ref[0, h : h + 1, :] = top + jnp.log(total)
    o_ref[...] = jnp.transpose(jnp.concatenate(outs, 0)).astype(BF)


def attend_fwd(proj, length):
    rows, width = proj.shape[0], proj.shape[1] // 3
    pairs = width // 128
    block = lambda part: pl.BlockSpec((length, 128), lambda b, h: (b, part * pairs + h))
    return pl.pallas_call(
        attend_fwd_kernel,
        grid=(rows // length, pairs),
        in_specs=[block(0), block(1), block(2)],
        out_specs=[block(0), pl.BlockSpec((1, 2, length), lambda b, h: (h, 0, b))],
        out_shape=[
            jax.ShapeDtypeStruct((rows, width), BF),
            jax.ShapeDtypeStruct((pairs, 2, rows), F32),
        ],
        compiler_params=pltpu.CompilerParams(vmem_limit_bytes=48 << 20),
        cost_estimate=pl.CostEstimate(
            flops=rows * length * width * 8,
            bytes_accessed=rows * width * 8,
            transcendentals=rows * length * HEADS,
        ),
    )(proj, proj, proj)


def attend_bwd_kernel(q_ref, k_ref, v_ref, do_ref, lse_ref, d_ref, dq_ref, dk_ref, dv_ref):
    q = q_ref[...] * 0.125
    k, v, do = k_ref[...], v_ref[...], do_ref[...]
    lane = lax.broadcasted_iota(jnp.int32, k.shape, 1)
    dqs, dks, dvs = [], [], []
    for h in range(2):
        keep = (lane < 64) if h == 0 else (lane >= 64)
        s = mm(jnp.where(keep, k, jnp.zeros_like(k)), q, 1, 1)
        p = jnp.exp(s - lse_ref[0, h : h + 1, :])
        dp = mm(jnp.where(keep, v, jnp.zeros_like(v)), do, 1, 1)
        ds = (p * (dp - d_ref[0, h : h + 1, :])).astype(BF)
        dvs.append(mm(p.astype(BF), do))
        dks.append(mm(ds, q))
        dqs.append(mm(ds, k, 0, 0))
    low = lane < 64
    dq_ref[...] = (jnp.where(low, dqs[0], dqs[1]) * 0.125).astype(BF)
    dk_ref[...] = jnp.where(low, dks[0], dks[1]).astype(BF)
    dv_ref[...] = jnp.where(low, dvs[0], dvs[1]).astype(BF)


def attend_bwd(proj, d_out, lse, inner, length):
    rows, width = proj.shape[0], proj.shape[1] // 3
    pairs = width // 128
    block = lambda part: pl.BlockSpec((length, 128), lambda b, h: (b, part * pairs + h))
    row = pl.BlockSpec((1, 2, length), lambda b, h: (h, 0, b))
    result = jax.ShapeDtypeStruct((rows, width), BF)
    return pl.pallas_call(
        attend_bwd_kernel,
        grid=(rows // length, pairs),
        in_specs=[block(0), block(1), block(2), block(0), row, row],
        out_specs=[block(0)] * 3,
        out_shape=[result] * 3,
        compiler_params=pltpu.CompilerParams(vmem_limit_bytes=56 << 20),
        cost_estimate=pl.CostEstimate(
            flops=rows * length * width * 20,
            bytes_accessed=rows * width * 16,
            transcendentals=rows * length * HEADS,
        ),
    )(proj, proj, proj, d_out, lse, inner)


def head_blocks(width):
    own = jnp.arange(width)[None, :] // (width // HEADS) == jnp.arange(HEADS)[:, None]
    return own.astype(F32)


def spread_heads(rows):
    n, width = rows.shape
    return (rows[:, None, :] * head_blocks(width)[None]).reshape(n * HEADS, width)


def fold_heads(rows):
    total, width = rows.shape
    return jnp.sum(rows.reshape(total // HEADS, HEADS, width) * head_blocks(width)[None], 1)


def device_program(
    patches, captions, pairs,
    image_attend_in, image_attend_out, image_up_weight, image_up_bias, image_down_weight,
    image_vectors, probe_query_weight, probe_pair_weight, probe_out_weight, probe_up_weight,
    probe_up_bias, probe_down_weight, text_attend_in, text_attend_out, text_up_weight,
    text_up_bias, text_down_weight, text_vectors, text_head_weight, temp_bias,
):
    seq = lax.axis_size("seq")
    world = seq * lax.axis_size("dp")
    me = lax.axis_index("dp") * seq + lax.axis_index("seq")
    width = patches.shape[-1]
    head_width = width // HEADS
    factor = head_width ** (-0.5)
    hidden_width = image_up_weight.shape[1]
    part = width // world
    wide_part = hidden_width // world

    def gather(*weights):
        flat = jnp.concatenate([w.reshape(-1, width) for w in weights], 0)
        full = lax.all_gather(flat, ALL, axis=0)
        out, at = [], 0
        for w in weights:
            count = w.size // width
            piece = full[:, at : at + count]
            out.append(piece.reshape(world * w.shape[0], w.shape[1]))
            at += count
        return out

    small = jnp.concatenate(
        [image_vectors.reshape(-1), text_vectors.reshape(-1), image_up_bias, probe_up_bias, text_up_bias]
    )
    small_all = lax.all_gather(small, ALL, axis=0)
    sizes = [image_vectors.size, text_vectors.size, image_up_bias.size, probe_up_bias.size, text_up_bias.size]
    cuts = [sum(sizes[:i]) for i in range(len(sizes) + 1)]
    pieces = [small_all[:, cuts[i] : cuts[i + 1]].astype(F32) for i in range(len(sizes))]
    ivec = pieces[0].reshape(world, -1, part).transpose(1, 0, 2).reshape(-1, width)
    tvec = pieces[1].reshape(world, -1, part).transpose(1, 0, 2).reshape(-1, width)
    i_bias, p_bias, t_bias = (p.reshape(-1) for p in pieces[2:])

    (w_in,) = gather(image_attend_in)
    w_out, w_up, w_down = gather(image_attend_out, image_up_weight, image_down_weight)
    tw_in, tw_out, tw_up, tw_down, tw_head, pw_query, pw_pair, pw_out, pw_up, pw_down = gather(
        text_attend_in, text_attend_out, text_up_weight, text_down_weight, text_head_weight,
        probe_query_weight, probe_pair_weight, probe_out_weight, probe_up_weight, probe_down_weight,
    )

    def to_owner(x):
        return lax.all_to_all(x, "seq", 0, 1, tiled=True)

    x = to_owner(patches)
    own, length = x.shape[0], x.shape[1]
    x = x.reshape(own * length, width).astype(F32)
    captions_own = to_owner(captions)
    text_length = captions_own.shape[1]

    normed = layer_norm(x, ivec[0], ivec[1]).astype(BF)
    proj = mm(normed, w_in).astype(BF)
    mixed, lse = attend_fwd(proj, length)
    hidden = x + mm(mixed, w_out)
    second = layer_norm(hidden, ivec[2], ivec[3]).astype(BF)
    value, slope = gelu_pair(mm(second, w_up) + i_bias)
    active, slope = value.astype(BF), slope.astype(BF)
    block_out = hidden + mm(active, w_down) + ivec[4]
    final = layer_norm(block_out, ivec[5], ivec[6]).astype(BF)

    t_x = captions_own.astype(F32)
    t_normed = layer_norm(t_x, tvec[0], tvec[1]).astype(BF)
    t_last = t_normed[:, -1]
    tw_q, tw_k, tw_v = tw_in[:, :width], tw_in[:, width : 2 * width], tw_in[:, 2 * width :]
    t_q = mm(t_last, tw_q).astype(BF)
    t_keys = mm(spread_heads(t_q.astype(F32)).astype(BF), tw_k, 1, 1) * factor
    t_keys = t_keys.reshape(own, HEADS, width)
    k_high, k_low = split_two(t_keys)
    scores = jnp.einsum("bsd,bhd->bsh", t_normed, k_high, preferred_element_type=F32)
    scores += jnp.einsum("bsd,bhd->bsh", t_normed, k_low, preferred_element_type=F32)
    t_probs = jax.nn.softmax(scores, axis=1)
    t_used = jnp.einsum("bsh,bsd->bhd", t_probs, t_normed.astype(F32), precision=HIGH)
    t_mixed = fold_heads(mm(t_used.reshape(own * HEADS, width).astype(BF), tw_v)).astype(BF)
    t_hidden = t_x[:, -1] + mm(t_mixed, tw_out)
    t_second = layer_norm(t_hidden, tvec[2], tvec[3]).astype(BF)
    t_value, t_slope = gelu_pair(mm(t_second, tw_up) + t_bias)
    t_active = t_value.astype(BF)
    t_out = t_hidden + mm(t_active, tw_down) + tvec[4]
    t_final = layer_norm(t_out, tvec[5], tvec[6]).astype(BF)
    text_embed = mm(t_final, tw_head)

    pw_k, pw_v = pw_pair[:, :width], pw_pair[:, width:]
    probe_query = mm_exact(ivec[7:8], pw_query.astype(F32))
    p_keys = mm_exact(spread_heads(probe_query), pw_k.astype(F32), 1, 1) * factor
    k_high, k_low = split_two(p_keys)
    pool_scores = mm(k_high, final, 1, 1) + mm(k_low, final, 1, 1)
    pool_scores = pool_scores.reshape(HEADS, own, length)
    pool_probs = jax.nn.softmax(pool_scores, axis=-1)
    final_own = final.reshape(own, length, width)
    p_high, p_low = split_two(pool_probs)
    used = jnp.einsum("hbt,btd->bhd", p_high, final_own, preferred_element_type=F32)
    used += jnp.einsum("hbt,btd->bhd", p_low, final_own, preferred_element_type=F32)
    pooled = fold_heads(mm_exact(used.reshape(own * HEADS, width), pw_v.astype(F32)))
    head_start = mm_exact(pooled, pw_out.astype(F32))
    head_normed = layer_norm(head_start, ivec[8], ivec[9]).astype(BF)
    h_value, h_slope = gelu_pair(mm(head_normed, pw_up) + p_bias)
    head_active = h_value.astype(BF)
    image_embed = head_start + mm(head_active, pw_down) + ivec[10]

    embeds = lax.all_gather(jnp.stack([image_embed, text_embed], 1), ALL, axis=0, tiled=True)
    every_image, every_text = embeds[:, 0], embeds[:, 1]
    labels = (2 * pairs - 1).astype(F32)
    total = every_image.shape[0]
    i_scale = lax.rsqrt(jnp.sum(every_image * every_image, -1, keepdims=True) + EPS)
    t_scale = lax.rsqrt(jnp.sum(every_text * every_text, -1, keepdims=True) + EPS)
    z_i, z_t = every_image * i_scale, every_text * t_scale
    cosine = mm_exact(z_i, z_t, 1, 1)
    temper = jnp.exp(temp_bias[0])
    logits = cosine * temper + temp_bias[1]
    loss = -jnp.sum(jax.nn.log_sigmoid(labels * logits)) / total
    g = -labels * jax.nn.sigmoid(-labels * logits) / total
    grad_temp = jnp.stack([temper * jnp.sum(g * cosine), jnp.sum(g)])
    dz_i = temper * mm_exact(g, z_t)
    dz_t = temper * mm_exact(g, z_i, 0, 0)
    all_d_image = (dz_i - z_i * jnp.sum(z_i * dz_i, -1, keepdims=True)) * i_scale
    all_d_text = (dz_t - z_t * jnp.sum(z_t * dz_t, -1, keepdims=True)) * t_scale
    d_image = lax.dynamic_slice_in_dim(all_d_image, me * own, own, 0)
    d_text = lax.dynamic_slice_in_dim(all_d_text, me * own, own, 0)

    h_upper = mm_exact(d_image, pw_down.astype(F32), 1, 1) * h_slope
    h_norm = mm_exact(h_upper, pw_up.astype(F32), 1, 1)
    d_start, dv8, dv9 = norm_back(head_start, ivec[8], h_norm)
    d_start = d_image + d_start
    dv10 = jnp.sum(d_image, 0)
    d_pooled = mm_exact(d_start, pw_out.astype(F32), 1, 1)
    p_values = mm_exact(spread_heads(d_pooled), pw_v.astype(F32), 1, 1).reshape(own, HEADS, width)
    v_high, v_low = split_two(p_values)
    d_probs = jnp.einsum("bhd,btd->hbt", v_high, final_own, preferred_element_type=F32)
    d_probs += jnp.einsum("bhd,btd->hbt", v_low, final_own, preferred_element_type=F32)
    d_scores = pool_probs * (d_probs - jnp.sum(pool_probs * d_probs, -1, keepdims=True))
    s_high, s_low = split_two(d_scores)
    p_used = jnp.einsum("hbt,btd->bhd", s_high, final_own, preferred_element_type=F32)
    p_used += jnp.einsum("hbt,btd->bhd", s_low, final_own, preferred_element_type=F32)
    d_query = jnp.sum(fold_heads(mm_exact(p_used.reshape(own * HEADS, width), pw_k.astype(F32))), 0) * factor
    d_final = jnp.einsum(
        "hbt,bhd->btd",
        jnp.concatenate([s_high, p_high], 0),
        jnp.concatenate([jnp.broadcast_to(k_high[None], (own, HEADS, width)), v_high], 1),
        preferred_element_type=F32,
    ).reshape(own * length, width)
    dy, dv5, dv6 = norm_back(block_out, ivec[5], d_final)

    d_branch = dy.astype(BF)
    g_down = mm(active, d_branch, 0, 0)
    dv4 = jnp.sum(dy, 0)
    d_upper_f = mm(d_branch, w_down, 1, 1) * slope.astype(F32)
    d_upper = d_upper_f.astype(BF)
    g_bias = jnp.sum(d_upper_f, 0)
    g_up = mm(second, d_upper, 0, 0)
    d_hidden, dv2, dv3 = norm_back(hidden, ivec[2], mm(d_upper, w_up, 1, 1))
    d_hidden = dy + d_hidden
    d_attend = d_hidden.astype(BF)
    g_out = mm(mixed, d_attend, 0, 0)
    d_mixed = mm(d_attend, w_out, 1, 1).astype(BF)

    def scatter(*grads):
        flat = jnp.concatenate([g.astype(BF).reshape(world, -1, width) for g in grads], 1)
        mine = lax.psum_scatter(flat, ALL, scatter_dimension=0, tiled=False).astype(F32)
        out, at = [], 0
        for g in grads:
            count = g.size // world // width
            out.append(mine[at : at + count].reshape(g.shape[0] // world, g.shape[1]))
            at += count
        return out

    own_up, own_down, own_out = scatter(g_up, g_down, g_out)
    inner_rows = jnp.sum(
        (d_mixed.astype(F32) * mixed.astype(F32)).reshape(own * length, HEADS, head_width), -1
    ).T.reshape(HEADS // 2, 2, own * length)
    d_q, d_k, d_v = attend_bwd(proj, d_mixed, lse, inner_rows, length)
    g_in = jnp.concatenate([mm(normed, d, 0, 0) for d in (d_q, d_k, d_v)], 1)
    (own_in,) = scatter(g_in)
    d_normed = (
        mm(d_q, w_in[:, :width], 1, 1)
        + mm(d_k, w_in[:, width : 2 * width], 1, 1)
        + mm(d_v, w_in[:, 2 * width :], 1, 1)
    )
    d_x, dv0, dv1 = norm_back(x, ivec[0], d_normed)
    d_x = (d_hidden + d_x).reshape(own, length, width)

    def to_tokens(v):
        return lax.all_to_all(v.astype(BF), "seq", 1, 0, tiled=True).astype(F32)

    grad_patches = to_tokens(d_x)

    dt_final = mm_exact(d_text, tw_head.astype(F32), 1, 1)
    dt_out, tv5, tv6 = norm_back(t_out, tvec[5], dt_final)
    dt_branch = dt_out.astype(BF)
    tv4 = jnp.sum(dt_out, 0)
    dt_upper = (mm(dt_branch, tw_down, 1, 1) * t_slope).astype(BF)
    dt_hidden, tv2, tv3 = norm_back(t_hidden, tvec[2], mm(dt_upper, tw_up, 1, 1))
    dt_hidden = dt_out + dt_hidden
    dt_attend = dt_hidden.astype(BF)
    dt_mixed = mm(dt_attend, tw_out, 1, 1).astype(BF)
    t_values = mm(spread_heads(dt_mixed.astype(F32)).astype(BF), tw_v, 1, 1).reshape(own, HEADS, width)
    tv_high, tv_low = split_two(t_values)
    dt_probs = jnp.einsum("bsd,bhd->bsh", t_normed, tv_high, preferred_element_type=F32)
    dt_probs += jnp.einsum("bsd,bhd->bsh", t_normed, tv_low, preferred_element_type=F32)
    dt_scores = t_probs * (dt_probs - jnp.sum(t_probs * dt_probs, 1, keepdims=True))
    tk_used = jnp.einsum("bsh,bsd->bhd", dt_scores, t_normed.astype(F32), precision=HIGH)
    dt_q = fold_heads(mm(tk_used.reshape(own * HEADS, width).astype(BF), tw_k)) * factor
    dt_q = dt_q.astype(BF)
    dt_normed = jnp.einsum("bsh,bhd->bsd", dt_scores, t_keys, precision=HIGH)
    dt_normed += jnp.einsum("bsh,bhd->bsd", t_probs, t_values, precision=HIGH)
    dt_normed = dt_normed.at[:, -1].add(mm(dt_q, tw_q, 1, 1))
    flat_x = t_x.reshape(own * text_length, width)
    dt_x, tv0, tv1 = norm_back(flat_x, tvec[0], dt_normed.reshape(own * text_length, width))
    dt_x = dt_x.reshape(own, text_length, width).at[:, -1].add(dt_hidden)
    grad_captions = to_tokens(dt_x)

    whole = jnp.concatenate(
        [v.astype(F32) for v in (h_upper, d_start, d_pooled, dt_branch, dt_upper, dt_attend, dt_q, t_q, dt_mixed)], 1
    )
    whole = lax.all_gather(whole, ALL, axis=0, tiled=True)
    at = [0]

    def take(count):
        at[0] += count
        return whole[:, at[0] - count : at[0]]

    a_h_upper, a_start, a_pooled, a_branch, a_upper, a_attend, a_q, a_query, a_mixed = (
        take(c) for c in (hidden_width, width, width, width, hidden_width, width, width, width, width)
    )
    columns = [pooled, head_normed, t_last, t_mixed, t_second, t_final]
    columns += [used, t_used, tk_used * factor]
    columns += [head_active, t_active]
    columns = jnp.concatenate(
        [v.astype(F32).reshape(own, -1, width) for v in columns], 1
    )
    wide = 2 * (hidden_width // width)
    narrow = columns.shape[1] - wide
    cut = jnp.concatenate(
        [
            columns[:, :narrow].reshape(own, narrow, world, part).transpose(2, 0, 1, 3).reshape(world, own, -1),
            columns[:, narrow:].reshape(own, 2, world, wide_part).transpose(2, 0, 1, 3).reshape(world, own, -1),
        ],
        2,
    )
    cut = lax.all_to_all(cut, ALL, 0, 0, tiled=True).reshape(total, -1)
    slim = cut[:, : narrow * part].reshape(total, narrow, part)
    broad = cut[:, narrow * part :].reshape(total, 2, wide_part)

    def outer(rows, cols):
        return mm_exact(rows, cols, 0, 0)

    def outer_heads(rows, cols):
        cols = cols.reshape(total, HEADS, head_width)
        return jnp.einsum("chm,che->mhe", rows, cols, precision=HIGH).reshape(part, width)

    c_pooled, c_head, c_last, c_mixed, c_second, c_final = (slim[:, i] for i in range(6))
    c_used, ct_used, ctk_used = (slim[:, 6 + i * HEADS : 6 + (i + 1) * HEADS] for i in range(3))
    own_t_in = jnp.concatenate(
        [outer(c_last, a_q), outer_heads(ctk_used, a_query), outer_heads(ct_used, a_mixed)], 1
    )
    own_t_out = outer(c_mixed, a_attend)
    own_t_up = outer(c_second, a_upper)
    own_t_down = outer(broad[:, 1], a_branch)
    own_t_head = outer(c_final, all_d_text)
    own_p_out = outer(c_pooled, a_start)
    own_p_up = outer(c_head, a_h_upper)
    own_p_down = outer(broad[:, 0], all_d_image)
    own_p_values = outer_heads(c_used, a_pooled)

    summed = jnp.concatenate(
        [
            jnp.stack([dv0, dv1, dv2, dv3, dv4, dv5, dv6, dv8, dv9, dv10]),
            jnp.stack([tv0, tv1, tv2, tv3, tv4, tv5, tv6]),
            d_query[None],
            jnp.sum(p_used, 0),
            g_bias.reshape(-1, width),
        ],
        0,
    )
    summed = lax.psum(summed, ALL)
    total_query = summed[17]
    mine = lambda v, n: lax.dynamic_slice_in_dim(v, me * n, n, -1)
    own_probe = mine(ivec[7], part)
    own_p_query = own_probe[:, None] * total_query[None, :]
    dv7 = jnp.sum(probe_query_weight.astype(F32) * total_query[None, :], 1)
    pk_used = mine(summed[18 : 18 + HEADS], part)
    own_p_keys = jnp.einsum(
        "hm,he->mhe", pk_used, probe_query.reshape(HEADS, head_width) * factor
    ).reshape(part, width)
    own_p_pair = jnp.concatenate([own_p_keys, own_p_values], 1)
    ten = mine(summed[:10], part)
    own_ivec = jnp.concatenate([ten[:7], dv7[None], ten[7:]], 0)
    own_tvec = mine(summed[10:17], part)
    own_bias = mine(summed[18 + HEADS :].reshape(-1), wide_part)
    own_p_bias = mine(jnp.sum(a_h_upper, 0), wide_part)
    own_t_bias = mine(jnp.sum(a_upper, 0), wide_part)
    return (
        loss, grad_patches, grad_captions,
        own_in, own_out, own_up, own_bias, own_down, own_ivec,
        own_p_query, own_p_pair, own_p_out, own_p_up, own_p_bias, own_p_down,
        own_t_in, own_t_out, own_t_up, own_t_bias, own_t_down, own_tvec, own_t_head,
        grad_temp,
    )


MESH = pl.DeviceIdType.MESH

class Place:
    def __init__(self):
        i = lax.axis_index("dp")
        self.i, self.z = i, lax.axis_index("seq")
        self.y, self.x, self.c = i // 4, (i // 2) % 2, i % 2
        self.at_y = (i + 4 - 8 * self.y, self.z)
        self.at_x = (i + 2 - 4 * self.x, self.z)
        self.at_c = (i + 1 - 2 * self.c, self.z)

    def at_z(self, k):
        return (self.i, (self.z + k) % 4)

def greet(peers):
    barrier = pltpu.get_barrier_semaphore()
    for p in peers:
        pl.semaphore_signal(barrier, inc=1, device_id=p, device_id_type=MESH)
    pl.semaphore_wait(barrier, len(peers))

def gather_kernel(kinds, order, *refs):
    n = len(kinds)
    srcs, outs = refs[:n], refs[n : 2 * n]
    send, recv, local = refs[2 * n :]
    me = Place()
    y, x, c, z = me.y, me.x, me.c, me.z
    greet([me.at_z(1), me.at_z(2), me.at_z(3), me.at_x, me.at_y, me.at_c])
    ends = []

    def copy_of(a, slot, src, dst, dev):
        return pltpu.make_async_remote_copy(
            src, dst, send.at[a, slot], recv.at[a, slot], device_id=dev, device_id_type=MESH
        )

    def push(a, slot, src, dst, dev, arriving):
        copy = copy_of(a, slot, src, dst, dev)
        copy.start()
        ends.append(copy.wait_send)
        return copy_of(a, slot, src, arriving, dev).wait_recv

    def along(a, step, up):
        home = outs[a].at[y, x, c]
        if up:
            slab, go, to = z - step, (z - step >= 0) & (z < 3), me.at_z(1)
        else:
            slab, go, to = z + step, (z + step < 4) & (z > 0), me.at_z(3)
        slab = jnp.clip(slab, 0, 3)
        src = srcs[a] if step == 0 else home.at[slab]
        copy = copy_of(a, step + (0 if up else 3), src, home.at[slab], to)
        pl.when(go)(lambda: copy.start())
        ends.append(lambda: pl.when(go)(lambda: copy.wait_send()))

    def arrived(a, step, up):
        home = outs[a].at[y, x, c]
        if up:
            slab, come = z - 1 - step, z - 1 - step >= 0
        else:
            slab, come = z + 1 + step, z + 1 + step < 4
        slab = jnp.clip(slab, 0, 3)
        copy = copy_of(a, step + (0 if up else 3), home.at[slab], home.at[slab], me.at_z(1))
        pl.when(come)(lambda: copy.wait_recv())

    waits = {}

    def half(r, which, order_):
        if order_ != "S":
            return r
        n_ = r.shape[-1] // 2
        return r.at[..., 0:n_] if which == "C" else r.at[..., n_ : 2 * n_]

    def stage(a, s):
        kind, turn = kinds[a]
        src, out = srcs[a], outs[a]
        if kind in ("za", "zg"):
            own = src.at[z] if kind == "za" else src
            keep = pltpu.make_async_copy(own, out.at[z], local.at[a])
            keep.start()
            ends.append(keep.wait)
            for k in (1, 2, 3):
                to, fro = (z + k) % 4, (z + 4 - k) % 4
                s_ref = src.at[to] if kind == "za" else src
                ends.append(push(a, k - 1, s_ref, out.at[z], me.at_z(k), out.at[fro]))
            return
        turns = "CD" if turn == "S" else turn
        if kind != "full" and s == 0:
            own = src.at[z] if kind == "cols" else src
            keep = pltpu.make_async_copy(own, out.at[y, x, c, z] if kind == "cols" else out.at[y, x, c], local.at[a])
            keep.start()
            waits[a] = [keep.wait]
            for k in (1, 2, 3) if kind == "cols" else ():
                to, fro = (z + k) % 4, (z + 4 - k) % 4
                waits[a].append(push(a, k - 1, src.at[to], out.at[y, x, c, z], me.at_z(k), out.at[y, x, c, fro]))
        elif s == 0:
            keep = pltpu.make_async_copy(src, out.at[y, x, c, z], local.at[a])
            keep.start()
            waits[a] = [keep.wait]
            along(a, 0, True)
            along(a, 0, False)
        elif s in (1, 2):
            for up in (True, False):
                arrived(a, s - 1, up)
                along(a, s, up)
        elif s == 3:
            for up in (True, False) if kind == "full" else ():
                arrived(a, 2, up)
            for w in waits.pop(a):
                w()
            waits[a] = []
            for t in turns:
                cut = lambda r: half(r, t, turn)
                to, fro = (me.at_x, (y, 1 - x)) if t == "C" else (me.at_y, (1 - y, x))
                mine = cut(out.at[y, x, c])
                waits[a].append(push(a, 6 + (t == "D"), mine, mine, to, cut(out.at[fro[0], fro[1], c])))
        elif s == 4:
            for w in waits.pop(a):
                w()
            waits[a] = []
            for t in turns:
                cut = lambda r: half(r, t, turn)
                if t == "C":
                    mine, come, to = cut(out.at[y, :, c]), cut(out.at[1 - y, :, c]), me.at_y
                else:
                    mine, come, to = cut(out.at[:, x, c]), cut(out.at[:, 1 - x, c]), me.at_x
                waits[a].append(push(a, 8 + (t == "D"), mine, mine, to, come))
        elif s == 5:
            for w in waits.pop(a):
                w()
            mine = out.at[:, :, c]
            ends.append(push(a, 10, mine, mine, me.at_c, out.at[:, :, 1 - c]))

    for a, s in order:
        stage(a, s)
    for e in ends:
        e()


def gather(ops, kinds, order, cid):
    shapes = []
    for o, (kind, _) in zip(ops, kinds):
        s = {"full": (2, 2, 2, 4) + o.shape, "zg": (4,) + o.shape, "za": o.shape, "cols": (2, 2, 2) + o.shape, "plane": (2, 2, 2) + o.shape}[kind]
        shapes.append(jax.ShapeDtypeStruct(s, o.dtype))
    n = len(ops)
    return pl.pallas_call(
        partial(gather_kernel, kinds, order),
        out_shape=shapes,
        in_specs=[pl.BlockSpec(memory_space=pl.ANY)] * n,
        out_specs=[pl.BlockSpec(memory_space=pl.ANY)] * n,
        scratch_shapes=[
            pltpu.SemaphoreType.DMA((n, 11)),
            pltpu.SemaphoreType.DMA((n, 11)),
            pltpu.SemaphoreType.DMA((n,)),
        ],
        compiler_params=pltpu.CompilerParams(collective_id=cid, has_side_effects=True),
    )(*ops)


def reduce_kernel(g_ref, dx_ref, own_ref, moved_ref, from_c, acc_c, from_1, acc_1, from_2, acc_2, from_z, send, recv, local):
    me = Place()
    y, x, c, z = me.y, me.x, me.c, me.z
    greet([me.at_z(1), me.at_z(2), me.at_z(3), me.at_x, me.at_y, me.at_c])
    half = g_ref.shape[-1] // 2
    started = []

    def push(slot, src, dst, dev, arriving):
        copy = pltpu.make_async_remote_copy(src, dst, send.at[slot], recv.at[slot], device_id=dev, device_id_type=MESH)
        copy.start()
        started.append(copy)
        return pltpu.make_async_remote_copy(src, arriving, send.at[slot], recv.at[slot], device_id=dev, device_id_type=MESH)

    a_c = push(0, g_ref.at[:, :, 1 - c], from_c, me.at_c, from_c)
    home = pltpu.make_async_copy(g_ref.at[:, :, c], acc_c, local.at[0])
    home.start()
    rest = []
    for k in (1, 2, 3):
        to, fro = (z + k) % 4, (z + 4 - k) % 4
        rest.append(push(k, dx_ref.at[to], moved_ref.at[z], me.at_z(k), moved_ref.at[fro]))
    keep = pltpu.make_async_copy(dx_ref.at[z], moved_ref.at[z], local.at[1])
    keep.start()
    home.wait()
    a_c.wait_recv()
    f32 = lambda v: v.astype(jnp.float32)
    for a in range(2):
        for b in range(2):
            for q in range(4):
                acc_c[a, b, q] = (f32(acc_c[a, b, q]) + f32(from_c[a, b, q])).astype(acc_c.dtype)
    left, right = slice(0, half), slice(half, 2 * half)
    a_y = push(4, acc_c.at[1 - y, :, :, :, left], from_1.at[0], me.at_y, from_1.at[0])
    a_x = push(5, acc_c.at[:, 1 - x, :, :, right], from_1.at[1], me.at_x, from_1.at[1])
    a_y.wait_recv()
    for b in range(2):
        for q in range(4):
            acc_1[0, b, q] = (f32(acc_c[y, b, q, :, left]) + f32(from_1[0, b, q])).astype(acc_1.dtype)
    b_x = push(6, acc_1.at[0, 1 - x], from_2.at[0], me.at_x, from_2.at[0])
    a_x.wait_recv()
    for b in range(2):
        for q in range(4):
            acc_1[1, b, q] = (f32(acc_c[b, x, q, :, right]) + f32(from_1[1, b, q])).astype(acc_1.dtype)
    b_y = push(7, acc_1.at[1, 1 - y], from_2.at[1], me.at_y, from_2.at[1])
    b_x.wait_recv()
    for q in range(4):
        acc_2[q, :, left] = (f32(acc_1[0, x, q]) + f32(from_2[0, q])).astype(acc_2.dtype)
    b_y.wait_recv()
    for q in range(4):
        acc_2[q, :, right] = (f32(acc_1[1, y, q]) + f32(from_2[1, q])).astype(acc_2.dtype)
    last = []
    for k in (1, 2, 3):
        to, fro = (z + k) % 4, (z + 4 - k) % 4
        last.append(push(7 + k, acc_2.at[to], from_z.at[k - 1], me.at_z(k), from_z.at[k - 1]))
    total = f32(acc_2[z])
    for k in (1, 2, 3):
        last[k - 1].wait_recv()
        total += f32(from_z[k - 1])
    own_ref[...] = total
    keep.wait()
    for r in rest:
        r.wait_recv()
    for copy in started:
        copy.wait_send()

def reduce_and_move(g, dx, cid):
    rows, n = g.shape[0] // 32, g.shape[1]
    g = g.reshape(2, 2, 2, 4, rows, n)
    dx = dx.reshape(4, dx.shape[0] // 4, dx.shape[1])
    hbm = pl.BlockSpec(memory_space=pl.ANY)
    v = lambda *s: pltpu.VMEM(s, g.dtype)
    return pl.pallas_call(
        reduce_kernel,
        in_specs=[hbm, hbm],
        out_specs=[pl.BlockSpec(memory_space=pltpu.VMEM), hbm],
        out_shape=[jax.ShapeDtypeStruct((rows, n), jnp.float32), jax.ShapeDtypeStruct(dx.shape, dx.dtype)],
        scratch_shapes=[
            v(2, 2, 4, rows, n), v(2, 2, 4, rows, n), v(2, 2, 4, rows, n // 2), v(2, 2, 4, rows, n // 2),
            v(2, 4, rows, n // 2), v(4, rows, n), v(3, rows, n),
            pltpu.SemaphoreType.DMA((11,)), pltpu.SemaphoreType.DMA((11,)), pltpu.SemaphoreType.DMA((2,)),
        ],
        compiler_params=pltpu.CompilerParams(collective_id=cid, has_side_effects=True, vmem_limit_bytes=40 << 20),
    )(g, dx)

ROWS = 80

def middle_kernel(final_ref, block_ref, tokens_ref, tp_ref, downs_ref, outs_ref, ivec_ref, tvec_ref, pbias_ref, tbias_ref,
                  label_ref, temp_ref,
                  dy_ref, branch_ref, rows_ref, sums_ref, dcap_ref, loss_ref, dz_ref,
                  tn_ref, dn_ref, send_a, recv_a, send_l, recv_l, send_t, recv_t, send_sem, recv_sem):
    me = Place()
    z, i = me.z, me.i
    n_dp = recv_l.shape[0]
    plane = [((i + k) % n_dp, z) for k in range(1, n_dp)]
    greet([me.at_z(1), me.at_z(2), me.at_z(3)] + plane)
    width = final_ref.shape[1]
    part = width // 4
    started = []

    def exchange(n, values_for):
        for q in range(4):
            send_a[n, q] = values_for(q)
        recv_a[n, z] = send_a[n, z]
        arrive = []
        for k in (1, 2, 3):
            to, fro = (z + k) % 4, (z + 4 - k) % 4
            copy = pltpu.make_async_remote_copy(send_a.at[n, to], recv_a.at[n, z], send_sem.at[n, k - 1],
                                                recv_sem.at[n, k - 1], device_id=me.at_z(k), device_id_type=MESH)
            copy.start()
            started.append(copy)
            arrive.append(pltpu.make_async_remote_copy(send_a.at[n, to], recv_a.at[n, fro], send_sem.at[n, k - 1],
                                                       recv_sem.at[n, k - 1], device_id=me.at_z(k), device_id_type=MESH))

        def done():
            for a in arrive:
                a.wait_recv()
            return [recv_a[n, q] for q in range(4)]

        return done

    pad4 = jnp.zeros((4, width), F32)
    pad1 = jnp.zeros((1, width), F32)
    ivec, tvec = ivec_ref[...], tvec_ref[...]
    iv = lambda k: ivec[k:k + 1]
    tv = lambda k: tvec[k:k + 1]
    names = ["tq", "tk", "tv", "thead", "pq", "pk", "pv"]
    col = {n: 2 * width + 256 * k for k, n in enumerate(names)}
    small = lambda n: tp_ref[:, col[n]:col[n] + 256]
    p_up = lambda: tp_ref[:, 0:width]
    t_up = lambda: tp_ref[:, width:2 * width]
    t_down = lambda: downs_ref[:, 0:width]
    p_down = lambda: downs_ref[:, width:2 * width]
    t_out_w = lambda: outs_ref[0:part, 0:width]
    p_out_w = lambda: outs_ref[0:part, width:2 * width]
    lane = lax.broadcasted_iota(jnp.int32, (1, 256), 1)
    own = [((lane >= 64 * h) & (lane < 64 * h + 64)).astype(F32) for h in range(3)]

    def spread(a):
        return jnp.concatenate([a * own[h] for h in range(3)], 0)

    def fold(a):
        n = a.shape[0] // 3
        return sum(a[h * n:(h + 1) * n] * own[h] for h in range(3))

    t_x = tokens_ref[...].astype(F32)
    tn = layer_norm(t_x, tv(0), tv(1)).astype(BF)
    tn_ref[...] = tn.astype(F32)
    last_at = [3 * 64 + 16 * c + 15 for c in range(4)]
    t_last = jnp.concatenate([tn_ref[r:r + 1, :] for r in last_at], 0)
    x_last = jnp.concatenate([tokens_ref[3 * 64 + 16 * c:3 * 64 + 16 * c + 16, :].astype(F32)[15:16] for c in range(4)], 0)
    t_q = mm(t_last.astype(BF), small("tq")).astype(BF).astype(F32)
    t_keys = mm(spread(t_q).astype(BF), small("tk"), 1, 1) * 0.125
    scores = mm_two(t_keys, tn, 1)
    col_id = (lax.broadcasted_iota(jnp.int32, scores.shape, 1) // 16) % 4
    row_id = lax.broadcasted_iota(jnp.int32, scores.shape, 0) % 4
    mine = col_id == row_id
    top = jnp.max(jnp.where(mine, scores, -1e30), -1, keepdims=True)
    e = jnp.where(mine, jnp.exp(jnp.where(mine, scores - top, 0.0)), 0.0)
    t_probs = e / jnp.sum(e, -1, keepdims=True)
    t_used = mm_two(t_probs, tn)
    t_mixed = fold(mm(t_used.astype(BF), small("tv"))).astype(BF)
    t_part = mm(t_mixed[:, 0:part], t_out_w())

    p_q = mm(iv(7).astype(BF), small("pq"))
    p_keys_my = mm_two(spread(p_q), small("pk"), 1) * 0.125
    block = jnp.concatenate([t_part, p_keys_my, pad1], 0)
    x0 = exchange(0, lambda q: block)()
    t_hidden = x_last + (x0[0] + x0[1] + x0[2] + x0[3])[0:4]
    p_keys = jnp.concatenate([x0[q][4:7] for q in range(4)], 0)
    t_second = layer_norm(t_hidden, tv(2), tv(3)).astype(BF)
    t_value, t_slope = gelu_pair(mm(t_second, t_up()) + tbias_ref[...])
    t_active = t_value.astype(BF)
    t_part = mm(t_active, t_down())
    final = final_ref[...]
    p_scores = mm_two(p_keys, final, 1)
    e = jnp.exp(p_scores - jnp.max(p_scores, -1, keepdims=True))
    p_probs = e / jnp.sum(e, -1, keepdims=True)
    used = mm_two(p_probs, final)
    x1 = exchange(1, lambda q: jnp.concatenate([t_part, used[3 * q:3 * q + 3], pad1], 0))()
    t_out = t_hidden + (x1[0] + x1[1] + x1[2] + x1[3])[0:4] + tv(4)
    t_final = layer_norm(t_out, tv(5), tv(6)).astype(BF)
    t_piece = mm(t_final, small("thead"))
    got = jnp.concatenate([x1[q][4 + h:5 + h] for h in range(3) for q in range(4)], 0)
    pooled = fold(mm_two(got, small("pv")))
    h_part = mm_two(pooled[:, 0:part], p_out_w())
    block = jnp.concatenate([h_part, jnp.concatenate([t_piece[:, 0:part], jnp.zeros((4, width - part), F32)], 1)], 0)
    x2 = exchange(2, lambda q: block)()
    h_start = (x2[0] + x2[1] + x2[2] + x2[3])[0:4]
    text_embed = jnp.concatenate([x2[q][4:8, 0:part] for q in range(4)], 1)
    h_normed = layer_norm(h_start, iv(8), iv(9)).astype(BF)
    h_value, h_slope = gelu_pair(mm(h_normed, p_up()) + pbias_ref[...])
    h_active = h_value.astype(BF)
    h_part = mm(h_active, p_down())
    block = jnp.concatenate([h_part, pad4], 0)
    x3 = exchange(3, lambda q: block)()
    image_embed = h_start + ((x3[0] + x3[1] + x3[2] + x3[3])[0:4] + iv(10))
    send_l[...] = jnp.concatenate([image_embed, text_embed], 0)
    recv_l[i] = send_l[...]
    arrive = []
    for k in range(1, n_dp):
        copy = pltpu.make_async_remote_copy(send_l, recv_l.at[i], send_sem.at[8, k], recv_sem.at[8, k],
                                            device_id=plane[k - 1], device_id_type=MESH)
        copy.start()
        started.append(copy)
        arrive.append(pltpu.make_async_remote_copy(send_l, recv_l.at[(i + n_dp - k) % n_dp], send_sem.at[8, k], recv_sem.at[8, k],
                                                   device_id=plane[k - 1], device_id_type=MESH))
    for a in arrive:
        a.wait_recv()
    every = jnp.concatenate([recv_l[k] for k in range(n_dp)], 0)
    scale = lax.rsqrt(jnp.sum(every * every, -1, keepdims=True) + EPS)
    unit = every * scale
    cosine = mm_exact(unit, unit, 1, 1)
    temper = jnp.exp(jnp.full((1, 1), temp_ref[0], F32))
    logits = cosine * temper + temp_ref[1]
    label = label_ref[...]
    valid = label != 0.0
    signed = label * logits
    total = n_dp * 4
    nll = jnp.maximum(-signed, 0.0) + jnp.log(1.0 + jnp.exp(-jnp.abs(signed)))
    add_all = lambda a: jnp.sum(jnp.sum(a, -1, keepdims=True), 0, keepdims=True)
    loss = add_all(jnp.where(valid, nll, 0.0)) / total
    g = jnp.where(valid, -label / (1.0 + jnp.exp(signed)), 0.0) / total
    gt0 = temper * add_all(g * cosine)
    gt1 = add_all(g)
    at = lax.broadcasted_iota(jnp.int32, (8, 128), 1)
    loss_ref[...] = jnp.where(at == 0, loss, jnp.where(at == 1, gt0, gt1))
    dz = temper * mm_exact(g + jnp.transpose(g), unit)
    dz_ref[...] = (dz - unit * jnp.sum(unit * dz, -1, keepdims=True)) * scale
    d_both = dz_ref[pl.ds(pl.multiple_of(8 * i, 8), 8), :]
    d_image, d_text = d_both[0:4], d_both[4:8]

    dh_upper = mm_two(d_image, p_down(), 1) * h_slope
    h_part = mm_two(dh_upper, p_up(), 1)
    d_text_my = sum(jnp.where(z == q, d_text[:, part * q:part * q + part], 0.0) for q in range(4))
    t_part = mm_two(d_text_my, small("thead")[:, 0:part], 1)
    block = jnp.concatenate([h_part, t_part], 0)
    x4 = exchange(4, lambda q: block)()
    both = x4[0] + x4[1] + x4[2] + x4[3]
    d_start, dv8, dv9 = norm_back_rows(h_start, iv(8), both[0:4])
    d_start = d_image + d_start
    dv10 = jnp.sum(d_image, 0, keepdims=True)
    d_pooled = mm_two(d_start, p_out_w(), 1)
    d_pooled = jnp.concatenate([d_pooled, jnp.zeros((4, 256 - part), F32)], 1)
    p_values_my = mm_two(spread(d_pooled), small("pv"), 1)
    dt_out, tv5, tv6 = norm_back_rows(t_out, tv(5), both[4:8])
    tv4 = jnp.sum(dt_out, 0, keepdims=True)
    dt_branch = dt_out.astype(BF)
    dt_upper = (mm(dt_branch, t_down(), 1, 1) * t_slope).astype(BF)
    t_part = mm(dt_upper, t_up(), 1, 1)
    x5 = exchange(5, lambda q: jnp.concatenate(
        [t_part] + [p_values_my[4 * h + q:4 * h + q + 1] for h in range(3)] + [pad1], 0))()
    dt_hidden, tv2, tv3 = norm_back_rows(t_hidden, tv(2), (x5[0] + x5[1] + x5[2] + x5[3])[0:4])
    dt_hidden = dt_out + dt_hidden
    dt_attend = dt_hidden.astype(BF)
    dt_mixed = mm(dt_attend, t_out_w(), 1, 1).astype(BF).astype(F32)
    dt_mixed = jnp.concatenate([dt_mixed, jnp.zeros((4, 256 - part), F32)], 1)
    t_values = mm(spread(dt_mixed).astype(BF), small("tv"), 1, 1)
    dt_probs = mm_two(t_values, tn, 1)
    dt_scores = t_probs * (dt_probs - jnp.sum(t_probs * dt_probs, -1, keepdims=True))
    tk_used = mm_two(dt_scores, tn) * 0.125
    dt_q = fold(mm(tk_used.astype(BF), small("tk"))).astype(BF)
    dn = mm(dt_scores.astype(BF), t_keys.astype(BF), 0, 0) + mm(t_probs.astype(BF), t_values.astype(BF), 0, 0)
    row_at = lax.broadcasted_iota(jnp.int32, dn.shape, 0)
    dq_back = mm(dt_q, small("tq"), 1, 1)
    for c in range(4):
        dn = dn + jnp.where(row_at == last_at[c], dq_back[c:c + 1], 0.0)
    dn_ref[...] = dn.astype(BF)
    p_values = jnp.concatenate([x5[q][4:7] for q in range(4)], 0)
    d_probs = mm_two(p_values, final, 1)
    d_scores = p_probs * (d_probs - jnp.sum(p_probs * d_probs, -1, keepdims=True))
    p_used = mm_two(d_scores, final) * 0.125
    x6 = exchange(6, lambda q: jnp.concatenate([p_used[3 * q:3 * q + 3], pad1, pad4], 0))
    arrive = []
    for k in (1, 2, 3):
        to, fro = (z + k) % 4, (z + 4 - k) % 4
        rows_to = dn_ref.at[pl.ds(pl.multiple_of(64 * to, 64), 64), :]
        copy = pltpu.make_async_remote_copy(rows_to, recv_t.at[z], send_sem.at[7, k], recv_sem.at[7, k],
                                            device_id=me.at_z(k), device_id_type=MESH)
        copy.start()
        started.append(copy)
        arrive.append(pltpu.make_async_remote_copy(rows_to, recv_t.at[fro], send_sem.at[7, k], recv_sem.at[7, k],
                                                   device_id=me.at_z(k), device_id_type=MESH))
    s_high, s_low = split_two(d_scores)
    q_high, q_low = split_two(p_probs)
    k_high, k_low = split_two(p_keys)
    v_high, v_low = split_two(p_values)
    left = jnp.concatenate([s_high.astype(F32), q_high.astype(F32)], 0)
    right = jnp.concatenate([k_high.astype(F32), v_high.astype(F32)], 0).astype(BF)
    send_t[...] = jnp.transpose(jnp.concatenate([left, jnp.zeros((104, left.shape[1]), F32)], 0))
    right = jnp.concatenate([right, jnp.zeros((104, width), BF)], 0)
    sums_ref[...] = jnp.zeros_like(sums_ref)
    tile = 128

    def step(n, carry):
        at_rows = pl.ds(pl.multiple_of(n * tile, tile), tile)
        d_final = mm(send_t[at_rows, :].astype(BF), right)
        d_y, gain, shift = norm_back_rows(block_ref[at_rows, :], iv(5), d_final)
        dy_ref[at_rows, :] = d_y
        branch_ref[at_rows, :] = d_y.astype(BF)
        sums_ref[5:6] += gain
        sums_ref[6:7] += shift
        sums_ref[4:5] += jnp.sum(d_y, 0, keepdims=True)
        return carry

    lax.fori_loop(0, final_ref.shape[0] // tile, step, 0)
    got6 = x6()
    w_got = jnp.concatenate([got6[q][h:h + 1] for h in range(3) for q in range(4)], 0)
    dq_rows = fold(mm_two(w_got, small("pk")))
    dq_my = jnp.sum(dq_rows, 0, keepdims=True)
    recv_t[z] = dn_ref[pl.ds(pl.multiple_of(64 * z, 64), 64), :]
    for a in arrive:
        a.wait_recv()
    dt_normed = sum(recv_t[q].astype(F32) for q in range(4))
    x_mine = tokens_ref[pl.ds(pl.multiple_of(64 * z, 64), 64), :].astype(F32)
    d_cap, tv0, tv1 = norm_back_rows(x_mine, tv(0), dt_normed)
    row_c = lax.broadcasted_iota(jnp.int32, d_cap.shape, 0)
    for c in range(4):
        d_cap = d_cap + jnp.where((row_c == 16 * c + 15) & (z == 3), dt_hidden[c:c + 1], 0.0)
    dcap_ref[...] = d_cap
    first = (z == 0).astype(F32)
    sums_ref[8:9] = dv8 * first
    sums_ref[9:10] = dv9 * first
    sums_ref[10:11] = dv10 * first
    sums_ref[11:12] = tv0
    sums_ref[12:13] = tv1
    sums_ref[13:14] = tv2 * first
    sums_ref[14:15] = tv3 * first
    sums_ref[15:16] = tv4 * first
    sums_ref[16:17] = tv5 * first
    sums_ref[17:18] = tv6 * first
    own_row = lambda a: sum(jnp.where(z == q, a[q:q + 1].astype(F32), 0.0) for q in range(4))
    pick = lambda a: a[:, 0:part].astype(F32)
    wide = jnp.concatenate
    pieces = [
        dh_upper, dt_upper.astype(F32), h_active.astype(F32), t_active.astype(F32),
        wide([pick(d_pooled), pick(pooled), pick(dt_q), pick(t_q)], 1),
        wide([pick(dt_mixed), pick(t_mixed), jnp.broadcast_to(pick(dq_my), (4, part)), jnp.broadcast_to(pick(p_q), (4, part))], 1),
        own_row(h_normed), own_row(d_start), own_row(t_last), own_row(t_second),
        own_row(dt_attend), own_row(dt_branch), own_row(t_final), pad1,
        used, t_used, tk_used, p_used,
    ]
    rows_ref[...] = jnp.concatenate(pieces, 0)
    for copy in started:
        copy.wait_send()

def middle(final, block_out, tokens, tp, downs, outs, ivec, tvec, pbias, tbias, label, temp, cid, n_dp):
    length, width = final.shape
    v = pl.BlockSpec(memory_space=pltpu.VMEM)
    f = lambda *s: jax.ShapeDtypeStruct(s, F32)
    return pl.pallas_call(
        middle_kernel,
        in_specs=[v] * 11 + [pl.BlockSpec(memory_space=pltpu.SMEM)],
        out_specs=[v] * 7,
        out_shape=[f(length, width), jax.ShapeDtypeStruct((length, width), BF), f(ROWS, width), f(24, width), f(64, width), f(8, 128), f(8 * n_dp, width)],
        scratch_shapes=[
            pltpu.VMEM((256, width), F32), pltpu.VMEM((256, width), BF),
            pltpu.VMEM((7, 4, 8, width), F32), pltpu.VMEM((7, 4, 8, width), F32),
            pltpu.VMEM((8, width), F32), pltpu.VMEM((n_dp, 8, width), F32),
            pltpu.VMEM((length, 128), F32), pltpu.VMEM((4, 64, width), BF),
            pltpu.SemaphoreType.DMA((9, 8)), pltpu.SemaphoreType.DMA((9, 8)),
        ],
        compiler_params=pltpu.CompilerParams(collective_id=cid, has_side_effects=True, vmem_limit_bytes=50 << 20),
    )(final, block_out, tokens, tp, downs, outs, ivec, tvec, pbias, tbias, label, temp)


def mlp_fwd_kernel(x_ref, mixed_ref, wo_ref, wu_ref, wd_ref, bias_ref, vec_ref,
                   hidden_ref, second_ref, active_ref, slope_ref, block_ref, final_ref, total):
    k = pl.program_id(0)
    vec = vec_ref[...]

    @pl.when(k == 0)
    def _():
        hidden = x_ref[...].astype(F32) + mm(mixed_ref[...], wo_ref[...])
        hidden_ref[...] = hidden
        second_ref[...] = layer_norm(hidden, vec[2:3], vec[3:4]).astype(BF)
        total[...] = hidden + vec[4:5]

    value, slope = gelu_pair(mm(second_ref[...], wu_ref[...]) + bias_ref[0])
    active = value.astype(BF)
    active_ref[...] = active
    slope_ref[...] = slope.astype(BF)
    total[...] += mm(active, wd_ref[...])

    @pl.when(k == pl.num_programs(0) - 1)
    def _():
        block_ref[...] = total[...]
        final_ref[...] = layer_norm(total[...], vec[5:6], vec[6:7]).astype(BF)


def mlp_fwd(x, mixed, main, bias, vec, fold):
    rows, width = mixed.shape
    whole = pl.BlockSpec((rows, width), lambda k: (0, 0))
    tile = pl.BlockSpec((rows, width), lambda k: (0, k))
    at = lambda f: pl.BlockSpec((width, width), lambda k: (0, f(k)))
    s = lambda n, t: jax.ShapeDtypeStruct((rows, n * width), t)
    return pl.pallas_call(
        mlp_fwd_kernel,
        grid=(fold,),
        in_specs=[whole, whole, at(lambda k: 0), at(lambda k: 1 + k), at(lambda k: 1 + fold + k),
                  pl.BlockSpec((1, 1, width), lambda k: (k, 0, 0)), pl.BlockSpec(vec.shape, lambda k: (0, 0))],
        out_specs=[whole, whole, tile, tile, whole, whole],
        out_shape=[s(1, F32), s(1, BF), s(fold, BF), s(fold, BF), s(1, F32), s(1, BF)],
        scratch_shapes=[pltpu.VMEM((rows, width), F32)],
        compiler_params=pltpu.CompilerParams(vmem_limit_bytes=56 << 20),
    )(x, mixed, main, main, main, bias.reshape(fold, 1, width), vec)


def mlp_bwd_kernel(dy_ref, branch_ref, active_ref, slope_ref, second_ref, hidden_ref, mixed_ref,
                   wo_ref, wu_ref, wd_ref, vec_ref,
                   g_ref, dhid_ref, dmix_ref, inner_ref, bias_ref, dvec_ref, total):
    k = pl.program_id(0)
    fold = pl.num_programs(0)
    width = mixed_ref.shape[1]
    branch = branch_ref[...]
    columns = lambda n: pl.ds(pl.multiple_of(n * width, width), width)
    g_ref[:, columns(1 + fold + k)] = mm(active_ref[...], branch, 0, 0).astype(BF)
    d_upper_f = mm(branch, wd_ref[...], 1, 1) * slope_ref[...].astype(F32)
    bias_ref[0] = jnp.sum(d_upper_f, 0, keepdims=True)
    d_upper = d_upper_f.astype(BF)
    g_ref[:, columns(1 + k)] = mm(second_ref[...], d_upper, 0, 0).astype(BF)
    back = mm(d_upper, wu_ref[...], 1, 1)

    @pl.when(k == 0)
    def _():
        total[...] = back

    @pl.when(k > 0)
    def _():
        total[...] += back

    @pl.when(k == fold - 1)
    def _():
        vec = vec_ref[...]
        d_hidden, gain, shift = norm_back_rows(hidden_ref[...], vec[2:3], total[...])
        dvec_ref[0:1] = gain
        dvec_ref[1:2] = shift
        d_hidden = dy_ref[...] + d_hidden
        dhid_ref[...] = d_hidden
        d_attend = d_hidden.astype(BF)
        mixed = mixed_ref[...]
        g_ref[:, 0:width] = mm(mixed, d_attend, 0, 0).astype(BF)
        d_mixed = mm(d_attend, wo_ref[...], 1, 1).astype(BF)
        dmix_ref[...] = d_mixed
        head = lax.broadcasted_iota(jnp.int32, (16, width), 0)
        lane = lax.broadcasted_iota(jnp.int32, (16, width), 1)
        own = (lane // (width // HEADS) == head).astype(BF)
        high, low = split_two(d_mixed.astype(F32) * mixed.astype(F32))
        sums = mm(own, high, 1, 1) + mm(own, low, 1, 1)
        for h in range(HEADS // 2):
            inner_ref[h] = sums[2 * h : 2 * h + 2]


def mlp_bwd(dy, branch, active, slope, second, hidden, mixed, main, vec, fold):
    rows, width = mixed.shape
    whole = pl.BlockSpec((rows, width), lambda k: (0, 0))
    tile = pl.BlockSpec((rows, width), lambda k: (0, k))
    at = lambda f: pl.BlockSpec((width, width), lambda k: (0, f(k)))
    f = lambda *s: jax.ShapeDtypeStruct(s, F32)
    return pl.pallas_call(
        mlp_bwd_kernel,
        grid=(fold,),
        in_specs=[whole, whole, tile, tile, whole, whole, whole,
                  at(lambda k: 0), at(lambda k: 1 + k), at(lambda k: 1 + fold + k), pl.BlockSpec(vec.shape, lambda k: (0, 0))],
        out_specs=[pl.BlockSpec((width, (1 + 2 * fold) * width), lambda k: (0, 0)), whole, whole,
                   pl.BlockSpec((HEADS // 2, 2, rows), lambda k: (0, 0, 0)),
                   pl.BlockSpec((1, 1, width), lambda k: (k, 0, 0)), pl.BlockSpec((8, width), lambda k: (0, 0))],
        out_shape=[jax.ShapeDtypeStruct((width, (1 + 2 * fold) * width), BF), f(rows, width),
                   jax.ShapeDtypeStruct((rows, width), BF), f(HEADS // 2, 2, rows), f(fold, 1, width), f(8, width)],
        scratch_shapes=[pltpu.VMEM((rows, width), F32)],
        compiler_params=pltpu.CompilerParams(vmem_limit_bytes=60 << 20),
    )(dy, branch, active, slope, second, hidden, mixed, main, main, main, vec)


def project_bwd_kernel(dq_ref, dk_ref, dv_ref, normed_ref, w_ref, x_ref, dhid_ref, sums_ref, vec_ref, g_ref, dx_ref):
    width = dq_ref.shape[1]
    normed = normed_ref[...]
    back = None
    for n, ref in enumerate((dq_ref, dk_ref, dv_ref)):
        d = ref[...]
        g_ref[:, n * width : (n + 1) * width] = mm(normed, d, 0, 0).astype(BF)
        part = mm(d, w_ref[:, n * width : (n + 1) * width], 1, 1)
        back = part if back is None else back + part
    d_x, gain, shift = norm_back_rows(x_ref[...].astype(F32), vec_ref[0:1], back)
    dx_ref[...] = (dhid_ref[...] + d_x).astype(BF)
    sums = jnp.concatenate([gain, shift, sums_ref[2:, :]], 0)
    sums = jnp.concatenate([sums, jnp.zeros((128 - sums.shape[0], width), F32)], 0)
    g_ref[:, 3 * width : 3 * width + 128] = jnp.transpose(sums).astype(BF)
    g_ref[:, 3 * width + 128 : 3 * width + 256] = jnp.zeros((width, 128), BF)


def project_bwd(dq, dk, dv, normed, w_in, x, d_hidden, sums, vec):
    rows, width = dq.shape
    v = pl.BlockSpec(memory_space=pltpu.VMEM)
    return pl.pallas_call(
        project_bwd_kernel,
        in_specs=[v] * 9,
        out_specs=[v] * 2,
        out_shape=[jax.ShapeDtypeStruct((width, 3 * width + 256), BF), jax.ShapeDtypeStruct((rows, width), BF)],
        compiler_params=pltpu.CompilerParams(vmem_limit_bytes=56 << 20),
    )(dq, dk, dv, normed, w_in, x, d_hidden, sums, vec)


def outer_kernel(rows_ref, dimage_ref, dtext_ref,
                 pup_ref, tup_ref, pdown_ref, tdown_ref, pout_ref, tout_ref, thead_ref,
                 tq_ref, tk_ref, tv_ref, pv_ref, pk_ref, bias_ref):
    at_dp, z = lax.axis_index("dp"), lax.axis_index("seq")
    n_dp, n_z = 8, 4
    me = at_dp * n_z + z
    width = rows_ref.shape[2]
    part, quarter = width // 32, width // n_z
    wide_part = 4 * part
    n = n_dp * n_z
    each = quarter // part

    def iota(shape, d):
        return lax.broadcasted_iota(jnp.int32, shape, d)

    def selector(count, first):
        return (iota((count, width), 1) == iota((count, width), 0) + first).astype(BF)

    def group(r):
        return jnp.concatenate([rows_ref[r + c] for c in range(4)], 0)

    cols = jnp.concatenate(
        [mm(selector(part, part * me), rows_ref[r], 1, 1) for r in range(24, 80)], 1
    ).astype(BF)
    get = lambda r, count=1: cols[:, n * (r - 24) : n * (r - 24 + count)]
    a, b = iota((4 * n, n), 0), iota((4 * n, n), 1)
    same = ((a % n) // n_z == b // n_z) & (a // n == b % n_z)
    keep = lambda which: (same & (a % n_z == which)).astype(BF)
    units = selector(wide_part, wide_part * at_dp)
    heads = selector(part, quarter + part * (me % each))
    to_mine, to_head = keep(z), keep(me // each)
    chosen = lambda sel, r, perm: mm(mm(sel, group(r), 1, 1).astype(BF), perm).astype(BF)
    pdown_ref[...] = mm(chosen(units, 8, to_mine), dimage_ref[...])
    tdown_ref[...] = mm(chosen(units, 12, to_mine), rows_ref[29])
    pout_ref[...] = mm(chosen(heads, 16, to_head), rows_ref[25])
    tout_ref[...] = mm(chosen(heads, 20, to_head), rows_ref[28])
    thead_ref[...] = mm(get(30), dtext_ref[...])
    ones = jnp.ones((n, 128), BF)
    bias_ref[0] = mm(chosen(units, 0, to_mine), ones)
    bias_ref[1] = mm(chosen(units, 4, to_mine), ones)
    a, b = iota((n, 4 * n), 0), iota((n, 4 * n), 1)
    spread = ((b % n) // n_z == a // n_z) & (b // n == a % n_z)
    spread = spread.astype(BF)
    lane_z = iota((1, 4 * n), 1) % n_z
    masks = [(lane_z == q).astype(BF) for q in range(n_z)]

    def blocks(values):
        return jnp.concatenate([v * m for v, m in zip(values, masks)], 0)

    by_image = lambda r: mm(get(r), spread).astype(BF)
    g16, g20 = group(16), group(20)

    def put(ref, value, first):
        for q in range(n_z):
            ref[q] = value[q * part : (q + 1) * part, first : first + ref.shape[2]]

    put(pup_ref, mm(blocks([by_image(24)] * 4), group(0)), 0)
    put(tup_ref, mm(blocks([by_image(27)] * 4), group(4)), 0)
    put(tq_ref, mm(blocks([by_image(26)] * 4), g16), 2 * quarter)
    lane = iota((1, width), 1)
    count = HEADS // n_z
    hw = quarter // count

    def by_head(values_of, rhs, first):
        total = None
        for h in range(count):
            own = ((lane >= first + hw * h) & (lane < first + hw * h + hw)).astype(F32)
            one = mm(blocks(values_of(h)), rhs) * own
            total = one if total is None else total + one
        return total

    put(tk_ref, by_head(lambda h: [get(56 + 4 * h, 4)] * 4, g16, 3 * quarter), 3 * quarter)
    put(tv_ref, by_head(lambda h: [get(44 + 4 * h, 4)] * 4, g20, 0), 0)
    put(pv_ref, by_head(lambda h: [by_image(32 + count * q + h) for q in range(n_z)], g16, 0), 0)
    a, b = iota((HEADS * n, 128), 0), iota((HEADS * n, 128), 1)
    pk_ref[...] = mm(get(68, HEADS), (a // n == b).astype(BF))


def outer_grads(rows, d_image, d_text):
    width = rows.shape[2]
    part, quarter = width // 32, width // 4
    v = pl.BlockSpec(memory_space=pltpu.VMEM)
    f = lambda *s: jax.ShapeDtypeStruct(s, F32)
    return pl.pallas_call(
        outer_kernel,
        in_specs=[v] * 3,
        out_specs=[v] * 13,
        out_shape=[f(4, part, width), f(4, part, width), f(4 * part, width), f(4 * part, width), f(part, width), f(part, width),
                   f(part, width), f(4, part, quarter), f(4, part, quarter), f(4, part, quarter), f(4, part, quarter),
                   f(part, 128), f(2, 4 * part, 128)],
        compiler_params=pltpu.CompilerParams(vmem_limit_bytes=48 << 20),
    )(rows, d_image, d_text)


def fast_program(
    patches, captions, pairs,
    image_attend_in, image_attend_out, image_up_weight, image_up_bias, image_down_weight,
    image_vectors, probe_query_weight, probe_pair_weight, probe_out_weight, probe_up_weight,
    probe_up_bias, probe_down_weight, text_attend_in, text_attend_out, text_up_weight,
    text_up_bias, text_down_weight, text_vectors, text_head_weight, temp_bias,
):
    n_dp, n_z = lax.axis_size("dp"), lax.axis_size("seq")
    world = n_dp * n_z
    at_dp, at_z = lax.axis_index("dp"), lax.axis_index("seq")
    me = at_dp * n_z + at_z
    width = patches.shape[-1]
    head_width = width // HEADS
    hidden_width = image_up_weight.shape[1]
    part, quarter = width // world, width // n_z
    wide_part = hidden_width // world
    fold = hidden_width // width
    length = patches.shape[1] * n_z

    small = jnp.concatenate(
        [image_vectors.reshape(-1), text_vectors.reshape(-1), image_up_bias, probe_up_bias, text_up_bias]
    )
    sizes = [image_vectors.size, text_vectors.size, image_up_bias.size, probe_up_bias.size, text_up_bias.size]
    small = jnp.pad(small, (0, 2048 - small.shape[0])).reshape(16, 128)

    def by_units(w):
        return w.reshape(part, n_dp, n_z, wide_part).transpose(2, 0, 1, 3).reshape(n_z, part, width)

    def by_heads(w):
        cut = w.reshape(part, n_z, quarter).transpose(1, 0, 2)
        return jnp.pad(cut, ((0, 0), (0, 0), (0, 256 - quarter)))

    split = [by_units(probe_up_weight), by_units(text_up_weight)]
    split += [by_heads(text_attend_in[:, k * width : (k + 1) * width]) for k in range(3)]
    split += [by_heads(text_head_weight), by_heads(probe_query_weight)]
    split += [by_heads(probe_pair_weight[:, k * width : (k + 1) * width]) for k in range(2)]
    split = jnp.concatenate(split, 2)
    downs = jnp.concatenate([text_down_weight, probe_down_weight], 1)
    w_in, tp, downs, small_all, x, tokens = gather(
        [image_attend_in, split, downs, small, patches, captions],
        [("full", "S"), ("cols", "S"), ("plane", "S"), ("full", "C"), ("za", None), ("zg", None)],
        [(0, 0), (2, 0), (2, 3), (3, 0), (0, 1), (3, 1), (1, 0), (0, 2), (3, 2), (0, 3), (4, 0), (5, 0), (3, 3)]
        + [(1, 3), (0, 4), (2, 4), (3, 4), (1, 4), (0, 5), (2, 5), (3, 5), (1, 5)],
        1,
    )
    tp, downs = tp.reshape(width, -1), downs.reshape(width, -1)
    w_in = w_in.reshape(width, 3 * width)
    x = x.reshape(length, width)
    main = jnp.concatenate(
        [
            image_attend_out,
            image_up_weight.reshape(part, width, fold).transpose(0, 2, 1).reshape(part, hidden_width),
            image_down_weight.reshape(part, hidden_width),
            text_attend_out,
            probe_out_weight,
        ],
        1,
    )
    main = lax.all_gather(main, ALL, axis=0, tiled=True)
    outs = lax.dynamic_slice_in_dim(main[:, width + 2 * hidden_width :], at_z * quarter, quarter, 0)

    small_all = small_all.reshape(world, -1)
    cuts = [sum(sizes[:i]) for i in range(len(sizes) + 1)]
    pieces = [small_all[:, cuts[i] : cuts[i + 1]].astype(F32) for i in range(len(sizes))]
    ivec = pieces[0].reshape(world, -1, part).transpose(1, 0, 2).reshape(-1, width)
    tvec = pieces[1].reshape(world, -1, part).transpose(1, 0, 2).reshape(-1, width)
    i_bias = pieces[2].reshape(width, fold).T.reshape(1, hidden_width)

    def own_units(p):
        p = p.reshape(n_dp, n_z, wide_part)
        return lax.dynamic_index_in_dim(p, at_z, 1, False).reshape(1, width)

    p_bias, t_bias = own_units(pieces[3]), own_units(pieces[4])

    normed = layer_norm(x.astype(F32), ivec[0], ivec[1]).astype(BF)
    proj = mm(normed, w_in).astype(BF)
    mixed, lse = attend_fwd(proj, length)
    hidden, second, active, slope, block_out, final = mlp_fwd(x, mixed, main, i_bias, ivec, fold)

    labels = (2 * pairs - 1).astype(F32).reshape(n_dp, n_z, n_dp, n_z)
    labels = jnp.pad(labels, ((0, 0), (0, n_z), (0, 0), (n_z, 0))).reshape(2 * world, 2 * world)
    dy, d_branch, rows, sums, d_captions, loss_row, d_embeds = middle(
        final, block_out, tokens.reshape(-1, width), tp, downs, outs, ivec, tvec, p_bias, t_bias, labels, temp_bias, 2, n_dp
    )
    loss, grad_temp = loss_row[0, 0], loss_row[0, 1:3]
    grad_captions = d_captions.reshape(captions.shape)
    rows = lax.all_gather(rows.astype(BF), ALL, axis=1, tiled=False)

    g_main, d_hidden, d_mixed, inner, g_bias, dvec = mlp_bwd(
        dy, d_branch, active, slope, second, hidden, mixed, main, ivec, fold
    )
    g_main = lax.psum_scatter(g_main, ALL, scatter_dimension=0, tiled=True).astype(F32)
    own_out = g_main[:, :width]
    own_up = g_main[:, width : width + hidden_width].reshape(part, fold, width)
    own_up = own_up.transpose(0, 2, 1).reshape(part, hidden_width)
    own_down = g_main[:, width + hidden_width :].reshape(wide_part, width)
    d_q, d_k, d_v = attend_bwd(proj, d_mixed, lse, inner, length)
    sums = jnp.concatenate([dvec[0:2], dvec[0:2], sums[4:], g_bias.reshape(fold, width)], 0)
    g_in, d_x = project_bwd(d_q, d_k, d_v, normed, w_in, x, d_hidden, sums, ivec)
    own_in, moved = reduce_and_move(g_in, d_x, 3)
    grad_patches = moved.astype(F32)
    own_sums = own_in[:, 3 * width : 3 * width + 128].T
    own_in = own_in[:, : 3 * width]

    d_embeds = d_embeds.reshape(n_dp, 2, n_z, width).astype(BF)
    pup, tup, own_p_down, own_t_down, own_p_out, own_t_out, own_t_head, tq, tk, tv, pv, pk, biases = outer_grads(
        rows, d_embeds[:, 0].reshape(world, width), d_embeds[:, 1].reshape(world, width)
    )

    def wide(g):
        return g.reshape(n_z, part, n_dp, wide_part).transpose(1, 2, 0, 3).reshape(part, hidden_width)

    own_p_up, own_t_up = wide(pup), wide(tup)
    own_t_in = jnp.stack([tq, tk, tv]).transpose(2, 0, 1, 3).reshape(part, 3 * width)
    row20 = rows[20].reshape(n_dp, n_z, n_z, quarter).astype(F32)
    probe_query = row20[0, :, 3].reshape(HEADS, head_width)
    own_p_k = (pk[:, :HEADS, None] * probe_query[None]).reshape(part, width)
    own_p_pair = jnp.concatenate([own_p_k, pv.transpose(1, 0, 2).reshape(part, width)], 1)
    d_query = jnp.sum(row20[:, :, 2], 0).reshape(width)
    mine = lambda v, n: lax.dynamic_slice_in_dim(v, me * n, n, -1)
    own_p_query = mine(ivec[7], part)[:, None] * d_query[None, :]
    dv7 = jnp.sum(probe_query_weight.astype(F32) * d_query[None, :], 1)
    own_ivec = jnp.concatenate([own_sums[0:7], dv7[None], own_sums[8:11]], 0)
    own_tvec = own_sums[11:18]
    own_bias = own_sums[24 : 24 + fold].T.reshape(wide_part)
    return (
        loss, grad_patches, grad_captions,
        own_in, own_out, own_up, own_bias, own_down, own_ivec,
        own_p_query, own_p_pair, own_p_out, own_p_up, biases[0, :, 0], own_p_down,
        own_t_in, own_t_out, own_t_up, biases[1, :, 0], own_t_down, own_tvec, own_t_head,
        grad_temp,
    )


def solution(mesh):
    tokens, matrix, vector, table = P("dp", "seq", None), P(ALL, None), P(ALL), P(None, ALL)
    weights = (
        (matrix, matrix, matrix, vector, matrix, table, matrix, matrix, matrix, matrix, vector, matrix)
        + (matrix, matrix, matrix, vector, matrix, table, matrix)
    )
    return jax.shard_map(
        fast_program if mesh.shape["dp"] == 8 and mesh.shape["seq"] == 4 else device_program,
        mesh=mesh,
        in_specs=(tokens, tokens, P()) + weights + (P(),),
        out_specs=(P(), tokens, tokens) + weights + (P(),),
        check_vma=False,
    )
```

```python
from functools import partial

import jax
import jax.numpy as jnp
from jax import lax
from jax.experimental import pallas as pl
from jax.experimental.pallas import tpu as pltpu
from jax.sharding import PartitionSpec as P

HEADS = 12
ALL = ("dp", "seq")
F32, BF = jnp.float32, jnp.bfloat16
HIGH = lax.Precision.HIGHEST
EPS = 1e-06


def mm(a, b, ca=1, cb=0):
    return lax.dot_general(a, b, (((ca,), (cb,)), ((), ())), preferred_element_type=F32)


def mm_exact(a, b, ca=1, cb=0):
    return lax.dot_general(a, b, (((ca,), (cb,)), ((), ())), precision=HIGH, preferred_element_type=F32)


def split_two(a):
    high = a.astype(BF)
    return high, (a - high.astype(F32)).astype(BF)


def layer_norm(x, gain, shift):
    center = x - jnp.mean(x, -1, keepdims=True)
    spread = jnp.mean(center * center, -1, keepdims=True)
    return center * lax.rsqrt(spread + EPS) * gain + shift


def norm_back(x, gain, upstream):
    center = x - jnp.mean(x, -1, keepdims=True)
    inverse = lax.rsqrt(jnp.mean(center * center, -1, keepdims=True) + EPS)
    unit = center * inverse
    scaled = upstream * gain
    d_x = inverse * (
        scaled
        - jnp.mean(scaled, -1, keepdims=True)
        - unit * jnp.mean(scaled * unit, -1, keepdims=True)
    )
    return d_x, jnp.sum(upstream * unit, 0), jnp.sum(upstream, 0)


def norm_back_rows(x, gain, upstream):
    d_x, d_gain, d_shift = norm_back(x, gain, upstream)
    return d_x, d_gain[None], d_shift[None]


def mm_two(a, b, cb=0):
    high, low = split_two(a)
    return mm(high, b, 1, cb) + mm(low, b, 1, cb)


def gelu_pair(u):
    c = 0.7978845608028654
    t = jnp.tanh(c * (u + 0.044715 * u * u * u))
    value = 0.5 * u * (1.0 + t)
    slope = 0.5 * (1.0 + t) + 0.5 * u * (1.0 - t * t) * c * (1.0 + 3 * 0.044715 * u * u)
    return value, slope


def attend_fwd_kernel(q_ref, k_ref, v_ref, o_ref, lse_ref):
    q = q_ref[...] * 0.125
    k = k_ref[...]
    lane = lax.broadcasted_iota(jnp.int32, k.shape, 1)
    v_turned = jnp.transpose(v_ref[...])
    outs = []
    for h in range(2):
        keep = (lane < 64) if h == 0 else (lane >= 64)
        own_k = jnp.where(keep, k, jnp.zeros_like(k))
        s = mm(own_k, q, 1, 1)
        top = jnp.max(s, 0, keepdims=True)
        p = jnp.exp(s - top)
        total = jnp.sum(p, 0, keepdims=True)
        outs.append(mm(v_turned[64 * h : 64 * h + 64], p.astype(BF)) / total)
        lse_ref[0, h : h + 1, :] = top + jnp.log(total)
    o_ref[...] = jnp.transpose(jnp.concatenate(outs, 0)).astype(BF)


def attend_fwd(proj, length):
    rows, width = proj.shape[0], proj.shape[1] // 3
    pairs = width // 128
    block = lambda part: pl.BlockSpec((length, 128), lambda b, h: (b, part * pairs + h))
    return pl.pallas_call(
        attend_fwd_kernel,
        grid=(rows // length, pairs),
        in_specs=[block(0), block(1), block(2)],
        out_specs=[block(0), pl.BlockSpec((1, 2, length), lambda b, h: (h, 0, b))],
        out_shape=[
            jax.ShapeDtypeStruct((rows, width), BF),
            jax.ShapeDtypeStruct((pairs, 2, rows), F32),
        ],
        compiler_params=pltpu.CompilerParams(vmem_limit_bytes=48 << 20),
        cost_estimate=pl.CostEstimate(
            flops=rows * length * width * 8,
            bytes_accessed=rows * width * 8,
            transcendentals=rows * length * HEADS,
        ),
    )(proj, proj, proj)


def attend_bwd_kernel(q_ref, k_ref, v_ref, do_ref, lse_ref, d_ref, dq_ref, dk_ref, dv_ref):
    q = q_ref[...] * 0.125
    k, v, do = k_ref[...], v_ref[...], do_ref[...]
    lane = lax.broadcasted_iota(jnp.int32, k.shape, 1)
    dqs, dks, dvs = [], [], []
    for h in range(2):
        keep = (lane < 64) if h == 0 else (lane >= 64)
        s = mm(jnp.where(keep, k, jnp.zeros_like(k)), q, 1, 1)
        p = jnp.exp(s - lse_ref[0, h : h + 1, :])
        dp = mm(jnp.where(keep, v, jnp.zeros_like(v)), do, 1, 1)
        ds = (p * (dp - d_ref[0, h : h + 1, :])).astype(BF)
        dvs.append(mm(p.astype(BF), do))
        dks.append(mm(ds, q))
        dqs.append(mm(ds, k, 0, 0))
    low = lane < 64
    dq_ref[...] = (jnp.where(low, dqs[0], dqs[1]) * 0.125).astype(BF)
    dk_ref[...] = jnp.where(low, dks[0], dks[1]).astype(BF)
    dv_ref[...] = jnp.where(low, dvs[0], dvs[1]).astype(BF)


def attend_bwd(proj, d_out, lse, inner, length):
    rows, width = proj.shape[0], proj.shape[1] // 3
    pairs = width // 128
    block = lambda part: pl.BlockSpec((length, 128), lambda b, h: (b, part * pairs + h))
    row = pl.BlockSpec((1, 2, length), lambda b, h: (h, 0, b))
    result = jax.ShapeDtypeStruct((rows, width), BF)
    return pl.pallas_call(
        attend_bwd_kernel,
        grid=(rows // length, pairs),
        in_specs=[block(0), block(1), block(2), block(0), row, row],
        out_specs=[block(0)] * 3,
        out_shape=[result] * 3,
        compiler_params=pltpu.CompilerParams(vmem_limit_bytes=56 << 20),
        cost_estimate=pl.CostEstimate(
            flops=rows * length * width * 20,
            bytes_accessed=rows * width * 16,
            transcendentals=rows * length * HEADS,
        ),
    )(proj, proj, proj, d_out, lse, inner)


def head_blocks(width):
    own = jnp.arange(width)[None, :] // (width // HEADS) == jnp.arange(HEADS)[:, None]
    return own.astype(F32)


def spread_heads(rows):
    n, width = rows.shape
    return (rows[:, None, :] * head_blocks(width)[None]).reshape(n * HEADS, width)


def fold_heads(rows):
    total, width = rows.shape
    return jnp.sum(rows.reshape(total // HEADS, HEADS, width) * head_blocks(width)[None], 1)


def device_program(
    patches, captions, pairs,
    image_attend_in, image_attend_out, image_up_weight, image_up_bias, image_down_weight,
    image_vectors, probe_query_weight, probe_pair_weight, probe_out_weight, probe_up_weight,
    probe_up_bias, probe_down_weight, text_attend_in, text_attend_out, text_up_weight,
    text_up_bias, text_down_weight, text_vectors, text_head_weight, temp_bias,
):
    seq = lax.axis_size("seq")
    world = seq * lax.axis_size("dp")
    me = lax.axis_index("dp") * seq + lax.axis_index("seq")
    width = patches.shape[-1]
    head_width = width // HEADS
    factor = head_width ** (-0.5)
    hidden_width = image_up_weight.shape[1]
    part = width // world
    wide_part = hidden_width // world

    def gather(*weights):
        flat = jnp.concatenate([w.reshape(-1, width) for w in weights], 0)
        full = lax.all_gather(flat, ALL, axis=0)
        out, at = [], 0
        for w in weights:
            count = w.size // width
            piece = full[:, at : at + count]
            out.append(piece.reshape(world * w.shape[0], w.shape[1]))
            at += count
        return out

    small = jnp.concatenate(
        [image_vectors.reshape(-1), text_vectors.reshape(-1), image_up_bias, probe_up_bias, text_up_bias]
    )
    small_all = lax.all_gather(small, ALL, axis=0)
    sizes = [image_vectors.size, text_vectors.size, image_up_bias.size, probe_up_bias.size, text_up_bias.size]
    cuts = [sum(sizes[:i]) for i in range(len(sizes) + 1)]
    pieces = [small_all[:, cuts[i] : cuts[i + 1]].astype(F32) for i in range(len(sizes))]
    ivec = pieces[0].reshape(world, -1, part).transpose(1, 0, 2).reshape(-1, width)
    tvec = pieces[1].reshape(world, -1, part).transpose(1, 0, 2).reshape(-1, width)
    i_bias, p_bias, t_bias = (p.reshape(-1) for p in pieces[2:])

    (w_in,) = gather(image_attend_in)
    w_out, w_up, w_down = gather(image_attend_out, image_up_weight, image_down_weight)
    tw_in, tw_out, tw_up, tw_down, tw_head, pw_query, pw_pair, pw_out, pw_up, pw_down = gather(
        text_attend_in, text_attend_out, text_up_weight, text_down_weight, text_head_weight,
        probe_query_weight, probe_pair_weight, probe_out_weight, probe_up_weight, probe_down_weight,
    )

    def to_owner(x):
        return lax.all_to_all(x, "seq", 0, 1, tiled=True)

    x = to_owner(patches)
    own, length = x.shape[0], x.shape[1]
    x = x.reshape(own * length, width).astype(F32)
    captions_own = to_owner(captions)
    text_length = captions_own.shape[1]

    normed = layer_norm(x, ivec[0], ivec[1]).astype(BF)
    proj = mm(normed, w_in).astype(BF)
    mixed, lse = attend_fwd(proj, length)
    hidden = x + mm(mixed, w_out)
    second = layer_norm(hidden, ivec[2], ivec[3]).astype(BF)
    value, slope = gelu_pair(mm(second, w_up) + i_bias)
    active, slope = value.astype(BF), slope.astype(BF)
    block_out = hidden + mm(active, w_down) + ivec[4]
    final = layer_norm(block_out, ivec[5], ivec[6]).astype(BF)

    t_x = captions_own.astype(F32)
    t_normed = layer_norm(t_x, tvec[0], tvec[1]).astype(BF)
    t_last = t_normed[:, -1]
    tw_q, tw_k, tw_v = tw_in[:, :width], tw_in[:, width : 2 * width], tw_in[:, 2 * width :]
    t_q = mm(t_last, tw_q).astype(BF)
    t_keys = mm(spread_heads(t_q.astype(F32)).astype(BF), tw_k, 1, 1) * factor
    t_keys = t_keys.reshape(own, HEADS, width)
    k_high, k_low = split_two(t_keys)
    scores = jnp.einsum("bsd,bhd->bsh", t_normed, k_high, preferred_element_type=F32)
    scores += jnp.einsum("bsd,bhd->bsh", t_normed, k_low, preferred_element_type=F32)
    t_probs = jax.nn.softmax(scores, axis=1)
    t_used = jnp.einsum("bsh,bsd->bhd", t_probs, t_normed.astype(F32), precision=HIGH)
    t_mixed = fold_heads(mm(t_used.reshape(own * HEADS, width).astype(BF), tw_v)).astype(BF)
    t_hidden = t_x[:, -1] + mm(t_mixed, tw_out)
    t_second = layer_norm(t_hidden, tvec[2], tvec[3]).astype(BF)
    t_value, t_slope = gelu_pair(mm(t_second, tw_up) + t_bias)
    t_active = t_value.astype(BF)
    t_out = t_hidden + mm(t_active, tw_down) + tvec[4]
    t_final = layer_norm(t_out, tvec[5], tvec[6]).astype(BF)
    text_embed = mm(t_final, tw_head)

    pw_k, pw_v = pw_pair[:, :width], pw_pair[:, width:]
    probe_query = mm_exact(ivec[7:8], pw_query.astype(F32))
    p_keys = mm_exact(spread_heads(probe_query), pw_k.astype(F32), 1, 1) * factor
    k_high, k_low = split_two(p_keys)
    pool_scores = mm(k_high, final, 1, 1) + mm(k_low, final, 1, 1)
    pool_scores = pool_scores.reshape(HEADS, own, length)
    pool_probs = jax.nn.softmax(pool_scores, axis=-1)
    final_own = final.reshape(own, length, width)
    p_high, p_low = split_two(pool_probs)
    used = jnp.einsum("hbt,btd->bhd", p_high, final_own, preferred_element_type=F32)
    used += jnp.einsum("hbt,btd->bhd", p_low, final_own, preferred_element_type=F32)
    pooled = fold_heads(mm_exact(used.reshape(own * HEADS, width), pw_v.astype(F32)))
    head_start = mm_exact(pooled, pw_out.astype(F32))
    head_normed = layer_norm(head_start, ivec[8], ivec[9]).astype(BF)
    h_value, h_slope = gelu_pair(mm(head_normed, pw_up) + p_bias)
    head_active = h_value.astype(BF)
    image_embed = head_start + mm(head_active, pw_down) + ivec[10]

    embeds = lax.all_gather(jnp.stack([image_embed, text_embed], 1), ALL, axis=0, tiled=True)
    every_image, every_text = embeds[:, 0], embeds[:, 1]
    labels = (2 * pairs - 1).astype(F32)
    total = every_image.shape[0]
    i_scale = lax.rsqrt(jnp.sum(every_image * every_image, -1, keepdims=True) + EPS)
    t_scale = lax.rsqrt(jnp.sum(every_text * every_text, -1, keepdims=True) + EPS)
    z_i, z_t = every_image * i_scale, every_text * t_scale
    cosine = mm_exact(z_i, z_t, 1, 1)
    temper = jnp.exp(temp_bias[0])
    logits = cosine * temper + temp_bias[1]
    loss = -jnp.sum(jax.nn.log_sigmoid(labels * logits)) / total
    g = -labels * jax.nn.sigmoid(-labels * logits) / total
    grad_temp = jnp.stack([temper * jnp.sum(g * cosine), jnp.sum(g)])
    dz_i = temper * mm_exact(g, z_t)
    dz_t = temper * mm_exact(g, z_i, 0, 0)
    all_d_image = (dz_i - z_i * jnp.sum(z_i * dz_i, -1, keepdims=True)) * i_scale
    all_d_text = (dz_t - z_t * jnp.sum(z_t * dz_t, -1, keepdims=True)) * t_scale
    d_image = lax.dynamic_slice_in_dim(all_d_image, me * own, own, 0)
    d_text = lax.dynamic_slice_in_dim(all_d_text, me * own, own, 0)

    h_upper = mm_exact(d_image, pw_down.astype(F32), 1, 1) * h_slope
    h_norm = mm_exact(h_upper, pw_up.astype(F32), 1, 1)
    d_start, dv8, dv9 = norm_back(head_start, ivec[8], h_norm)
    d_start = d_image + d_start
    dv10 = jnp.sum(d_image, 0)
    d_pooled = mm_exact(d_start, pw_out.astype(F32), 1, 1)
    p_values = mm_exact(spread_heads(d_pooled), pw_v.astype(F32), 1, 1).reshape(own, HEADS, width)
    v_high, v_low = split_two(p_values)
    d_probs = jnp.einsum("bhd,btd->hbt", v_high, final_own, preferred_element_type=F32)
    d_probs += jnp.einsum("bhd,btd->hbt", v_low, final_own, preferred_element_type=F32)
    d_scores = pool_probs * (d_probs - jnp.sum(pool_probs * d_probs, -1, keepdims=True))
    s_high, s_low = split_two(d_scores)
    p_used = jnp.einsum("hbt,btd->bhd", s_high, final_own, preferred_element_type=F32)
    p_used += jnp.einsum("hbt,btd->bhd", s_low, final_own, preferred_element_type=F32)
    d_query = jnp.sum(fold_heads(mm_exact(p_used.reshape(own * HEADS, width), pw_k.astype(F32))), 0) * factor
    d_final = jnp.einsum(
        "hbt,bhd->btd",
        jnp.concatenate([s_high, p_high], 0),
        jnp.concatenate([jnp.broadcast_to(k_high[None], (own, HEADS, width)), v_high], 1),
        preferred_element_type=F32,
    ).reshape(own * length, width)
    dy, dv5, dv6 = norm_back(block_out, ivec[5], d_final)

    d_branch = dy.astype(BF)
    g_down = mm(active, d_branch, 0, 0)
    dv4 = jnp.sum(dy, 0)
    d_upper_f = mm(d_branch, w_down, 1, 1) * slope.astype(F32)
    d_upper = d_upper_f.astype(BF)
    g_bias = jnp.sum(d_upper_f, 0)
    g_up = mm(second, d_upper, 0, 0)
    d_hidden, dv2, dv3 = norm_back(hidden, ivec[2], mm(d_upper, w_up, 1, 1))
    d_hidden = dy + d_hidden
    d_attend = d_hidden.astype(BF)
    g_out = mm(mixed, d_attend, 0, 0)
    d_mixed = mm(d_attend, w_out, 1, 1).astype(BF)

    def scatter(*grads):
        flat = jnp.concatenate([g.astype(BF).reshape(world, -1, width) for g in grads], 1)
        mine = lax.psum_scatter(flat, ALL, scatter_dimension=0, tiled=False).astype(F32)
        out, at = [], 0
        for g in grads:
            count = g.size // world // width
            out.append(mine[at : at + count].reshape(g.shape[0] // world, g.shape[1]))
            at += count
        return out

    own_up, own_down, own_out = scatter(g_up, g_down, g_out)
    inner_rows = jnp.sum(
        (d_mixed.astype(F32) * mixed.astype(F32)).reshape(own * length, HEADS, head_width), -1
    ).T.reshape(HEADS // 2, 2, own * length)
    d_q, d_k, d_v = attend_bwd(proj, d_mixed, lse, inner_rows, length)
    g_in = jnp.concatenate([mm(normed, d, 0, 0) for d in (d_q, d_k, d_v)], 1)
    (own_in,) = scatter(g_in)
    d_normed = (
        mm(d_q, w_in[:, :width], 1, 1)
        + mm(d_k, w_in[:, width : 2 * width], 1, 1)
        + mm(d_v, w_in[:, 2 * width :], 1, 1)
    )
    d_x, dv0, dv1 = norm_back(x, ivec[0], d_normed)
    d_x = (d_hidden + d_x).reshape(own, length, width)

    def to_tokens(v):
        return lax.all_to_all(v.astype(BF), "seq", 1, 0, tiled=True).astype(F32)

    grad_patches = to_tokens(d_x)

    dt_final = mm_exact(d_text, tw_head.astype(F32), 1, 1)
    dt_out, tv5, tv6 = norm_back(t_out, tvec[5], dt_final)
    dt_branch = dt_out.astype(BF)
    tv4 = jnp.sum(dt_out, 0)
    dt_upper = (mm(dt_branch, tw_down, 1, 1) * t_slope).astype(BF)
    dt_hidden, tv2, tv3 = norm_back(t_hidden, tvec[2], mm(dt_upper, tw_up, 1, 1))
    dt_hidden = dt_out + dt_hidden
    dt_attend = dt_hidden.astype(BF)
    dt_mixed = mm(dt_attend, tw_out, 1, 1).astype(BF)
    t_values = mm(spread_heads(dt_mixed.astype(F32)).astype(BF), tw_v, 1, 1).reshape(own, HEADS, width)
    tv_high, tv_low = split_two(t_values)
    dt_probs = jnp.einsum("bsd,bhd->bsh", t_normed, tv_high, preferred_element_type=F32)
    dt_probs += jnp.einsum("bsd,bhd->bsh", t_normed, tv_low, preferred_element_type=F32)
    dt_scores = t_probs * (dt_probs - jnp.sum(t_probs * dt_probs, 1, keepdims=True))
    tk_used = jnp.einsum("bsh,bsd->bhd", dt_scores, t_normed.astype(F32), precision=HIGH)
    dt_q = fold_heads(mm(tk_used.reshape(own * HEADS, width).astype(BF), tw_k)) * factor
    dt_q = dt_q.astype(BF)
    dt_normed = jnp.einsum("bsh,bhd->bsd", dt_scores, t_keys, precision=HIGH)
    dt_normed += jnp.einsum("bsh,bhd->bsd", t_probs, t_values, precision=HIGH)
    dt_normed = dt_normed.at[:, -1].add(mm(dt_q, tw_q, 1, 1))
    flat_x = t_x.reshape(own * text_length, width)
    dt_x, tv0, tv1 = norm_back(flat_x, tvec[0], dt_normed.reshape(own * text_length, width))
    dt_x = dt_x.reshape(own, text_length, width).at[:, -1].add(dt_hidden)
    grad_captions = to_tokens(dt_x)

    whole = jnp.concatenate(
        [v.astype(F32) for v in (h_upper, d_start, d_pooled, dt_branch, dt_upper, dt_attend, dt_q, t_q, dt_mixed)], 1
    )
    whole = lax.all_gather(whole, ALL, axis=0, tiled=True)
    at = [0]

    def take(count):
        at[0] += count
        return whole[:, at[0] - count : at[0]]

    a_h_upper, a_start, a_pooled, a_branch, a_upper, a_attend, a_q, a_query, a_mixed = (
        take(c) for c in (hidden_width, width, width, width, hidden_width, width, width, width, width)
    )
    columns = [pooled, head_normed, t_last, t_mixed, t_second, t_final]
    columns += [used, t_used, tk_used * factor]
    columns += [head_active, t_active]
    columns = jnp.concatenate(
        [v.astype(F32).reshape(own, -1, width) for v in columns], 1
    )
    wide = 2 * (hidden_width // width)
    narrow = columns.shape[1] - wide
    cut = jnp.concatenate(
        [
            columns[:, :narrow].reshape(own, narrow, world, part).transpose(2, 0, 1, 3).reshape(world, own, -1),
            columns[:, narrow:].reshape(own, 2, world, wide_part).transpose(2, 0, 1, 3).reshape(world, own, -1),
        ],
        2,
    )
    cut = lax.all_to_all(cut, ALL, 0, 0, tiled=True).reshape(total, -1)
    slim = cut[:, : narrow * part].reshape(total, narrow, part)
    broad = cut[:, narrow * part :].reshape(total, 2, wide_part)

    def outer(rows, cols):
        return mm_exact(rows, cols, 0, 0)

    def outer_heads(rows, cols):
        cols = cols.reshape(total, HEADS, head_width)
        return jnp.einsum("chm,che->mhe", rows, cols, precision=HIGH).reshape(part, width)

    c_pooled, c_head, c_last, c_mixed, c_second, c_final = (slim[:, i] for i in range(6))
    c_used, ct_used, ctk_used = (slim[:, 6 + i * HEADS : 6 + (i + 1) * HEADS] for i in range(3))
    own_t_in = jnp.concatenate(
        [outer(c_last, a_q), outer_heads(ctk_used, a_query), outer_heads(ct_used, a_mixed)], 1
    )
    own_t_out = outer(c_mixed, a_attend)
    own_t_up = outer(c_second, a_upper)
    own_t_down = outer(broad[:, 1], a_branch)
    own_t_head = outer(c_final, all_d_text)
    own_p_out = outer(c_pooled, a_start)
    own_p_up = outer(c_head, a_h_upper)
    own_p_down = outer(broad[:, 0], all_d_image)
    own_p_values = outer_heads(c_used, a_pooled)

    summed = jnp.concatenate(
        [
            jnp.stack([dv0, dv1, dv2, dv3, dv4, dv5, dv6, dv8, dv9, dv10]),
            jnp.stack([tv0, tv1, tv2, tv3, tv4, tv5, tv6]),
            d_query[None],
            jnp.sum(p_used, 0),
            g_bias.reshape(-1, width),
        ],
        0,
    )
    summed = lax.psum(summed, ALL)
    total_query = summed[17]
    mine = lambda v, n: lax.dynamic_slice_in_dim(v, me * n, n, -1)
    own_probe = mine(ivec[7], part)
    own_p_query = own_probe[:, None] * total_query[None, :]
    dv7 = jnp.sum(probe_query_weight.astype(F32) * total_query[None, :], 1)
    pk_used = mine(summed[18 : 18 + HEADS], part)
    own_p_keys = jnp.einsum(
        "hm,he->mhe", pk_used, probe_query.reshape(HEADS, head_width) * factor
    ).reshape(part, width)
    own_p_pair = jnp.concatenate([own_p_keys, own_p_values], 1)
    ten = mine(summed[:10], part)
    own_ivec = jnp.concatenate([ten[:7], dv7[None], ten[7:]], 0)
    own_tvec = mine(summed[10:17], part)
    own_bias = mine(summed[18 + HEADS :].reshape(-1), wide_part)
    own_p_bias = mine(jnp.sum(a_h_upper, 0), wide_part)
    own_t_bias = mine(jnp.sum(a_upper, 0), wide_part)
    return (
        loss, grad_patches, grad_captions,
        own_in, own_out, own_up, own_bias, own_down, own_ivec,
        own_p_query, own_p_pair, own_p_out, own_p_up, own_p_bias, own_p_down,
        own_t_in, own_t_out, own_t_up, own_t_bias, own_t_down, own_tvec, own_t_head,
        grad_temp,
    )


MESH = pl.DeviceIdType.MESH

class Place:
    def __init__(self):
        i = lax.axis_index("dp")
        self.i, self.z = i, lax.axis_index("seq")
        self.y, self.x, self.c = i // 4, (i // 2) % 2, i % 2
        self.at_y = (i + 4 - 8 * self.y, self.z)
        self.at_x = (i + 2 - 4 * self.x, self.z)
        self.at_c = (i + 1 - 2 * self.c, self.z)

    def at_z(self, k):
        return (self.i, (self.z + k) % 4)

def greet(peers):
    barrier = pltpu.get_barrier_semaphore()
    for p in peers:
        pl.semaphore_signal(barrier, inc=1, device_id=p, device_id_type=MESH)
    pl.semaphore_wait(barrier, len(peers))

def gather_kernel(kinds, order, *refs):
    n = len(kinds)
    srcs, outs = refs[:n], refs[n : 2 * n]
    send, recv, local = refs[2 * n :]
    me = Place()
    y, x, c, z = me.y, me.x, me.c, me.z
    greet([me.at_z(1), me.at_z(2), me.at_z(3), me.at_x, me.at_y, me.at_c])
    ends = []

    def copy_of(a, slot, src, dst, dev):
        return pltpu.make_async_remote_copy(
            src, dst, send.at[a, slot], recv.at[a, slot], device_id=dev, device_id_type=MESH
        )

    def push(a, slot, src, dst, dev, arriving):
        copy = copy_of(a, slot, src, dst, dev)
        copy.start()
        ends.append(copy.wait_send)
        return copy_of(a, slot, src, arriving, dev).wait_recv

    def along(a, step, up):
        home = outs[a].at[y, x, c]
        if up:
            slab, go, to = z - step, (z - step >= 0) & (z < 3), me.at_z(1)
        else:
            slab, go, to = z + step, (z + step < 4) & (z > 0), me.at_z(3)
        slab = jnp.clip(slab, 0, 3)
        src = srcs[a] if step == 0 else home.at[slab]
        copy = copy_of(a, step + (0 if up else 3), src, home.at[slab], to)
        pl.when(go)(lambda: copy.start())
        ends.append(lambda: pl.when(go)(lambda: copy.wait_send()))

    def arrived(a, step, up):
        home = outs[a].at[y, x, c]
        if up:
            slab, come = z - 1 - step, z - 1 - step >= 0
        else:
            slab, come = z + 1 + step, z + 1 + step < 4
        slab = jnp.clip(slab, 0, 3)
        copy = copy_of(a, step + (0 if up else 3), home.at[slab], home.at[slab], me.at_z(1))
        pl.when(come)(lambda: copy.wait_recv())

    waits = {}

    def half(r, which, order_):
        if order_ != "S":
            return r
        n_ = r.shape[-1] // 2
        return r.at[..., 0:n_] if which == "C" else r.at[..., n_ : 2 * n_]

    def stage(a, s):
        kind, turn = kinds[a]
        src, out = srcs[a], outs[a]
        if kind in ("za", "zg"):
            own = src.at[z] if kind == "za" else src
            keep = pltpu.make_async_copy(own, out.at[z], local.at[a])
            keep.start()
            ends.append(keep.wait)
            for k in (1, 2, 3):
                to, fro = (z + k) % 4, (z + 4 - k) % 4
                s_ref = src.at[to] if kind == "za" else src
                ends.append(push(a, k - 1, s_ref, out.at[z], me.at_z(k), out.at[fro]))
            return
        turns = "CD" if turn == "S" else turn
        if kind != "full" and s == 0:
            own = src.at[z] if kind == "cols" else src
            keep = pltpu.make_async_copy(own, out.at[y, x, c, z] if kind == "cols" else out.at[y, x, c], local.at[a])
            keep.start()
            waits[a] = [keep.wait]
            for k in (1, 2, 3) if kind == "cols" else ():
                to, fro = (z + k) % 4, (z + 4 - k) % 4
                waits[a].append(push(a, k - 1, src.at[to], out.at[y, x, c, z], me.at_z(k), out.at[y, x, c, fro]))
        elif s == 0:
            keep = pltpu.make_async_copy(src, out.at[y, x, c, z], local.at[a])
            keep.start()
            waits[a] = [keep.wait]
            along(a, 0, True)
            along(a, 0, False)
        elif s in (1, 2):
            for up in (True, False):
                arrived(a, s - 1, up)
                along(a, s, up)
        elif s == 3:
            for up in (True, False) if kind == "full" else ():
                arrived(a, 2, up)
            for w in waits.pop(a):
                w()
            waits[a] = []
            for t in turns:
                cut = lambda r: half(r, t, turn)
                to, fro = (me.at_x, (y, 1 - x)) if t == "C" else (me.at_y, (1 - y, x))
                mine = cut(out.at[y, x, c])
                waits[a].append(push(a, 6 + (t == "D"), mine, mine, to, cut(out.at[fro[0], fro[1], c])))
        elif s == 4:
            for w in waits.pop(a):
                w()
            waits[a] = []
            for t in turns:
                cut = lambda r: half(r, t, turn)
                if t == "C":
                    mine, come, to = cut(out.at[y, :, c]), cut(out.at[1 - y, :, c]), me.at_y
                else:
                    mine, come, to = cut(out.at[:, x, c]), cut(out.at[:, 1 - x, c]), me.at_x
                waits[a].append(push(a, 8 + (t == "D"), mine, mine, to, come))
        elif s == 5:
            for w in waits.pop(a):
                w()
            mine = out.at[:, :, c]
            ends.append(push(a, 10, mine, mine, me.at_c, out.at[:, :, 1 - c]))

    for a, s in order:
        stage(a, s)
    for e in ends:
        e()


def gather(ops, kinds, order, cid):
    shapes = []
    for o, (kind, _) in zip(ops, kinds):
        s = {"full": (2, 2, 2, 4) + o.shape, "zg": (4,) + o.shape, "za": o.shape, "cols": (2, 2, 2) + o.shape, "plane": (2, 2, 2) + o.shape}[kind]
        shapes.append(jax.ShapeDtypeStruct(s, o.dtype))
    n = len(ops)
    return pl.pallas_call(
        partial(gather_kernel, kinds, order),
        out_shape=shapes,
        in_specs=[pl.BlockSpec(memory_space=pl.ANY)] * n,
        out_specs=[pl.BlockSpec(memory_space=pl.ANY)] * n,
        scratch_shapes=[
            pltpu.SemaphoreType.DMA((n, 11)),
            pltpu.SemaphoreType.DMA((n, 11)),
            pltpu.SemaphoreType.DMA((n,)),
        ],
        compiler_params=pltpu.CompilerParams(collective_id=cid, has_side_effects=True),
    )(*ops)


def reduce_kernel(g_ref, dx_ref, own_ref, moved_ref, from_c, acc_c, from_1, acc_1, from_2, acc_2, from_z, send, recv, local):
    me = Place()
    y, x, c, z = me.y, me.x, me.c, me.z
    greet([me.at_z(1), me.at_z(2), me.at_z(3), me.at_x, me.at_y, me.at_c])
    half = g_ref.shape[-1] // 2
    started = []

    def push(slot, src, dst, dev, arriving):
        copy = pltpu.make_async_remote_copy(src, dst, send.at[slot], recv.at[slot], device_id=dev, device_id_type=MESH)
        copy.start()
        started.append(copy)
        return pltpu.make_async_remote_copy(src, arriving, send.at[slot], recv.at[slot], device_id=dev, device_id_type=MESH)

    a_c = push(0, g_ref.at[:, :, 1 - c], from_c, me.at_c, from_c)
    home = pltpu.make_async_copy(g_ref.at[:, :, c], acc_c, local.at[0])
    home.start()
    rest = []
    for k in (1, 2, 3):
        to, fro = (z + k) % 4, (z + 4 - k) % 4
        rest.append(push(k, dx_ref.at[to], moved_ref.at[z], me.at_z(k), moved_ref.at[fro]))
    keep = pltpu.make_async_copy(dx_ref.at[z], moved_ref.at[z], local.at[1])
    keep.start()
    home.wait()
    a_c.wait_recv()
    f32 = lambda v: v.astype(jnp.float32)
    for a in range(2):
        for b in range(2):
            for q in range(4):
                acc_c[a, b, q] = (f32(acc_c[a, b, q]) + f32(from_c[a, b, q])).astype(acc_c.dtype)
    left, right = slice(0, half), slice(half, 2 * half)
    a_y = push(4, acc_c.at[1 - y, :, :, :, left], from_1.at[0], me.at_y, from_1.at[0])
    a_x = push(5, acc_c.at[:, 1 - x, :, :, right], from_1.at[1], me.at_x, from_1.at[1])
    a_y.wait_recv()
    for b in range(2):
        for q in range(4):
            acc_1[0, b, q] = (f32(acc_c[y, b, q, :, left]) + f32(from_1[0, b, q])).astype(acc_1.dtype)
    b_x = push(6, acc_1.at[0, 1 - x], from_2.at[0], me.at_x, from_2.at[0])
    a_x.wait_recv()
    for b in range(2):
        for q in range(4):
            acc_1[1, b, q] = (f32(acc_c[b, x, q, :, right]) + f32(from_1[1, b, q])).astype(acc_1.dtype)
    b_y = push(7, acc_1.at[1, 1 - y], from_2.at[1], me.at_y, from_2.at[1])
    b_x.wait_recv()
    for q in range(4):
        acc_2[q, :, left] = (f32(acc_1[0, x, q]) + f32(from_2[0, q])).astype(acc_2.dtype)
    b_y.wait_recv()
    for q in range(4):
        acc_2[q, :, right] = (f32(acc_1[1, y, q]) + f32(from_2[1, q])).astype(acc_2.dtype)
    last = []
    for k in (1, 2, 3):
        to, fro = (z + k) % 4, (z + 4 - k) % 4
        last.append(push(7 + k, acc_2.at[to], from_z.at[k - 1], me.at_z(k), from_z.at[k - 1]))
    total = f32(acc_2[z])
    for k in (1, 2, 3):
        last[k - 1].wait_recv()
        total += f32(from_z[k - 1])
    own_ref[...] = total
    keep.wait()
    for r in rest:
        r.wait_recv()
    for copy in started:
        copy.wait_send()

def reduce_and_move(g, dx, cid):
    rows, n = g.shape[0] // 32, g.shape[1]
    g = g.reshape(2, 2, 2, 4, rows, n)
    dx = dx.reshape(4, dx.shape[0] // 4, dx.shape[1])
    hbm = pl.BlockSpec(memory_space=pl.ANY)
    v = lambda *s: pltpu.VMEM(s, g.dtype)
    return pl.pallas_call(
        reduce_kernel,
        in_specs=[hbm, hbm],
        out_specs=[pl.BlockSpec(memory_space=pltpu.VMEM), hbm],
        out_shape=[jax.ShapeDtypeStruct((rows, n), jnp.float32), jax.ShapeDtypeStruct(dx.shape, dx.dtype)],
        scratch_shapes=[
            v(2, 2, 4, rows, n), v(2, 2, 4, rows, n), v(2, 2, 4, rows, n // 2), v(2, 2, 4, rows, n // 2),
            v(2, 4, rows, n // 2), v(4, rows, n), v(3, rows, n),
            pltpu.SemaphoreType.DMA((11,)), pltpu.SemaphoreType.DMA((11,)), pltpu.SemaphoreType.DMA((2,)),
        ],
        compiler_params=pltpu.CompilerParams(collective_id=cid, has_side_effects=True, vmem_limit_bytes=40 << 20),
    )(g, dx)

ROWS = 80

def middle_kernel(final_ref, block_ref, tokens_ref, tp_ref, downs_ref, outs_ref, ivec_ref, tvec_ref, pbias_ref, tbias_ref,
                  label_ref, temp_ref,
                  dy_ref, branch_ref, rows_ref, sums_ref, dcap_ref, loss_ref, dz_ref,
                  tn_ref, dn_ref, send_a, recv_a, send_l, recv_l, send_t, recv_t, send_sem, recv_sem):
    me = Place()
    z, i = me.z, me.i
    n_dp = recv_l.shape[0]
    plane = [((i + k) % n_dp, z) for k in range(1, n_dp)]
    greet([me.at_z(1), me.at_z(2), me.at_z(3)] + plane)
    width = final_ref.shape[1]
    part = width // 4
    started = []

    def exchange(n, values_for):
        for q in range(4):
            send_a[n, q] = values_for(q)
        recv_a[n, z] = send_a[n, z]
        arrive = []
        for k in (1, 2, 3):
            to, fro = (z + k) % 4, (z + 4 - k) % 4
            copy = pltpu.make_async_remote_copy(send_a.at[n, to], recv_a.at[n, z], send_sem.at[n, k - 1],
                                                recv_sem.at[n, k - 1], device_id=me.at_z(k), device_id_type=MESH)
            copy.start()
            started.append(copy)
            arrive.append(pltpu.make_async_remote_copy(send_a.at[n, to], recv_a.at[n, fro], send_sem.at[n, k - 1],
                                                       recv_sem.at[n, k - 1], device_id=me.at_z(k), device_id_type=MESH))

        def done():
            for a in arrive:
                a.wait_recv()
            return [recv_a[n, q] for q in range(4)]

        return done

    pad4 = jnp.zeros((4, width), F32)
    pad1 = jnp.zeros((1, width), F32)
    ivec, tvec = ivec_ref[...], tvec_ref[...]
    iv = lambda k: ivec[k:k + 1]
    tv = lambda k: tvec[k:k + 1]
    names = ["tq", "tk", "tv", "thead", "pq", "pk", "pv"]
    col = {n: 2 * width + 256 * k for k, n in enumerate(names)}
    small = lambda n: tp_ref[:, col[n]:col[n] + 256]
    p_up = lambda: tp_ref[:, 0:width]
    t_up = lambda: tp_ref[:, width:2 * width]
    t_down = lambda: downs_ref[:, 0:width]
    p_down = lambda: downs_ref[:, width:2 * width]
    t_out_w = lambda: outs_ref[0:part, 0:width]
    p_out_w = lambda: outs_ref[0:part, width:2 * width]
    lane = lax.broadcasted_iota(jnp.int32, (1, 256), 1)
    own = [((lane >= 64 * h) & (lane < 64 * h + 64)).astype(F32) for h in range(3)]

    def spread(a):
        return jnp.concatenate([a * own[h] for h in range(3)], 0)

    def fold(a):
        n = a.shape[0] // 3
        return sum(a[h * n:(h + 1) * n] * own[h] for h in range(3))

    t_x = tokens_ref[...].astype(F32)
    tn = layer_norm(t_x, tv(0), tv(1)).astype(BF)
    tn_ref[...] = tn.astype(F32)
    last_at = [3 * 64 + 16 * c + 15 for c in range(4)]
    t_last = jnp.concatenate([tn_ref[r:r + 1, :] for r in last_at], 0)
    x_last = jnp.concatenate([tokens_ref[3 * 64 + 16 * c:3 * 64 + 16 * c + 16, :].astype(F32)[15:16] for c in range(4)], 0)
    t_q = mm(t_last.astype(BF), small("tq")).astype(BF).astype(F32)
    t_keys = mm(spread(t_q).astype(BF), small("tk"), 1, 1) * 0.125
    scores = mm_two(t_keys, tn, 1)
    col_id = (lax.broadcasted_iota(jnp.int32, scores.shape, 1) // 16) % 4
    row_id = lax.broadcasted_iota(jnp.int32, scores.shape, 0) % 4
    mine = col_id == row_id
    top = jnp.max(jnp.where(mine, scores, -1e30), -1, keepdims=True)
    e = jnp.where(mine, jnp.exp(jnp.where(mine, scores - top, 0.0)), 0.0)
    t_probs = e / jnp.sum(e, -1, keepdims=True)
    t_used = mm_two(t_probs, tn)
    t_mixed = fold(mm(t_used.astype(BF), small("tv"))).astype(BF)
    t_part = mm(t_mixed[:, 0:part], t_out_w())

    p_q = mm(iv(7).astype(BF), small("pq"))
    p_keys_my = mm_two(spread(p_q), small("pk"), 1) * 0.125
    block = jnp.concatenate([t_part, p_keys_my, pad1], 0)
    x0 = exchange(0, lambda q: block)()
    t_hidden = x_last + (x0[0] + x0[1] + x0[2] + x0[3])[0:4]
    p_keys = jnp.concatenate([x0[q][4:7] for q in range(4)], 0)
    t_second = layer_norm(t_hidden, tv(2), tv(3)).astype(BF)
    t_value, t_slope = gelu_pair(mm(t_second, t_up()) + tbias_ref[...])
    t_active = t_value.astype(BF)
    t_part = mm(t_active, t_down())
    final = final_ref[...]
    p_scores = mm_two(p_keys, final, 1)
    e = jnp.exp(p_scores - jnp.max(p_scores, -1, keepdims=True))
    p_probs = e / jnp.sum(e, -1, keepdims=True)
    used = mm_two(p_probs, final)
    x1 = exchange(1, lambda q: jnp.concatenate([t_part, used[3 * q:3 * q + 3], pad1], 0))()
    t_out = t_hidden + (x1[0] + x1[1] + x1[2] + x1[3])[0:4] + tv(4)
    t_final = layer_norm(t_out, tv(5), tv(6)).astype(BF)
    t_piece = mm(t_final, small("thead"))
    got = jnp.concatenate([x1[q][4 + h:5 + h] for h in range(3) for q in range(4)], 0)
    pooled = fold(mm_two(got, small("pv")))
    h_part = mm_two(pooled[:, 0:part], p_out_w())
    block = jnp.concatenate([h_part, jnp.concatenate([t_piece[:, 0:part], jnp.zeros((4, width - part), F32)], 1)], 0)
    x2 = exchange(2, lambda q: block)()
    h_start = (x2[0] + x2[1] + x2[2] + x2[3])[0:4]
    text_embed = jnp.concatenate([x2[q][4:8, 0:part] for q in range(4)], 1)
    h_normed = layer_norm(h_start, iv(8), iv(9)).astype(BF)
    h_value, h_slope = gelu_pair(mm(h_normed, p_up()) + pbias_ref[...])
    h_active = h_value.astype(BF)
    h_part = mm(h_active, p_down())
    block = jnp.concatenate([h_part, pad4], 0)
    x3 = exchange(3, lambda q: block)()
    image_embed = h_start + ((x3[0] + x3[1] + x3[2] + x3[3])[0:4] + iv(10))
    send_l[...] = jnp.concatenate([image_embed, text_embed], 0)
    recv_l[i] = send_l[...]
    arrive = []
    for k in range(1, n_dp):
        copy = pltpu.make_async_remote_copy(send_l, recv_l.at[i], send_sem.at[8, k], recv_sem.at[8, k],
                                            device_id=plane[k - 1], device_id_type=MESH)
        copy.start()
        started.append(copy)
        arrive.append(pltpu.make_async_remote_copy(send_l, recv_l.at[(i + n_dp - k) % n_dp], send_sem.at[8, k], recv_sem.at[8, k],
                                                   device_id=plane[k - 1], device_id_type=MESH))
    for a in arrive:
        a.wait_recv()
    every = jnp.concatenate([recv_l[k] for k in range(n_dp)], 0)
    scale = lax.rsqrt(jnp.sum(every * every, -1, keepdims=True) + EPS)
    unit = every * scale
    cosine = mm_exact(unit, unit, 1, 1)
    temper = jnp.exp(jnp.full((1, 1), temp_ref[0], F32))
    logits = cosine * temper + temp_ref[1]
    label = label_ref[...]
    valid = label != 0.0
    signed = label * logits
    total = n_dp * 4
    nll = jnp.maximum(-signed, 0.0) + jnp.log(1.0 + jnp.exp(-jnp.abs(signed)))
    add_all = lambda a: jnp.sum(jnp.sum(a, -1, keepdims=True), 0, keepdims=True)
    loss = add_all(jnp.where(valid, nll, 0.0)) / total
    g = jnp.where(valid, -label / (1.0 + jnp.exp(signed)), 0.0) / total
    gt0 = temper * add_all(g * cosine)
    gt1 = add_all(g)
    at = lax.broadcasted_iota(jnp.int32, (8, 128), 1)
    loss_ref[...] = jnp.where(at == 0, loss, jnp.where(at == 1, gt0, gt1))
    dz = temper * mm_exact(g + jnp.transpose(g), unit)
    dz_ref[...] = (dz - unit * jnp.sum(unit * dz, -1, keepdims=True)) * scale
    d_both = dz_ref[pl.ds(pl.multiple_of(8 * i, 8), 8), :]
    d_image, d_text = d_both[0:4], d_both[4:8]

    dh_upper = mm_two(d_image, p_down(), 1) * h_slope
    h_part = mm_two(dh_upper, p_up(), 1)
    d_text_my = sum(jnp.where(z == q, d_text[:, part * q:part * q + part], 0.0) for q in range(4))
    t_part = mm_two(d_text_my, small("thead")[:, 0:part], 1)
    block = jnp.concatenate([h_part, t_part], 0)
    x4 = exchange(4, lambda q: block)()
    both = x4[0] + x4[1] + x4[2] + x4[3]
    d_start, dv8, dv9 = norm_back_rows(h_start, iv(8), both[0:4])
    d_start = d_image + d_start
    dv10 = jnp.sum(d_image, 0, keepdims=True)
    d_pooled = mm_two(d_start, p_out_w(), 1)
    d_pooled = jnp.concatenate([d_pooled, jnp.zeros((4, 256 - part), F32)], 1)
    p_values_my = mm_two(spread(d_pooled), small("pv"), 1)
    dt_out, tv5, tv6 = norm_back_rows(t_out, tv(5), both[4:8])
    tv4 = jnp.sum(dt_out, 0, keepdims=True)
    dt_branch = dt_out.astype(BF)
    dt_upper = (mm(dt_branch, t_down(), 1, 1) * t_slope).astype(BF)
    t_part = mm(dt_upper, t_up(), 1, 1)
    x5 = exchange(5, lambda q: jnp.concatenate(
        [t_part] + [p_values_my[4 * h + q:4 * h + q + 1] for h in range(3)] + [pad1], 0))()
    dt_hidden, tv2, tv3 = norm_back_rows(t_hidden, tv(2), (x5[0] + x5[1] + x5[2] + x5[3])[0:4])
    dt_hidden = dt_out + dt_hidden
    dt_attend = dt_hidden.astype(BF)
    dt_mixed = mm(dt_attend, t_out_w(), 1, 1).astype(BF).astype(F32)
    dt_mixed = jnp.concatenate([dt_mixed, jnp.zeros((4, 256 - part), F32)], 1)
    t_values = mm(spread(dt_mixed).astype(BF), small("tv"), 1, 1)
    dt_probs = mm_two(t_values, tn, 1)
    dt_scores = t_probs * (dt_probs - jnp.sum(t_probs * dt_probs, -1, keepdims=True))
    tk_used = mm_two(dt_scores, tn) * 0.125
    dt_q = fold(mm(tk_used.astype(BF), small("tk"))).astype(BF)
    dn = mm(dt_scores.astype(BF), t_keys.astype(BF), 0, 0) + mm(t_probs.astype(BF), t_values.astype(BF), 0, 0)
    row_at = lax.broadcasted_iota(jnp.int32, dn.shape, 0)
    dq_back = mm(dt_q, small("tq"), 1, 1)
    for c in range(4):
        dn = dn + jnp.where(row_at == last_at[c], dq_back[c:c + 1], 0.0)
    dn_ref[...] = dn.astype(BF)
    p_values = jnp.concatenate([x5[q][4:7] for q in range(4)], 0)
    d_probs = mm_two(p_values, final, 1)
    d_scores = p_probs * (d_probs - jnp.sum(p_probs * d_probs, -1, keepdims=True))
    p_used = mm_two(d_scores, final) * 0.125
    x6 = exchange(6, lambda q: jnp.concatenate([p_used[3 * q:3 * q + 3], pad1, pad4], 0))
    arrive = []
    for k in (1, 2, 3):
        to, fro = (z + k) % 4, (z + 4 - k) % 4
        rows_to = dn_ref.at[pl.ds(pl.multiple_of(64 * to, 64), 64), :]
        copy = pltpu.make_async_remote_copy(rows_to, recv_t.at[z], send_sem.at[7, k], recv_sem.at[7, k],
                                            device_id=me.at_z(k), device_id_type=MESH)
        copy.start()
        started.append(copy)
        arrive.append(pltpu.make_async_remote_copy(rows_to, recv_t.at[fro], send_sem.at[7, k], recv_sem.at[7, k],
                                                   device_id=me.at_z(k), device_id_type=MESH))
    s_high, s_low = split_two(d_scores)
    q_high, q_low = split_two(p_probs)
    k_high, k_low = split_two(p_keys)
    v_high, v_low = split_two(p_values)
    left = jnp.concatenate([s_high.astype(F32), q_high.astype(F32)], 0)
    right = jnp.concatenate([k_high.astype(F32), v_high.astype(F32)], 0).astype(BF)
    send_t[...] = jnp.transpose(jnp.concatenate([left, jnp.zeros((104, left.shape[1]), F32)], 0))
    right = jnp.concatenate([right, jnp.zeros((104, width), BF)], 0)
    sums_ref[...] = jnp.zeros_like(sums_ref)
    tile = 128

    def step(n, carry):
        at_rows = pl.ds(pl.multiple_of(n * tile, tile), tile)
        d_final = mm(send_t[at_rows, :].astype(BF), right)
        d_y, gain, shift = norm_back_rows(block_ref[at_rows, :], iv(5), d_final)
        dy_ref[at_rows, :] = d_y
        branch_ref[at_rows, :] = d_y.astype(BF)
        sums_ref[5:6] += gain
        sums_ref[6:7] += shift
        sums_ref[4:5] += jnp.sum(d_y, 0, keepdims=True)
        return carry

    lax.fori_loop(0, final_ref.shape[0] // tile, step, 0)
    got6 = x6()
    w_got = jnp.concatenate([got6[q][h:h + 1] for h in range(3) for q in range(4)], 0)
    dq_rows = fold(mm_two(w_got, small("pk")))
    dq_my = jnp.sum(dq_rows, 0, keepdims=True)
    recv_t[z] = dn_ref[pl.ds(pl.multiple_of(64 * z, 64), 64), :]
    for a in arrive:
        a.wait_recv()
    dt_normed = sum(recv_t[q].astype(F32) for q in range(4))
    x_mine = tokens_ref[pl.ds(pl.multiple_of(64 * z, 64), 64), :].astype(F32)
    d_cap, tv0, tv1 = norm_back_rows(x_mine, tv(0), dt_normed)
    row_c = lax.broadcasted_iota(jnp.int32, d_cap.shape, 0)
    for c in range(4):
        d_cap = d_cap + jnp.where((row_c == 16 * c + 15) & (z == 3), dt_hidden[c:c + 1], 0.0)
    dcap_ref[...] = d_cap
    first = (z == 0).astype(F32)
    sums_ref[8:9] = dv8 * first
    sums_ref[9:10] = dv9 * first
    sums_ref[10:11] = dv10 * first
    sums_ref[11:12] = tv0
    sums_ref[12:13] = tv1
    sums_ref[13:14] = tv2 * first
    sums_ref[14:15] = tv3 * first
    sums_ref[15:16] = tv4 * first
    sums_ref[16:17] = tv5 * first
    sums_ref[17:18] = tv6 * first
    own_row = lambda a: sum(jnp.where(z == q, a[q:q + 1].astype(F32), 0.0) for q in range(4))
    pick = lambda a: a[:, 0:part].astype(F32)
    wide = jnp.concatenate
    pieces = [
        dh_upper, dt_upper.astype(F32), h_active.astype(F32), t_active.astype(F32),
        wide([pick(d_pooled), pick(pooled), pick(dt_q), pick(t_q)], 1),
        wide([pick(dt_mixed), pick(t_mixed), jnp.broadcast_to(pick(dq_my), (4, part)), jnp.broadcast_to(pick(p_q), (4, part))], 1),
        own_row(h_normed), own_row(d_start), own_row(t_last), own_row(t_second),
        own_row(dt_attend), own_row(dt_branch), own_row(t_final), pad1,
        used, t_used, tk_used, p_used,
    ]
    rows_ref[...] = jnp.concatenate(pieces, 0).astype(BF)
    for copy in started:
        copy.wait_send()

def middle(final, block_out, tokens, tp, downs, outs, ivec, tvec, pbias, tbias, label, temp, cid, n_dp):
    length, width = final.shape
    v = pl.BlockSpec(memory_space=pltpu.VMEM)
    f = lambda *s: jax.ShapeDtypeStruct(s, F32)
    return pl.pallas_call(
        middle_kernel,
        in_specs=[v] * 11 + [pl.BlockSpec(memory_space=pltpu.SMEM)],
        out_specs=[v] * 7,
        out_shape=[f(length, width), jax.ShapeDtypeStruct((length, width), BF), jax.ShapeDtypeStruct((ROWS, width), BF), f(24, width), f(64, width), f(8, 128), f(8 * n_dp, width)],
        scratch_shapes=[
            pltpu.VMEM((256, width), F32), pltpu.VMEM((256, width), BF),
            pltpu.VMEM((7, 4, 8, width), F32), pltpu.VMEM((7, 4, 8, width), F32),
            pltpu.VMEM((8, width), F32), pltpu.VMEM((n_dp, 8, width), F32),
            pltpu.VMEM((length, 128), F32), pltpu.VMEM((4, 64, width), BF),
            pltpu.SemaphoreType.DMA((9, 8)), pltpu.SemaphoreType.DMA((9, 8)),
        ],
        compiler_params=pltpu.CompilerParams(collective_id=cid, has_side_effects=True, vmem_limit_bytes=50 << 20),
    )(final, block_out, tokens, tp, downs, outs, ivec, tvec, pbias, tbias, label, temp)


class Spread:
    stages = 6

    def __init__(self, me, src, out, send, recv, local):
        self.me, self.src, self.out, self.send, self.recv, self.local = me, src, out, send, recv, local

    def moves(self, s):
        me, out = self.me, self.out
        y, x, c, z = me.y, me.x, me.c, me.z
        if s < 3:
            home = out.at[y, x, c]
            for up in (True, False):
                step = -s if up else s
                slab, come = z + step, z + step + (-1 if up else 1)
                go = ((slab >= 0) & (z < 3)) if up else ((slab < 4) & (z > 0))
                arrives = (come >= 0) & (come < 4)
                slab, come = jnp.clip(slab, 0, 3), jnp.clip(come, 0, 3)
                src = self.src if s == 0 else home.at[slab]
                yield s + (0 if up else 3), src, home.at[slab], me.at_z(1 if up else 3), go, home.at[come], arrives
        elif s == 5:
            mine = out.at[:, :, c]
            yield 10, mine, mine, me.at_c, None, out.at[:, :, 1 - c], None
        else:
            n = out.shape[-1] // 2
            left, right = (lambda r: r.at[..., 0:n]), (lambda r: r.at[..., n : 2 * n])
            if s == 3:
                own = out.at[y, x, c]
                yield 6, left(own), left(own), me.at_x, None, left(out.at[y, 1 - x, c]), None
                yield 7, right(own), right(own), me.at_y, None, right(out.at[1 - y, x, c]), None
            else:
                own = out.at[y, :, c]
                yield 8, left(own), left(own), me.at_y, None, left(out.at[1 - y, :, c]), None
                own = out.at[:, x, c]
                yield 9, right(own), right(own), me.at_x, None, right(out.at[:, 1 - x, c]), None

    def each(self, s, act):
        for slot, src, dst, dev, go, come, arrives in self.moves(s):
            make = lambda a, b: pltpu.make_async_remote_copy(
                a, b, self.send.at[slot], self.recv.at[slot], device_id=dev, device_id_type=MESH
            )
            if act == "arrived":
                copy, when = make(src, come).wait_recv, arrives
            else:
                copy, when = getattr(make(src, dst), "start" if act == "start" else "wait_send"), go
            if when is None:
                copy()
            else:
                pl.when(when)(lambda: copy())

    def keep(self):
        me = self.me
        return pltpu.make_async_copy(self.src, self.out.at[me.y, me.x, me.c, me.z], self.local)

    def begin(self, s):
        if s == 0:
            self.keep().start()
        else:
            self.each(s - 1, "arrived")
        if s == 3:
            self.keep().wait()
        self.each(s, "start")

    def finish(self):
        self.each(5, "arrived")
        for s in range(6):
            self.each(s, "sent")


def attend_bwd_kernel_hosting(q_ref, k_ref, v_ref, do_ref, lse_ref, d_ref, rows_ref, dq_ref, dk_ref, dv_ref, all_ref, send, recv, local):
    h_at = pl.program_id(0)
    me = Place()
    spread = Spread(me, rows_ref, all_ref, send, recv, local)

    def first():
        greet([me.at_z(1), me.at_z(2), me.at_z(3), me.at_x, me.at_y, me.at_c])
        spread.begin(0)

    pl.when(h_at == 0)(first)
    for s in range(1, 6):
        pl.when(h_at == s)(partial(spread.begin, s))
    q = q_ref[...] * 0.125
    k, v, do = k_ref[...], v_ref[...], do_ref[...]
    lane = lax.broadcasted_iota(jnp.int32, k.shape, 1)
    dqs, dks, dvs = [], [], []
    for h in range(2):
        keep = (lane < 64) if h == 0 else (lane >= 64)
        s = mm(jnp.where(keep, k, jnp.zeros_like(k)), q, 1, 1)
        p = jnp.exp(s - lse_ref[0, h : h + 1, :])
        dp = mm(jnp.where(keep, v, jnp.zeros_like(v)), do, 1, 1)
        ds = (p * (dp - d_ref[0, h : h + 1, :])).astype(BF)
        dvs.append(mm(p.astype(BF), do))
        dks.append(mm(ds, q))
        dqs.append(mm(ds, k, 0, 0))
    low = lane < 64
    dq_ref[...] = (jnp.where(low, dqs[0], dqs[1]) * 0.125).astype(BF)
    dk_ref[...] = jnp.where(low, dks[0], dks[1]).astype(BF)
    dv_ref[...] = jnp.where(low, dvs[0], dvs[1]).astype(BF)
    pl.when(h_at == 5)(spread.finish)


def attend_bwd_and_spread(proj, d_out, lse, inner, rows, cid):
    length, width = proj.shape[0], proj.shape[1] // 3
    pairs = width // 128
    block = lambda part: pl.BlockSpec((length, 128), lambda h: (0, part * pairs + h))
    row = pl.BlockSpec((1, 2, length), lambda h: (h, 0, 0))
    hbm = pl.BlockSpec(memory_space=pl.ANY)
    result = jax.ShapeDtypeStruct((length, width), BF)
    return pl.pallas_call(
        attend_bwd_kernel_hosting,
        grid=(pairs,),
        in_specs=[block(0), block(1), block(2), block(0), row, row, hbm],
        out_specs=[block(0)] * 3 + [hbm],
        out_shape=[result] * 3 + [jax.ShapeDtypeStruct((2, 2, 2, 4) + rows.shape, rows.dtype)],
        scratch_shapes=[pltpu.SemaphoreType.DMA((11,)), pltpu.SemaphoreType.DMA((11,)), pltpu.SemaphoreType.DMA],
        compiler_params=pltpu.CompilerParams(collective_id=cid, has_side_effects=True, vmem_limit_bytes=56 << 20),
    )(proj, proj, proj, d_out, lse, inner, rows)


def mlp_fwd_kernel(x_ref, mixed_ref, wo_ref, wu_ref, wd_ref, bias_ref, vec_ref,
                   hidden_ref, second_ref, active_ref, slope_ref, block_ref, final_ref, total):
    k = pl.program_id(0)
    vec = vec_ref[...]

    @pl.when(k == 0)
    def _():
        hidden = x_ref[...].astype(F32) + mm(mixed_ref[...], wo_ref[...])
        hidden_ref[...] = hidden
        second_ref[...] = layer_norm(hidden, vec[2:3], vec[3:4]).astype(BF)
        total[...] = hidden + vec[4:5]

    value, slope = gelu_pair(mm(second_ref[...], wu_ref[...]) + bias_ref[0])
    active = value.astype(BF)
    active_ref[...] = active
    slope_ref[...] = slope.astype(BF)
    total[...] += mm(active, wd_ref[...])

    @pl.when(k == pl.num_programs(0) - 1)
    def _():
        block_ref[...] = total[...]
        final_ref[...] = layer_norm(total[...], vec[5:6], vec[6:7]).astype(BF)


def mlp_fwd(x, mixed, main, bias, vec, fold):
    rows, width = mixed.shape
    whole = pl.BlockSpec((rows, width), lambda k: (0, 0))
    tile = pl.BlockSpec((rows, width), lambda k: (0, k))
    at = lambda f: pl.BlockSpec((width, width), lambda k: (0, f(k)))
    s = lambda n, t: jax.ShapeDtypeStruct((rows, n * width), t)
    return pl.pallas_call(
        mlp_fwd_kernel,
        grid=(fold,),
        in_specs=[whole, whole, at(lambda k: 0), at(lambda k: 1 + k), at(lambda k: 1 + fold + k),
                  pl.BlockSpec((1, 1, width), lambda k: (k, 0, 0)), pl.BlockSpec(vec.shape, lambda k: (0, 0))],
        out_specs=[whole, whole, tile, tile, whole, whole],
        out_shape=[s(1, F32), s(1, BF), s(fold, BF), s(fold, BF), s(1, F32), s(1, BF)],
        scratch_shapes=[pltpu.VMEM((rows, width), F32)],
        compiler_params=pltpu.CompilerParams(vmem_limit_bytes=56 << 20),
    )(x, mixed, main, main, main, bias.reshape(fold, 1, width), vec)


def mlp_bwd_kernel(dy_ref, branch_ref, active_ref, slope_ref, second_ref, hidden_ref, mixed_ref,
                   wo_ref, wu_ref, wd_ref, vec_ref,
                   g_ref, dhid_ref, dmix_ref, inner_ref, bias_ref, dvec_ref, total):
    k = pl.program_id(0)
    fold = pl.num_programs(0)
    width = mixed_ref.shape[1]
    branch = branch_ref[...]
    columns = lambda n: pl.ds(pl.multiple_of(n * width, width), width)
    g_ref[:, columns(1 + fold + k)] = mm(active_ref[...], branch, 0, 0).astype(BF)
    d_upper_f = mm(branch, wd_ref[...], 1, 1) * slope_ref[...].astype(F32)
    bias_ref[0] = jnp.sum(d_upper_f, 0, keepdims=True)
    d_upper = d_upper_f.astype(BF)
    g_ref[:, columns(1 + k)] = mm(second_ref[...], d_upper, 0, 0).astype(BF)
    back = mm(d_upper, wu_ref[...], 1, 1)

    @pl.when(k == 0)
    def _():
        total[...] = back

    @pl.when(k > 0)
    def _():
        total[...] += back

    @pl.when(k == fold - 1)
    def _():
        vec = vec_ref[...]
        d_hidden, gain, shift = norm_back_rows(hidden_ref[...], vec[2:3], total[...])
        dvec_ref[0:1] = gain
        dvec_ref[1:2] = shift
        d_hidden = dy_ref[...] + d_hidden
        dhid_ref[...] = d_hidden
        d_attend = d_hidden.astype(BF)
        mixed = mixed_ref[...]
        g_ref[:, 0:width] = mm(mixed, d_attend, 0, 0).astype(BF)
        d_mixed = mm(d_attend, wo_ref[...], 1, 1).astype(BF)
        dmix_ref[...] = d_mixed
        head = lax.broadcasted_iota(jnp.int32, (16, width), 0)
        lane = lax.broadcasted_iota(jnp.int32, (16, width), 1)
        own = (lane // (width // HEADS) == head).astype(BF)
        high, low = split_two(d_mixed.astype(F32) * mixed.astype(F32))
        sums = mm(own, high, 1, 1) + mm(own, low, 1, 1)
        for h in range(HEADS // 2):
            inner_ref[h] = sums[2 * h : 2 * h + 2]


def mlp_bwd(dy, branch, active, slope, second, hidden, mixed, main, vec, fold):
    rows, width = mixed.shape
    whole = pl.BlockSpec((rows, width), lambda k: (0, 0))
    tile = pl.BlockSpec((rows, width), lambda k: (0, k))
    at = lambda f: pl.BlockSpec((width, width), lambda k: (0, f(k)))
    f = lambda *s: jax.ShapeDtypeStruct(s, F32)
    return pl.pallas_call(
        mlp_bwd_kernel,
        grid=(fold,),
        in_specs=[whole, whole, tile, tile, whole, whole, whole,
                  at(lambda k: 0), at(lambda k: 1 + k), at(lambda k: 1 + fold + k), pl.BlockSpec(vec.shape, lambda k: (0, 0))],
        out_specs=[pl.BlockSpec((width, (1 + 2 * fold) * width), lambda k: (0, 0)), whole, whole,
                   pl.BlockSpec((HEADS // 2, 2, rows), lambda k: (0, 0, 0)),
                   pl.BlockSpec((1, 1, width), lambda k: (k, 0, 0)), pl.BlockSpec((8, width), lambda k: (0, 0))],
        out_shape=[jax.ShapeDtypeStruct((width, (1 + 2 * fold) * width), BF), f(rows, width),
                   jax.ShapeDtypeStruct((rows, width), BF), f(HEADS // 2, 2, rows), f(fold, 1, width), f(8, width)],
        scratch_shapes=[pltpu.VMEM((rows, width), F32)],
        compiler_params=pltpu.CompilerParams(vmem_limit_bytes=60 << 20),
    )(dy, branch, active, slope, second, hidden, mixed, main, main, main, vec)


def project_bwd_kernel(dq_ref, dk_ref, dv_ref, normed_ref, w_ref, x_ref, dhid_ref, sums_ref, vec_ref, g_ref, dx_ref):
    width = dq_ref.shape[1]
    normed = normed_ref[...]
    back = None
    for n, ref in enumerate((dq_ref, dk_ref, dv_ref)):
        d = ref[...]
        g_ref[:, n * width : (n + 1) * width] = mm(normed, d, 0, 0).astype(BF)
        part = mm(d, w_ref[:, n * width : (n + 1) * width], 1, 1)
        back = part if back is None else back + part
    d_x, gain, shift = norm_back_rows(x_ref[...].astype(F32), vec_ref[0:1], back)
    dx_ref[...] = (dhid_ref[...] + d_x).astype(BF)
    sums = jnp.concatenate([gain, shift, sums_ref[2:, :]], 0)
    sums = jnp.concatenate([sums, jnp.zeros((128 - sums.shape[0], width), F32)], 0)
    g_ref[:, 3 * width : 3 * width + 128] = jnp.transpose(sums).astype(BF)
    g_ref[:, 3 * width + 128 : 3 * width + 256] = jnp.zeros((width, 128), BF)


def project_bwd(dq, dk, dv, normed, w_in, x, d_hidden, sums, vec):
    rows, width = dq.shape
    v = pl.BlockSpec(memory_space=pltpu.VMEM)
    return pl.pallas_call(
        project_bwd_kernel,
        in_specs=[v] * 9,
        out_specs=[v] * 2,
        out_shape=[jax.ShapeDtypeStruct((width, 3 * width + 256), BF), jax.ShapeDtypeStruct((rows, width), BF)],
        compiler_params=pltpu.CompilerParams(vmem_limit_bytes=56 << 20),
    )(dq, dk, dv, normed, w_in, x, d_hidden, sums, vec)


def outer_kernel(rows_ref, dimage_ref, dtext_ref,
                 pup_ref, tup_ref, pdown_ref, tdown_ref, pout_ref, tout_ref, thead_ref,
                 tq_ref, tk_ref, tv_ref, pv_ref, pk_ref, bias_ref):
    at_dp, z = lax.axis_index("dp"), lax.axis_index("seq")
    n_dp, n_z = 8, 4
    me = at_dp * n_z + z
    width = rows_ref.shape[2]
    part, quarter = width // 32, width // n_z
    wide_part = 4 * part
    n = n_dp * n_z
    each = quarter // part

    def iota(shape, d):
        return lax.broadcasted_iota(jnp.int32, shape, d)

    def selector(count, first):
        return (iota((count, width), 1) == iota((count, width), 0) + first).astype(BF)

    def group(r):
        return jnp.concatenate([rows_ref[r + c] for c in range(4)], 0)

    cols = jnp.concatenate(
        [mm(selector(part, part * me), rows_ref[r], 1, 1) for r in range(24, 80)], 1
    ).astype(BF)
    get = lambda r, count=1: cols[:, n * (r - 24) : n * (r - 24 + count)]
    a, b = iota((4 * n, n), 0), iota((4 * n, n), 1)
    same = ((a % n) // n_z == b // n_z) & (a // n == b % n_z)
    keep = lambda which: (same & (a % n_z == which)).astype(BF)
    units = selector(wide_part, wide_part * at_dp)
    heads = selector(part, quarter + part * (me % each))
    to_mine, to_head = keep(z), keep(me // each)
    chosen = lambda sel, r, perm: mm(mm(sel, group(r), 1, 1).astype(BF), perm).astype(BF)
    pdown_ref[...] = mm(chosen(units, 8, to_mine), dimage_ref[...])
    tdown_ref[...] = mm(chosen(units, 12, to_mine), rows_ref[29])
    pout_ref[...] = mm(chosen(heads, 16, to_head), rows_ref[25])
    tout_ref[...] = mm(chosen(heads, 20, to_head), rows_ref[28])
    thead_ref[...] = mm(get(30), dtext_ref[...])
    ones = jnp.ones((n, 128), BF)
    bias_ref[0] = mm(chosen(units, 0, to_mine), ones)
    bias_ref[1] = mm(chosen(units, 4, to_mine), ones)
    a, b = iota((n, 4 * n), 0), iota((n, 4 * n), 1)
    spread = ((b % n) // n_z == a // n_z) & (b // n == a % n_z)
    spread = spread.astype(BF)
    lane_z = iota((1, 4 * n), 1) % n_z
    masks = [(lane_z == q).astype(BF) for q in range(n_z)]

    def blocks(values):
        return jnp.concatenate([v * m for v, m in zip(values, masks)], 0)

    by_image = lambda r: mm(get(r), spread).astype(BF)
    g16, g20 = group(16), group(20)

    def put(ref, value, first):
        for q in range(n_z):
            ref[q] = value[q * part : (q + 1) * part, first : first + ref.shape[2]]

    put(pup_ref, mm(blocks([by_image(24)] * 4), group(0)), 0)
    put(tup_ref, mm(blocks([by_image(27)] * 4), group(4)), 0)
    put(tq_ref, mm(blocks([by_image(26)] * 4), g16), 2 * quarter)
    lane = iota((1, width), 1)
    count = HEADS // n_z
    hw = quarter // count

    def by_head(values_of, rhs, first):
        total = None
        for h in range(count):
            own = ((lane >= first + hw * h) & (lane < first + hw * h + hw)).astype(F32)
            one = mm(blocks(values_of(h)), rhs) * own
            total = one if total is None else total + one
        return total

    put(tk_ref, by_head(lambda h: [get(56 + 4 * h, 4)] * 4, g16, 3 * quarter), 3 * quarter)
    put(tv_ref, by_head(lambda h: [get(44 + 4 * h, 4)] * 4, g20, 0), 0)
    put(pv_ref, by_head(lambda h: [by_image(32 + count * q + h) for q in range(n_z)], g16, 0), 0)
    a, b = iota((HEADS * n, 128), 0), iota((HEADS * n, 128), 1)
    pk_ref[...] = mm(get(68, HEADS), (a // n == b).astype(BF))


def outer_grads(rows, d_image, d_text):
    width = rows.shape[2]
    part, quarter = width // 32, width // 4
    v = pl.BlockSpec(memory_space=pltpu.VMEM)
    f = lambda *s: jax.ShapeDtypeStruct(s, F32)
    return pl.pallas_call(
        outer_kernel,
        in_specs=[v] * 3,
        out_specs=[v] * 13,
        out_shape=[f(4, part, width), f(4, part, width), f(4 * part, width), f(4 * part, width), f(part, width), f(part, width),
                   f(part, width), f(4, part, quarter), f(4, part, quarter), f(4, part, quarter), f(4, part, quarter),
                   f(part, 128), f(2, 4 * part, 128)],
        compiler_params=pltpu.CompilerParams(vmem_limit_bytes=48 << 20),
    )(rows, d_image, d_text)


def fast_program(
    patches, captions, pairs,
    image_attend_in, image_attend_out, image_up_weight, image_up_bias, image_down_weight,
    image_vectors, probe_query_weight, probe_pair_weight, probe_out_weight, probe_up_weight,
    probe_up_bias, probe_down_weight, text_attend_in, text_attend_out, text_up_weight,
    text_up_bias, text_down_weight, text_vectors, text_head_weight, temp_bias,
):
    n_dp, n_z = lax.axis_size("dp"), lax.axis_size("seq")
    world = n_dp * n_z
    at_dp, at_z = lax.axis_index("dp"), lax.axis_index("seq")
    me = at_dp * n_z + at_z
    width = patches.shape[-1]
    head_width = width // HEADS
    hidden_width = image_up_weight.shape[1]
    part, quarter = width // world, width // n_z
    wide_part = hidden_width // world
    fold = hidden_width // width
    length = patches.shape[1] * n_z

    small = jnp.concatenate(
        [image_vectors.reshape(-1), text_vectors.reshape(-1), image_up_bias, probe_up_bias, text_up_bias]
    )
    sizes = [image_vectors.size, text_vectors.size, image_up_bias.size, probe_up_bias.size, text_up_bias.size]
    small = jnp.pad(small, (0, 2048 - small.shape[0])).reshape(16, 128)

    def by_units(w):
        return w.reshape(part, n_dp, n_z, wide_part).transpose(2, 0, 1, 3).reshape(n_z, part, width)

    def by_heads(w):
        cut = w.reshape(part, n_z, quarter).transpose(1, 0, 2)
        return jnp.pad(cut, ((0, 0), (0, 0), (0, 256 - quarter)))

    split = [by_units(probe_up_weight), by_units(text_up_weight)]
    split += [by_heads(text_attend_in[:, k * width : (k + 1) * width]) for k in range(3)]
    split += [by_heads(text_head_weight), by_heads(probe_query_weight)]
    split += [by_heads(probe_pair_weight[:, k * width : (k + 1) * width]) for k in range(2)]
    split = jnp.concatenate(split, 2)
    downs = jnp.concatenate([text_down_weight, probe_down_weight], 1)
    w_in, tp, downs, small_all, x, tokens = gather(
        [image_attend_in, split, downs, small, patches, captions],
        [("full", "S"), ("cols", "S"), ("plane", "S"), ("full", "C"), ("za", None), ("zg", None)],
        [(0, 0), (2, 0), (2, 3), (3, 0), (0, 1), (3, 1), (1, 0), (0, 2), (3, 2), (0, 3), (4, 0), (5, 0), (3, 3)]
        + [(1, 3), (0, 4), (2, 4), (3, 4), (1, 4), (0, 5), (2, 5), (3, 5), (1, 5)],
        1,
    )
    tp, downs = tp.reshape(width, -1), downs.reshape(width, -1)
    w_in = w_in.reshape(width, 3 * width)
    x = x.reshape(length, width)
    main = jnp.concatenate(
        [
            image_attend_out,
            image_up_weight.reshape(part, width, fold).transpose(0, 2, 1).reshape(part, hidden_width),
            image_down_weight.reshape(part, hidden_width),
            text_attend_out,
            probe_out_weight,
        ],
        1,
    )
    main = lax.all_gather(main, ALL, axis=0, tiled=True)
    outs = lax.dynamic_slice_in_dim(main[:, width + 2 * hidden_width :], at_z * quarter, quarter, 0)

    small_all = small_all.reshape(world, -1)
    cuts = [sum(sizes[:i]) for i in range(len(sizes) + 1)]
    pieces = [small_all[:, cuts[i] : cuts[i + 1]].astype(F32) for i in range(len(sizes))]
    ivec = pieces[0].reshape(world, -1, part).transpose(1, 0, 2).reshape(-1, width)
    tvec = pieces[1].reshape(world, -1, part).transpose(1, 0, 2).reshape(-1, width)
    i_bias = pieces[2].reshape(width, fold).T.reshape(1, hidden_width)

    def own_units(p):
        p = p.reshape(n_dp, n_z, wide_part)
        return lax.dynamic_index_in_dim(p, at_z, 1, False).reshape(1, width)

    p_bias, t_bias = own_units(pieces[3]), own_units(pieces[4])

    normed = layer_norm(x.astype(F32), ivec[0], ivec[1]).astype(BF)
    proj = mm(normed, w_in).astype(BF)
    mixed, lse = attend_fwd(proj, length)
    hidden, second, active, slope, block_out, final = mlp_fwd(x, mixed, main, i_bias, ivec, fold)

    labels = (2 * pairs - 1).astype(F32).reshape(n_dp, n_z, n_dp, n_z)
    labels = jnp.pad(labels, ((0, 0), (0, n_z), (0, 0), (n_z, 0))).reshape(2 * world, 2 * world)
    dy, d_branch, rows, sums, d_captions, loss_row, d_embeds = middle(
        final, block_out, tokens.reshape(-1, width), tp, downs, outs, ivec, tvec, p_bias, t_bias, labels, temp_bias, 2, n_dp
    )
    loss, grad_temp = loss_row[0, 0], loss_row[0, 1:3]
    grad_captions = d_captions.reshape(captions.shape)

    g_main, d_hidden, d_mixed, inner, g_bias, dvec = mlp_bwd(
        dy, d_branch, active, slope, second, hidden, mixed, main, ivec, fold
    )
    g_main = lax.psum_scatter(g_main, ALL, scatter_dimension=0, tiled=True).astype(F32)
    own_out = g_main[:, :width]
    own_up = g_main[:, width : width + hidden_width].reshape(part, fold, width)
    own_up = own_up.transpose(0, 2, 1).reshape(part, hidden_width)
    own_down = g_main[:, width + hidden_width :].reshape(wide_part, width)
    d_q, d_k, d_v, rows = attend_bwd_and_spread(proj, d_mixed, lse, inner, rows, 4)
    rows = rows.reshape(world, ROWS, width).transpose(1, 0, 2)
    sums = jnp.concatenate([dvec[0:2], dvec[0:2], sums[4:], g_bias.reshape(fold, width)], 0)
    g_in, d_x = project_bwd(d_q, d_k, d_v, normed, w_in, x, d_hidden, sums, ivec)
    own_in, moved = reduce_and_move(g_in, d_x, 3)
    grad_patches = moved.astype(F32)
    own_sums = own_in[:, 3 * width : 3 * width + 128].T
    own_in = own_in[:, : 3 * width]

    d_embeds = d_embeds.reshape(n_dp, 2, n_z, width).astype(BF)
    pup, tup, own_p_down, own_t_down, own_p_out, own_t_out, own_t_head, tq, tk, tv, pv, pk, biases = outer_grads(
        rows, d_embeds[:, 0].reshape(world, width), d_embeds[:, 1].reshape(world, width)
    )

    def wide(g):
        return g.reshape(n_z, part, n_dp, wide_part).transpose(1, 2, 0, 3).reshape(part, hidden_width)

    own_p_up, own_t_up = wide(pup), wide(tup)
    own_t_in = jnp.stack([tq, tk, tv]).transpose(2, 0, 1, 3).reshape(part, 3 * width)
    row20 = rows[20].reshape(n_dp, n_z, n_z, quarter).astype(F32)
    probe_query = row20[0, :, 3].reshape(HEADS, head_width)
    own_p_k = (pk[:, :HEADS, None] * probe_query[None]).reshape(part, width)
    own_p_pair = jnp.concatenate([own_p_k, pv.transpose(1, 0, 2).reshape(part, width)], 1)
    d_query = jnp.sum(row20[:, :, 2], 0).reshape(width)
    mine = lambda v, n: lax.dynamic_slice_in_dim(v, me * n, n, -1)
    own_p_query = mine(ivec[7], part)[:, None] * d_query[None, :]
    dv7 = jnp.sum(probe_query_weight.astype(F32) * d_query[None, :], 1)
    own_ivec = jnp.concatenate([own_sums[0:7], dv7[None], own_sums[8:11]], 0)
    own_tvec = own_sums[11:18]
    own_bias = own_sums[24 : 24 + fold].T.reshape(wide_part)
    return (
        loss, grad_patches, grad_captions,
        own_in, own_out, own_up, own_bias, own_down, own_ivec,
        own_p_query, own_p_pair, own_p_out, own_p_up, biases[0, :, 0], own_p_down,
        own_t_in, own_t_out, own_t_up, biases[1, :, 0], own_t_down, own_tvec, own_t_head,
        grad_temp,
    )


def solution(mesh):
    tokens, matrix, vector, table = P("dp", "seq", None), P(ALL, None), P(ALL), P(None, ALL)
    weights = (
        (matrix, matrix, matrix, vector, matrix, table, matrix, matrix, matrix, matrix, vector, matrix)
        + (matrix, matrix, matrix, vector, matrix, table, matrix)
    )
    return jax.shard_map(
        fast_program if mesh.shape["dp"] == 8 and mesh.shape["seq"] == 4 else device_program,
        mesh=mesh,
        in_specs=(tokens, tokens, P()) + weights + (P(),),
        out_specs=(P(), tokens, tokens) + weights + (P(),),
        check_vma=False,
    )
```

```python
from functools import partial

import jax
import jax.numpy as jnp
from jax import lax
from jax.experimental import pallas as pl
from jax.experimental.pallas import tpu as pltpu
from jax.sharding import PartitionSpec as P

HEADS = 12
ALL = ("dp", "seq")
F32, BF = jnp.float32, jnp.bfloat16
HIGH = lax.Precision.HIGHEST
EPS = 1e-06


def mm(a, b, ca=1, cb=0):
    return lax.dot_general(a, b, (((ca,), (cb,)), ((), ())), preferred_element_type=F32)


def mm_exact(a, b, ca=1, cb=0):
    return lax.dot_general(a, b, (((ca,), (cb,)), ((), ())), precision=HIGH, preferred_element_type=F32)


def split_two(a):
    high = a.astype(BF)
    return high, (a - high.astype(F32)).astype(BF)


def layer_norm(x, gain, shift):
    center = x - jnp.mean(x, -1, keepdims=True)
    spread = jnp.mean(center * center, -1, keepdims=True)
    return center * lax.rsqrt(spread + EPS) * gain + shift


def norm_back(x, gain, upstream):
    center = x - jnp.mean(x, -1, keepdims=True)
    inverse = lax.rsqrt(jnp.mean(center * center, -1, keepdims=True) + EPS)
    unit = center * inverse
    scaled = upstream * gain
    d_x = inverse * (
        scaled
        - jnp.mean(scaled, -1, keepdims=True)
        - unit * jnp.mean(scaled * unit, -1, keepdims=True)
    )
    return d_x, jnp.sum(upstream * unit, 0), jnp.sum(upstream, 0)


def norm_back_rows(x, gain, upstream):
    d_x, d_gain, d_shift = norm_back(x, gain, upstream)
    return d_x, d_gain[None], d_shift[None]


def mm_two(a, b, cb=0):
    n = a.shape[0]
    high = a.astype(BF).astype(F32)
    both = mm(jnp.concatenate([high, a - high], 0).astype(BF), b, 1, cb)
    return both[0:n] + both[n : 2 * n]


def gelu_pair(u):
    c = 0.7978845608028654
    t = jnp.tanh(c * (u + 0.044715 * u * u * u))
    value = 0.5 * u * (1.0 + t)
    slope = 0.5 * (1.0 + t) + 0.5 * u * (1.0 - t * t) * c * (1.0 + 3 * 0.044715 * u * u)
    return value, slope


def attend_fwd_kernel(q_ref, k_ref, v_ref, o_ref, lse_ref):
    q = q_ref[...] * 0.125
    k = k_ref[...]
    lane = lax.broadcasted_iota(jnp.int32, k.shape, 1)
    v_turned = jnp.transpose(v_ref[...])
    outs = []
    for h in range(2):
        keep = (lane < 64) if h == 0 else (lane >= 64)
        own_k = jnp.where(keep, k, jnp.zeros_like(k))
        s = mm(own_k, q, 1, 1)
        top = jnp.max(s, 0, keepdims=True)
        p = jnp.exp(s - top)
        total = jnp.sum(p, 0, keepdims=True)
        outs.append(mm(v_turned[64 * h : 64 * h + 64], p.astype(BF)) / total)
        lse_ref[0, h : h + 1, :] = top + jnp.log(total)
    o_ref[...] = jnp.transpose(jnp.concatenate(outs, 0)).astype(BF)


def attend_fwd(proj, length):
    rows, width = proj.shape[0], proj.shape[1] // 3
    pairs = width // 128
    block = lambda part: pl.BlockSpec((length, 128), lambda b, h: (b, part * pairs + h))
    return pl.pallas_call(
        attend_fwd_kernel,
        grid=(rows // length, pairs),
        in_specs=[block(0), block(1), block(2)],
        out_specs=[block(0), pl.BlockSpec((1, 2, length), lambda b, h: (h, 0, b))],
        out_shape=[
            jax.ShapeDtypeStruct((rows, width), BF),
            jax.ShapeDtypeStruct((pairs, 2, rows), F32),
        ],
        compiler_params=pltpu.CompilerParams(vmem_limit_bytes=48 << 20),
        cost_estimate=pl.CostEstimate(
            flops=rows * length * width * 8,
            bytes_accessed=rows * width * 8,
            transcendentals=rows * length * HEADS,
        ),
    )(proj, proj, proj)


def attend_bwd_kernel(q_ref, k_ref, v_ref, do_ref, lse_ref, d_ref, dq_ref, dk_ref, dv_ref):
    q = q_ref[...] * 0.125
    k, v, do = k_ref[...], v_ref[...], do_ref[...]
    lane = lax.broadcasted_iota(jnp.int32, k.shape, 1)
    dqs, dks, dvs = [], [], []
    for h in range(2):
        keep = (lane < 64) if h == 0 else (lane >= 64)
        s = mm(jnp.where(keep, k, jnp.zeros_like(k)), q, 1, 1)
        p = jnp.exp(s - lse_ref[0, h : h + 1, :])
        dp = mm(jnp.where(keep, v, jnp.zeros_like(v)), do, 1, 1)
        ds = (p * (dp - d_ref[0, h : h + 1, :])).astype(BF)
        dvs.append(mm(p.astype(BF), do))
        dks.append(mm(ds, q))
        dqs.append(mm(ds, k, 0, 0))
    low = lane < 64
    dq_ref[...] = (jnp.where(low, dqs[0], dqs[1]) * 0.125).astype(BF)
    dk_ref[...] = jnp.where(low, dks[0], dks[1]).astype(BF)
    dv_ref[...] = jnp.where(low, dvs[0], dvs[1]).astype(BF)


def attend_bwd(proj, d_out, lse, inner, length):
    rows, width = proj.shape[0], proj.shape[1] // 3
    pairs = width // 128
    block = lambda part: pl.BlockSpec((length, 128), lambda b, h: (b, part * pairs + h))
    row = pl.BlockSpec((1, 2, length), lambda b, h: (h, 0, b))
    result = jax.ShapeDtypeStruct((rows, width), BF)
    return pl.pallas_call(
        attend_bwd_kernel,
        grid=(rows // length, pairs),
        in_specs=[block(0), block(1), block(2), block(0), row, row],
        out_specs=[block(0)] * 3,
        out_shape=[result] * 3,
        compiler_params=pltpu.CompilerParams(vmem_limit_bytes=56 << 20),
        cost_estimate=pl.CostEstimate(
            flops=rows * length * width * 20,
            bytes_accessed=rows * width * 16,
            transcendentals=rows * length * HEADS,
        ),
    )(proj, proj, proj, d_out, lse, inner)


def head_blocks(width):
    own = jnp.arange(width)[None, :] // (width // HEADS) == jnp.arange(HEADS)[:, None]
    return own.astype(F32)


def spread_heads(rows):
    n, width = rows.shape
    return (rows[:, None, :] * head_blocks(width)[None]).reshape(n * HEADS, width)


def fold_heads(rows):
    total, width = rows.shape
    return jnp.sum(rows.reshape(total // HEADS, HEADS, width) * head_blocks(width)[None], 1)


def device_program(
    patches, captions, pairs,
    image_attend_in, image_attend_out, image_up_weight, image_up_bias, image_down_weight,
    image_vectors, probe_query_weight, probe_pair_weight, probe_out_weight, probe_up_weight,
    probe_up_bias, probe_down_weight, text_attend_in, text_attend_out, text_up_weight,
    text_up_bias, text_down_weight, text_vectors, text_head_weight, temp_bias,
):
    seq = lax.axis_size("seq")
    world = seq * lax.axis_size("dp")
    me = lax.axis_index("dp") * seq + lax.axis_index("seq")
    width = patches.shape[-1]
    head_width = width // HEADS
    factor = head_width ** (-0.5)
    hidden_width = image_up_weight.shape[1]
    part = width // world
    wide_part = hidden_width // world

    def gather(*weights):
        flat = jnp.concatenate([w.reshape(-1, width) for w in weights], 0)
        full = lax.all_gather(flat, ALL, axis=0)
        out, at = [], 0
        for w in weights:
            count = w.size // width
            piece = full[:, at : at + count]
            out.append(piece.reshape(world * w.shape[0], w.shape[1]))
            at += count
        return out

    small = jnp.concatenate(
        [image_vectors.reshape(-1), text_vectors.reshape(-1), image_up_bias, probe_up_bias, text_up_bias]
    )
    small_all = lax.all_gather(small, ALL, axis=0)
    sizes = [image_vectors.size, text_vectors.size, image_up_bias.size, probe_up_bias.size, text_up_bias.size]
    cuts = [sum(sizes[:i]) for i in range(len(sizes) + 1)]
    pieces = [small_all[:, cuts[i] : cuts[i + 1]].astype(F32) for i in range(len(sizes))]
    ivec = pieces[0].reshape(world, -1, part).transpose(1, 0, 2).reshape(-1, width)
    tvec = pieces[1].reshape(world, -1, part).transpose(1, 0, 2).reshape(-1, width)
    i_bias, p_bias, t_bias = (p.reshape(-1) for p in pieces[2:])

    (w_in,) = gather(image_attend_in)
    w_out, w_up, w_down = gather(image_attend_out, image_up_weight, image_down_weight)
    tw_in, tw_out, tw_up, tw_down, tw_head, pw_query, pw_pair, pw_out, pw_up, pw_down = gather(
        text_attend_in, text_attend_out, text_up_weight, text_down_weight, text_head_weight,
        probe_query_weight, probe_pair_weight, probe_out_weight, probe_up_weight, probe_down_weight,
    )

    def to_owner(x):
        return lax.all_to_all(x, "seq", 0, 1, tiled=True)

    x = to_owner(patches)
    own, length = x.shape[0], x.shape[1]
    x = x.reshape(own * length, width).astype(F32)
    captions_own = to_owner(captions)
    text_length = captions_own.shape[1]

    normed = layer_norm(x, ivec[0], ivec[1]).astype(BF)
    proj = mm(normed, w_in).astype(BF)
    mixed, lse = attend_fwd(proj, length)
    hidden = x + mm(mixed, w_out)
    second = layer_norm(hidden, ivec[2], ivec[3]).astype(BF)
    value, slope = gelu_pair(mm(second, w_up) + i_bias)
    active, slope = value.astype(BF), slope.astype(BF)
    block_out = hidden + mm(active, w_down) + ivec[4]
    final = layer_norm(block_out, ivec[5], ivec[6]).astype(BF)

    t_x = captions_own.astype(F32)
    t_normed = layer_norm(t_x, tvec[0], tvec[1]).astype(BF)
    t_last = t_normed[:, -1]
    tw_q, tw_k, tw_v = tw_in[:, :width], tw_in[:, width : 2 * width], tw_in[:, 2 * width :]
    t_q = mm(t_last, tw_q).astype(BF)
    t_keys = mm(spread_heads(t_q.astype(F32)).astype(BF), tw_k, 1, 1) * factor
    t_keys = t_keys.reshape(own, HEADS, width)
    k_high, k_low = split_two(t_keys)
    scores = jnp.einsum("bsd,bhd->bsh", t_normed, k_high, preferred_element_type=F32)
    scores += jnp.einsum("bsd,bhd->bsh", t_normed, k_low, preferred_element_type=F32)
    t_probs = jax.nn.softmax(scores, axis=1)
    t_used = jnp.einsum("bsh,bsd->bhd", t_probs, t_normed.astype(F32), precision=HIGH)
    t_mixed = fold_heads(mm(t_used.reshape(own * HEADS, width).astype(BF), tw_v)).astype(BF)
    t_hidden = t_x[:, -1] + mm(t_mixed, tw_out)
    t_second = layer_norm(t_hidden, tvec[2], tvec[3]).astype(BF)
    t_value, t_slope = gelu_pair(mm(t_second, tw_up) + t_bias)
    t_active = t_value.astype(BF)
    t_out = t_hidden + mm(t_active, tw_down) + tvec[4]
    t_final = layer_norm(t_out, tvec[5], tvec[6]).astype(BF)
    text_embed = mm(t_final, tw_head)

    pw_k, pw_v = pw_pair[:, :width], pw_pair[:, width:]
    probe_query = mm_exact(ivec[7:8], pw_query.astype(F32))
    p_keys = mm_exact(spread_heads(probe_query), pw_k.astype(F32), 1, 1) * factor
    k_high, k_low = split_two(p_keys)
    pool_scores = mm(k_high, final, 1, 1) + mm(k_low, final, 1, 1)
    pool_scores = pool_scores.reshape(HEADS, own, length)
    pool_probs = jax.nn.softmax(pool_scores, axis=-1)
    final_own = final.reshape(own, length, width)
    p_high, p_low = split_two(pool_probs)
    used = jnp.einsum("hbt,btd->bhd", p_high, final_own, preferred_element_type=F32)
    used += jnp.einsum("hbt,btd->bhd", p_low, final_own, preferred_element_type=F32)
    pooled = fold_heads(mm_exact(used.reshape(own * HEADS, width), pw_v.astype(F32)))
    head_start = mm_exact(pooled, pw_out.astype(F32))
    head_normed = layer_norm(head_start, ivec[8], ivec[9]).astype(BF)
    h_value, h_slope = gelu_pair(mm(head_normed, pw_up) + p_bias)
    head_active = h_value.astype(BF)
    image_embed = head_start + mm(head_active, pw_down) + ivec[10]

    embeds = lax.all_gather(jnp.stack([image_embed, text_embed], 1), ALL, axis=0, tiled=True)
    every_image, every_text = embeds[:, 0], embeds[:, 1]
    labels = (2 * pairs - 1).astype(F32)
    total = every_image.shape[0]
    i_scale = lax.rsqrt(jnp.sum(every_image * every_image, -1, keepdims=True) + EPS)
    t_scale = lax.rsqrt(jnp.sum(every_text * every_text, -1, keepdims=True) + EPS)
    z_i, z_t = every_image * i_scale, every_text * t_scale
    cosine = mm_exact(z_i, z_t, 1, 1)
    temper = jnp.exp(temp_bias[0])
    logits = cosine * temper + temp_bias[1]
    loss = -jnp.sum(jax.nn.log_sigmoid(labels * logits)) / total
    g = -labels * jax.nn.sigmoid(-labels * logits) / total
    grad_temp = jnp.stack([temper * jnp.sum(g * cosine), jnp.sum(g)])
    dz_i = temper * mm_exact(g, z_t)
    dz_t = temper * mm_exact(g, z_i, 0, 0)
    all_d_image = (dz_i - z_i * jnp.sum(z_i * dz_i, -1, keepdims=True)) * i_scale
    all_d_text = (dz_t - z_t * jnp.sum(z_t * dz_t, -1, keepdims=True)) * t_scale
    d_image = lax.dynamic_slice_in_dim(all_d_image, me * own, own, 0)
    d_text = lax.dynamic_slice_in_dim(all_d_text, me * own, own, 0)

    h_upper = mm_exact(d_image, pw_down.astype(F32), 1, 1) * h_slope
    h_norm = mm_exact(h_upper, pw_up.astype(F32), 1, 1)
    d_start, dv8, dv9 = norm_back(head_start, ivec[8], h_norm)
    d_start = d_image + d_start
    dv10 = jnp.sum(d_image, 0)
    d_pooled = mm_exact(d_start, pw_out.astype(F32), 1, 1)
    p_values = mm_exact(spread_heads(d_pooled), pw_v.astype(F32), 1, 1).reshape(own, HEADS, width)
    v_high, v_low = split_two(p_values)
    d_probs = jnp.einsum("bhd,btd->hbt", v_high, final_own, preferred_element_type=F32)
    d_probs += jnp.einsum("bhd,btd->hbt", v_low, final_own, preferred_element_type=F32)
    d_scores = pool_probs * (d_probs - jnp.sum(pool_probs * d_probs, -1, keepdims=True))
    s_high, s_low = split_two(d_scores)
    p_used = jnp.einsum("hbt,btd->bhd", s_high, final_own, preferred_element_type=F32)
    p_used += jnp.einsum("hbt,btd->bhd", s_low, final_own, preferred_element_type=F32)
    d_query = jnp.sum(fold_heads(mm_exact(p_used.reshape(own * HEADS, width), pw_k.astype(F32))), 0) * factor
    d_final = jnp.einsum(
        "hbt,bhd->btd",
        jnp.concatenate([s_high, p_high], 0),
        jnp.concatenate([jnp.broadcast_to(k_high[None], (own, HEADS, width)), v_high], 1),
        preferred_element_type=F32,
    ).reshape(own * length, width)
    dy, dv5, dv6 = norm_back(block_out, ivec[5], d_final)

    d_branch = dy.astype(BF)
    g_down = mm(active, d_branch, 0, 0)
    dv4 = jnp.sum(dy, 0)
    d_upper_f = mm(d_branch, w_down, 1, 1) * slope.astype(F32)
    d_upper = d_upper_f.astype(BF)
    g_bias = jnp.sum(d_upper_f, 0)
    g_up = mm(second, d_upper, 0, 0)
    d_hidden, dv2, dv3 = norm_back(hidden, ivec[2], mm(d_upper, w_up, 1, 1))
    d_hidden = dy + d_hidden
    d_attend = d_hidden.astype(BF)
    g_out = mm(mixed, d_attend, 0, 0)
    d_mixed = mm(d_attend, w_out, 1, 1).astype(BF)

    def scatter(*grads):
        flat = jnp.concatenate([g.astype(BF).reshape(world, -1, width) for g in grads], 1)
        mine = lax.psum_scatter(flat, ALL, scatter_dimension=0, tiled=False).astype(F32)
        out, at = [], 0
        for g in grads:
            count = g.size // world // width
            out.append(mine[at : at + count].reshape(g.shape[0] // world, g.shape[1]))
            at += count
        return out

    own_up, own_down, own_out = scatter(g_up, g_down, g_out)
    inner_rows = jnp.sum(
        (d_mixed.astype(F32) * mixed.astype(F32)).reshape(own * length, HEADS, head_width), -1
    ).T.reshape(HEADS // 2, 2, own * length)
    d_q, d_k, d_v = attend_bwd(proj, d_mixed, lse, inner_rows, length)
    g_in = jnp.concatenate([mm(normed, d, 0, 0) for d in (d_q, d_k, d_v)], 1)
    (own_in,) = scatter(g_in)
    d_normed = (
        mm(d_q, w_in[:, :width], 1, 1)
        + mm(d_k, w_in[:, width : 2 * width], 1, 1)
        + mm(d_v, w_in[:, 2 * width :], 1, 1)
    )
    d_x, dv0, dv1 = norm_back(x, ivec[0], d_normed)
    d_x = (d_hidden + d_x).reshape(own, length, width)

    def to_tokens(v):
        return lax.all_to_all(v.astype(BF), "seq", 1, 0, tiled=True).astype(F32)

    grad_patches = to_tokens(d_x)

    dt_final = mm_exact(d_text, tw_head.astype(F32), 1, 1)
    dt_out, tv5, tv6 = norm_back(t_out, tvec[5], dt_final)
    dt_branch = dt_out.astype(BF)
    tv4 = jnp.sum(dt_out, 0)
    dt_upper = (mm(dt_branch, tw_down, 1, 1) * t_slope).astype(BF)
    dt_hidden, tv2, tv3 = norm_back(t_hidden, tvec[2], mm(dt_upper, tw_up, 1, 1))
    dt_hidden = dt_out + dt_hidden
    dt_attend = dt_hidden.astype(BF)
    dt_mixed = mm(dt_attend, tw_out, 1, 1).astype(BF)
    t_values = mm(spread_heads(dt_mixed.astype(F32)).astype(BF), tw_v, 1, 1).reshape(own, HEADS, width)
    tv_high, tv_low = split_two(t_values)
    dt_probs = jnp.einsum("bsd,bhd->bsh", t_normed, tv_high, preferred_element_type=F32)
    dt_probs += jnp.einsum("bsd,bhd->bsh", t_normed, tv_low, preferred_element_type=F32)
    dt_scores = t_probs * (dt_probs - jnp.sum(t_probs * dt_probs, 1, keepdims=True))
    tk_used = jnp.einsum("bsh,bsd->bhd", dt_scores, t_normed.astype(F32), precision=HIGH)
    dt_q = fold_heads(mm(tk_used.reshape(own * HEADS, width).astype(BF), tw_k)) * factor
    dt_q = dt_q.astype(BF)
    dt_normed = jnp.einsum("bsh,bhd->bsd", dt_scores, t_keys, precision=HIGH)
    dt_normed += jnp.einsum("bsh,bhd->bsd", t_probs, t_values, precision=HIGH)
    dt_normed = dt_normed.at[:, -1].add(mm(dt_q, tw_q, 1, 1))
    flat_x = t_x.reshape(own * text_length, width)
    dt_x, tv0, tv1 = norm_back(flat_x, tvec[0], dt_normed.reshape(own * text_length, width))
    dt_x = dt_x.reshape(own, text_length, width).at[:, -1].add(dt_hidden)
    grad_captions = to_tokens(dt_x)

    whole = jnp.concatenate(
        [v.astype(F32) for v in (h_upper, d_start, d_pooled, dt_branch, dt_upper, dt_attend, dt_q, t_q, dt_mixed)], 1
    )
    whole = lax.all_gather(whole, ALL, axis=0, tiled=True)
    at = [0]

    def take(count):
        at[0] += count
        return whole[:, at[0] - count : at[0]]

    a_h_upper, a_start, a_pooled, a_branch, a_upper, a_attend, a_q, a_query, a_mixed = (
        take(c) for c in (hidden_width, width, width, width, hidden_width, width, width, width, width)
    )
    columns = [pooled, head_normed, t_last, t_mixed, t_second, t_final]
    columns += [used, t_used, tk_used * factor]
    columns += [head_active, t_active]
    columns = jnp.concatenate(
        [v.astype(F32).reshape(own, -1, width) for v in columns], 1
    )
    wide = 2 * (hidden_width // width)
    narrow = columns.shape[1] - wide
    cut = jnp.concatenate(
        [
            columns[:, :narrow].reshape(own, narrow, world, part).transpose(2, 0, 1, 3).reshape(world, own, -1),
            columns[:, narrow:].reshape(own, 2, world, wide_part).transpose(2, 0, 1, 3).reshape(world, own, -1),
        ],
        2,
    )
    cut = lax.all_to_all(cut, ALL, 0, 0, tiled=True).reshape(total, -1)
    slim = cut[:, : narrow * part].reshape(total, narrow, part)
    broad = cut[:, narrow * part :].reshape(total, 2, wide_part)

    def outer(rows, cols):
        return mm_exact(rows, cols, 0, 0)

    def outer_heads(rows, cols):
        cols = cols.reshape(total, HEADS, head_width)
        return jnp.einsum("chm,che->mhe", rows, cols, precision=HIGH).reshape(part, width)

    c_pooled, c_head, c_last, c_mixed, c_second, c_final = (slim[:, i] for i in range(6))
    c_used, ct_used, ctk_used = (slim[:, 6 + i * HEADS : 6 + (i + 1) * HEADS] for i in range(3))
    own_t_in = jnp.concatenate(
        [outer(c_last, a_q), outer_heads(ctk_used, a_query), outer_heads(ct_used, a_mixed)], 1
    )
    own_t_out = outer(c_mixed, a_attend)
    own_t_up = outer(c_second, a_upper)
    own_t_down = outer(broad[:, 1], a_branch)
    own_t_head = outer(c_final, all_d_text)
    own_p_out = outer(c_pooled, a_start)
    own_p_up = outer(c_head, a_h_upper)
    own_p_down = outer(broad[:, 0], all_d_image)
    own_p_values = outer_heads(c_used, a_pooled)

    summed = jnp.concatenate(
        [
            jnp.stack([dv0, dv1, dv2, dv3, dv4, dv5, dv6, dv8, dv9, dv10]),
            jnp.stack([tv0, tv1, tv2, tv3, tv4, tv5, tv6]),
            d_query[None],
            jnp.sum(p_used, 0),
            g_bias.reshape(-1, width),
        ],
        0,
    )
    summed = lax.psum(summed, ALL)
    total_query = summed[17]
    mine = lambda v, n: lax.dynamic_slice_in_dim(v, me * n, n, -1)
    own_probe = mine(ivec[7], part)
    own_p_query = own_probe[:, None] * total_query[None, :]
    dv7 = jnp.sum(probe_query_weight.astype(F32) * total_query[None, :], 1)
    pk_used = mine(summed[18 : 18 + HEADS], part)
    own_p_keys = jnp.einsum(
        "hm,he->mhe", pk_used, probe_query.reshape(HEADS, head_width) * factor
    ).reshape(part, width)
    own_p_pair = jnp.concatenate([own_p_keys, own_p_values], 1)
    ten = mine(summed[:10], part)
    own_ivec = jnp.concatenate([ten[:7], dv7[None], ten[7:]], 0)
    own_tvec = mine(summed[10:17], part)
    own_bias = mine(summed[18 + HEADS :].reshape(-1), wide_part)
    own_p_bias = mine(jnp.sum(a_h_upper, 0), wide_part)
    own_t_bias = mine(jnp.sum(a_upper, 0), wide_part)
    return (
        loss, grad_patches, grad_captions,
        own_in, own_out, own_up, own_bias, own_down, own_ivec,
        own_p_query, own_p_pair, own_p_out, own_p_up, own_p_bias, own_p_down,
        own_t_in, own_t_out, own_t_up, own_t_bias, own_t_down, own_tvec, own_t_head,
        grad_temp,
    )


MESH = pl.DeviceIdType.MESH

class Place:
    def __init__(self):
        i = lax.axis_index("dp")
        self.i, self.z = i, lax.axis_index("seq")
        self.y, self.x, self.c = i // 4, (i // 2) % 2, i % 2
        self.at_y = (i + 4 - 8 * self.y, self.z)
        self.at_x = (i + 2 - 4 * self.x, self.z)
        self.at_c = (i + 1 - 2 * self.c, self.z)

    def at_z(self, k):
        return (self.i, (self.z + k) % 4)

def greet(peers):
    barrier = pltpu.get_barrier_semaphore()
    for p in peers:
        pl.semaphore_signal(barrier, inc=1, device_id=p, device_id_type=MESH)
    pl.semaphore_wait(barrier, len(peers))

def gather_kernel(kinds, order, *refs):
    n = len(kinds)
    srcs, outs = refs[:n], refs[n : 2 * n]
    send, recv, local = refs[2 * n :]
    me = Place()
    y, x, c, z = me.y, me.x, me.c, me.z
    greet([me.at_z(1), me.at_z(2), me.at_z(3), me.at_x, me.at_y, me.at_c])
    ends = []

    def copy_of(a, slot, src, dst, dev):
        return pltpu.make_async_remote_copy(
            src, dst, send.at[a, slot], recv.at[a, slot], device_id=dev, device_id_type=MESH
        )

    def push(a, slot, src, dst, dev, arriving):
        copy = copy_of(a, slot, src, dst, dev)
        copy.start()
        ends.append(copy.wait_send)
        return copy_of(a, slot, src, arriving, dev).wait_recv

    def along(a, step, up):
        home = outs[a].at[y, x, c]
        if up:
            slab, go, to = z - step, (z - step >= 0) & (z < 3), me.at_z(1)
        else:
            slab, go, to = z + step, (z + step < 4) & (z > 0), me.at_z(3)
        slab = jnp.clip(slab, 0, 3)
        src = srcs[a] if step == 0 else home.at[slab]
        copy = copy_of(a, step + (0 if up else 3), src, home.at[slab], to)
        pl.when(go)(lambda: copy.start())
        ends.append(lambda: pl.when(go)(lambda: copy.wait_send()))

    def arrived(a, step, up):
        home = outs[a].at[y, x, c]
        if up:
            slab, come = z - 1 - step, z - 1 - step >= 0
        else:
            slab, come = z + 1 + step, z + 1 + step < 4
        slab = jnp.clip(slab, 0, 3)
        copy = copy_of(a, step + (0 if up else 3), home.at[slab], home.at[slab], me.at_z(1))
        pl.when(come)(lambda: copy.wait_recv())

    waits = {}

    def half(r, which, order_):
        if order_ != "S":
            return r
        n_ = r.shape[-1] // 2
        return r.at[..., 0:n_] if which == "C" else r.at[..., n_ : 2 * n_]

    def stage(a, s):
        kind, turn = kinds[a]
        src, out = srcs[a], outs[a]
        if kind in ("za", "zg"):
            own = src.at[z] if kind == "za" else src
            keep = pltpu.make_async_copy(own, out.at[z], local.at[a])
            keep.start()
            ends.append(keep.wait)
            for k in (1, 2, 3):
                to, fro = (z + k) % 4, (z + 4 - k) % 4
                s_ref = src.at[to] if kind == "za" else src
                ends.append(push(a, k - 1, s_ref, out.at[z], me.at_z(k), out.at[fro]))
            return
        turns = "CD" if turn == "S" else turn
        if kind != "full" and s == 0:
            own = src.at[z] if kind == "cols" else src
            keep = pltpu.make_async_copy(own, out.at[y, x, c, z] if kind == "cols" else out.at[y, x, c], local.at[a])
            keep.start()
            waits[a] = [keep.wait]
            for k in (1, 2, 3) if kind == "cols" else ():
                to, fro = (z + k) % 4, (z + 4 - k) % 4
                waits[a].append(push(a, k - 1, src.at[to], out.at[y, x, c, z], me.at_z(k), out.at[y, x, c, fro]))
        elif s == 0:
            keep = pltpu.make_async_copy(src, out.at[y, x, c, z], local.at[a])
            keep.start()
            waits[a] = [keep.wait]
            along(a, 0, True)
            along(a, 0, False)
        elif s in (1, 2):
            for up in (True, False):
                arrived(a, s - 1, up)
                along(a, s, up)
        elif s == 3:
            for up in (True, False) if kind == "full" else ():
                arrived(a, 2, up)
            for w in waits.pop(a):
                w()
            waits[a] = []
            for t in turns:
                cut = lambda r: half(r, t, turn)
                to, fro = (me.at_x, (y, 1 - x)) if t == "C" else (me.at_y, (1 - y, x))
                mine = cut(out.at[y, x, c])
                waits[a].append(push(a, 6 + (t == "D"), mine, mine, to, cut(out.at[fro[0], fro[1], c])))
        elif s == 4:
            for w in waits.pop(a):
                w()
            waits[a] = []
            for t in turns:
                cut = lambda r: half(r, t, turn)
                if t == "C":
                    mine, come, to = cut(out.at[y, :, c]), cut(out.at[1 - y, :, c]), me.at_y
                else:
                    mine, come, to = cut(out.at[:, x, c]), cut(out.at[:, 1 - x, c]), me.at_x
                waits[a].append(push(a, 8 + (t == "D"), mine, mine, to, come))
        elif s == 5:
            for w in waits.pop(a):
                w()
            mine = out.at[:, :, c]
            ends.append(push(a, 10, mine, mine, me.at_c, out.at[:, :, 1 - c]))

    for a, s in order:
        stage(a, s)
    for e in ends:
        e()


def gather(ops, kinds, order, cid):
    shapes = []
    for o, (kind, _) in zip(ops, kinds):
        s = {"full": (2, 2, 2, 4) + o.shape, "zg": (4,) + o.shape, "za": o.shape, "cols": (2, 2, 2) + o.shape, "plane": (2, 2, 2) + o.shape}[kind]
        shapes.append(jax.ShapeDtypeStruct(s, o.dtype))
    n = len(ops)
    return pl.pallas_call(
        partial(gather_kernel, kinds, order),
        out_shape=shapes,
        in_specs=[pl.BlockSpec(memory_space=pl.ANY)] * n,
        out_specs=[pl.BlockSpec(memory_space=pl.ANY)] * n,
        scratch_shapes=[
            pltpu.SemaphoreType.DMA((n, 11)),
            pltpu.SemaphoreType.DMA((n, 11)),
            pltpu.SemaphoreType.DMA((n,)),
        ],
        compiler_params=pltpu.CompilerParams(collective_id=cid, has_side_effects=True),
    )(*ops)


def reduce_kernel(g_ref, dx_ref, own_ref, moved_ref, from_c, acc_c, from_1, acc_1, from_2, acc_2, from_z, send, recv, local):
    me = Place()
    y, x, c, z = me.y, me.x, me.c, me.z
    greet([me.at_z(1), me.at_z(2), me.at_z(3), me.at_x, me.at_y, me.at_c])
    half = g_ref.shape[-1] // 2
    started = []

    def push(slot, src, dst, dev, arriving):
        copy = pltpu.make_async_remote_copy(src, dst, send.at[slot], recv.at[slot], device_id=dev, device_id_type=MESH)
        copy.start()
        started.append(copy)
        return pltpu.make_async_remote_copy(src, arriving, send.at[slot], recv.at[slot], device_id=dev, device_id_type=MESH)

    a_c = push(0, g_ref.at[:, :, 1 - c], from_c, me.at_c, from_c)
    home = pltpu.make_async_copy(g_ref.at[:, :, c], acc_c, local.at[0])
    home.start()
    rest = []
    for k in (1, 2, 3):
        to, fro = (z + k) % 4, (z + 4 - k) % 4
        rest.append(push(k, dx_ref.at[to], moved_ref.at[z], me.at_z(k), moved_ref.at[fro]))
    keep = pltpu.make_async_copy(dx_ref.at[z], moved_ref.at[z], local.at[1])
    keep.start()
    home.wait()
    a_c.wait_recv()
    f32 = lambda v: v.astype(jnp.float32)
    for a in range(2):
        for b in range(2):
            for q in range(4):
                acc_c[a, b, q] = (f32(acc_c[a, b, q]) + f32(from_c[a, b, q])).astype(acc_c.dtype)
    left, right = slice(0, half), slice(half, 2 * half)
    a_y = push(4, acc_c.at[1 - y, :, :, :, left], from_1.at[0], me.at_y, from_1.at[0])
    a_x = push(5, acc_c.at[:, 1 - x, :, :, right], from_1.at[1], me.at_x, from_1.at[1])
    a_y.wait_recv()
    for b in range(2):
        for q in range(4):
            acc_1[0, b, q] = (f32(acc_c[y, b, q, :, left]) + f32(from_1[0, b, q])).astype(acc_1.dtype)
    b_x = push(6, acc_1.at[0, 1 - x], from_2.at[0], me.at_x, from_2.at[0])
    a_x.wait_recv()
    for b in range(2):
        for q in range(4):
            acc_1[1, b, q] = (f32(acc_c[b, x, q, :, right]) + f32(from_1[1, b, q])).astype(acc_1.dtype)
    b_y = push(7, acc_1.at[1, 1 - y], from_2.at[1], me.at_y, from_2.at[1])
    b_x.wait_recv()
    for q in range(4):
        acc_2[q, :, left] = (f32(acc_1[0, x, q]) + f32(from_2[0, q])).astype(acc_2.dtype)
    b_y.wait_recv()
    for q in range(4):
        acc_2[q, :, right] = (f32(acc_1[1, y, q]) + f32(from_2[1, q])).astype(acc_2.dtype)
    last = []
    for k in (1, 2, 3):
        to, fro = (z + k) % 4, (z + 4 - k) % 4
        last.append(push(7 + k, acc_2.at[to], from_z.at[k - 1], me.at_z(k), from_z.at[k - 1]))
    total = f32(acc_2[z])
    for k in (1, 2, 3):
        last[k - 1].wait_recv()
        total += f32(from_z[k - 1])
    own_ref[...] = total
    keep.wait()
    for r in rest:
        r.wait_recv()
    for copy in started:
        copy.wait_send()

def reduce_and_move(g, dx, cid):
    rows, n = g.shape[0] // 32, g.shape[1]
    g = g.reshape(2, 2, 2, 4, rows, n)
    dx = dx.reshape(4, dx.shape[0] // 4, dx.shape[1])
    hbm = pl.BlockSpec(memory_space=pl.ANY)
    v = lambda *s: pltpu.VMEM(s, g.dtype)
    return pl.pallas_call(
        reduce_kernel,
        in_specs=[hbm, hbm],
        out_specs=[pl.BlockSpec(memory_space=pltpu.VMEM), hbm],
        out_shape=[jax.ShapeDtypeStruct((rows, n), jnp.float32), jax.ShapeDtypeStruct(dx.shape, dx.dtype)],
        scratch_shapes=[
            v(2, 2, 4, rows, n), v(2, 2, 4, rows, n), v(2, 2, 4, rows, n // 2), v(2, 2, 4, rows, n // 2),
            v(2, 4, rows, n // 2), v(4, rows, n), v(3, rows, n),
            pltpu.SemaphoreType.DMA((11,)), pltpu.SemaphoreType.DMA((11,)), pltpu.SemaphoreType.DMA((2,)),
        ],
        compiler_params=pltpu.CompilerParams(collective_id=cid, has_side_effects=True, vmem_limit_bytes=40 << 20),
    )(g, dx)

ROWS = 80

def middle_kernel(final_ref, block_ref, tokens_ref, tp_ref, downs_ref, outs_ref, ivec_ref, tvec_ref, pbias_ref, tbias_ref,
                  label_ref, temp_ref,
                  dy_ref, branch_ref, rows_ref, sums_ref, dcap_ref, loss_ref, dz_ref,
                  tn_ref, dn_ref, send_a, recv_a, send_l, recv_l, send_t, recv_t, send_sem, recv_sem):
    me = Place()
    z, i = me.z, me.i
    n_dp = recv_l.shape[0]
    plane = [((i + k) % n_dp, z) for k in range(1, n_dp)]
    greet([me.at_z(1), me.at_z(2), me.at_z(3)] + plane)
    width = final_ref.shape[1]
    part = width // 4
    started = []

    def exchange(n, values, rows=4):
        if not isinstance(values, list):
            values = [values] * 4
        for q in range(4):
            send_a[n, q, 0:rows] = values[q]
        recv_a[n, z] = send_a[n, z]
        copies = []
        for k in (3, 2, 1):
            to, fro = (z + k) % 4, (z + 4 - k) % 4
            make = lambda dst: pltpu.make_async_remote_copy(
                send_a.at[n, to], dst, send_sem.at[n, k], recv_sem.at[n, k], device_id=me.at_z(k), device_id_type=MESH)
            copy = make(recv_a.at[n, z])
            copy.start()
            started.append(copy)
            copies.append(make(recv_a.at[n, fro]))

        def done():
            for a in copies:
                a.wait_recv()
            return [recv_a[n, q, 0:rows] for q in range(4)]

        return done

    total = lambda blocks: (blocks[0] + blocks[1]) + (blocks[2] + blocks[3])
    by_head = lambda blocks, n=3: jnp.concatenate([blocks[q][h : h + 1] for h in range(n) for q in range(4)], 0)
    pad1 = jnp.zeros((1, width), F32)
    ivec, tvec = ivec_ref[...], tvec_ref[...]
    iv = lambda k: ivec[k:k + 1]
    tv = lambda k: tvec[k:k + 1]
    names = ["tq", "tk", "tv", "thead", "pq", "pk", "pv"]
    col = {n: 2 * width + 256 * k for k, n in enumerate(names)}
    small = lambda n: tp_ref[:, col[n]:col[n] + 256]
    p_up = lambda: tp_ref[:, 0:width]
    t_up = lambda: tp_ref[:, width:2 * width]
    t_down = lambda: downs_ref[:, 0:width]
    p_down = lambda: downs_ref[:, width:2 * width]
    t_out_w = lambda: outs_ref[0:part, 0:width]
    p_out_w = lambda: outs_ref[0:part, width:2 * width]
    lane = lax.broadcasted_iota(jnp.int32, (1, 256), 1)
    own = [((lane >= 64 * h) & (lane < 64 * h + 64)).astype(F32) for h in range(3)]

    def spread(a):
        return jnp.concatenate([a * own[h] for h in range(3)], 0)

    def fold(a):
        n = a.shape[0] // 3
        return sum(a[h * n:(h + 1) * n] * own[h] for h in range(3))

    p_q = mm(iv(7).astype(BF), small("pq"))
    get_keys = exchange(0, mm_two(spread(p_q), small("pk"), 1) * 0.125, 3)
    t_x = tokens_ref[...].astype(F32)
    tn = layer_norm(t_x, tv(0), tv(1)).astype(BF)
    tn_ref[...] = tn.astype(F32)
    last_at = [3 * 64 + 16 * c + 15 for c in range(4)]
    t_last = jnp.concatenate([tn_ref[r:r + 1, :] for r in last_at], 0)
    x_last = jnp.concatenate([tokens_ref[3 * 64 + 16 * c:3 * 64 + 16 * c + 16, :].astype(F32)[15:16] for c in range(4)], 0)
    t_q = mm(t_last.astype(BF), small("tq")).astype(BF).astype(F32)
    t_keys = mm(spread(t_q).astype(BF), small("tk"), 1, 1) * 0.125
    scores = mm_two(t_keys, tn, 1)
    col_id = (lax.broadcasted_iota(jnp.int32, scores.shape, 1) // 16) % 4
    row_id = lax.broadcasted_iota(jnp.int32, scores.shape, 0) % 4
    mine = col_id == row_id
    top = jnp.max(jnp.where(mine, scores, -1e30), -1, keepdims=True)
    e = jnp.where(mine, jnp.exp(jnp.where(mine, scores - top, 0.0)), 0.0)
    t_probs = e / jnp.sum(e, -1, keepdims=True)
    t_used = mm_two(t_probs, tn)
    t_mixed = fold(mm(t_used.astype(BF), small("tv"))).astype(BF)
    get_t = exchange(1, mm(t_mixed[:, 0:part], t_out_w()), 4)
    final = final_ref[...]
    p_keys = jnp.concatenate(get_keys(), 0)
    p_scores = mm_two(p_keys, final, 1)
    e = jnp.exp(p_scores - jnp.max(p_scores, -1, keepdims=True))
    p_probs = e / jnp.sum(e, -1, keepdims=True)
    used = mm_two(p_probs, final)
    get_p = exchange(2, [used[3 * q:3 * q + 3] for q in range(4)], 3)
    t_hidden = x_last + total(get_t())
    t_second = layer_norm(t_hidden, tv(2), tv(3)).astype(BF)
    t_value, t_slope = gelu_pair(mm(t_second, t_up()) + tbias_ref[...])
    t_active = t_value.astype(BF)
    get_t = exchange(3, mm(t_active, t_down()), 4)
    pooled = fold(mm_two(by_head(get_p()), small("pv")))
    get_p = exchange(4, mm_two(pooled[:, 0:part], p_out_w()), 4)
    t_out = t_hidden + total(get_t()) + tv(4)
    t_final = layer_norm(t_out, tv(5), tv(6)).astype(BF)
    t_piece = mm(t_final, small("thead"))
    get_t = exchange(5, jnp.concatenate([t_piece[:, 0:part], jnp.zeros((4, width - part), F32)], 1), 4)
    h_start = total(get_p())
    h_normed = layer_norm(h_start, iv(8), iv(9)).astype(BF)
    h_value, h_slope = gelu_pair(mm(h_normed, p_up()) + pbias_ref[...])
    h_active = h_value.astype(BF)
    get_p = exchange(6, mm(h_active, p_down()), 4)
    text_embed = jnp.concatenate([blk[:, 0:part] for blk in get_t()], 1)
    image_embed = h_start + (total(get_p()) + iv(10))
    send_l[...] = jnp.concatenate([image_embed, text_embed], 0)
    recv_l[i] = send_l[...]
    arrive = []
    for k in range(1, n_dp):
        copy = pltpu.make_async_remote_copy(send_l, recv_l.at[i], send_sem.at[15, k], recv_sem.at[15, k],
                                            device_id=plane[k - 1], device_id_type=MESH)
        copy.start()
        started.append(copy)
        arrive.append(pltpu.make_async_remote_copy(send_l, recv_l.at[(i + n_dp - k) % n_dp], send_sem.at[15, k], recv_sem.at[15, k],
                                                   device_id=plane[k - 1], device_id_type=MESH))
    for a in arrive:
        a.wait_recv()
    every = jnp.concatenate([recv_l[k] for k in range(n_dp)], 0)
    scale = lax.rsqrt(jnp.sum(every * every, -1, keepdims=True) + EPS)
    unit = every * scale
    cosine = mm_exact(unit, unit, 1, 1)
    temper = jnp.exp(jnp.full((1, 1), temp_ref[0], F32))
    logits = cosine * temper + temp_ref[1]
    label = label_ref[...]
    valid = label != 0.0
    signed = label * logits
    n_all = n_dp * 4
    nll = jnp.maximum(-signed, 0.0) + jnp.log(1.0 + jnp.exp(-jnp.abs(signed)))
    add_all = lambda a: jnp.sum(jnp.sum(a, -1, keepdims=True), 0, keepdims=True)
    loss = add_all(jnp.where(valid, nll, 0.0)) / n_all
    g = jnp.where(valid, -label / (1.0 + jnp.exp(signed)), 0.0) / n_all
    gt0 = temper * add_all(g * cosine)
    gt1 = add_all(g)
    at = lax.broadcasted_iota(jnp.int32, (8, 128), 1)
    loss_ref[...] = jnp.where(at == 0, loss, jnp.where(at == 1, gt0, gt1))
    dz = temper * mm_exact(g + jnp.transpose(g), unit)
    dz_ref[...] = (dz - unit * jnp.sum(unit * dz, -1, keepdims=True)) * scale
    d_both = dz_ref[pl.ds(pl.multiple_of(8 * i, 8), 8), :]
    d_image, d_text = d_both[0:4], d_both[4:8]

    dh_upper = mm_two(d_image, p_down(), 1) * h_slope
    get_p = exchange(7, mm_two(dh_upper, p_up(), 1), 4)
    d_text_my = sum(jnp.where(z == q, d_text[:, part * q:part * q + part], 0.0) for q in range(4))
    get_t = exchange(8, mm_two(d_text_my, small("thead")[:, 0:part], 1), 4)
    d_start, dv8, dv9 = norm_back_rows(h_start, iv(8), total(get_p()))
    d_start = d_image + d_start
    dv10 = jnp.sum(d_image, 0, keepdims=True)
    d_pooled = mm_two(d_start, p_out_w(), 1)
    d_pooled = jnp.concatenate([d_pooled, jnp.zeros((4, 256 - part), F32)], 1)
    p_values_my = mm_two(spread(d_pooled), small("pv"), 1)
    get_p = exchange(9, [jnp.concatenate([p_values_my[4 * h + q:4 * h + q + 1] for h in range(3)], 0) for q in range(4)], 3)
    dt_out, tv5, tv6 = norm_back_rows(t_out, tv(5), total(get_t()))
    tv4 = jnp.sum(dt_out, 0, keepdims=True)
    dt_branch = dt_out.astype(BF)
    dt_upper = (mm(dt_branch, t_down(), 1, 1) * t_slope).astype(BF)
    get_t = exchange(10, mm(dt_upper, t_up(), 1, 1), 4)
    p_values = jnp.concatenate(get_p(), 0)
    d_probs = mm_two(p_values, final, 1)
    d_scores = p_probs * (d_probs - jnp.sum(p_probs * d_probs, -1, keepdims=True))
    p_used = mm_two(d_scores, final) * 0.125
    get_p = exchange(11, [p_used[3 * q:3 * q + 3] for q in range(4)], 3)
    dt_hidden, tv2, tv3 = norm_back_rows(t_hidden, tv(2), total(get_t()))
    dt_hidden = dt_out + dt_hidden
    dt_attend = dt_hidden.astype(BF)
    dt_mixed = mm(dt_attend, t_out_w(), 1, 1).astype(BF).astype(F32)
    dt_mixed = jnp.concatenate([dt_mixed, jnp.zeros((4, 256 - part), F32)], 1)
    t_values = mm(spread(dt_mixed).astype(BF), small("tv"), 1, 1)
    dt_probs = mm_two(t_values, tn, 1)
    dt_scores = t_probs * (dt_probs - jnp.sum(t_probs * dt_probs, -1, keepdims=True))
    tk_used = mm_two(dt_scores, tn) * 0.125
    dt_q = fold(mm(tk_used.astype(BF), small("tk"))).astype(BF)
    dn = mm(dt_scores.astype(BF), t_keys.astype(BF), 0, 0) + mm(t_probs.astype(BF), t_values.astype(BF), 0, 0)
    row_at = lax.broadcasted_iota(jnp.int32, dn.shape, 0)
    dq_back = mm(dt_q, small("tq"), 1, 1)
    for c in range(4):
        dn = dn + jnp.where(row_at == last_at[c], dq_back[c:c + 1], 0.0)
    dn_ref[...] = dn.astype(BF)
    arrive = []
    for k in (1, 2, 3):
        to, fro = (z + k) % 4, (z + 4 - k) % 4
        rows_to = dn_ref.at[pl.ds(pl.multiple_of(64 * to, 64), 64), :]
        copy = pltpu.make_async_remote_copy(rows_to, recv_t.at[z], send_sem.at[14, k], recv_sem.at[14, k],
                                            device_id=me.at_z(k), device_id_type=MESH)
        copy.start()
        started.append(copy)
        arrive.append(pltpu.make_async_remote_copy(rows_to, recv_t.at[fro], send_sem.at[14, k], recv_sem.at[14, k],
                                                   device_id=me.at_z(k), device_id_type=MESH))
    s_high, s_low = split_two(d_scores)
    q_high, q_low = split_two(p_probs)
    k_high, k_low = split_two(p_keys)
    v_high, v_low = split_two(p_values)
    left = jnp.concatenate([s_high.astype(F32), q_high.astype(F32)], 0)
    right = jnp.concatenate([k_high.astype(F32), v_high.astype(F32)], 0).astype(BF)
    send_t[...] = jnp.transpose(jnp.concatenate([left, jnp.zeros((104, left.shape[1]), F32)], 0))
    right = jnp.concatenate([right, jnp.zeros((104, width), BF)], 0)
    sums_ref[...] = jnp.zeros_like(sums_ref)
    tile = 128

    def step(n, carry):
        at_rows = pl.ds(pl.multiple_of(n * tile, tile), tile)
        d_final = mm(send_t[at_rows, :].astype(BF), right)
        d_y, gain, shift = norm_back_rows(block_ref[at_rows, :], iv(5), d_final)
        dy_ref[at_rows, :] = d_y
        branch_ref[at_rows, :] = d_y.astype(BF)
        sums_ref[5:6] += gain
        sums_ref[6:7] += shift
        sums_ref[4:5] += jnp.sum(d_y, 0, keepdims=True)
        return carry

    lax.fori_loop(0, final_ref.shape[0] // tile, step, 0)
    w_got = by_head(get_p())
    dq_rows = fold(mm_two(w_got, small("pk")))
    dq_my = jnp.sum(dq_rows, 0, keepdims=True)
    recv_t[z] = dn_ref[pl.ds(pl.multiple_of(64 * z, 64), 64), :]
    for a in arrive:
        a.wait_recv()
    dt_normed = sum(recv_t[q].astype(F32) for q in range(4))
    x_mine = tokens_ref[pl.ds(pl.multiple_of(64 * z, 64), 64), :].astype(F32)
    d_cap, tv0, tv1 = norm_back_rows(x_mine, tv(0), dt_normed)
    row_c = lax.broadcasted_iota(jnp.int32, d_cap.shape, 0)
    for c in range(4):
        d_cap = d_cap + jnp.where((row_c == 16 * c + 15) & (z == 3), dt_hidden[c:c + 1], 0.0)
    dcap_ref[...] = d_cap
    first = (z == 0).astype(F32)
    sums_ref[8:9] = dv8 * first
    sums_ref[9:10] = dv9 * first
    sums_ref[10:11] = dv10 * first
    sums_ref[11:12] = tv0
    sums_ref[12:13] = tv1
    sums_ref[13:14] = tv2 * first
    sums_ref[14:15] = tv3 * first
    sums_ref[15:16] = tv4 * first
    sums_ref[16:17] = tv5 * first
    sums_ref[17:18] = tv6 * first
    own_row = lambda a: sum(jnp.where(z == q, a[q:q + 1].astype(F32), 0.0) for q in range(4))
    pick = lambda a: a[:, 0:part].astype(F32)
    wide = jnp.concatenate
    pieces = [
        dh_upper, dt_upper.astype(F32), h_active.astype(F32), t_active.astype(F32),
        wide([pick(d_pooled), pick(pooled), pick(dt_q), pick(t_q)], 1),
        wide([pick(dt_mixed), pick(t_mixed), jnp.broadcast_to(pick(dq_my), (4, part)), jnp.broadcast_to(pick(p_q), (4, part))], 1),
        own_row(h_normed), own_row(d_start), own_row(t_last), own_row(t_second),
        own_row(dt_attend), own_row(dt_branch), own_row(t_final), pad1,
        used, t_used, tk_used, p_used,
    ]
    rows_ref[...] = jnp.concatenate(pieces, 0).astype(BF)
    for copy in started:
        copy.wait_send()

def middle(final, block_out, tokens, tp, downs, outs, ivec, tvec, pbias, tbias, label, temp, cid, n_dp):
    length, width = final.shape
    v = pl.BlockSpec(memory_space=pltpu.VMEM)
    f = lambda *s: jax.ShapeDtypeStruct(s, F32)
    return pl.pallas_call(
        middle_kernel,
        in_specs=[v] * 11 + [pl.BlockSpec(memory_space=pltpu.SMEM)],
        out_specs=[v] * 7,
        out_shape=[f(length, width), jax.ShapeDtypeStruct((length, width), BF), jax.ShapeDtypeStruct((ROWS, width), BF), f(24, width), f(64, width), f(8, 128), f(8 * n_dp, width)],
        scratch_shapes=[
            pltpu.VMEM((256, width), F32), pltpu.VMEM((256, width), BF),
            pltpu.VMEM((12, 4, 4, width), F32), pltpu.VMEM((12, 4, 4, width), F32),
            pltpu.VMEM((8, width), F32), pltpu.VMEM((n_dp, 8, width), F32),
            pltpu.VMEM((length, 128), F32), pltpu.VMEM((4, 64, width), BF),
            pltpu.SemaphoreType.DMA((16, 8)), pltpu.SemaphoreType.DMA((16, 8)),
        ],
        compiler_params=pltpu.CompilerParams(collective_id=cid, has_side_effects=True, vmem_limit_bytes=50 << 20),
    )(final, block_out, tokens, tp, downs, outs, ivec, tvec, pbias, tbias, label, temp)


def plane_moves(me, out, s):
    y, x, c = me.y, me.x, me.c
    n = out.shape[-1] // 2
    left, right = (lambda r: r.at[..., 0:n]), (lambda r: r.at[..., n : 2 * n])
    if s == 3:
        own = out.at[y, x, c]
        yield 6, left(own), left(own), me.at_x, None, left(out.at[y, 1 - x, c]), None
        yield 7, right(own), right(own), me.at_y, None, right(out.at[1 - y, x, c]), None
    elif s == 4:
        own = out.at[y, :, c]
        yield 8, left(own), left(own), me.at_y, None, left(out.at[1 - y, :, c]), None
        own = out.at[:, x, c]
        yield 9, right(own), right(own), me.at_x, None, right(out.at[:, 1 - x, c]), None
    else:
        mine = out.at[:, :, c]
        yield 10, mine, mine, me.at_c, None, out.at[:, :, 1 - c], None


def turn_moves(me, src, home, split):
    z = me.z
    for k in (3, 2, 1):
        to, fro = (z + k) % 4, (z + 4 - k) % 4
        yield k - 1, src.at[to] if split else src, home.at[z], me.at_z(k), None, home.at[fro], None


def run_moves(moves, act, send, recv):
    for slot, src, dst, dev, go, come, arrives in moves:
        make = lambda a, b: pltpu.make_async_remote_copy(
            a, b, send.at[slot], recv.at[slot], device_id=dev, device_id_type=MESH
        )
        if act == "arrived":
            copy, when = make(src, come).wait_recv, arrives
        else:
            copy, when = getattr(make(src, dst), "start" if act == "start" else "wait_send"), go
        if when is None:
            copy()
        else:
            pl.when(when)(lambda: copy())


class Spread:
    stages = 6

    def __init__(self, me, src, out, send, recv, local):
        self.me, self.src, self.out, self.send, self.recv, self.local = me, src, out, send, recv, local

    def moves(self, s):
        me, out = self.me, self.out
        y, x, c, z = me.y, me.x, me.c, me.z
        if s < 3:
            home = out.at[y, x, c]
            for up in (True, False):
                step = -s if up else s
                slab, come = z + step, z + step + (-1 if up else 1)
                go = ((slab >= 0) & (z < 3)) if up else ((slab < 4) & (z > 0))
                arrives = (come >= 0) & (come < 4)
                slab, come = jnp.clip(slab, 0, 3), jnp.clip(come, 0, 3)
                src = self.src if s == 0 else home.at[slab]
                yield s + (0 if up else 3), src, home.at[slab], me.at_z(1 if up else 3), go, home.at[come], arrives
        else:
            yield from plane_moves(me, out, s)

    def each(self, s, act):
        run_moves(self.moves(s), act, self.send, self.recv)

    def keep(self):
        me = self.me
        return pltpu.make_async_copy(self.src, self.out.at[me.y, me.x, me.c, me.z], self.local)

    def begin(self, s):
        if s == 0:
            self.keep().start()
        else:
            self.each(s - 1, "arrived")
        if s == 3:
            self.keep().wait()
        self.each(s, "start")

    def finish(self):
        self.each(5, "arrived")
        for s in range(6):
            self.each(s, "sent")


def attend_bwd_kernel_hosting(q_ref, k_ref, v_ref, do_ref, lse_ref, d_ref, rows_ref, dq_ref, dk_ref, dv_ref, all_ref, send, recv, local):
    h_at = pl.program_id(0)
    me = Place()
    spread = Spread(me, rows_ref, all_ref, send, recv, local)

    def first():
        greet([me.at_z(1), me.at_z(2), me.at_z(3), me.at_x, me.at_y, me.at_c])
        spread.begin(0)

    pl.when(h_at == 0)(first)
    for s in range(1, 6):
        pl.when(h_at == s)(partial(spread.begin, s))
    q = q_ref[...] * 0.125
    k, v, do = k_ref[...], v_ref[...], do_ref[...]
    lane = lax.broadcasted_iota(jnp.int32, k.shape, 1)
    dqs, dks, dvs = [], [], []
    for h in range(2):
        keep = (lane < 64) if h == 0 else (lane >= 64)
        s = mm(jnp.where(keep, k, jnp.zeros_like(k)), q, 1, 1)
        p = jnp.exp(s - lse_ref[0, h : h + 1, :])
        dp = mm(jnp.where(keep, v, jnp.zeros_like(v)), do, 1, 1)
        ds = (p * (dp - d_ref[0, h : h + 1, :])).astype(BF)
        dvs.append(mm(p.astype(BF), do))
        dks.append(mm(ds, q))
        dqs.append(mm(ds, k, 0, 0))
    low = lane < 64
    dq_ref[...] = (jnp.where(low, dqs[0], dqs[1]) * 0.125).astype(BF)
    dk_ref[...] = jnp.where(low, dks[0], dks[1]).astype(BF)
    dv_ref[...] = jnp.where(low, dvs[0], dvs[1]).astype(BF)
    pl.when(h_at == 5)(spread.finish)


def attend_bwd_and_spread(proj, d_out, lse, inner, rows, cid):
    length, width = proj.shape[0], proj.shape[1] // 3
    pairs = width // 128
    block = lambda part: pl.BlockSpec((length, 128), lambda h: (0, part * pairs + h))
    row = pl.BlockSpec((1, 2, length), lambda h: (h, 0, 0))
    hbm = pl.BlockSpec(memory_space=pl.ANY)
    result = jax.ShapeDtypeStruct((length, width), BF)
    return pl.pallas_call(
        attend_bwd_kernel_hosting,
        grid=(pairs,),
        in_specs=[block(0), block(1), block(2), block(0), row, row, hbm],
        out_specs=[block(0)] * 3 + [hbm],
        out_shape=[result] * 3 + [jax.ShapeDtypeStruct((2, 2, 2, 4) + rows.shape, rows.dtype)],
        scratch_shapes=[pltpu.SemaphoreType.DMA((11,)), pltpu.SemaphoreType.DMA((11,)), pltpu.SemaphoreType.DMA],
        compiler_params=pltpu.CompilerParams(collective_id=cid, has_side_effects=True, vmem_limit_bytes=56 << 20),
    )(proj, proj, proj, d_out, lse, inner, rows)


def attend_fwd_kernel_hosting(q_ref, k_ref, v_ref, split_ref, downs_ref, tokens_ref,
                              o_ref, lse_ref, tp_ref, down_ref, token_ref, send, recv, local):
    h_at = pl.program_id(0)
    me = Place()
    home = tp_ref.at[me.y, me.x, me.c]
    down_home = down_ref.at[me.y, me.x, me.c]
    keeps = [
        pltpu.make_async_copy(split_ref.at[me.z], home.at[me.z], local.at[0]),
        pltpu.make_async_copy(downs_ref, down_home, local.at[1]),
        pltpu.make_async_copy(tokens_ref, token_ref.at[me.z], local.at[2]),
    ]
    groups = {
        "split": (lambda: turn_moves(me, split_ref, home, True), 0),
        "tokens": (lambda: turn_moves(me, tokens_ref, token_ref, False), 2),
        "split_xy": (lambda: plane_moves(me, tp_ref, 3), 0),
        "down_xy": (lambda: plane_moves(me, down_ref, 3), 1),
    }

    def act(name, what):
        moves, a = groups[name]
        run_moves(moves(), what, send.at[a], recv.at[a])

    def first():
        greet([me.at_z(1), me.at_z(2), me.at_z(3), me.at_x, me.at_y])
        for keep in keeps:
            keep.start()
        act("split", "start")
        keeps[1].wait()
        act("down_xy", "start")

    def middle_step():
        act("split", "arrived")
        keeps[0].wait()
        act("split_xy", "start")
        act("tokens", "start")

    def last():
        for name in ("split_xy", "down_xy", "tokens"):
            act(name, "arrived")
        keeps[2].wait()
        for name in groups:
            act(name, "sent")

    pl.when(h_at == 0)(first)
    pl.when(h_at == 3)(middle_step)
    attend_fwd_kernel(q_ref, k_ref, v_ref, o_ref, lse_ref)
    pl.when(h_at == pl.num_programs(0) - 1)(last)


def attend_fwd_and_gather(proj, split, downs, tokens, cid):
    length, width = proj.shape[0], proj.shape[1] // 3
    pairs = width // 128
    block = lambda part: pl.BlockSpec((length, 128), lambda h: (0, part * pairs + h))
    hbm = pl.BlockSpec(memory_space=pl.ANY)
    s = jax.ShapeDtypeStruct
    return pl.pallas_call(
        attend_fwd_kernel_hosting,
        grid=(pairs,),
        in_specs=[block(0), block(1), block(2), hbm, hbm, hbm],
        out_specs=[block(0), pl.BlockSpec((1, 2, length), lambda h: (h, 0, 0)), hbm, hbm, hbm],
        out_shape=[
            s((length, width), BF),
            s((pairs, 2, length), F32),
            s((2, 2, 2) + split.shape, BF),
            s((2, 2, 2) + downs.shape, BF),
            s((4,) + tokens.shape, BF),
        ],
        scratch_shapes=[pltpu.SemaphoreType.DMA((3, 11)), pltpu.SemaphoreType.DMA((3, 11)), pltpu.SemaphoreType.DMA((3,))],
        compiler_params=pltpu.CompilerParams(collective_id=cid, has_side_effects=True, vmem_limit_bytes=48 << 20),
    )(proj, proj, proj, split, downs, tokens)


def mlp_fwd_kernel(x_ref, mixed_ref, wo_ref, wu_ref, wd_ref, bias_ref, vec_ref, tp_in, down_in,
                   hidden_ref, second_ref, active_ref, slope_ref, block_ref, final_ref, tp_ref, down_ref, total, send, recv):
    k = pl.program_id(0)
    me = Place()

    def act(s, what):
        for a, ref in enumerate((tp_ref, down_ref)):
            run_moves(plane_moves(me, ref, s), what, send.at[a], recv.at[a])

    def first():
        greet([me.at_x, me.at_y, me.at_c])
        act(4, "start")

    def then():
        act(4, "arrived")
        act(5, "start")

    pl.when(k == 0)(first)
    pl.when(k == pl.num_programs(0) - 1)(then)
    vec = vec_ref[...]

    @pl.when(k == 0)
    def _():
        hidden = x_ref[...].astype(F32) + mm(mixed_ref[...], wo_ref[...])
        hidden_ref[...] = hidden
        second_ref[...] = layer_norm(hidden, vec[2:3], vec[3:4]).astype(BF)
        total[...] = hidden + vec[4:5]

    value, slope = gelu_pair(mm(second_ref[...], wu_ref[...]) + bias_ref[0])
    active = value.astype(BF)
    active_ref[...] = active
    slope_ref[...] = slope.astype(BF)
    total[...] += mm(active, wd_ref[...])

    @pl.when(k == pl.num_programs(0) - 1)
    def _():
        block_ref[...] = total[...]
        final_ref[...] = layer_norm(total[...], vec[5:6], vec[6:7]).astype(BF)
        act(5, "arrived")
        act(4, "sent")
        act(5, "sent")


def mlp_fwd(x, mixed, main, bias, vec, fold, tp, downs, cid):
    rows, width = mixed.shape
    whole = pl.BlockSpec((rows, width), lambda k: (0, 0))
    tile = pl.BlockSpec((rows, width), lambda k: (0, k))
    at = lambda f: pl.BlockSpec((width, width), lambda k: (0, f(k)))
    s = lambda n, t: jax.ShapeDtypeStruct((rows, n * width), t)
    hbm = pl.BlockSpec(memory_space=pl.ANY)
    return pl.pallas_call(
        mlp_fwd_kernel,
        grid=(fold,),
        in_specs=[whole, whole, at(lambda k: 0), at(lambda k: 1 + k), at(lambda k: 1 + fold + k),
                  pl.BlockSpec((1, 1, width), lambda k: (k, 0, 0)), pl.BlockSpec(vec.shape, lambda k: (0, 0)), hbm, hbm],
        out_specs=[whole, whole, tile, tile, whole, whole, hbm, hbm],
        out_shape=[s(1, F32), s(1, BF), s(fold, BF), s(fold, BF), s(1, F32), s(1, BF),
                   jax.ShapeDtypeStruct(tp.shape, BF), jax.ShapeDtypeStruct(downs.shape, BF)],
        scratch_shapes=[pltpu.VMEM((rows, width), F32), pltpu.SemaphoreType.DMA((2, 11)), pltpu.SemaphoreType.DMA((2, 11))],
        input_output_aliases={7: 6, 8: 7},
        compiler_params=pltpu.CompilerParams(collective_id=cid, has_side_effects=True, vmem_limit_bytes=56 << 20),
    )(x, mixed, main, main, main, bias.reshape(fold, 1, width), vec, tp, downs)


def mlp_bwd_kernel(dy_ref, branch_ref, active_ref, slope_ref, second_ref, hidden_ref, mixed_ref,
                   wo_ref, wu_ref, wd_ref, vec_ref,
                   g_ref, dhid_ref, dmix_ref, inner_ref, bias_ref, dvec_ref, total):
    k = pl.program_id(0)
    fold = pl.num_programs(0)
    width = mixed_ref.shape[1]
    branch = branch_ref[...]
    columns = lambda n: pl.ds(pl.multiple_of(n * width, width), width)
    g_ref[:, columns(1 + fold + k)] = mm(active_ref[...], branch, 0, 0).astype(BF)
    d_upper_f = mm(branch, wd_ref[...], 1, 1) * slope_ref[...].astype(F32)
    bias_ref[0] = jnp.sum(d_upper_f, 0, keepdims=True)
    d_upper = d_upper_f.astype(BF)
    g_ref[:, columns(1 + k)] = mm(second_ref[...], d_upper, 0, 0).astype(BF)
    back = mm(d_upper, wu_ref[...], 1, 1)

    @pl.when(k == 0)
    def _():
        total[...] = back

    @pl.when(k > 0)
    def _():
        total[...] += back

    @pl.when(k == fold - 1)
    def _():
        vec = vec_ref[...]
        d_hidden, gain, shift = norm_back_rows(hidden_ref[...], vec[2:3], total[...])
        dvec_ref[0:1] = gain
        dvec_ref[1:2] = shift
        d_hidden = dy_ref[...] + d_hidden
        dhid_ref[...] = d_hidden
        d_attend = d_hidden.astype(BF)
        mixed = mixed_ref[...]
        g_ref[:, 0:width] = mm(mixed, d_attend, 0, 0).astype(BF)
        d_mixed = mm(d_attend, wo_ref[...], 1, 1).astype(BF)
        dmix_ref[...] = d_mixed
        head = lax.broadcasted_iota(jnp.int32, (16, width), 0)
        lane = lax.broadcasted_iota(jnp.int32, (16, width), 1)
        own = (lane // (width // HEADS) == head).astype(BF)
        high, low = split_two(d_mixed.astype(F32) * mixed.astype(F32))
        sums = mm(own, high, 1, 1) + mm(own, low, 1, 1)
        for h in range(HEADS // 2):
            inner_ref[h] = sums[2 * h : 2 * h + 2]


def mlp_bwd(dy, branch, active, slope, second, hidden, mixed, main, vec, fold):
    rows, width = mixed.shape
    whole = pl.BlockSpec((rows, width), lambda k: (0, 0))
    tile = pl.BlockSpec((rows, width), lambda k: (0, k))
    at = lambda f: pl.BlockSpec((width, width), lambda k: (0, f(k)))
    f = lambda *s: jax.ShapeDtypeStruct(s, F32)
    return pl.pallas_call(
        mlp_bwd_kernel,
        grid=(fold,),
        in_specs=[whole, whole, tile, tile, whole, whole, whole,
                  at(lambda k: 0), at(lambda k: 1 + k), at(lambda k: 1 + fold + k), pl.BlockSpec(vec.shape, lambda k: (0, 0))],
        out_specs=[pl.BlockSpec((width, (1 + 2 * fold) * width), lambda k: (0, 0)), whole, whole,
                   pl.BlockSpec((HEADS // 2, 2, rows), lambda k: (0, 0, 0)),
                   pl.BlockSpec((1, 1, width), lambda k: (k, 0, 0)), pl.BlockSpec((8, width), lambda k: (0, 0))],
        out_shape=[jax.ShapeDtypeStruct((width, (1 + 2 * fold) * width), BF), f(rows, width),
                   jax.ShapeDtypeStruct((rows, width), BF), f(HEADS // 2, 2, rows), f(fold, 1, width), f(8, width)],
        scratch_shapes=[pltpu.VMEM((rows, width), F32)],
        compiler_params=pltpu.CompilerParams(vmem_limit_bytes=60 << 20),
    )(dy, branch, active, slope, second, hidden, mixed, main, main, main, vec)


def project_bwd_kernel(dq_ref, dk_ref, dv_ref, normed_ref, w_ref, x_ref, dhid_ref, sums_ref, vec_ref, g_ref, dx_ref):
    width = dq_ref.shape[1]
    normed = normed_ref[...]
    back = None
    for n, ref in enumerate((dq_ref, dk_ref, dv_ref)):
        d = ref[...]
        g_ref[:, n * width : (n + 1) * width] = mm(normed, d, 0, 0).astype(BF)
        part = mm(d, w_ref[:, n * width : (n + 1) * width], 1, 1)
        back = part if back is None else back + part
    d_x, gain, shift = norm_back_rows(x_ref[...].astype(F32), vec_ref[0:1], back)
    dx_ref[...] = (dhid_ref[...] + d_x).astype(BF)
    sums = jnp.concatenate([gain, shift, sums_ref[2:, :]], 0)
    sums = jnp.concatenate([sums, jnp.zeros((128 - sums.shape[0], width), F32)], 0)
    g_ref[:, 3 * width : 3 * width + 128] = jnp.transpose(sums).astype(BF)
    g_ref[:, 3 * width + 128 : 3 * width + 256] = jnp.zeros((width, 128), BF)


def project_bwd(dq, dk, dv, normed, w_in, x, d_hidden, sums, vec):
    rows, width = dq.shape
    v = pl.BlockSpec(memory_space=pltpu.VMEM)
    return pl.pallas_call(
        project_bwd_kernel,
        in_specs=[v] * 9,
        out_specs=[v] * 2,
        out_shape=[jax.ShapeDtypeStruct((width, 3 * width + 256), BF), jax.ShapeDtypeStruct((rows, width), BF)],
        compiler_params=pltpu.CompilerParams(vmem_limit_bytes=56 << 20),
    )(dq, dk, dv, normed, w_in, x, d_hidden, sums, vec)


def outer_kernel(rows_ref, dimage_ref, dtext_ref,
                 pup_ref, tup_ref, pdown_ref, tdown_ref, pout_ref, tout_ref, thead_ref,
                 tq_ref, tk_ref, tv_ref, pv_ref, pk_ref, bias_ref):
    at_dp, z = lax.axis_index("dp"), lax.axis_index("seq")
    n_dp, n_z = 8, 4
    me = at_dp * n_z + z
    width = rows_ref.shape[2]
    part, quarter = width // 32, width // n_z
    wide_part = 4 * part
    n = n_dp * n_z
    each = quarter // part

    def iota(shape, d):
        return lax.broadcasted_iota(jnp.int32, shape, d)

    def selector(count, first):
        return (iota((count, width), 1) == iota((count, width), 0) + first).astype(BF)

    def group(r):
        return jnp.concatenate([rows_ref[r + c] for c in range(4)], 0)

    cols = jnp.concatenate(
        [mm(selector(part, part * me), rows_ref[r], 1, 1) for r in range(24, 80)], 1
    ).astype(BF)
    get = lambda r, count=1: cols[:, n * (r - 24) : n * (r - 24 + count)]
    a, b = iota((4 * n, n), 0), iota((4 * n, n), 1)
    same = ((a % n) // n_z == b // n_z) & (a // n == b % n_z)
    keep = lambda which: (same & (a % n_z == which)).astype(BF)
    units = selector(wide_part, wide_part * at_dp)
    heads = selector(part, quarter + part * (me % each))
    to_mine, to_head = keep(z), keep(me // each)
    chosen = lambda sel, r, perm: mm(mm(sel, group(r), 1, 1).astype(BF), perm).astype(BF)
    pdown_ref[...] = mm(chosen(units, 8, to_mine), dimage_ref[...])
    tdown_ref[...] = mm(chosen(units, 12, to_mine), rows_ref[29])
    pout_ref[...] = mm(chosen(heads, 16, to_head), rows_ref[25])
    tout_ref[...] = mm(chosen(heads, 20, to_head), rows_ref[28])
    thead_ref[...] = mm(get(30), dtext_ref[...])
    ones = jnp.ones((n, 128), BF)
    bias_ref[0] = mm(chosen(units, 0, to_mine), ones)
    bias_ref[1] = mm(chosen(units, 4, to_mine), ones)
    a, b = iota((n, 4 * n), 0), iota((n, 4 * n), 1)
    spread = ((b % n) // n_z == a // n_z) & (b // n == a % n_z)
    spread = spread.astype(BF)
    lane_z = iota((1, 4 * n), 1) % n_z
    masks = [(lane_z == q).astype(BF) for q in range(n_z)]

    def blocks(values):
        return jnp.concatenate([v * m for v, m in zip(values, masks)], 0)

    by_image = lambda r: mm(get(r), spread).astype(BF)
    g16, g20 = group(16), group(20)

    def put(ref, value, first):
        for q in range(n_z):
            ref[q] = value[q * part : (q + 1) * part, first : first + ref.shape[2]]

    put(pup_ref, mm(blocks([by_image(24)] * 4), group(0)), 0)
    put(tup_ref, mm(blocks([by_image(27)] * 4), group(4)), 0)
    put(tq_ref, mm(blocks([by_image(26)] * 4), g16), 2 * quarter)
    lane = iota((1, width), 1)
    count = HEADS // n_z
    hw = quarter // count

    def by_head(values_of, rhs, first):
        total = None
        for h in range(count):
            own = ((lane >= first + hw * h) & (lane < first + hw * h + hw)).astype(F32)
            one = mm(blocks(values_of(h)), rhs) * own
            total = one if total is None else total + one
        return total

    put(tk_ref, by_head(lambda h: [get(56 + 4 * h, 4)] * 4, g16, 3 * quarter), 3 * quarter)
    put(tv_ref, by_head(lambda h: [get(44 + 4 * h, 4)] * 4, g20, 0), 0)
    put(pv_ref, by_head(lambda h: [by_image(32 + count * q + h) for q in range(n_z)], g16, 0), 0)
    a, b = iota((HEADS * n, 128), 0), iota((HEADS * n, 128), 1)
    pk_ref[...] = mm(get(68, HEADS), (a // n == b).astype(BF))


def outer_grads(rows, d_image, d_text):
    width = rows.shape[2]
    part, quarter = width // 32, width // 4
    v = pl.BlockSpec(memory_space=pltpu.VMEM)
    f = lambda *s: jax.ShapeDtypeStruct(s, F32)
    return pl.pallas_call(
        outer_kernel,
        in_specs=[v] * 3,
        out_specs=[v] * 13,
        out_shape=[f(4, part, width), f(4, part, width), f(4 * part, width), f(4 * part, width), f(part, width), f(part, width),
                   f(part, width), f(4, part, quarter), f(4, part, quarter), f(4, part, quarter), f(4, part, quarter),
                   f(part, 128), f(2, 4 * part, 128)],
        compiler_params=pltpu.CompilerParams(vmem_limit_bytes=48 << 20),
    )(rows, d_image, d_text)


def fast_program(
    patches, captions, pairs,
    image_attend_in, image_attend_out, image_up_weight, image_up_bias, image_down_weight,
    image_vectors, probe_query_weight, probe_pair_weight, probe_out_weight, probe_up_weight,
    probe_up_bias, probe_down_weight, text_attend_in, text_attend_out, text_up_weight,
    text_up_bias, text_down_weight, text_vectors, text_head_weight, temp_bias,
):
    n_dp, n_z = lax.axis_size("dp"), lax.axis_size("seq")
    world = n_dp * n_z
    at_dp, at_z = lax.axis_index("dp"), lax.axis_index("seq")
    me = at_dp * n_z + at_z
    width = patches.shape[-1]
    head_width = width // HEADS
    hidden_width = image_up_weight.shape[1]
    part, quarter = width // world, width // n_z
    wide_part = hidden_width // world
    fold = hidden_width // width
    length = patches.shape[1] * n_z

    small = jnp.concatenate(
        [image_vectors.reshape(-1), text_vectors.reshape(-1), image_up_bias, probe_up_bias, text_up_bias]
    )
    sizes = [image_vectors.size, text_vectors.size, image_up_bias.size, probe_up_bias.size, text_up_bias.size]
    small = jnp.pad(small, (0, 2048 - small.shape[0])).reshape(16, 128)

    def by_units(w):
        return w.reshape(part, n_dp, n_z, wide_part).transpose(2, 0, 1, 3).reshape(n_z, part, width)

    def by_heads(w):
        cut = w.reshape(part, n_z, quarter).transpose(1, 0, 2)
        return jnp.pad(cut, ((0, 0), (0, 0), (0, 256 - quarter)))

    split = [by_units(probe_up_weight), by_units(text_up_weight)]
    split += [by_heads(text_attend_in[:, k * width : (k + 1) * width]) for k in range(3)]
    split += [by_heads(text_head_weight), by_heads(probe_query_weight)]
    split += [by_heads(probe_pair_weight[:, k * width : (k + 1) * width]) for k in range(2)]
    split = jnp.concatenate(split, 2)
    downs = jnp.concatenate([text_down_weight, probe_down_weight], 1)
    w_in, small_all, x = gather(
        [image_attend_in, small, patches],
        [("full", "S"), ("full", "C"), ("za", None)],
        [(0, 0), (1, 0), (0, 1), (1, 1), (0, 2), (1, 2), (0, 3), (2, 0), (1, 3), (0, 4), (1, 4), (0, 5), (1, 5)],
        1,
    )
    w_in = w_in.reshape(width, 3 * width)
    x = x.reshape(length, width)
    main = jnp.concatenate(
        [
            image_attend_out,
            image_up_weight.reshape(part, width, fold).transpose(0, 2, 1).reshape(part, hidden_width),
            image_down_weight.reshape(part, hidden_width),
            text_attend_out,
            probe_out_weight,
        ],
        1,
    )
    main = lax.all_gather(main, ALL, axis=0, tiled=True)
    outs = lax.dynamic_slice_in_dim(main[:, width + 2 * hidden_width :], at_z * quarter, quarter, 0)

    small_all = small_all.reshape(world, -1)
    cuts = [sum(sizes[:i]) for i in range(len(sizes) + 1)]
    pieces = [small_all[:, cuts[i] : cuts[i + 1]].astype(F32) for i in range(len(sizes))]
    ivec = pieces[0].reshape(world, -1, part).transpose(1, 0, 2).reshape(-1, width)
    tvec = pieces[1].reshape(world, -1, part).transpose(1, 0, 2).reshape(-1, width)
    i_bias = pieces[2].reshape(width, fold).T.reshape(1, hidden_width)

    def own_units(p):
        p = p.reshape(n_dp, n_z, wide_part)
        return lax.dynamic_index_in_dim(p, at_z, 1, False).reshape(1, width)

    p_bias, t_bias = own_units(pieces[3]), own_units(pieces[4])

    normed = layer_norm(x.astype(F32), ivec[0], ivec[1]).astype(BF)
    proj = mm(normed, w_in).astype(BF)
    mixed, lse, tp, downs, tokens = attend_fwd_and_gather(proj, split, downs, captions, 5)
    hidden, second, active, slope, block_out, final, tp, downs = mlp_fwd(
        x, mixed, main, i_bias, ivec, fold, tp, downs, 6
    )
    tp, downs = tp.reshape(width, -1), downs.reshape(width, -1)

    labels = (2 * pairs - 1).astype(F32).reshape(n_dp, n_z, n_dp, n_z)
    labels = jnp.pad(labels, ((0, 0), (0, n_z), (0, 0), (n_z, 0))).reshape(2 * world, 2 * world)
    dy, d_branch, rows, sums, d_captions, loss_row, d_embeds = middle(
        final, block_out, tokens.reshape(-1, width), tp, downs, outs, ivec, tvec, p_bias, t_bias, labels, temp_bias, 2, n_dp
    )
    loss, grad_temp = loss_row[0, 0], loss_row[0, 1:3]
    grad_captions = d_captions.reshape(captions.shape)

    g_main, d_hidden, d_mixed, inner, g_bias, dvec = mlp_bwd(
        dy, d_branch, active, slope, second, hidden, mixed, main, ivec, fold
    )
    g_main = lax.psum_scatter(g_main, ALL, scatter_dimension=0, tiled=True).astype(F32)
    own_out = g_main[:, :width]
    own_up = g_main[:, width : width + hidden_width].reshape(part, fold, width)
    own_up = own_up.transpose(0, 2, 1).reshape(part, hidden_width)
    own_down = g_main[:, width + hidden_width :].reshape(wide_part, width)
    d_q, d_k, d_v, rows = attend_bwd_and_spread(proj, d_mixed, lse, inner, rows, 4)
    rows = rows.reshape(world, ROWS, width).transpose(1, 0, 2)
    sums = jnp.concatenate([dvec[0:2], dvec[0:2], sums[4:], g_bias.reshape(fold, width)], 0)
    g_in, d_x = project_bwd(d_q, d_k, d_v, normed, w_in, x, d_hidden, sums, ivec)
    own_in, moved = reduce_and_move(g_in, d_x, 3)
    grad_patches = moved.astype(F32)
    own_sums = own_in[:, 3 * width : 3 * width + 128].T
    own_in = own_in[:, : 3 * width]

    d_embeds = d_embeds.reshape(n_dp, 2, n_z, width).astype(BF)
    pup, tup, own_p_down, own_t_down, own_p_out, own_t_out, own_t_head, tq, tk, tv, pv, pk, biases = outer_grads(
        rows, d_embeds[:, 0].reshape(world, width), d_embeds[:, 1].reshape(world, width)
    )

    def wide(g):
        return g.reshape(n_z, part, n_dp, wide_part).transpose(1, 2, 0, 3).reshape(part, hidden_width)

    own_p_up, own_t_up = wide(pup), wide(tup)
    own_t_in = jnp.stack([tq, tk, tv]).transpose(2, 0, 1, 3).reshape(part, 3 * width)
    row20 = rows[20].reshape(n_dp, n_z, n_z, quarter).astype(F32)
    probe_query = row20[0, :, 3].reshape(HEADS, head_width)
    own_p_k = (pk[:, :HEADS, None] * probe_query[None]).reshape(part, width)
    own_p_pair = jnp.concatenate([own_p_k, pv.transpose(1, 0, 2).reshape(part, width)], 1)
    d_query = jnp.sum(row20[:, :, 2], 0).reshape(width)
    mine = lambda v, n: lax.dynamic_slice_in_dim(v, me * n, n, -1)
    own_p_query = mine(ivec[7], part)[:, None] * d_query[None, :]
    dv7 = jnp.sum(probe_query_weight.astype(F32) * d_query[None, :], 1)
    own_ivec = jnp.concatenate([own_sums[0:7], dv7[None], own_sums[8:11]], 0)
    own_tvec = own_sums[11:18]
    own_bias = own_sums[24 : 24 + fold].T.reshape(wide_part)
    return (
        loss, grad_patches, grad_captions,
        own_in, own_out, own_up, own_bias, own_down, own_ivec,
        own_p_query, own_p_pair, own_p_out, own_p_up, biases[0, :, 0], own_p_down,
        own_t_in, own_t_out, own_t_up, biases[1, :, 0], own_t_down, own_tvec, own_t_head,
        grad_temp,
    )


def solution(mesh):
    tokens, matrix, vector, table = P("dp", "seq", None), P(ALL, None), P(ALL), P(None, ALL)
    weights = (
        (matrix, matrix, matrix, vector, matrix, table, matrix, matrix, matrix, matrix, vector, matrix)
        + (matrix, matrix, matrix, vector, matrix, table, matrix)
    )
    return jax.shard_map(
        fast_program if mesh.shape["dp"] == 8 and mesh.shape["seq"] == 4 else device_program,
        mesh=mesh,
        in_specs=(tokens, tokens, P()) + weights + (P(),),
        out_specs=(P(), tokens, tokens) + weights + (P(),),
        check_vma=False,
    )
```

```python
from functools import partial

import jax
import jax.numpy as jnp
from jax import lax
from jax.experimental import pallas as pl
from jax.experimental.pallas import tpu as pltpu
from jax.sharding import PartitionSpec as P

HEADS = 12
ALL = ("dp", "seq")
F32, BF = jnp.float32, jnp.bfloat16
HIGH = lax.Precision.HIGHEST
EPS = 1e-06


def mm(a, b, ca=1, cb=0):
    return lax.dot_general(a, b, (((ca,), (cb,)), ((), ())), preferred_element_type=F32)


def mm_exact(a, b, ca=1, cb=0):
    return lax.dot_general(a, b, (((ca,), (cb,)), ((), ())), precision=HIGH, preferred_element_type=F32)


def split_two(a):
    high = a.astype(BF)
    return high, (a - high.astype(F32)).astype(BF)


def layer_norm(x, gain, shift):
    center = x - jnp.mean(x, -1, keepdims=True)
    spread = jnp.mean(center * center, -1, keepdims=True)
    return center * lax.rsqrt(spread + EPS) * gain + shift


def norm_back(x, gain, upstream):
    center = x - jnp.mean(x, -1, keepdims=True)
    inverse = lax.rsqrt(jnp.mean(center * center, -1, keepdims=True) + EPS)
    unit = center * inverse
    scaled = upstream * gain
    d_x = inverse * (
        scaled
        - jnp.mean(scaled, -1, keepdims=True)
        - unit * jnp.mean(scaled * unit, -1, keepdims=True)
    )
    return d_x, jnp.sum(upstream * unit, 0), jnp.sum(upstream, 0)


def norm_back_rows(x, gain, upstream):
    d_x, d_gain, d_shift = norm_back(x, gain, upstream)
    return d_x, d_gain[None], d_shift[None]


def mm_two(a, b, cb=0):
    n = a.shape[0]
    high = a.astype(BF).astype(F32)
    both = mm(jnp.concatenate([high, a - high], 0).astype(BF), b, 1, cb)
    return both[0:n] + both[n : 2 * n]


def gelu_pair(u):
    c = 0.7978845608028654
    t = jnp.tanh(c * (u + 0.044715 * u * u * u))
    value = 0.5 * u * (1.0 + t)
    slope = 0.5 * (1.0 + t) + 0.5 * u * (1.0 - t * t) * c * (1.0 + 3 * 0.044715 * u * u)
    return value, slope


def attend_fwd_kernel(q_ref, k_ref, v_ref, o_ref, lse_ref):
    q = q_ref[...] * 0.125
    k = k_ref[...]
    lane = lax.broadcasted_iota(jnp.int32, k.shape, 1)
    v_turned = jnp.transpose(v_ref[...])
    outs = []
    for h in range(2):
        keep = (lane < 64) if h == 0 else (lane >= 64)
        own_k = jnp.where(keep, k, jnp.zeros_like(k))
        s = mm(own_k, q, 1, 1)
        top = jnp.max(s, 0, keepdims=True)
        p = jnp.exp(s - top)
        total = jnp.sum(p, 0, keepdims=True)
        outs.append(mm(v_turned[64 * h : 64 * h + 64], p.astype(BF)) / total)
        lse_ref[0, h : h + 1, :] = top + jnp.log(total)
    o_ref[...] = jnp.transpose(jnp.concatenate(outs, 0)).astype(BF)


def attend_fwd(proj, length):
    rows, width = proj.shape[0], proj.shape[1] // 3
    pairs = width // 128
    block = lambda part: pl.BlockSpec((length, 128), lambda b, h: (b, part * pairs + h))
    return pl.pallas_call(
        attend_fwd_kernel,
        grid=(rows // length, pairs),
        in_specs=[block(0), block(1), block(2)],
        out_specs=[block(0), pl.BlockSpec((1, 2, length), lambda b, h: (h, 0, b))],
        out_shape=[
            jax.ShapeDtypeStruct((rows, width), BF),
            jax.ShapeDtypeStruct((pairs, 2, rows), F32),
        ],
        compiler_params=pltpu.CompilerParams(vmem_limit_bytes=48 << 20),
        cost_estimate=pl.CostEstimate(
            flops=rows * length * width * 8,
            bytes_accessed=rows * width * 8,
            transcendentals=rows * length * HEADS,
        ),
    )(proj, proj, proj)


def attend_bwd_kernel(q_ref, k_ref, v_ref, do_ref, lse_ref, d_ref, dq_ref, dk_ref, dv_ref):
    q = q_ref[...] * 0.125
    k, v, do = k_ref[...], v_ref[...], do_ref[...]
    lane = lax.broadcasted_iota(jnp.int32, k.shape, 1)
    dqs, dks, dvs = [], [], []
    for h in range(2):
        keep = (lane < 64) if h == 0 else (lane >= 64)
        s = mm(jnp.where(keep, k, jnp.zeros_like(k)), q, 1, 1)
        p = jnp.exp(s - lse_ref[0, h : h + 1, :])
        dp = mm(jnp.where(keep, v, jnp.zeros_like(v)), do, 1, 1)
        ds = (p * (dp - d_ref[0, h : h + 1, :])).astype(BF)
        dvs.append(mm(p.astype(BF), do))
        dks.append(mm(ds, q))
        dqs.append(mm(ds, k, 0, 0))
    low = lane < 64
    dq_ref[...] = (jnp.where(low, dqs[0], dqs[1]) * 0.125).astype(BF)
    dk_ref[...] = jnp.where(low, dks[0], dks[1]).astype(BF)
    dv_ref[...] = jnp.where(low, dvs[0], dvs[1]).astype(BF)


def attend_bwd(proj, d_out, lse, inner, length):
    rows, width = proj.shape[0], proj.shape[1] // 3
    pairs = width // 128
    block = lambda part: pl.BlockSpec((length, 128), lambda b, h: (b, part * pairs + h))
    row = pl.BlockSpec((1, 2, length), lambda b, h: (h, 0, b))
    result = jax.ShapeDtypeStruct((rows, width), BF)
    return pl.pallas_call(
        attend_bwd_kernel,
        grid=(rows // length, pairs),
        in_specs=[block(0), block(1), block(2), block(0), row, row],
        out_specs=[block(0)] * 3,
        out_shape=[result] * 3,
        compiler_params=pltpu.CompilerParams(vmem_limit_bytes=56 << 20),
        cost_estimate=pl.CostEstimate(
            flops=rows * length * width * 20,
            bytes_accessed=rows * width * 16,
            transcendentals=rows * length * HEADS,
        ),
    )(proj, proj, proj, d_out, lse, inner)


def head_blocks(width):
    own = jnp.arange(width)[None, :] // (width // HEADS) == jnp.arange(HEADS)[:, None]
    return own.astype(F32)


def spread_heads(rows):
    n, width = rows.shape
    return (rows[:, None, :] * head_blocks(width)[None]).reshape(n * HEADS, width)


def fold_heads(rows):
    total, width = rows.shape
    return jnp.sum(rows.reshape(total // HEADS, HEADS, width) * head_blocks(width)[None], 1)


def device_program(
    patches, captions, pairs,
    image_attend_in, image_attend_out, image_up_weight, image_up_bias, image_down_weight,
    image_vectors, probe_query_weight, probe_pair_weight, probe_out_weight, probe_up_weight,
    probe_up_bias, probe_down_weight, text_attend_in, text_attend_out, text_up_weight,
    text_up_bias, text_down_weight, text_vectors, text_head_weight, temp_bias,
):
    seq = lax.axis_size("seq")
    world = seq * lax.axis_size("dp")
    me = lax.axis_index("dp") * seq + lax.axis_index("seq")
    width = patches.shape[-1]
    head_width = width // HEADS
    factor = head_width ** (-0.5)
    hidden_width = image_up_weight.shape[1]
    part = width // world
    wide_part = hidden_width // world

    def gather(*weights):
        flat = jnp.concatenate([w.reshape(-1, width) for w in weights], 0)
        full = lax.all_gather(flat, ALL, axis=0)
        out, at = [], 0
        for w in weights:
            count = w.size // width
            piece = full[:, at : at + count]
            out.append(piece.reshape(world * w.shape[0], w.shape[1]))
            at += count
        return out

    small = jnp.concatenate(
        [image_vectors.reshape(-1), text_vectors.reshape(-1), image_up_bias, probe_up_bias, text_up_bias]
    )
    small_all = lax.all_gather(small, ALL, axis=0)
    sizes = [image_vectors.size, text_vectors.size, image_up_bias.size, probe_up_bias.size, text_up_bias.size]
    cuts = [sum(sizes[:i]) for i in range(len(sizes) + 1)]
    pieces = [small_all[:, cuts[i] : cuts[i + 1]].astype(F32) for i in range(len(sizes))]
    ivec = pieces[0].reshape(world, -1, part).transpose(1, 0, 2).reshape(-1, width)
    tvec = pieces[1].reshape(world, -1, part).transpose(1, 0, 2).reshape(-1, width)
    i_bias, p_bias, t_bias = (p.reshape(-1) for p in pieces[2:])

    (w_in,) = gather(image_attend_in)
    w_out, w_up, w_down = gather(image_attend_out, image_up_weight, image_down_weight)
    tw_in, tw_out, tw_up, tw_down, tw_head, pw_query, pw_pair, pw_out, pw_up, pw_down = gather(
        text_attend_in, text_attend_out, text_up_weight, text_down_weight, text_head_weight,
        probe_query_weight, probe_pair_weight, probe_out_weight, probe_up_weight, probe_down_weight,
    )

    def to_owner(x):
        return lax.all_to_all(x, "seq", 0, 1, tiled=True)

    x = to_owner(patches)
    own, length = x.shape[0], x.shape[1]
    x = x.reshape(own * length, width).astype(F32)
    captions_own = to_owner(captions)
    text_length = captions_own.shape[1]

    normed = layer_norm(x, ivec[0], ivec[1]).astype(BF)
    proj = mm(normed, w_in).astype(BF)
    mixed, lse = attend_fwd(proj, length)
    hidden = x + mm(mixed, w_out)
    second = layer_norm(hidden, ivec[2], ivec[3]).astype(BF)
    value, slope = gelu_pair(mm(second, w_up) + i_bias)
    active, slope = value.astype(BF), slope.astype(BF)
    block_out = hidden + mm(active, w_down) + ivec[4]
    final = layer_norm(block_out, ivec[5], ivec[6]).astype(BF)

    t_x = captions_own.astype(F32)
    t_normed = layer_norm(t_x, tvec[0], tvec[1]).astype(BF)
    t_last = t_normed[:, -1]
    tw_q, tw_k, tw_v = tw_in[:, :width], tw_in[:, width : 2 * width], tw_in[:, 2 * width :]
    t_q = mm(t_last, tw_q).astype(BF)
    t_keys = mm(spread_heads(t_q.astype(F32)).astype(BF), tw_k, 1, 1) * factor
    t_keys = t_keys.reshape(own, HEADS, width)
    k_high, k_low = split_two(t_keys)
    scores = jnp.einsum("bsd,bhd->bsh", t_normed, k_high, preferred_element_type=F32)
    scores += jnp.einsum("bsd,bhd->bsh", t_normed, k_low, preferred_element_type=F32)
    t_probs = jax.nn.softmax(scores, axis=1)
    t_used = jnp.einsum("bsh,bsd->bhd", t_probs, t_normed.astype(F32), precision=HIGH)
    t_mixed = fold_heads(mm(t_used.reshape(own * HEADS, width).astype(BF), tw_v)).astype(BF)
    t_hidden = t_x[:, -1] + mm(t_mixed, tw_out)
    t_second = layer_norm(t_hidden, tvec[2], tvec[3]).astype(BF)
    t_value, t_slope = gelu_pair(mm(t_second, tw_up) + t_bias)
    t_active = t_value.astype(BF)
    t_out = t_hidden + mm(t_active, tw_down) + tvec[4]
    t_final = layer_norm(t_out, tvec[5], tvec[6]).astype(BF)
    text_embed = mm(t_final, tw_head)

    pw_k, pw_v = pw_pair[:, :width], pw_pair[:, width:]
    probe_query = mm_exact(ivec[7:8], pw_query.astype(F32))
    p_keys = mm_exact(spread_heads(probe_query), pw_k.astype(F32), 1, 1) * factor
    k_high, k_low = split_two(p_keys)
    pool_scores = mm(k_high, final, 1, 1) + mm(k_low, final, 1, 1)
    pool_scores = pool_scores.reshape(HEADS, own, length)
    pool_probs = jax.nn.softmax(pool_scores, axis=-1)
    final_own = final.reshape(own, length, width)
    p_high, p_low = split_two(pool_probs)
    used = jnp.einsum("hbt,btd->bhd", p_high, final_own, preferred_element_type=F32)
    used += jnp.einsum("hbt,btd->bhd", p_low, final_own, preferred_element_type=F32)
    pooled = fold_heads(mm_exact(used.reshape(own * HEADS, width), pw_v.astype(F32)))
    head_start = mm_exact(pooled, pw_out.astype(F32))
    head_normed = layer_norm(head_start, ivec[8], ivec[9]).astype(BF)
    h_value, h_slope = gelu_pair(mm(head_normed, pw_up) + p_bias)
    head_active = h_value.astype(BF)
    image_embed = head_start + mm(head_active, pw_down) + ivec[10]

    embeds = lax.all_gather(jnp.stack([image_embed, text_embed], 1), ALL, axis=0, tiled=True)
    every_image, every_text = embeds[:, 0], embeds[:, 1]
    labels = (2 * pairs - 1).astype(F32)
    total = every_image.shape[0]
    i_scale = lax.rsqrt(jnp.sum(every_image * every_image, -1, keepdims=True) + EPS)
    t_scale = lax.rsqrt(jnp.sum(every_text * every_text, -1, keepdims=True) + EPS)
    z_i, z_t = every_image * i_scale, every_text * t_scale
    cosine = mm_exact(z_i, z_t, 1, 1)
    temper = jnp.exp(temp_bias[0])
    logits = cosine * temper + temp_bias[1]
    loss = -jnp.sum(jax.nn.log_sigmoid(labels * logits)) / total
    g = -labels * jax.nn.sigmoid(-labels * logits) / total
    grad_temp = jnp.stack([temper * jnp.sum(g * cosine), jnp.sum(g)])
    dz_i = temper * mm_exact(g, z_t)
    dz_t = temper * mm_exact(g, z_i, 0, 0)
    all_d_image = (dz_i - z_i * jnp.sum(z_i * dz_i, -1, keepdims=True)) * i_scale
    all_d_text = (dz_t - z_t * jnp.sum(z_t * dz_t, -1, keepdims=True)) * t_scale
    d_image = lax.dynamic_slice_in_dim(all_d_image, me * own, own, 0)
    d_text = lax.dynamic_slice_in_dim(all_d_text, me * own, own, 0)

    h_upper = mm_exact(d_image, pw_down.astype(F32), 1, 1) * h_slope
    h_norm = mm_exact(h_upper, pw_up.astype(F32), 1, 1)
    d_start, dv8, dv9 = norm_back(head_start, ivec[8], h_norm)
    d_start = d_image + d_start
    dv10 = jnp.sum(d_image, 0)
    d_pooled = mm_exact(d_start, pw_out.astype(F32), 1, 1)
    p_values = mm_exact(spread_heads(d_pooled), pw_v.astype(F32), 1, 1).reshape(own, HEADS, width)
    v_high, v_low = split_two(p_values)
    d_probs = jnp.einsum("bhd,btd->hbt", v_high, final_own, preferred_element_type=F32)
    d_probs += jnp.einsum("bhd,btd->hbt", v_low, final_own, preferred_element_type=F32)
    d_scores = pool_probs * (d_probs - jnp.sum(pool_probs * d_probs, -1, keepdims=True))
    s_high, s_low = split_two(d_scores)
    p_used = jnp.einsum("hbt,btd->bhd", s_high, final_own, preferred_element_type=F32)
    p_used += jnp.einsum("hbt,btd->bhd", s_low, final_own, preferred_element_type=F32)
    d_query = jnp.sum(fold_heads(mm_exact(p_used.reshape(own * HEADS, width), pw_k.astype(F32))), 0) * factor
    d_final = jnp.einsum(
        "hbt,bhd->btd",
        jnp.concatenate([s_high, p_high], 0),
        jnp.concatenate([jnp.broadcast_to(k_high[None], (own, HEADS, width)), v_high], 1),
        preferred_element_type=F32,
    ).reshape(own * length, width)
    dy, dv5, dv6 = norm_back(block_out, ivec[5], d_final)

    d_branch = dy.astype(BF)
    g_down = mm(active, d_branch, 0, 0)
    dv4 = jnp.sum(dy, 0)
    d_upper_f = mm(d_branch, w_down, 1, 1) * slope.astype(F32)
    d_upper = d_upper_f.astype(BF)
    g_bias = jnp.sum(d_upper_f, 0)
    g_up = mm(second, d_upper, 0, 0)
    d_hidden, dv2, dv3 = norm_back(hidden, ivec[2], mm(d_upper, w_up, 1, 1))
    d_hidden = dy + d_hidden
    d_attend = d_hidden.astype(BF)
    g_out = mm(mixed, d_attend, 0, 0)
    d_mixed = mm(d_attend, w_out, 1, 1).astype(BF)

    def scatter(*grads):
        flat = jnp.concatenate([g.astype(BF).reshape(world, -1, width) for g in grads], 1)
        mine = lax.psum_scatter(flat, ALL, scatter_dimension=0, tiled=False).astype(F32)
        out, at = [], 0
        for g in grads:
            count = g.size // world // width
            out.append(mine[at : at + count].reshape(g.shape[0] // world, g.shape[1]))
            at += count
        return out

    own_up, own_down, own_out = scatter(g_up, g_down, g_out)
    inner_rows = jnp.sum(
        (d_mixed.astype(F32) * mixed.astype(F32)).reshape(own * length, HEADS, head_width), -1
    ).T.reshape(HEADS // 2, 2, own * length)
    d_q, d_k, d_v = attend_bwd(proj, d_mixed, lse, inner_rows, length)
    g_in = jnp.concatenate([mm(normed, d, 0, 0) for d in (d_q, d_k, d_v)], 1)
    (own_in,) = scatter(g_in)
    d_normed = (
        mm(d_q, w_in[:, :width], 1, 1)
        + mm(d_k, w_in[:, width : 2 * width], 1, 1)
        + mm(d_v, w_in[:, 2 * width :], 1, 1)
    )
    d_x, dv0, dv1 = norm_back(x, ivec[0], d_normed)
    d_x = (d_hidden + d_x).reshape(own, length, width)

    def to_tokens(v):
        return lax.all_to_all(v.astype(BF), "seq", 1, 0, tiled=True).astype(F32)

    grad_patches = to_tokens(d_x)

    dt_final = mm_exact(d_text, tw_head.astype(F32), 1, 1)
    dt_out, tv5, tv6 = norm_back(t_out, tvec[5], dt_final)
    dt_branch = dt_out.astype(BF)
    tv4 = jnp.sum(dt_out, 0)
    dt_upper = (mm(dt_branch, tw_down, 1, 1) * t_slope).astype(BF)
    dt_hidden, tv2, tv3 = norm_back(t_hidden, tvec[2], mm(dt_upper, tw_up, 1, 1))
    dt_hidden = dt_out + dt_hidden
    dt_attend = dt_hidden.astype(BF)
    dt_mixed = mm(dt_attend, tw_out, 1, 1).astype(BF)
    t_values = mm(spread_heads(dt_mixed.astype(F32)).astype(BF), tw_v, 1, 1).reshape(own, HEADS, width)
    tv_high, tv_low = split_two(t_values)
    dt_probs = jnp.einsum("bsd,bhd->bsh", t_normed, tv_high, preferred_element_type=F32)
    dt_probs += jnp.einsum("bsd,bhd->bsh", t_normed, tv_low, preferred_element_type=F32)
    dt_scores = t_probs * (dt_probs - jnp.sum(t_probs * dt_probs, 1, keepdims=True))
    tk_used = jnp.einsum("bsh,bsd->bhd", dt_scores, t_normed.astype(F32), precision=HIGH)
    dt_q = fold_heads(mm(tk_used.reshape(own * HEADS, width).astype(BF), tw_k)) * factor
    dt_q = dt_q.astype(BF)
    dt_normed = jnp.einsum("bsh,bhd->bsd", dt_scores, t_keys, precision=HIGH)
    dt_normed += jnp.einsum("bsh,bhd->bsd", t_probs, t_values, precision=HIGH)
    dt_normed = dt_normed.at[:, -1].add(mm(dt_q, tw_q, 1, 1))
    flat_x = t_x.reshape(own * text_length, width)
    dt_x, tv0, tv1 = norm_back(flat_x, tvec[0], dt_normed.reshape(own * text_length, width))
    dt_x = dt_x.reshape(own, text_length, width).at[:, -1].add(dt_hidden)
    grad_captions = to_tokens(dt_x)

    whole = jnp.concatenate(
        [v.astype(F32) for v in (h_upper, d_start, d_pooled, dt_branch, dt_upper, dt_attend, dt_q, t_q, dt_mixed)], 1
    )
    whole = lax.all_gather(whole, ALL, axis=0, tiled=True)
    at = [0]

    def take(count):
        at[0] += count
        return whole[:, at[0] - count : at[0]]

    a_h_upper, a_start, a_pooled, a_branch, a_upper, a_attend, a_q, a_query, a_mixed = (
        take(c) for c in (hidden_width, width, width, width, hidden_width, width, width, width, width)
    )
    columns = [pooled, head_normed, t_last, t_mixed, t_second, t_final]
    columns += [used, t_used, tk_used * factor]
    columns += [head_active, t_active]
    columns = jnp.concatenate(
        [v.astype(F32).reshape(own, -1, width) for v in columns], 1
    )
    wide = 2 * (hidden_width // width)
    narrow = columns.shape[1] - wide
    cut = jnp.concatenate(
        [
            columns[:, :narrow].reshape(own, narrow, world, part).transpose(2, 0, 1, 3).reshape(world, own, -1),
            columns[:, narrow:].reshape(own, 2, world, wide_part).transpose(2, 0, 1, 3).reshape(world, own, -1),
        ],
        2,
    )
    cut = lax.all_to_all(cut, ALL, 0, 0, tiled=True).reshape(total, -1)
    slim = cut[:, : narrow * part].reshape(total, narrow, part)
    broad = cut[:, narrow * part :].reshape(total, 2, wide_part)

    def outer(rows, cols):
        return mm_exact(rows, cols, 0, 0)

    def outer_heads(rows, cols):
        cols = cols.reshape(total, HEADS, head_width)
        return jnp.einsum("chm,che->mhe", rows, cols, precision=HIGH).reshape(part, width)

    c_pooled, c_head, c_last, c_mixed, c_second, c_final = (slim[:, i] for i in range(6))
    c_used, ct_used, ctk_used = (slim[:, 6 + i * HEADS : 6 + (i + 1) * HEADS] for i in range(3))
    own_t_in = jnp.concatenate(
        [outer(c_last, a_q), outer_heads(ctk_used, a_query), outer_heads(ct_used, a_mixed)], 1
    )
    own_t_out = outer(c_mixed, a_attend)
    own_t_up = outer(c_second, a_upper)
    own_t_down = outer(broad[:, 1], a_branch)
    own_t_head = outer(c_final, all_d_text)
    own_p_out = outer(c_pooled, a_start)
    own_p_up = outer(c_head, a_h_upper)
    own_p_down = outer(broad[:, 0], all_d_image)
    own_p_values = outer_heads(c_used, a_pooled)

    summed = jnp.concatenate(
        [
            jnp.stack([dv0, dv1, dv2, dv3, dv4, dv5, dv6, dv8, dv9, dv10]),
            jnp.stack([tv0, tv1, tv2, tv3, tv4, tv5, tv6]),
            d_query[None],
            jnp.sum(p_used, 0),
            g_bias.reshape(-1, width),
        ],
        0,
    )
    summed = lax.psum(summed, ALL)
    total_query = summed[17]
    mine = lambda v, n: lax.dynamic_slice_in_dim(v, me * n, n, -1)
    own_probe = mine(ivec[7], part)
    own_p_query = own_probe[:, None] * total_query[None, :]
    dv7 = jnp.sum(probe_query_weight.astype(F32) * total_query[None, :], 1)
    pk_used = mine(summed[18 : 18 + HEADS], part)
    own_p_keys = jnp.einsum(
        "hm,he->mhe", pk_used, probe_query.reshape(HEADS, head_width) * factor
    ).reshape(part, width)
    own_p_pair = jnp.concatenate([own_p_keys, own_p_values], 1)
    ten = mine(summed[:10], part)
    own_ivec = jnp.concatenate([ten[:7], dv7[None], ten[7:]], 0)
    own_tvec = mine(summed[10:17], part)
    own_bias = mine(summed[18 + HEADS :].reshape(-1), wide_part)
    own_p_bias = mine(jnp.sum(a_h_upper, 0), wide_part)
    own_t_bias = mine(jnp.sum(a_upper, 0), wide_part)
    return (
        loss, grad_patches, grad_captions,
        own_in, own_out, own_up, own_bias, own_down, own_ivec,
        own_p_query, own_p_pair, own_p_out, own_p_up, own_p_bias, own_p_down,
        own_t_in, own_t_out, own_t_up, own_t_bias, own_t_down, own_tvec, own_t_head,
        grad_temp,
    )


MESH = pl.DeviceIdType.MESH

class Place:
    def __init__(self):
        i = lax.axis_index("dp")
        self.i, self.z = i, lax.axis_index("seq")
        self.y, self.x, self.c = i // 4, (i // 2) % 2, i % 2
        self.at_y = (i + 4 - 8 * self.y, self.z)
        self.at_x = (i + 2 - 4 * self.x, self.z)
        self.at_c = (i + 1 - 2 * self.c, self.z)

    def at_z(self, k):
        return (self.i, (self.z + k) % 4)

def greet(peers):
    barrier = pltpu.get_barrier_semaphore()
    for p in peers:
        pl.semaphore_signal(barrier, inc=1, device_id=p, device_id_type=MESH)
    pl.semaphore_wait(barrier, len(peers))

def gather_kernel(kinds, order, *refs):
    n = len(kinds)
    srcs, outs = refs[:n], refs[n : 2 * n]
    send, recv, local = refs[2 * n :]
    me = Place()
    y, x, c, z = me.y, me.x, me.c, me.z
    greet([me.at_z(1), me.at_z(2), me.at_z(3), me.at_x, me.at_y, me.at_c])
    ends = []

    def copy_of(a, slot, src, dst, dev):
        return pltpu.make_async_remote_copy(
            src, dst, send.at[a, slot], recv.at[a, slot], device_id=dev, device_id_type=MESH
        )

    def push(a, slot, src, dst, dev, arriving):
        copy = copy_of(a, slot, src, dst, dev)
        copy.start()
        ends.append(copy.wait_send)
        return copy_of(a, slot, src, arriving, dev).wait_recv

    def along(a, step, up):
        home = outs[a].at[y, x, c]
        if up:
            slab, go, to = z - step, (z - step >= 0) & (z < 3), me.at_z(1)
        else:
            slab, go, to = z + step, (z + step < 4) & (z > 0), me.at_z(3)
        slab = jnp.clip(slab, 0, 3)
        src = srcs[a] if step == 0 else home.at[slab]
        copy = copy_of(a, step + (0 if up else 3), src, home.at[slab], to)
        pl.when(go)(lambda: copy.start())
        ends.append(lambda: pl.when(go)(lambda: copy.wait_send()))

    def arrived(a, step, up):
        home = outs[a].at[y, x, c]
        if up:
            slab, come = z - 1 - step, z - 1 - step >= 0
        else:
            slab, come = z + 1 + step, z + 1 + step < 4
        slab = jnp.clip(slab, 0, 3)
        copy = copy_of(a, step + (0 if up else 3), home.at[slab], home.at[slab], me.at_z(1))
        pl.when(come)(lambda: copy.wait_recv())

    waits = {}

    def half(r, which, order_):
        if order_ != "S":
            return r
        n_ = r.shape[-1] // 2
        return r.at[..., 0:n_] if which == "C" else r.at[..., n_ : 2 * n_]

    def stage(a, s):
        kind, turn = kinds[a]
        src, out = srcs[a], outs[a]
        if kind in ("za", "zg"):
            own = src.at[z] if kind == "za" else src
            keep = pltpu.make_async_copy(own, out.at[z], local.at[a])
            keep.start()
            ends.append(keep.wait)
            for k in (1, 2, 3):
                to, fro = (z + k) % 4, (z + 4 - k) % 4
                s_ref = src.at[to] if kind == "za" else src
                ends.append(push(a, k - 1, s_ref, out.at[z], me.at_z(k), out.at[fro]))
            return
        turns = "CD" if turn == "S" else turn
        if kind != "full" and s == 0:
            own = src.at[z] if kind == "cols" else src
            keep = pltpu.make_async_copy(own, out.at[y, x, c, z] if kind == "cols" else out.at[y, x, c], local.at[a])
            keep.start()
            waits[a] = [keep.wait]
            for k in (1, 2, 3) if kind == "cols" else ():
                to, fro = (z + k) % 4, (z + 4 - k) % 4
                waits[a].append(push(a, k - 1, src.at[to], out.at[y, x, c, z], me.at_z(k), out.at[y, x, c, fro]))
        elif s == 0:
            keep = pltpu.make_async_copy(src, out.at[y, x, c, z], local.at[a])
            keep.start()
            waits[a] = [keep.wait]
            along(a, 0, True)
            along(a, 0, False)
        elif s in (1, 2):
            for up in (True, False):
                arrived(a, s - 1, up)
                along(a, s, up)
        elif s == 3:
            for up in (True, False) if kind == "full" else ():
                arrived(a, 2, up)
            for w in waits.pop(a):
                w()
            waits[a] = []
            for t in turns:
                cut = lambda r: half(r, t, turn)
                to, fro = (me.at_x, (y, 1 - x)) if t == "C" else (me.at_y, (1 - y, x))
                mine = cut(out.at[y, x, c])
                waits[a].append(push(a, 6 + (t == "D"), mine, mine, to, cut(out.at[fro[0], fro[1], c])))
        elif s == 4:
            for w in waits.pop(a):
                w()
            waits[a] = []
            for t in turns:
                cut = lambda r: half(r, t, turn)
                if t == "C":
                    mine, come, to = cut(out.at[y, :, c]), cut(out.at[1 - y, :, c]), me.at_y
                else:
                    mine, come, to = cut(out.at[:, x, c]), cut(out.at[:, 1 - x, c]), me.at_x
                waits[a].append(push(a, 8 + (t == "D"), mine, mine, to, come))
        elif s == 5:
            for w in waits.pop(a):
                w()
            mine = out.at[:, :, c]
            ends.append(push(a, 10, mine, mine, me.at_c, out.at[:, :, 1 - c]))

    for a, s in order:
        stage(a, s)
    for e in ends:
        e()


def gather(ops, kinds, order, cid):
    shapes = []
    for o, (kind, _) in zip(ops, kinds):
        s = {"full": (2, 2, 2, 4) + o.shape, "zg": (4,) + o.shape, "za": o.shape, "cols": (2, 2, 2) + o.shape, "plane": (2, 2, 2) + o.shape}[kind]
        shapes.append(jax.ShapeDtypeStruct(s, o.dtype))
    n = len(ops)
    return pl.pallas_call(
        partial(gather_kernel, kinds, order),
        out_shape=shapes,
        in_specs=[pl.BlockSpec(memory_space=pl.ANY)] * n,
        out_specs=[pl.BlockSpec(memory_space=pl.ANY)] * n,
        scratch_shapes=[
            pltpu.SemaphoreType.DMA((n, 11)),
            pltpu.SemaphoreType.DMA((n, 11)),
            pltpu.SemaphoreType.DMA((n,)),
        ],
        compiler_params=pltpu.CompilerParams(collective_id=cid, has_side_effects=True),
    )(*ops)


def reduce_kernel(g_ref, dx_ref, own_ref, moved_ref, from_c, acc_c, from_1, acc_1, from_2, acc_2, from_z, send, recv, local):
    me = Place()
    y, x, c, z = me.y, me.x, me.c, me.z
    greet([me.at_z(1), me.at_z(2), me.at_z(3), me.at_x, me.at_y, me.at_c])
    half = g_ref.shape[-1] // 2
    started = []

    def push(slot, src, dst, dev, arriving):
        copy = pltpu.make_async_remote_copy(src, dst, send.at[slot], recv.at[slot], device_id=dev, device_id_type=MESH)
        copy.start()
        started.append(copy)
        return pltpu.make_async_remote_copy(src, arriving, send.at[slot], recv.at[slot], device_id=dev, device_id_type=MESH)

    a_c = push(0, g_ref.at[:, :, 1 - c], from_c, me.at_c, from_c)
    home = pltpu.make_async_copy(g_ref.at[:, :, c], acc_c, local.at[0])
    home.start()
    rest = []
    for k in (1, 2, 3):
        to, fro = (z + k) % 4, (z + 4 - k) % 4
        rest.append(push(k, dx_ref.at[to], moved_ref.at[z], me.at_z(k), moved_ref.at[fro]))
    keep = pltpu.make_async_copy(dx_ref.at[z], moved_ref.at[z], local.at[1])
    keep.start()
    home.wait()
    a_c.wait_recv()
    f32 = lambda v: v.astype(jnp.float32)
    for a in range(2):
        for b in range(2):
            for q in range(4):
                acc_c[a, b, q] = (f32(acc_c[a, b, q]) + f32(from_c[a, b, q])).astype(acc_c.dtype)
    left, right = slice(0, half), slice(half, 2 * half)
    a_y = push(4, acc_c.at[1 - y, :, :, :, left], from_1.at[0], me.at_y, from_1.at[0])
    a_x = push(5, acc_c.at[:, 1 - x, :, :, right], from_1.at[1], me.at_x, from_1.at[1])
    a_y.wait_recv()
    for b in range(2):
        for q in range(4):
            acc_1[0, b, q] = (f32(acc_c[y, b, q, :, left]) + f32(from_1[0, b, q])).astype(acc_1.dtype)
    b_x = push(6, acc_1.at[0, 1 - x], from_2.at[0], me.at_x, from_2.at[0])
    a_x.wait_recv()
    for b in range(2):
        for q in range(4):
            acc_1[1, b, q] = (f32(acc_c[b, x, q, :, right]) + f32(from_1[1, b, q])).astype(acc_1.dtype)
    b_y = push(7, acc_1.at[1, 1 - y], from_2.at[1], me.at_y, from_2.at[1])
    b_x.wait_recv()
    for q in range(4):
        acc_2[q, :, left] = (f32(acc_1[0, x, q]) + f32(from_2[0, q])).astype(acc_2.dtype)
    b_y.wait_recv()
    for q in range(4):
        acc_2[q, :, right] = (f32(acc_1[1, y, q]) + f32(from_2[1, q])).astype(acc_2.dtype)
    last = []
    for k in (1, 2, 3):
        to, fro = (z + k) % 4, (z + 4 - k) % 4
        last.append(push(7 + k, acc_2.at[to], from_z.at[k - 1], me.at_z(k), from_z.at[k - 1]))
    total = f32(acc_2[z])
    for k in (1, 2, 3):
        last[k - 1].wait_recv()
        total += f32(from_z[k - 1])
    own_ref[...] = total
    keep.wait()
    for r in rest:
        r.wait_recv()
    for copy in started:
        copy.wait_send()

def reduce_and_move(g, dx, cid):
    rows, n = g.shape[0] // 32, g.shape[1]
    g = g.reshape(2, 2, 2, 4, rows, n)
    dx = dx.reshape(4, dx.shape[0] // 4, dx.shape[1])
    hbm = pl.BlockSpec(memory_space=pl.ANY)
    v = lambda *s: pltpu.VMEM(s, g.dtype)
    return pl.pallas_call(
        reduce_kernel,
        in_specs=[hbm, hbm],
        out_specs=[pl.BlockSpec(memory_space=pltpu.VMEM), hbm],
        out_shape=[jax.ShapeDtypeStruct((rows, n), jnp.float32), jax.ShapeDtypeStruct(dx.shape, dx.dtype)],
        scratch_shapes=[
            v(2, 2, 4, rows, n), v(2, 2, 4, rows, n), v(2, 2, 4, rows, n // 2), v(2, 2, 4, rows, n // 2),
            v(2, 4, rows, n // 2), v(4, rows, n), v(3, rows, n),
            pltpu.SemaphoreType.DMA((11,)), pltpu.SemaphoreType.DMA((11,)), pltpu.SemaphoreType.DMA((2,)),
        ],
        compiler_params=pltpu.CompilerParams(collective_id=cid, has_side_effects=True, vmem_limit_bytes=40 << 20),
    )(g, dx)

ROWS = 80

def middle_kernel(final_ref, block_ref, tokens_ref, tp_ref, downs_ref, outs_ref, ivec_ref, tvec_ref, pbias_ref, tbias_ref,
                  label_ref, temp_ref,
                  dy_ref, branch_ref, rows_ref, sums_ref, dcap_ref, loss_ref, dz_ref,
                  tn_ref, dn_ref, send_a, recv_a, send_l, recv_l, send_t, recv_t, send_sem, recv_sem):
    me = Place()
    z, i = me.z, me.i
    n_dp = recv_l.shape[0]
    plane = [((i + k) % n_dp, z) for k in range(1, n_dp)]
    greet([me.at_z(1), me.at_z(2), me.at_z(3)] + plane)
    width = final_ref.shape[1]
    part = width // 4
    started = []

    def exchange(n, values, rows=4):
        if not isinstance(values, list):
            values = [values] * 4
        for q in range(4):
            send_a[n, q, 0:rows] = values[q]
        recv_a[n, z] = send_a[n, z]
        copies = []
        for k in (3, 2, 1):
            to, fro = (z + k) % 4, (z + 4 - k) % 4
            make = lambda dst: pltpu.make_async_remote_copy(
                send_a.at[n, to], dst, send_sem.at[n, k], recv_sem.at[n, k], device_id=me.at_z(k), device_id_type=MESH)
            copy = make(recv_a.at[n, z])
            copy.start()
            started.append(copy)
            copies.append(make(recv_a.at[n, fro]))

        def done():
            for a in copies:
                a.wait_recv()
            return [recv_a[n, q, 0:rows] for q in range(4)]

        return done

    total = lambda blocks: (blocks[0] + blocks[1]) + (blocks[2] + blocks[3])
    by_head = lambda blocks, n=3: jnp.concatenate([blocks[q][h : h + 1] for h in range(n) for q in range(4)], 0)
    pad1 = jnp.zeros((1, width), F32)
    ivec, tvec = ivec_ref[...], tvec_ref[...]
    iv = lambda k: ivec[k:k + 1]
    tv = lambda k: tvec[k:k + 1]
    names = ["tq", "tk", "tv", "thead", "pq", "pk", "pv"]
    col = {n: 2 * width + 256 * k for k, n in enumerate(names)}
    small = lambda n: tp_ref[:, col[n]:col[n] + 256]
    p_up = lambda: tp_ref[:, 0:width]
    t_up = lambda: tp_ref[:, width:2 * width]
    t_down = lambda: downs_ref[:, 0:width]
    p_down = lambda: downs_ref[:, width:2 * width]
    t_out_w = lambda: outs_ref[0:part, 0:width]
    p_out_w = lambda: outs_ref[0:part, width:2 * width]
    lane = lax.broadcasted_iota(jnp.int32, (1, 256), 1)
    own = [((lane >= 64 * h) & (lane < 64 * h + 64)).astype(F32) for h in range(3)]

    def spread(a):
        return jnp.concatenate([a * own[h] for h in range(3)], 0)

    def fold(a):
        n = a.shape[0] // 3
        return sum(a[h * n:(h + 1) * n] * own[h] for h in range(3))

    p_q = mm(iv(7).astype(BF), small("pq"))
    get_keys = exchange(0, mm_two(spread(p_q), small("pk"), 1) * 0.125, 3)
    t_x = tokens_ref[...].astype(F32)
    tn = layer_norm(t_x, tv(0), tv(1)).astype(BF)
    tn_ref[...] = tn.astype(F32)
    last_at = [3 * 64 + 16 * c + 15 for c in range(4)]
    t_last = jnp.concatenate([tn_ref[r:r + 1, :] for r in last_at], 0)
    x_last = jnp.concatenate([tokens_ref[3 * 64 + 16 * c:3 * 64 + 16 * c + 16, :].astype(F32)[15:16] for c in range(4)], 0)
    t_q = mm(t_last.astype(BF), small("tq")).astype(BF).astype(F32)
    t_keys = mm(spread(t_q).astype(BF), small("tk"), 1, 1) * 0.125
    scores = mm_two(t_keys, tn, 1)
    col_id = (lax.broadcasted_iota(jnp.int32, scores.shape, 1) // 16) % 4
    row_id = lax.broadcasted_iota(jnp.int32, scores.shape, 0) % 4
    mine = col_id == row_id
    top = jnp.max(jnp.where(mine, scores, -1e30), -1, keepdims=True)
    e = jnp.where(mine, jnp.exp(jnp.where(mine, scores - top, 0.0)), 0.0)
    t_probs = e / jnp.sum(e, -1, keepdims=True)
    t_used = mm_two(t_probs, tn)
    t_mixed = fold(mm(t_used.astype(BF), small("tv"))).astype(BF)
    get_t = exchange(1, mm(t_mixed[:, 0:part], t_out_w()), 4)
    final = final_ref[...]
    p_keys = jnp.concatenate(get_keys(), 0)
    p_scores = mm_two(p_keys, final, 1)
    e = jnp.exp(p_scores - jnp.max(p_scores, -1, keepdims=True))
    p_probs = e / jnp.sum(e, -1, keepdims=True)
    used = mm_two(p_probs, final)
    get_p = exchange(2, [used[3 * q:3 * q + 3] for q in range(4)], 3)
    t_hidden = x_last + total(get_t())
    t_second = layer_norm(t_hidden, tv(2), tv(3)).astype(BF)
    t_value, t_slope = gelu_pair(mm(t_second, t_up()) + tbias_ref[...])
    t_active = t_value.astype(BF)
    get_t = exchange(3, mm(t_active, t_down()), 4)
    pooled = fold(mm_two(by_head(get_p()), small("pv")))
    get_p = exchange(4, mm_two(pooled[:, 0:part], p_out_w()), 4)
    t_out = t_hidden + total(get_t()) + tv(4)
    t_final = layer_norm(t_out, tv(5), tv(6)).astype(BF)
    t_piece = mm(t_final, small("thead"))
    get_t = exchange(5, jnp.concatenate([t_piece[:, 0:part], jnp.zeros((4, width - part), F32)], 1), 4)
    h_start = total(get_p())
    h_normed = layer_norm(h_start, iv(8), iv(9)).astype(BF)
    h_value, h_slope = gelu_pair(mm(h_normed, p_up()) + pbias_ref[...])
    h_active = h_value.astype(BF)
    get_p = exchange(6, mm(h_active, p_down()), 4)
    text_embed = jnp.concatenate([blk[:, 0:part] for blk in get_t()], 1)
    image_embed = h_start + (total(get_p()) + iv(10))
    send_l[...] = jnp.concatenate([image_embed, text_embed], 0)
    recv_l[i] = send_l[...]
    arrive = []
    for k in range(1, n_dp):
        copy = pltpu.make_async_remote_copy(send_l, recv_l.at[i], send_sem.at[15, k], recv_sem.at[15, k],
                                            device_id=plane[k - 1], device_id_type=MESH)
        copy.start()
        started.append(copy)
        arrive.append(pltpu.make_async_remote_copy(send_l, recv_l.at[(i + n_dp - k) % n_dp], send_sem.at[15, k], recv_sem.at[15, k],
                                                   device_id=plane[k - 1], device_id_type=MESH))
    for a in arrive:
        a.wait_recv()
    every = jnp.concatenate([recv_l[k] for k in range(n_dp)], 0)
    scale = lax.rsqrt(jnp.sum(every * every, -1, keepdims=True) + EPS)
    unit = every * scale
    cosine = mm_exact(unit, unit, 1, 1)
    temper = jnp.exp(jnp.full((1, 1), temp_ref[0], F32))
    logits = cosine * temper + temp_ref[1]
    label = label_ref[...]
    valid = label != 0.0
    signed = label * logits
    n_all = n_dp * 4
    nll = jnp.maximum(-signed, 0.0) + jnp.log(1.0 + jnp.exp(-jnp.abs(signed)))
    add_all = lambda a: jnp.sum(jnp.sum(a, -1, keepdims=True), 0, keepdims=True)
    loss = add_all(jnp.where(valid, nll, 0.0)) / n_all
    g = jnp.where(valid, -label / (1.0 + jnp.exp(signed)), 0.0) / n_all
    gt0 = temper * add_all(g * cosine)
    gt1 = add_all(g)
    at = lax.broadcasted_iota(jnp.int32, (8, 128), 1)
    loss_ref[...] = jnp.where(at == 0, loss, jnp.where(at == 1, gt0, gt1))
    dz = temper * mm_exact(g + jnp.transpose(g), unit)
    dz_ref[...] = (dz - unit * jnp.sum(unit * dz, -1, keepdims=True)) * scale
    d_both = dz_ref[pl.ds(pl.multiple_of(8 * i, 8), 8), :]
    d_image, d_text = d_both[0:4], d_both[4:8]

    dh_upper = mm_two(d_image, p_down(), 1) * h_slope
    get_p = exchange(7, mm_two(dh_upper, p_up(), 1), 4)
    d_text_my = sum(jnp.where(z == q, d_text[:, part * q:part * q + part], 0.0) for q in range(4))
    get_t = exchange(8, mm_two(d_text_my, small("thead")[:, 0:part], 1), 4)
    d_start, dv8, dv9 = norm_back_rows(h_start, iv(8), total(get_p()))
    d_start = d_image + d_start
    dv10 = jnp.sum(d_image, 0, keepdims=True)
    d_pooled = mm_two(d_start, p_out_w(), 1)
    d_pooled = jnp.concatenate([d_pooled, jnp.zeros((4, 256 - part), F32)], 1)
    p_values_my = mm_two(spread(d_pooled), small("pv"), 1)
    get_p = exchange(9, [jnp.concatenate([p_values_my[4 * h + q:4 * h + q + 1] for h in range(3)], 0) for q in range(4)], 3)
    dt_out, tv5, tv6 = norm_back_rows(t_out, tv(5), total(get_t()))
    tv4 = jnp.sum(dt_out, 0, keepdims=True)
    dt_branch = dt_out.astype(BF)
    dt_upper = (mm(dt_branch, t_down(), 1, 1) * t_slope).astype(BF)
    get_t = exchange(10, mm(dt_upper, t_up(), 1, 1), 4)
    p_values = jnp.concatenate(get_p(), 0)
    d_probs = mm_two(p_values, final, 1)
    d_scores = p_probs * (d_probs - jnp.sum(p_probs * d_probs, -1, keepdims=True))
    p_used = mm_two(d_scores, final) * 0.125
    get_p = exchange(11, [p_used[3 * q:3 * q + 3] for q in range(4)], 3)
    dt_hidden, tv2, tv3 = norm_back_rows(t_hidden, tv(2), total(get_t()))
    dt_hidden = dt_out + dt_hidden
    dt_attend = dt_hidden.astype(BF)
    dt_mixed = mm(dt_attend, t_out_w(), 1, 1).astype(BF).astype(F32)
    dt_mixed = jnp.concatenate([dt_mixed, jnp.zeros((4, 256 - part), F32)], 1)
    t_values = mm(spread(dt_mixed).astype(BF), small("tv"), 1, 1)
    dt_probs = mm_two(t_values, tn, 1)
    dt_scores = t_probs * (dt_probs - jnp.sum(t_probs * dt_probs, -1, keepdims=True))
    tk_used = mm_two(dt_scores, tn) * 0.125
    dt_q = fold(mm(tk_used.astype(BF), small("tk"))).astype(BF)
    dn = mm(dt_scores.astype(BF), t_keys.astype(BF), 0, 0) + mm(t_probs.astype(BF), t_values.astype(BF), 0, 0)
    row_at = lax.broadcasted_iota(jnp.int32, dn.shape, 0)
    dq_back = mm(dt_q, small("tq"), 1, 1)
    for c in range(4):
        dn = dn + jnp.where(row_at == last_at[c], dq_back[c:c + 1], 0.0)
    dn_ref[...] = dn.astype(BF)
    arrive = []
    for k in (1, 2, 3):
        to, fro = (z + k) % 4, (z + 4 - k) % 4
        rows_to = dn_ref.at[pl.ds(pl.multiple_of(64 * to, 64), 64), :]
        copy = pltpu.make_async_remote_copy(rows_to, recv_t.at[z], send_sem.at[14, k], recv_sem.at[14, k],
                                            device_id=me.at_z(k), device_id_type=MESH)
        copy.start()
        started.append(copy)
        arrive.append(pltpu.make_async_remote_copy(rows_to, recv_t.at[fro], send_sem.at[14, k], recv_sem.at[14, k],
                                                   device_id=me.at_z(k), device_id_type=MESH))
    s_high, s_low = split_two(d_scores)
    q_high, q_low = split_two(p_probs)
    k_high, k_low = split_two(p_keys)
    v_high, v_low = split_two(p_values)
    left = jnp.concatenate([s_high.astype(F32), q_high.astype(F32)], 0)
    right = jnp.concatenate([k_high.astype(F32), v_high.astype(F32)], 0).astype(BF)
    send_t[...] = jnp.transpose(jnp.concatenate([left, jnp.zeros((104, left.shape[1]), F32)], 0))
    right = jnp.concatenate([right, jnp.zeros((104, width), BF)], 0)
    sums_ref[...] = jnp.zeros_like(sums_ref)
    tile = 128

    def step(n, carry):
        at_rows = pl.ds(pl.multiple_of(n * tile, tile), tile)
        d_final = mm(send_t[at_rows, :].astype(BF), right)
        d_y, gain, shift = norm_back_rows(block_ref[at_rows, :], iv(5), d_final)
        dy_ref[at_rows, :] = d_y
        branch_ref[at_rows, :] = d_y.astype(BF)
        sums_ref[5:6] += gain
        sums_ref[6:7] += shift
        sums_ref[4:5] += jnp.sum(d_y, 0, keepdims=True)
        return carry

    lax.fori_loop(0, final_ref.shape[0] // tile, step, 0)
    w_got = by_head(get_p())
    dq_rows = fold(mm_two(w_got, small("pk")))
    dq_my = jnp.sum(dq_rows, 0, keepdims=True)
    recv_t[z] = dn_ref[pl.ds(pl.multiple_of(64 * z, 64), 64), :]
    for a in arrive:
        a.wait_recv()
    dt_normed = sum(recv_t[q].astype(F32) for q in range(4))
    x_mine = tokens_ref[pl.ds(pl.multiple_of(64 * z, 64), 64), :].astype(F32)
    d_cap, tv0, tv1 = norm_back_rows(x_mine, tv(0), dt_normed)
    row_c = lax.broadcasted_iota(jnp.int32, d_cap.shape, 0)
    for c in range(4):
        d_cap = d_cap + jnp.where((row_c == 16 * c + 15) & (z == 3), dt_hidden[c:c + 1], 0.0)
    dcap_ref[...] = d_cap
    first = (z == 0).astype(F32)
    sums_ref[8:9] = dv8 * first
    sums_ref[9:10] = dv9 * first
    sums_ref[10:11] = dv10 * first
    sums_ref[11:12] = tv0
    sums_ref[12:13] = tv1
    sums_ref[13:14] = tv2 * first
    sums_ref[14:15] = tv3 * first
    sums_ref[15:16] = tv4 * first
    sums_ref[16:17] = tv5 * first
    sums_ref[17:18] = tv6 * first
    own_row = lambda a: sum(jnp.where(z == q, a[q:q + 1].astype(F32), 0.0) for q in range(4))
    pick = lambda a: a[:, 0:part].astype(F32)
    wide = jnp.concatenate
    pieces = [
        dh_upper, dt_upper.astype(F32), h_active.astype(F32), t_active.astype(F32),
        wide([pick(d_pooled), pick(pooled), pick(dt_q), pick(t_q)], 1),
        wide([pick(dt_mixed), pick(t_mixed), jnp.broadcast_to(pick(dq_my), (4, part)), jnp.broadcast_to(pick(p_q), (4, part))], 1),
        own_row(h_normed), own_row(d_start), own_row(t_last), own_row(t_second),
        own_row(dt_attend), own_row(dt_branch), own_row(t_final), pad1,
        used, t_used, tk_used, p_used,
    ]
    rows_ref[...] = jnp.concatenate(pieces, 0).astype(BF)
    for copy in started:
        copy.wait_send()

def middle(final, block_out, tokens, tp, downs, outs, ivec, tvec, pbias, tbias, label, temp, cid, n_dp):
    length, width = final.shape
    v = pl.BlockSpec(memory_space=pltpu.VMEM)
    f = lambda *s: jax.ShapeDtypeStruct(s, F32)
    return pl.pallas_call(
        middle_kernel,
        in_specs=[v] * 11 + [pl.BlockSpec(memory_space=pltpu.SMEM)],
        out_specs=[v] * 7,
        out_shape=[f(length, width), jax.ShapeDtypeStruct((length, width), BF), jax.ShapeDtypeStruct((ROWS, width), BF), f(24, width), f(64, width), f(8, 128), f(8 * n_dp, width)],
        scratch_shapes=[
            pltpu.VMEM((256, width), F32), pltpu.VMEM((256, width), BF),
            pltpu.VMEM((12, 4, 4, width), F32), pltpu.VMEM((12, 4, 4, width), F32),
            pltpu.VMEM((8, width), F32), pltpu.VMEM((n_dp, 8, width), F32),
            pltpu.VMEM((length, 128), F32), pltpu.VMEM((4, 64, width), BF),
            pltpu.SemaphoreType.DMA((16, 8)), pltpu.SemaphoreType.DMA((16, 8)),
        ],
        compiler_params=pltpu.CompilerParams(collective_id=cid, has_side_effects=True, vmem_limit_bytes=50 << 20),
    )(final, block_out, tokens, tp, downs, outs, ivec, tvec, pbias, tbias, label, temp)


def plane_moves(me, out, s):
    y, x, c = me.y, me.x, me.c
    n = out.shape[-1] // 2
    left, right = (lambda r: r.at[..., 0:n]), (lambda r: r.at[..., n : 2 * n])
    if s == 3:
        own = out.at[y, x, c]
        yield 6, left(own), left(own), me.at_x, None, left(out.at[y, 1 - x, c]), None
        yield 7, right(own), right(own), me.at_y, None, right(out.at[1 - y, x, c]), None
    elif s == 4:
        own = out.at[y, :, c]
        yield 8, left(own), left(own), me.at_y, None, left(out.at[1 - y, :, c]), None
        own = out.at[:, x, c]
        yield 9, right(own), right(own), me.at_x, None, right(out.at[:, 1 - x, c]), None
    else:
        mine = out.at[:, :, c]
        yield 10, mine, mine, me.at_c, None, out.at[:, :, 1 - c], None


def turn_moves(me, src, home, split):
    z = me.z
    for k in (3, 2, 1):
        to, fro = (z + k) % 4, (z + 4 - k) % 4
        yield k - 1, src.at[to] if split else src, home.at[z], me.at_z(k), None, home.at[fro], None


def run_moves(moves, act, send, recv):
    for slot, src, dst, dev, go, come, arrives in moves:
        make = lambda a, b: pltpu.make_async_remote_copy(
            a, b, send.at[slot], recv.at[slot], device_id=dev, device_id_type=MESH
        )
        if act == "arrived":
            copy, when = make(src, come).wait_recv, arrives
        else:
            copy, when = getattr(make(src, dst), "start" if act == "start" else "wait_send"), go
        if when is None:
            copy()
        else:
            pl.when(when)(lambda: copy())


class Spread:
    stages = 6

    def __init__(self, me, src, out, send, recv, local):
        self.me, self.src, self.out, self.send, self.recv, self.local = me, src, out, send, recv, local

    def moves(self, s):
        me, out = self.me, self.out
        y, x, c, z = me.y, me.x, me.c, me.z
        if s < 3:
            home = out.at[y, x, c]
            for up in (True, False):
                step = -s if up else s
                slab, come = z + step, z + step + (-1 if up else 1)
                go = ((slab >= 0) & (z < 3)) if up else ((slab < 4) & (z > 0))
                arrives = (come >= 0) & (come < 4)
                slab, come = jnp.clip(slab, 0, 3), jnp.clip(come, 0, 3)
                src = self.src if s == 0 else home.at[slab]
                yield s + (0 if up else 3), src, home.at[slab], me.at_z(1 if up else 3), go, home.at[come], arrives
        else:
            yield from plane_moves(me, out, s)

    def each(self, s, act):
        run_moves(self.moves(s), act, self.send, self.recv)

    def keep(self):
        me = self.me
        return pltpu.make_async_copy(self.src, self.out.at[me.y, me.x, me.c, me.z], self.local)

    def begin(self, s):
        if s == 0:
            self.keep().start()
        else:
            self.each(s - 1, "arrived")
        if s == 3:
            self.keep().wait()
        self.each(s, "start")

    def finish(self):
        self.each(5, "arrived")
        for s in range(6):
            self.each(s, "sent")


class Reduce:
    def __init__(self, me, g, own, acc, from_c, from_1, from_2, from_z, send, recv, local):
        self.me, self.g, self.own, self.acc = me, g, own, acc
        self.from_c, self.from_1, self.from_2, self.from_z = from_c, from_1, from_2, from_z
        self.send, self.recv, self.local = send, recv, local
        self.size = acc.shape[-1]
        self.left, self.right = slice(0, self.size // 2), slice(self.size // 2, self.size)

    def moves(self, n, stage):
        me, acc = self.me, self.acc.at[n]
        y, x, z = me.y, me.x, me.z
        if stage == "core":
            src = self.g.at[:, :, 1 - me.c, :, :, n * self.size : (n + 1) * self.size]
            yield 0, src, self.from_c.at[n], me.at_c, None, self.from_c.at[n], None
        elif stage == "one":
            a, b = self.from_1.at[n, 0], self.from_1.at[n, 1]
            yield 1, acc.at[1 - y, :, :, :, self.left], a, me.at_y, None, a, None
            yield 2, acc.at[:, 1 - x, :, :, self.right], b, me.at_x, None, b, None
        elif stage == "two":
            a, b = self.from_2.at[n, 0], self.from_2.at[n, 1]
            yield 3, acc.at[y, 1 - x, :, :, self.left], a, me.at_x, None, a, None
            yield 4, acc.at[1 - y, x, :, :, self.right], b, me.at_y, None, b, None
        else:
            for k in (3, 2, 1):
                got = self.from_z.at[n, k - 1]
                yield 4 + k, acc.at[y, x, (z + k) % 4], got, me.at_z(k), None, got, None

    def act(self, n, stage, what):
        run_moves(self.moves(n, stage), what, self.send.at[n], self.recv.at[n])

    def keep(self, n):
        src = self.g.at[:, :, self.me.c, :, :, n * self.size : (n + 1) * self.size]
        return pltpu.make_async_copy(src, self.acc.at[n], self.local.at[n])

    def start(self, n, stage):
        if stage == "core":
            self.keep(n).start()
        self.act(n, stage, "start")

    def done(self, n, stage):
        me, acc = self.me, self.acc
        y, x = me.y, me.x
        f32 = lambda v: v.astype(F32)

        def each(count, body):
            lax.fori_loop(0, count, lambda q, carry: body(q) or carry, 0)

        if stage == "core":
            self.keep(n).wait()
        self.act(n, stage, "arrived")
        if stage == "core":

            def add(q):
                for a in range(2):
                    for b in range(2):
                        acc[n, a, b, q] = (f32(acc[n, a, b, q]) + f32(self.from_c[n, a, b, q])).astype(BF)

            each(4, add)
        elif stage == "one":

            def add(q):
                for b in range(2):
                    at = (n, y, b, q, slice(None), self.left)
                    acc[at] = (f32(acc[at]) + f32(self.from_1[n, 0, b, q])).astype(BF)
                    at = (n, b, x, q, slice(None), self.right)
                    acc[at] = (f32(acc[at]) + f32(self.from_1[n, 1, b, q])).astype(BF)

            each(4, add)
        elif stage == "two":

            def add(q):
                for half, cut in enumerate((self.left, self.right)):
                    at = (n, y, x, q, slice(None), cut)
                    acc[at] = (f32(acc[at]) + f32(self.from_2[n, half, q])).astype(BF)

            each(4, add)
        else:
            total = f32(acc[n, y, x, me.z])
            for k in range(3):
                total += f32(self.from_z[n, k])
            self.own[:, n * self.size : (n + 1) * self.size] = total

    def finish(self, n):
        for stage in ("core", "one", "two", "z"):
            self.act(n, stage, "sent")


REDUCE_STEPS = {
    0: [("start", 0, "core"), ("start", 1, "core")],
    1: [("done", 0, "core"), ("start", 0, "one")],
    2: [("done", 1, "core")],
    3: [("start", 1, "one")],
    5: [("done", 0, "one"), ("start", 0, "two")],
    7: [("done", 1, "one"), ("done", 0, "two"), ("start", 0, "z"), ("start", 1, "two")],
    9: [("done", 1, "two"), ("start", 1, "z")],
    12: [("done", 0, "z"), ("done", 1, "z")],
}
CHUNKS = 2


def attend_bwd_kernel_hosting(q_ref, k_ref, v_ref, do_ref, lse_ref, d_ref, g_ref, rows_ref, dq_ref, dk_ref, dv_ref, own_ref, all_ref,
                              acc, from_c, from_1, from_2, from_z, send, recv, local, rows_send, rows_recv, rows_local):
    h_at = pl.program_id(0)
    me = Place()
    spread = Spread(me, rows_ref, all_ref, rows_send, rows_recv, rows_local)
    reduce = Reduce(me, g_ref, own_ref, acc, from_c, from_1, from_2, from_z, send, recv, local)

    def tick(step):
        if step not in REDUCE_STEPS:
            return

        def go():
            if step == 0:
                greet([me.at_z(1), me.at_z(2), me.at_z(3), me.at_x, me.at_y, me.at_c])
            for what, n, stage in REDUCE_STEPS[step]:
                getattr(reduce, what)(n, stage)

        pl.when(h_at == step // 2)(go)

    for step in range(0, 12, 2):
        tick(step)
    for s in range(6):
        pl.when(h_at == s)(partial(spread.begin, s))
    q = q_ref[...] * 0.125
    k, v, do = k_ref[...], v_ref[...], do_ref[...]
    lane = lax.broadcasted_iota(jnp.int32, k.shape, 1)
    low = lane < 64
    for h in range(2):
        if h == 1:
            for step in range(1, 12, 2):
                tick(step)
        keep = low if h == 0 else ~low
        s = mm(jnp.where(keep, k, jnp.zeros_like(k)), q, 1, 1)
        p = jnp.exp(s - lse_ref[0, h : h + 1, :])
        dp = mm(jnp.where(keep, v, jnp.zeros_like(v)), do, 1, 1)
        ds = (p * (dp - d_ref[0, h : h + 1, :])).astype(BF)
        d_v = mm(p.astype(BF), do).astype(BF)
        d_k = mm(ds, q).astype(BF)
        d_q = (mm(ds, k, 0, 0) * 0.125).astype(BF)
        for ref, value in ((dq_ref, d_q), (dk_ref, d_k), (dv_ref, d_v)):
            ref[...] = value if h == 0 else jnp.where(low, ref[...], value)

    def last():
        for what, n, stage in REDUCE_STEPS[12]:
            getattr(reduce, what)(n, stage)
        for n in range(CHUNKS):
            reduce.finish(n)
        spread.finish()

    pl.when(h_at == pl.num_programs(0) - 1)(last)


def attend_bwd_and_reduce(proj, d_out, lse, inner, g, own_rows, cid):
    length, width = proj.shape[0], proj.shape[1] // 3
    pairs = width // 128
    rows, n = g.shape[0] // 32, g.shape[1]
    size = n // CHUNKS
    block = lambda part: pl.BlockSpec((length, 128), lambda h: (0, part * pairs + h))
    row = pl.BlockSpec((1, 2, length), lambda h: (h, 0, 0))
    hbm = pl.BlockSpec(memory_space=pl.ANY)
    result = jax.ShapeDtypeStruct((length, width), BF)
    v = lambda *s: pltpu.VMEM(s, BF)
    return pl.pallas_call(
        attend_bwd_kernel_hosting,
        grid=(pairs,),
        in_specs=[block(0), block(1), block(2), block(0), row, row, hbm, hbm],
        out_specs=[block(0)] * 3 + [pl.BlockSpec((rows, n), lambda h: (0, 0)), hbm],
        out_shape=[result] * 3
        + [jax.ShapeDtypeStruct((rows, n), F32), jax.ShapeDtypeStruct((2, 2, 2, 4) + own_rows.shape, BF)],
        scratch_shapes=[
            v(CHUNKS, 2, 2, 4, rows, size), v(CHUNKS, 2, 2, 4, rows, size), v(CHUNKS, 2, 2, 4, rows, size // 2),
            v(CHUNKS, 2, 4, rows, size // 2), v(CHUNKS, 3, rows, size),
            pltpu.SemaphoreType.DMA((CHUNKS, 8)), pltpu.SemaphoreType.DMA((CHUNKS, 8)), pltpu.SemaphoreType.DMA((CHUNKS,)),
            pltpu.SemaphoreType.DMA((11,)), pltpu.SemaphoreType.DMA((11,)), pltpu.SemaphoreType.DMA,
        ],
        compiler_params=pltpu.CompilerParams(collective_id=cid, has_side_effects=True, vmem_limit_bytes=60 << 20),
    )(proj, proj, proj, d_out, lse, inner, g.reshape(2, 2, 2, 4, rows, n), own_rows)


def attend_fwd_kernel_hosting(q_ref, k_ref, v_ref, split_ref, downs_ref, tokens_ref,
                              o_ref, lse_ref, tp_ref, down_ref, token_ref, send, recv, local):
    h_at = pl.program_id(0)
    me = Place()
    home = tp_ref.at[me.y, me.x, me.c]
    down_home = down_ref.at[me.y, me.x, me.c]
    keeps = [
        pltpu.make_async_copy(split_ref.at[me.z], home.at[me.z], local.at[0]),
        pltpu.make_async_copy(downs_ref, down_home, local.at[1]),
        pltpu.make_async_copy(tokens_ref, token_ref.at[me.z], local.at[2]),
    ]
    groups = {
        "split": (lambda: turn_moves(me, split_ref, home, True), 0),
        "tokens": (lambda: turn_moves(me, tokens_ref, token_ref, False), 2),
        "split_xy": (lambda: plane_moves(me, tp_ref, 3), 0),
        "down_xy": (lambda: plane_moves(me, down_ref, 3), 1),
    }

    def act(name, what):
        moves, a = groups[name]
        run_moves(moves(), what, send.at[a], recv.at[a])

    def first():
        greet([me.at_z(1), me.at_z(2), me.at_z(3), me.at_x, me.at_y])
        for keep in keeps:
            keep.start()
        act("split", "start")
        keeps[1].wait()
        act("down_xy", "start")

    def middle_step():
        act("split", "arrived")
        keeps[0].wait()
        act("split_xy", "start")
        act("tokens", "start")

    def last():
        for name in ("split_xy", "down_xy", "tokens"):
            act(name, "arrived")
        keeps[2].wait()
        for name in groups:
            act(name, "sent")

    pl.when(h_at == 0)(first)
    pl.when(h_at == 3)(middle_step)
    attend_fwd_kernel(q_ref, k_ref, v_ref, o_ref, lse_ref)
    pl.when(h_at == pl.num_programs(0) - 1)(last)


def attend_fwd_and_gather(proj, split, downs, tokens, cid):
    length, width = proj.shape[0], proj.shape[1] // 3
    pairs = width // 128
    block = lambda part: pl.BlockSpec((length, 128), lambda h: (0, part * pairs + h))
    hbm = pl.BlockSpec(memory_space=pl.ANY)
    s = jax.ShapeDtypeStruct
    return pl.pallas_call(
        attend_fwd_kernel_hosting,
        grid=(pairs,),
        in_specs=[block(0), block(1), block(2), hbm, hbm, hbm],
        out_specs=[block(0), pl.BlockSpec((1, 2, length), lambda h: (h, 0, 0)), hbm, hbm, hbm],
        out_shape=[
            s((length, width), BF),
            s((pairs, 2, length), F32),
            s((2, 2, 2) + split.shape, BF),
            s((2, 2, 2) + downs.shape, BF),
            s((4,) + tokens.shape, BF),
        ],
        scratch_shapes=[pltpu.SemaphoreType.DMA((3, 11)), pltpu.SemaphoreType.DMA((3, 11)), pltpu.SemaphoreType.DMA((3,))],
        compiler_params=pltpu.CompilerParams(collective_id=cid, has_side_effects=True, vmem_limit_bytes=48 << 20),
    )(proj, proj, proj, split, downs, tokens)


def mlp_fwd_kernel(x_ref, mixed_ref, wo_ref, wu_ref, wd_ref, bias_ref, vec_ref, tp_in, down_in,
                   hidden_ref, second_ref, active_ref, slope_ref, block_ref, final_ref, tp_ref, down_ref, total, send, recv):
    k = pl.program_id(0)
    me = Place()

    def act(s, what):
        for a, ref in enumerate((tp_ref, down_ref)):
            run_moves(plane_moves(me, ref, s), what, send.at[a], recv.at[a])

    def first():
        greet([me.at_x, me.at_y, me.at_c])
        act(4, "start")

    def then():
        act(4, "arrived")
        act(5, "start")

    pl.when(k == 0)(first)
    pl.when(k == pl.num_programs(0) - 1)(then)
    vec = vec_ref[...]

    @pl.when(k == 0)
    def _():
        hidden = x_ref[...].astype(F32) + mm(mixed_ref[...], wo_ref[...])
        hidden_ref[...] = hidden
        second_ref[...] = layer_norm(hidden, vec[2:3], vec[3:4]).astype(BF)
        total[...] = hidden + vec[4:5]

    value, slope = gelu_pair(mm(second_ref[...], wu_ref[...]) + bias_ref[0])
    active = value.astype(BF)
    active_ref[...] = active
    slope_ref[...] = slope.astype(BF)
    total[...] += mm(active, wd_ref[...])

    @pl.when(k == pl.num_programs(0) - 1)
    def _():
        block_ref[...] = total[...]
        final_ref[...] = layer_norm(total[...], vec[5:6], vec[6:7]).astype(BF)
        act(5, "arrived")
        act(4, "sent")
        act(5, "sent")


def mlp_fwd(x, mixed, main, bias, vec, fold, tp, downs, cid):
    rows, width = mixed.shape
    whole = pl.BlockSpec((rows, width), lambda k: (0, 0))
    tile = pl.BlockSpec((rows, width), lambda k: (0, k))
    at = lambda f: pl.BlockSpec((width, width), lambda k: (0, f(k)))
    s = lambda n, t: jax.ShapeDtypeStruct((rows, n * width), t)
    hbm = pl.BlockSpec(memory_space=pl.ANY)
    return pl.pallas_call(
        mlp_fwd_kernel,
        grid=(fold,),
        in_specs=[whole, whole, at(lambda k: 0), at(lambda k: 1 + k), at(lambda k: 1 + fold + k),
                  pl.BlockSpec((1, 1, width), lambda k: (k, 0, 0)), pl.BlockSpec(vec.shape, lambda k: (0, 0)), hbm, hbm],
        out_specs=[whole, whole, tile, tile, whole, whole, hbm, hbm],
        out_shape=[s(1, F32), s(1, BF), s(fold, BF), s(fold, BF), s(1, F32), s(1, BF),
                   jax.ShapeDtypeStruct(tp.shape, BF), jax.ShapeDtypeStruct(downs.shape, BF)],
        scratch_shapes=[pltpu.VMEM((rows, width), F32), pltpu.SemaphoreType.DMA((2, 11)), pltpu.SemaphoreType.DMA((2, 11))],
        input_output_aliases={7: 6, 8: 7},
        compiler_params=pltpu.CompilerParams(collective_id=cid, has_side_effects=True, vmem_limit_bytes=56 << 20),
    )(x, mixed, main, main, main, bias.reshape(fold, 1, width), vec, tp, downs)


def mlp_bwd_kernel(dy_ref, branch_ref, active_ref, slope_ref, second_ref, hidden_ref, mixed_ref,
                   wo_ref, wu_ref, wd_ref, vec_ref,
                   g_ref, gs_ref, dhid_ref, dmix_ref, inner_ref, bias_ref, dvec_ref, total):
    k = pl.program_id(0)
    fold = pl.num_programs(0)
    width = mixed_ref.shape[1]
    branch = branch_ref[...]
    columns = lambda n: pl.ds(pl.multiple_of(n * width, width), width)
    gs_ref[:, columns(1 + k)] = mm(active_ref[...], branch, 0, 0).astype(BF)
    d_upper_f = mm(branch, wd_ref[...], 1, 1) * slope_ref[...].astype(F32)
    bias_ref[0] = jnp.sum(d_upper_f, 0, keepdims=True)
    d_upper = d_upper_f.astype(BF)
    g_ref[:, columns(k)] = mm(second_ref[...], d_upper, 0, 0).astype(BF)
    back = mm(d_upper, wu_ref[...], 1, 1)

    @pl.when(k == 0)
    def _():
        total[...] = back

    @pl.when(k > 0)
    def _():
        total[...] += back

    @pl.when(k == fold - 1)
    def _():
        vec = vec_ref[...]
        d_hidden, gain, shift = norm_back_rows(hidden_ref[...], vec[2:3], total[...])
        dvec_ref[0:1] = gain
        dvec_ref[1:2] = shift
        d_hidden = dy_ref[...] + d_hidden
        dhid_ref[...] = d_hidden
        d_attend = d_hidden.astype(BF)
        mixed = mixed_ref[...]
        gs_ref[:, 0:width] = mm(mixed, d_attend, 0, 0).astype(BF)
        d_mixed = mm(d_attend, wo_ref[...], 1, 1).astype(BF)
        dmix_ref[...] = d_mixed
        head = lax.broadcasted_iota(jnp.int32, (16, width), 0)
        lane = lax.broadcasted_iota(jnp.int32, (16, width), 1)
        own = (lane // (width // HEADS) == head).astype(BF)
        high, low = split_two(d_mixed.astype(F32) * mixed.astype(F32))
        sums = mm(own, high, 1, 1) + mm(own, low, 1, 1)
        for h in range(HEADS // 2):
            inner_ref[h] = sums[2 * h : 2 * h + 2]


def mlp_bwd(dy, branch, active, slope, second, hidden, mixed, main, vec, fold):
    rows, width = mixed.shape
    whole = pl.BlockSpec((rows, width), lambda k: (0, 0))
    tile = pl.BlockSpec((rows, width), lambda k: (0, k))
    at = lambda f: pl.BlockSpec((width, width), lambda k: (0, f(k)))
    f = lambda *s: jax.ShapeDtypeStruct(s, F32)
    return pl.pallas_call(
        mlp_bwd_kernel,
        grid=(fold,),
        in_specs=[whole, whole, tile, tile, whole, whole, whole,
                  at(lambda k: 0), at(lambda k: 1 + k), at(lambda k: 1 + fold + k), pl.BlockSpec(vec.shape, lambda k: (0, 0))],
        out_specs=[pl.BlockSpec((width, fold * width), lambda k: (0, 0)), pl.BlockSpec((width, (1 + fold) * width), lambda k: (0, 0)), whole, whole,
                   pl.BlockSpec((HEADS // 2, 2, rows), lambda k: (0, 0, 0)),
                   pl.BlockSpec((1, 1, width), lambda k: (k, 0, 0)), pl.BlockSpec((8, width), lambda k: (0, 0))],
        out_shape=[jax.ShapeDtypeStruct((width, fold * width), BF), jax.ShapeDtypeStruct((width, (1 + fold) * width), BF), f(rows, width),
                   jax.ShapeDtypeStruct((rows, width), BF), f(HEADS // 2, 2, rows), f(fold, 1, width), f(8, width)],
        scratch_shapes=[pltpu.VMEM((rows, width), F32)],
        compiler_params=pltpu.CompilerParams(vmem_limit_bytes=60 << 20),
    )(dy, branch, active, slope, second, hidden, mixed, main, main, main, vec)


def project_bwd_kernel(dq_ref, dk_ref, dv_ref, normed_ref, w_ref, x_ref, dhid_ref, sums_ref, vec_ref, g_ref, dx_ref):
    width = dq_ref.shape[1]
    normed = normed_ref[...]
    back = None
    for n, ref in enumerate((dq_ref, dk_ref, dv_ref)):
        d = ref[...]
        g_ref[:, n * width : (n + 1) * width] = mm(normed, d, 0, 0).astype(BF)
        part = mm(d, w_ref[:, n * width : (n + 1) * width], 1, 1)
        back = part if back is None else back + part
    d_x, gain, shift = norm_back_rows(x_ref[...].astype(F32), vec_ref[0:1], back)
    dx_ref[...] = (dhid_ref[...] + d_x).astype(BF)
    sums = jnp.concatenate([gain, shift, sums_ref[2:, :]], 0)
    sums = jnp.concatenate([sums, jnp.zeros((128 - sums.shape[0], width), F32)], 0)
    g_ref[:, 3 * width : 3 * width + 128] = jnp.transpose(sums).astype(BF)
    g_ref[:, 3 * width + 128 : 3 * width + 256] = jnp.zeros((width, 128), BF)


def project_bwd(dq, dk, dv, normed, w_in, x, d_hidden, sums, vec):
    rows, width = dq.shape
    v = pl.BlockSpec(memory_space=pltpu.VMEM)
    return pl.pallas_call(
        project_bwd_kernel,
        in_specs=[v] * 9,
        out_specs=[v] * 2,
        out_shape=[jax.ShapeDtypeStruct((width, 3 * width + 256), BF), jax.ShapeDtypeStruct((rows, width), BF)],
        compiler_params=pltpu.CompilerParams(vmem_limit_bytes=56 << 20),
    )(dq, dk, dv, normed, w_in, x, d_hidden, sums, vec)


def outer_kernel(rows_ref, dimage_ref, dtext_ref,
                 pup_ref, tup_ref, pdown_ref, tdown_ref, pout_ref, tout_ref, thead_ref,
                 tq_ref, tk_ref, tv_ref, pv_ref, pk_ref, bias_ref):
    at_dp, z = lax.axis_index("dp"), lax.axis_index("seq")
    n_dp, n_z = 8, 4
    me = at_dp * n_z + z
    width = rows_ref.shape[2]
    part, quarter = width // 32, width // n_z
    wide_part = 4 * part
    n = n_dp * n_z
    each = quarter // part

    def iota(shape, d):
        return lax.broadcasted_iota(jnp.int32, shape, d)

    def selector(count, first):
        return (iota((count, width), 1) == iota((count, width), 0) + first).astype(BF)

    def group(r):
        return jnp.concatenate([rows_ref[r + c] for c in range(4)], 0)

    cols = jnp.concatenate(
        [mm(selector(part, part * me), rows_ref[r], 1, 1) for r in range(24, 80)], 1
    ).astype(BF)
    get = lambda r, count=1: cols[:, n * (r - 24) : n * (r - 24 + count)]
    a, b = iota((4 * n, n), 0), iota((4 * n, n), 1)
    same = ((a % n) // n_z == b // n_z) & (a // n == b % n_z)
    keep = lambda which: (same & (a % n_z == which)).astype(BF)
    units = selector(wide_part, wide_part * at_dp)
    heads = selector(part, quarter + part * (me % each))
    to_mine, to_head = keep(z), keep(me // each)
    chosen = lambda sel, r, perm: mm(mm(sel, group(r), 1, 1).astype(BF), perm).astype(BF)
    pdown_ref[...] = mm(chosen(units, 8, to_mine), dimage_ref[...])
    tdown_ref[...] = mm(chosen(units, 12, to_mine), rows_ref[29])
    pout_ref[...] = mm(chosen(heads, 16, to_head), rows_ref[25])
    tout_ref[...] = mm(chosen(heads, 20, to_head), rows_ref[28])
    thead_ref[...] = mm(get(30), dtext_ref[...])
    ones = jnp.ones((n, 128), BF)
    bias_ref[0] = mm(chosen(units, 0, to_mine), ones)
    bias_ref[1] = mm(chosen(units, 4, to_mine), ones)
    a, b = iota((n, 4 * n), 0), iota((n, 4 * n), 1)
    spread = ((b % n) // n_z == a // n_z) & (b // n == a % n_z)
    spread = spread.astype(BF)
    lane_z = iota((1, 4 * n), 1) % n_z
    masks = [(lane_z == q).astype(BF) for q in range(n_z)]

    def blocks(values):
        return jnp.concatenate([v * m for v, m in zip(values, masks)], 0)

    by_image = lambda r: mm(get(r), spread).astype(BF)
    g16, g20 = group(16), group(20)

    def put(ref, value, first):
        for q in range(n_z):
            ref[q] = value[q * part : (q + 1) * part, first : first + ref.shape[2]]

    put(pup_ref, mm(blocks([by_image(24)] * 4), group(0)), 0)
    put(tup_ref, mm(blocks([by_image(27)] * 4), group(4)), 0)
    put(tq_ref, mm(blocks([by_image(26)] * 4), g16), 2 * quarter)
    lane = iota((1, width), 1)
    count = HEADS // n_z
    hw = quarter // count

    def by_head(values_of, rhs, first):
        total = None
        for h in range(count):
            own = ((lane >= first + hw * h) & (lane < first + hw * h + hw)).astype(F32)
            one = mm(blocks(values_of(h)), rhs) * own
            total = one if total is None else total + one
        return total

    put(tk_ref, by_head(lambda h: [get(56 + 4 * h, 4)] * 4, g16, 3 * quarter), 3 * quarter)
    put(tv_ref, by_head(lambda h: [get(44 + 4 * h, 4)] * 4, g20, 0), 0)
    put(pv_ref, by_head(lambda h: [by_image(32 + count * q + h) for q in range(n_z)], g16, 0), 0)
    a, b = iota((HEADS * n, 128), 0), iota((HEADS * n, 128), 1)
    pk_ref[...] = mm(get(68, HEADS), (a // n == b).astype(BF))


def outer_grads(rows, d_image, d_text):
    width = rows.shape[2]
    part, quarter = width // 32, width // 4
    v = pl.BlockSpec(memory_space=pltpu.VMEM)
    f = lambda *s: jax.ShapeDtypeStruct(s, F32)
    return pl.pallas_call(
        outer_kernel,
        in_specs=[v] * 3,
        out_specs=[v] * 13,
        out_shape=[f(4, part, width), f(4, part, width), f(4 * part, width), f(4 * part, width), f(part, width), f(part, width),
                   f(part, width), f(4, part, quarter), f(4, part, quarter), f(4, part, quarter), f(4, part, quarter),
                   f(part, 128), f(2, 4 * part, 128)],
        compiler_params=pltpu.CompilerParams(vmem_limit_bytes=48 << 20),
    )(rows, d_image, d_text)


def fast_program(
    patches, captions, pairs,
    image_attend_in, image_attend_out, image_up_weight, image_up_bias, image_down_weight,
    image_vectors, probe_query_weight, probe_pair_weight, probe_out_weight, probe_up_weight,
    probe_up_bias, probe_down_weight, text_attend_in, text_attend_out, text_up_weight,
    text_up_bias, text_down_weight, text_vectors, text_head_weight, temp_bias,
):
    n_dp, n_z = lax.axis_size("dp"), lax.axis_size("seq")
    world = n_dp * n_z
    at_dp, at_z = lax.axis_index("dp"), lax.axis_index("seq")
    me = at_dp * n_z + at_z
    width = patches.shape[-1]
    head_width = width // HEADS
    hidden_width = image_up_weight.shape[1]
    part, quarter = width // world, width // n_z
    wide_part = hidden_width // world
    fold = hidden_width // width
    length = patches.shape[1] * n_z

    small = jnp.concatenate(
        [image_vectors.reshape(-1), text_vectors.reshape(-1), image_up_bias, probe_up_bias, text_up_bias]
    )
    sizes = [image_vectors.size, text_vectors.size, image_up_bias.size, probe_up_bias.size, text_up_bias.size]
    small = jnp.pad(small, (0, 2048 - small.shape[0])).reshape(16, 128)

    def by_units(w):
        return w.reshape(part, n_dp, n_z, wide_part).transpose(2, 0, 1, 3).reshape(n_z, part, width)

    def by_heads(w):
        cut = w.reshape(part, n_z, quarter).transpose(1, 0, 2)
        return jnp.pad(cut, ((0, 0), (0, 0), (0, 256 - quarter)))

    split = [by_units(probe_up_weight), by_units(text_up_weight)]
    split += [by_heads(text_attend_in[:, k * width : (k + 1) * width]) for k in range(3)]
    split += [by_heads(text_head_weight), by_heads(probe_query_weight)]
    split += [by_heads(probe_pair_weight[:, k * width : (k + 1) * width]) for k in range(2)]
    split = jnp.concatenate(split, 2)
    downs = jnp.concatenate([text_down_weight, probe_down_weight], 1)
    w_in, small_all, x = gather(
        [image_attend_in, small, patches],
        [("full", "S"), ("full", "C"), ("za", None)],
        [(0, 0), (1, 0), (0, 1), (1, 1), (0, 2), (1, 2), (0, 3), (2, 0), (1, 3), (0, 4), (1, 4), (0, 5), (1, 5)],
        1,
    )
    w_in = w_in.reshape(width, 3 * width)
    x = x.reshape(length, width)
    main = jnp.concatenate(
        [
            image_attend_out,
            image_up_weight.reshape(part, width, fold).transpose(0, 2, 1).reshape(part, hidden_width),
            image_down_weight.reshape(part, hidden_width),
            text_attend_out,
            probe_out_weight,
        ],
        1,
    )
    main = lax.all_gather(main, ALL, axis=0, tiled=True)
    outs = lax.dynamic_slice_in_dim(main[:, width + 2 * hidden_width :], at_z * quarter, quarter, 0)

    small_all = small_all.reshape(world, -1)
    cuts = [sum(sizes[:i]) for i in range(len(sizes) + 1)]
    pieces = [small_all[:, cuts[i] : cuts[i + 1]].astype(F32) for i in range(len(sizes))]
    ivec = pieces[0].reshape(world, -1, part).transpose(1, 0, 2).reshape(-1, width)
    tvec = pieces[1].reshape(world, -1, part).transpose(1, 0, 2).reshape(-1, width)
    i_bias = pieces[2].reshape(width, fold).T.reshape(1, hidden_width)

    def own_units(p):
        p = p.reshape(n_dp, n_z, wide_part)
        return lax.dynamic_index_in_dim(p, at_z, 1, False).reshape(1, width)

    p_bias, t_bias = own_units(pieces[3]), own_units(pieces[4])

    normed = layer_norm(x.astype(F32), ivec[0], ivec[1]).astype(BF)
    proj = mm(normed, w_in).astype(BF)
    mixed, lse, tp, downs, tokens = attend_fwd_and_gather(proj, split, downs, captions, 5)
    hidden, second, active, slope, block_out, final, tp, downs = mlp_fwd(
        x, mixed, main, i_bias, ivec, fold, tp, downs, 6
    )
    tp, downs = tp.reshape(width, -1), downs.reshape(width, -1)

    labels = (2 * pairs - 1).astype(F32).reshape(n_dp, n_z, n_dp, n_z)
    labels = jnp.pad(labels, ((0, 0), (0, n_z), (0, 0), (n_z, 0))).reshape(2 * world, 2 * world)
    dy, d_branch, rows, sums, d_captions, loss_row, d_embeds = middle(
        final, block_out, tokens.reshape(-1, width), tp, downs, outs, ivec, tvec, p_bias, t_bias, labels, temp_bias, 2, n_dp
    )
    loss, grad_temp = loss_row[0, 0], loss_row[0, 1:3]
    grad_captions = d_captions.reshape(captions.shape)

    g_up, g_rest, d_hidden, d_mixed, inner, g_bias, dvec = mlp_bwd(
        dy, d_branch, active, slope, second, hidden, mixed, main, ivec, fold
    )
    g_rest = lax.psum_scatter(g_rest, ALL, scatter_dimension=0, tiled=True).astype(F32)
    own_out = g_rest[:, :width]
    own_down = g_rest[:, width:].reshape(wide_part, width)
    d_q, d_k, d_v, own_up, rows = attend_bwd_and_reduce(proj, d_mixed, lse, inner, g_up, rows, 4)
    own_up = own_up.reshape(part, fold, width).transpose(0, 2, 1).reshape(part, hidden_width)
    rows = rows.reshape(world, ROWS, width).transpose(1, 0, 2)
    sums = jnp.concatenate([dvec[0:2], dvec[0:2], sums[4:], g_bias.reshape(fold, width)], 0)
    g_in, d_x = project_bwd(d_q, d_k, d_v, normed, w_in, x, d_hidden, sums, ivec)
    own_in, moved = reduce_and_move(g_in, d_x, 3)
    grad_patches = moved.astype(F32)
    own_sums = own_in[:, 3 * width : 3 * width + 128].T
    own_in = own_in[:, : 3 * width]

    d_embeds = d_embeds.reshape(n_dp, 2, n_z, width).astype(BF)
    pup, tup, own_p_down, own_t_down, own_p_out, own_t_out, own_t_head, tq, tk, tv, pv, pk, biases = outer_grads(
        rows, d_embeds[:, 0].reshape(world, width), d_embeds[:, 1].reshape(world, width)
    )

    def wide(g):
        return g.reshape(n_z, part, n_dp, wide_part).transpose(1, 2, 0, 3).reshape(part, hidden_width)

    own_p_up, own_t_up = wide(pup), wide(tup)
    own_t_in = jnp.stack([tq, tk, tv]).transpose(2, 0, 1, 3).reshape(part, 3 * width)
    row20 = rows[20].reshape(n_dp, n_z, n_z, quarter).astype(F32)
    probe_query = row20[0, :, 3].reshape(HEADS, head_width)
    own_p_k = (pk[:, :HEADS, None] * probe_query[None]).reshape(part, width)
    own_p_pair = jnp.concatenate([own_p_k, pv.transpose(1, 0, 2).reshape(part, width)], 1)
    d_query = jnp.sum(row20[:, :, 2], 0).reshape(width)
    mine = lambda v, n: lax.dynamic_slice_in_dim(v, me * n, n, -1)
    own_p_query = mine(ivec[7], part)[:, None] * d_query[None, :]
    dv7 = jnp.sum(probe_query_weight.astype(F32) * d_query[None, :], 1)
    own_ivec = jnp.concatenate([own_sums[0:7], dv7[None], own_sums[8:11]], 0)
    own_tvec = own_sums[11:18]
    own_bias = own_sums[24 : 24 + fold].T.reshape(wide_part)
    return (
        loss, grad_patches, grad_captions,
        own_in, own_out, own_up, own_bias, own_down, own_ivec,
        own_p_query, own_p_pair, own_p_out, own_p_up, biases[0, :, 0], own_p_down,
        own_t_in, own_t_out, own_t_up, biases[1, :, 0], own_t_down, own_tvec, own_t_head,
        grad_temp,
    )


def solution(mesh):
    tokens, matrix, vector, table = P("dp", "seq", None), P(ALL, None), P(ALL), P(None, ALL)
    weights = (
        (matrix, matrix, matrix, vector, matrix, table, matrix, matrix, matrix, matrix, vector, matrix)
        + (matrix, matrix, matrix, vector, matrix, table, matrix)
    )
    return jax.shard_map(
        fast_program if mesh.shape["dp"] == 8 and mesh.shape["seq"] == 4 else device_program,
        mesh=mesh,
        in_specs=(tokens, tokens, P()) + weights + (P(),),
        out_specs=(P(), tokens, tokens) + weights + (P(),),
        check_vma=False,
    )
```

```python
from functools import partial

import jax
import jax.numpy as jnp
from jax import lax
from jax.experimental import pallas as pl
from jax.experimental.pallas import tpu as pltpu
from jax.sharding import PartitionSpec as P

HEADS = 12
ALL = ("dp", "seq")
F32, BF = jnp.float32, jnp.bfloat16
HIGH = lax.Precision.HIGHEST
EPS = 1e-06


def mm(a, b, ca=1, cb=0):
    return lax.dot_general(a, b, (((ca,), (cb,)), ((), ())), preferred_element_type=F32)


def mm_exact(a, b, ca=1, cb=0):
    return lax.dot_general(a, b, (((ca,), (cb,)), ((), ())), precision=HIGH, preferred_element_type=F32)


def split_two(a):
    high = a.astype(BF)
    return high, (a - high.astype(F32)).astype(BF)


def layer_norm(x, gain, shift):
    center = x - jnp.mean(x, -1, keepdims=True)
    spread = jnp.mean(center * center, -1, keepdims=True)
    return center * lax.rsqrt(spread + EPS) * gain + shift


def norm_back(x, gain, upstream):
    center = x - jnp.mean(x, -1, keepdims=True)
    inverse = lax.rsqrt(jnp.mean(center * center, -1, keepdims=True) + EPS)
    unit = center * inverse
    scaled = upstream * gain
    d_x = inverse * (
        scaled
        - jnp.mean(scaled, -1, keepdims=True)
        - unit * jnp.mean(scaled * unit, -1, keepdims=True)
    )
    return d_x, jnp.sum(upstream * unit, 0), jnp.sum(upstream, 0)


def norm_back_rows(x, gain, upstream):
    d_x, d_gain, d_shift = norm_back(x, gain, upstream)
    return d_x, d_gain[None], d_shift[None]


def mm_two(a, b, cb=0):
    n = a.shape[0]
    high = a.astype(BF).astype(F32)
    both = mm(jnp.concatenate([high, a - high], 0).astype(BF), b, 1, cb)
    return both[0:n] + both[n : 2 * n]


def gelu_pair(u):
    c = 0.7978845608028654
    t = jnp.tanh(c * (u + 0.044715 * u * u * u))
    value = 0.5 * u * (1.0 + t)
    slope = 0.5 * (1.0 + t) + 0.5 * u * (1.0 - t * t) * c * (1.0 + 3 * 0.044715 * u * u)
    return value, slope


def attend_fwd_kernel(q_ref, k_ref, v_ref, o_ref, lse_ref):
    q = q_ref[...] * 0.125
    k = k_ref[...]
    lane = lax.broadcasted_iota(jnp.int32, k.shape, 1)
    v_turned = jnp.transpose(v_ref[...])
    outs = []
    for h in range(2):
        keep = (lane < 64) if h == 0 else (lane >= 64)
        own_k = jnp.where(keep, k, jnp.zeros_like(k))
        s = mm(own_k, q, 1, 1)
        top = jnp.max(s, 0, keepdims=True)
        p = jnp.exp(s - top)
        total = jnp.sum(p, 0, keepdims=True)
        outs.append(mm(v_turned[64 * h : 64 * h + 64], p.astype(BF)) / total)
        lse_ref[0, h : h + 1, :] = top + jnp.log(total)
    o_ref[...] = jnp.transpose(jnp.concatenate(outs, 0)).astype(BF)


def attend_fwd(proj, length):
    rows, width = proj.shape[0], proj.shape[1] // 3
    pairs = width // 128
    block = lambda part: pl.BlockSpec((length, 128), lambda b, h: (b, part * pairs + h))
    return pl.pallas_call(
        attend_fwd_kernel,
        grid=(rows // length, pairs),
        in_specs=[block(0), block(1), block(2)],
        out_specs=[block(0), pl.BlockSpec((1, 2, length), lambda b, h: (h, 0, b))],
        out_shape=[
            jax.ShapeDtypeStruct((rows, width), BF),
            jax.ShapeDtypeStruct((pairs, 2, rows), F32),
        ],
        compiler_params=pltpu.CompilerParams(vmem_limit_bytes=48 << 20),
        cost_estimate=pl.CostEstimate(
            flops=rows * length * width * 8,
            bytes_accessed=rows * width * 8,
            transcendentals=rows * length * HEADS,
        ),
    )(proj, proj, proj)


def attend_bwd_kernel(q_ref, k_ref, v_ref, do_ref, lse_ref, d_ref, dq_ref, dk_ref, dv_ref):
    q = q_ref[...] * 0.125
    k, v, do = k_ref[...], v_ref[...], do_ref[...]
    lane = lax.broadcasted_iota(jnp.int32, k.shape, 1)
    dqs, dks, dvs = [], [], []
    for h in range(2):
        keep = (lane < 64) if h == 0 else (lane >= 64)
        s = mm(jnp.where(keep, k, jnp.zeros_like(k)), q, 1, 1)
        p = jnp.exp(s - lse_ref[0, h : h + 1, :])
        dp = mm(jnp.where(keep, v, jnp.zeros_like(v)), do, 1, 1)
        ds = (p * (dp - d_ref[0, h : h + 1, :])).astype(BF)
        dvs.append(mm(p.astype(BF), do))
        dks.append(mm(ds, q))
        dqs.append(mm(ds, k, 0, 0))
    low = lane < 64
    dq_ref[...] = (jnp.where(low, dqs[0], dqs[1]) * 0.125).astype(BF)
    dk_ref[...] = jnp.where(low, dks[0], dks[1]).astype(BF)
    dv_ref[...] = jnp.where(low, dvs[0], dvs[1]).astype(BF)


def attend_bwd(proj, d_out, lse, inner, length):
    rows, width = proj.shape[0], proj.shape[1] // 3
    pairs = width // 128
    block = lambda part: pl.BlockSpec((length, 128), lambda b, h: (b, part * pairs + h))
    row = pl.BlockSpec((1, 2, length), lambda b, h: (h, 0, b))
    result = jax.ShapeDtypeStruct((rows, width), BF)
    return pl.pallas_call(
        attend_bwd_kernel,
        grid=(rows // length, pairs),
        in_specs=[block(0), block(1), block(2), block(0), row, row],
        out_specs=[block(0)] * 3,
        out_shape=[result] * 3,
        compiler_params=pltpu.CompilerParams(vmem_limit_bytes=56 << 20),
        cost_estimate=pl.CostEstimate(
            flops=rows * length * width * 20,
            bytes_accessed=rows * width * 16,
            transcendentals=rows * length * HEADS,
        ),
    )(proj, proj, proj, d_out, lse, inner)


def head_blocks(width):
    own = jnp.arange(width)[None, :] // (width // HEADS) == jnp.arange(HEADS)[:, None]
    return own.astype(F32)


def spread_heads(rows):
    n, width = rows.shape
    return (rows[:, None, :] * head_blocks(width)[None]).reshape(n * HEADS, width)


def fold_heads(rows):
    total, width = rows.shape
    return jnp.sum(rows.reshape(total // HEADS, HEADS, width) * head_blocks(width)[None], 1)


def device_program(
    patches, captions, pairs,
    image_attend_in, image_attend_out, image_up_weight, image_up_bias, image_down_weight,
    image_vectors, probe_query_weight, probe_pair_weight, probe_out_weight, probe_up_weight,
    probe_up_bias, probe_down_weight, text_attend_in, text_attend_out, text_up_weight,
    text_up_bias, text_down_weight, text_vectors, text_head_weight, temp_bias,
):
    seq = lax.axis_size("seq")
    world = seq * lax.axis_size("dp")
    me = lax.axis_index("dp") * seq + lax.axis_index("seq")
    width = patches.shape[-1]
    head_width = width // HEADS
    factor = head_width ** (-0.5)
    hidden_width = image_up_weight.shape[1]
    part = width // world
    wide_part = hidden_width // world

    def gather(*weights):
        flat = jnp.concatenate([w.reshape(-1, width) for w in weights], 0)
        full = lax.all_gather(flat, ALL, axis=0)
        out, at = [], 0
        for w in weights:
            count = w.size // width
            piece = full[:, at : at + count]
            out.append(piece.reshape(world * w.shape[0], w.shape[1]))
            at += count
        return out

    small = jnp.concatenate(
        [image_vectors.reshape(-1), text_vectors.reshape(-1), image_up_bias, probe_up_bias, text_up_bias]
    )
    small_all = lax.all_gather(small, ALL, axis=0)
    sizes = [image_vectors.size, text_vectors.size, image_up_bias.size, probe_up_bias.size, text_up_bias.size]
    cuts = [sum(sizes[:i]) for i in range(len(sizes) + 1)]
    pieces = [small_all[:, cuts[i] : cuts[i + 1]].astype(F32) for i in range(len(sizes))]
    ivec = pieces[0].reshape(world, -1, part).transpose(1, 0, 2).reshape(-1, width)
    tvec = pieces[1].reshape(world, -1, part).transpose(1, 0, 2).reshape(-1, width)
    i_bias, p_bias, t_bias = (p.reshape(-1) for p in pieces[2:])

    (w_in,) = gather(image_attend_in)
    w_out, w_up, w_down = gather(image_attend_out, image_up_weight, image_down_weight)
    tw_in, tw_out, tw_up, tw_down, tw_head, pw_query, pw_pair, pw_out, pw_up, pw_down = gather(
        text_attend_in, text_attend_out, text_up_weight, text_down_weight, text_head_weight,
        probe_query_weight, probe_pair_weight, probe_out_weight, probe_up_weight, probe_down_weight,
    )

    def to_owner(x):
        return lax.all_to_all(x, "seq", 0, 1, tiled=True)

    x = to_owner(patches)
    own, length = x.shape[0], x.shape[1]
    x = x.reshape(own * length, width).astype(F32)
    captions_own = to_owner(captions)
    text_length = captions_own.shape[1]

    normed = layer_norm(x, ivec[0], ivec[1]).astype(BF)
    proj = mm(normed, w_in).astype(BF)
    mixed, lse = attend_fwd(proj, length)
    hidden = x + mm(mixed, w_out)
    second = layer_norm(hidden, ivec[2], ivec[3]).astype(BF)
    value, slope = gelu_pair(mm(second, w_up) + i_bias)
    active, slope = value.astype(BF), slope.astype(BF)
    block_out = hidden + mm(active, w_down) + ivec[4]
    final = layer_norm(block_out, ivec[5], ivec[6]).astype(BF)

    t_x = captions_own.astype(F32)
    t_normed = layer_norm(t_x, tvec[0], tvec[1]).astype(BF)
    t_last = t_normed[:, -1]
    tw_q, tw_k, tw_v = tw_in[:, :width], tw_in[:, width : 2 * width], tw_in[:, 2 * width :]
    t_q = mm(t_last, tw_q).astype(BF)
    t_keys = mm(spread_heads(t_q.astype(F32)).astype(BF), tw_k, 1, 1) * factor
    t_keys = t_keys.reshape(own, HEADS, width)
    k_high, k_low = split_two(t_keys)
    scores = jnp.einsum("bsd,bhd->bsh", t_normed, k_high, preferred_element_type=F32)
    scores += jnp.einsum("bsd,bhd->bsh", t_normed, k_low, preferred_element_type=F32)
    t_probs = jax.nn.softmax(scores, axis=1)
    t_used = jnp.einsum("bsh,bsd->bhd", t_probs, t_normed.astype(F32), precision=HIGH)
    t_mixed = fold_heads(mm(t_used.reshape(own * HEADS, width).astype(BF), tw_v)).astype(BF)
    t_hidden = t_x[:, -1] + mm(t_mixed, tw_out)
    t_second = layer_norm(t_hidden, tvec[2], tvec[3]).astype(BF)
    t_value, t_slope = gelu_pair(mm(t_second, tw_up) + t_bias)
    t_active = t_value.astype(BF)
    t_out = t_hidden + mm(t_active, tw_down) + tvec[4]
    t_final = layer_norm(t_out, tvec[5], tvec[6]).astype(BF)
    text_embed = mm(t_final, tw_head)

    pw_k, pw_v = pw_pair[:, :width], pw_pair[:, width:]
    probe_query = mm_exact(ivec[7:8], pw_query.astype(F32))
    p_keys = mm_exact(spread_heads(probe_query), pw_k.astype(F32), 1, 1) * factor
    k_high, k_low = split_two(p_keys)
    pool_scores = mm(k_high, final, 1, 1) + mm(k_low, final, 1, 1)
    pool_scores = pool_scores.reshape(HEADS, own, length)
    pool_probs = jax.nn.softmax(pool_scores, axis=-1)
    final_own = final.reshape(own, length, width)
    p_high, p_low = split_two(pool_probs)
    used = jnp.einsum("hbt,btd->bhd", p_high, final_own, preferred_element_type=F32)
    used += jnp.einsum("hbt,btd->bhd", p_low, final_own, preferred_element_type=F32)
    pooled = fold_heads(mm_exact(used.reshape(own * HEADS, width), pw_v.astype(F32)))
    head_start = mm_exact(pooled, pw_out.astype(F32))
    head_normed = layer_norm(head_start, ivec[8], ivec[9]).astype(BF)
    h_value, h_slope = gelu_pair(mm(head_normed, pw_up) + p_bias)
    head_active = h_value.astype(BF)
    image_embed = head_start + mm(head_active, pw_down) + ivec[10]

    embeds = lax.all_gather(jnp.stack([image_embed, text_embed], 1), ALL, axis=0, tiled=True)
    every_image, every_text = embeds[:, 0], embeds[:, 1]
    labels = (2 * pairs - 1).astype(F32)
    total = every_image.shape[0]
    i_scale = lax.rsqrt(jnp.sum(every_image * every_image, -1, keepdims=True) + EPS)
    t_scale = lax.rsqrt(jnp.sum(every_text * every_text, -1, keepdims=True) + EPS)
    z_i, z_t = every_image * i_scale, every_text * t_scale
    cosine = mm_exact(z_i, z_t, 1, 1)
    temper = jnp.exp(temp_bias[0])
    logits = cosine * temper + temp_bias[1]
    loss = -jnp.sum(jax.nn.log_sigmoid(labels * logits)) / total
    g = -labels * jax.nn.sigmoid(-labels * logits) / total
    grad_temp = jnp.stack([temper * jnp.sum(g * cosine), jnp.sum(g)])
    dz_i = temper * mm_exact(g, z_t)
    dz_t = temper * mm_exact(g, z_i, 0, 0)
    all_d_image = (dz_i - z_i * jnp.sum(z_i * dz_i, -1, keepdims=True)) * i_scale
    all_d_text = (dz_t - z_t * jnp.sum(z_t * dz_t, -1, keepdims=True)) * t_scale
    d_image = lax.dynamic_slice_in_dim(all_d_image, me * own, own, 0)
    d_text = lax.dynamic_slice_in_dim(all_d_text, me * own, own, 0)

    h_upper = mm_exact(d_image, pw_down.astype(F32), 1, 1) * h_slope
    h_norm = mm_exact(h_upper, pw_up.astype(F32), 1, 1)
    d_start, dv8, dv9 = norm_back(head_start, ivec[8], h_norm)
    d_start = d_image + d_start
    dv10 = jnp.sum(d_image, 0)
    d_pooled = mm_exact(d_start, pw_out.astype(F32), 1, 1)
    p_values = mm_exact(spread_heads(d_pooled), pw_v.astype(F32), 1, 1).reshape(own, HEADS, width)
    v_high, v_low = split_two(p_values)
    d_probs = jnp.einsum("bhd,btd->hbt", v_high, final_own, preferred_element_type=F32)
    d_probs += jnp.einsum("bhd,btd->hbt", v_low, final_own, preferred_element_type=F32)
    d_scores = pool_probs * (d_probs - jnp.sum(pool_probs * d_probs, -1, keepdims=True))
    s_high, s_low = split_two(d_scores)
    p_used = jnp.einsum("hbt,btd->bhd", s_high, final_own, preferred_element_type=F32)
    p_used += jnp.einsum("hbt,btd->bhd", s_low, final_own, preferred_element_type=F32)
    d_query = jnp.sum(fold_heads(mm_exact(p_used.reshape(own * HEADS, width), pw_k.astype(F32))), 0) * factor
    d_final = jnp.einsum(
        "hbt,bhd->btd",
        jnp.concatenate([s_high, p_high], 0),
        jnp.concatenate([jnp.broadcast_to(k_high[None], (own, HEADS, width)), v_high], 1),
        preferred_element_type=F32,
    ).reshape(own * length, width)
    dy, dv5, dv6 = norm_back(block_out, ivec[5], d_final)

    d_branch = dy.astype(BF)
    g_down = mm(active, d_branch, 0, 0)
    dv4 = jnp.sum(dy, 0)
    d_upper_f = mm(d_branch, w_down, 1, 1) * slope.astype(F32)
    d_upper = d_upper_f.astype(BF)
    g_bias = jnp.sum(d_upper_f, 0)
    g_up = mm(second, d_upper, 0, 0)
    d_hidden, dv2, dv3 = norm_back(hidden, ivec[2], mm(d_upper, w_up, 1, 1))
    d_hidden = dy + d_hidden
    d_attend = d_hidden.astype(BF)
    g_out = mm(mixed, d_attend, 0, 0)
    d_mixed = mm(d_attend, w_out, 1, 1).astype(BF)

    def scatter(*grads):
        flat = jnp.concatenate([g.astype(BF).reshape(world, -1, width) for g in grads], 1)
        mine = lax.psum_scatter(flat, ALL, scatter_dimension=0, tiled=False).astype(F32)
        out, at = [], 0
        for g in grads:
            count = g.size // world // width
            out.append(mine[at : at + count].reshape(g.shape[0] // world, g.shape[1]))
            at += count
        return out

    own_up, own_down, own_out = scatter(g_up, g_down, g_out)
    inner_rows = jnp.sum(
        (d_mixed.astype(F32) * mixed.astype(F32)).reshape(own * length, HEADS, head_width), -1
    ).T.reshape(HEADS // 2, 2, own * length)
    d_q, d_k, d_v = attend_bwd(proj, d_mixed, lse, inner_rows, length)
    g_in = jnp.concatenate([mm(normed, d, 0, 0) for d in (d_q, d_k, d_v)], 1)
    (own_in,) = scatter(g_in)
    d_normed = (
        mm(d_q, w_in[:, :width], 1, 1)
        + mm(d_k, w_in[:, width : 2 * width], 1, 1)
        + mm(d_v, w_in[:, 2 * width :], 1, 1)
    )
    d_x, dv0, dv1 = norm_back(x, ivec[0], d_normed)
    d_x = (d_hidden + d_x).reshape(own, length, width)

    def to_tokens(v):
        return lax.all_to_all(v.astype(BF), "seq", 1, 0, tiled=True).astype(F32)

    grad_patches = to_tokens(d_x)

    dt_final = mm_exact(d_text, tw_head.astype(F32), 1, 1)
    dt_out, tv5, tv6 = norm_back(t_out, tvec[5], dt_final)
    dt_branch = dt_out.astype(BF)
    tv4 = jnp.sum(dt_out, 0)
    dt_upper = (mm(dt_branch, tw_down, 1, 1) * t_slope).astype(BF)
    dt_hidden, tv2, tv3 = norm_back(t_hidden, tvec[2], mm(dt_upper, tw_up, 1, 1))
    dt_hidden = dt_out + dt_hidden
    dt_attend = dt_hidden.astype(BF)
    dt_mixed = mm(dt_attend, tw_out, 1, 1).astype(BF)
    t_values = mm(spread_heads(dt_mixed.astype(F32)).astype(BF), tw_v, 1, 1).reshape(own, HEADS, width)
    tv_high, tv_low = split_two(t_values)
    dt_probs = jnp.einsum("bsd,bhd->bsh", t_normed, tv_high, preferred_element_type=F32)
    dt_probs += jnp.einsum("bsd,bhd->bsh", t_normed, tv_low, preferred_element_type=F32)
    dt_scores = t_probs * (dt_probs - jnp.sum(t_probs * dt_probs, 1, keepdims=True))
    tk_used = jnp.einsum("bsh,bsd->bhd", dt_scores, t_normed.astype(F32), precision=HIGH)
    dt_q = fold_heads(mm(tk_used.reshape(own * HEADS, width).astype(BF), tw_k)) * factor
    dt_q = dt_q.astype(BF)
    dt_normed = jnp.einsum("bsh,bhd->bsd", dt_scores, t_keys, precision=HIGH)
    dt_normed += jnp.einsum("bsh,bhd->bsd", t_probs, t_values, precision=HIGH)
    dt_normed = dt_normed.at[:, -1].add(mm(dt_q, tw_q, 1, 1))
    flat_x = t_x.reshape(own * text_length, width)
    dt_x, tv0, tv1 = norm_back(flat_x, tvec[0], dt_normed.reshape(own * text_length, width))
    dt_x = dt_x.reshape(own, text_length, width).at[:, -1].add(dt_hidden)
    grad_captions = to_tokens(dt_x)

    whole = jnp.concatenate(
        [v.astype(F32) for v in (h_upper, d_start, d_pooled, dt_branch, dt_upper, dt_attend, dt_q, t_q, dt_mixed)], 1
    )
    whole = lax.all_gather(whole, ALL, axis=0, tiled=True)
    at = [0]

    def take(count):
        at[0] += count
        return whole[:, at[0] - count : at[0]]

    a_h_upper, a_start, a_pooled, a_branch, a_upper, a_attend, a_q, a_query, a_mixed = (
        take(c) for c in (hidden_width, width, width, width, hidden_width, width, width, width, width)
    )
    columns = [pooled, head_normed, t_last, t_mixed, t_second, t_final]
    columns += [used, t_used, tk_used * factor]
    columns += [head_active, t_active]
    columns = jnp.concatenate(
        [v.astype(F32).reshape(own, -1, width) for v in columns], 1
    )
    wide = 2 * (hidden_width // width)
    narrow = columns.shape[1] - wide
    cut = jnp.concatenate(
        [
            columns[:, :narrow].reshape(own, narrow, world, part).transpose(2, 0, 1, 3).reshape(world, own, -1),
            columns[:, narrow:].reshape(own, 2, world, wide_part).transpose(2, 0, 1, 3).reshape(world, own, -1),
        ],
        2,
    )
    cut = lax.all_to_all(cut, ALL, 0, 0, tiled=True).reshape(total, -1)
    slim = cut[:, : narrow * part].reshape(total, narrow, part)
    broad = cut[:, narrow * part :].reshape(total, 2, wide_part)

    def outer(rows, cols):
        return mm_exact(rows, cols, 0, 0)

    def outer_heads(rows, cols):
        cols = cols.reshape(total, HEADS, head_width)
        return jnp.einsum("chm,che->mhe", rows, cols, precision=HIGH).reshape(part, width)

    c_pooled, c_head, c_last, c_mixed, c_second, c_final = (slim[:, i] for i in range(6))
    c_used, ct_used, ctk_used = (slim[:, 6 + i * HEADS : 6 + (i + 1) * HEADS] for i in range(3))
    own_t_in = jnp.concatenate(
        [outer(c_last, a_q), outer_heads(ctk_used, a_query), outer_heads(ct_used, a_mixed)], 1
    )
    own_t_out = outer(c_mixed, a_attend)
    own_t_up = outer(c_second, a_upper)
    own_t_down = outer(broad[:, 1], a_branch)
    own_t_head = outer(c_final, all_d_text)
    own_p_out = outer(c_pooled, a_start)
    own_p_up = outer(c_head, a_h_upper)
    own_p_down = outer(broad[:, 0], all_d_image)
    own_p_values = outer_heads(c_used, a_pooled)

    summed = jnp.concatenate(
        [
            jnp.stack([dv0, dv1, dv2, dv3, dv4, dv5, dv6, dv8, dv9, dv10]),
            jnp.stack([tv0, tv1, tv2, tv3, tv4, tv5, tv6]),
            d_query[None],
            jnp.sum(p_used, 0),
            g_bias.reshape(-1, width),
        ],
        0,
    )
    summed = lax.psum(summed, ALL)
    total_query = summed[17]
    mine = lambda v, n: lax.dynamic_slice_in_dim(v, me * n, n, -1)
    own_probe = mine(ivec[7], part)
    own_p_query = own_probe[:, None] * total_query[None, :]
    dv7 = jnp.sum(probe_query_weight.astype(F32) * total_query[None, :], 1)
    pk_used = mine(summed[18 : 18 + HEADS], part)
    own_p_keys = jnp.einsum(
        "hm,he->mhe", pk_used, probe_query.reshape(HEADS, head_width) * factor
    ).reshape(part, width)
    own_p_pair = jnp.concatenate([own_p_keys, own_p_values], 1)
    ten = mine(summed[:10], part)
    own_ivec = jnp.concatenate([ten[:7], dv7[None], ten[7:]], 0)
    own_tvec = mine(summed[10:17], part)
    own_bias = mine(summed[18 + HEADS :].reshape(-1), wide_part)
    own_p_bias = mine(jnp.sum(a_h_upper, 0), wide_part)
    own_t_bias = mine(jnp.sum(a_upper, 0), wide_part)
    return (
        loss, grad_patches, grad_captions,
        own_in, own_out, own_up, own_bias, own_down, own_ivec,
        own_p_query, own_p_pair, own_p_out, own_p_up, own_p_bias, own_p_down,
        own_t_in, own_t_out, own_t_up, own_t_bias, own_t_down, own_tvec, own_t_head,
        grad_temp,
    )


MESH = pl.DeviceIdType.MESH

class Place:
    def __init__(self):
        i = lax.axis_index("dp")
        self.i, self.z = i, lax.axis_index("seq")
        self.y, self.x, self.c = i // 4, (i // 2) % 2, i % 2
        self.at_y = (i + 4 - 8 * self.y, self.z)
        self.at_x = (i + 2 - 4 * self.x, self.z)
        self.at_c = (i + 1 - 2 * self.c, self.z)

    def at_z(self, k):
        return (self.i, (self.z + k) % 4)

def greet(peers):
    barrier = pltpu.get_barrier_semaphore()
    for p in peers:
        pl.semaphore_signal(barrier, inc=1, device_id=p, device_id_type=MESH)
    pl.semaphore_wait(barrier, len(peers))

def gather_kernel(kinds, order, *refs):
    n = len(kinds)
    srcs, outs = refs[:n], refs[n : 2 * n]
    send, recv, local = refs[2 * n :]
    me = Place()
    y, x, c, z = me.y, me.x, me.c, me.z
    greet([me.at_z(1), me.at_z(2), me.at_z(3), me.at_x, me.at_y, me.at_c])
    ends = []

    def copy_of(a, slot, src, dst, dev):
        return pltpu.make_async_remote_copy(
            src, dst, send.at[a, slot], recv.at[a, slot], device_id=dev, device_id_type=MESH
        )

    def push(a, slot, src, dst, dev, arriving):
        copy = copy_of(a, slot, src, dst, dev)
        copy.start()
        ends.append(copy.wait_send)
        return copy_of(a, slot, src, arriving, dev).wait_recv

    def along(a, step, up):
        home = outs[a].at[y, x, c]
        if up:
            slab, go, to = z - step, (z - step >= 0) & (z < 3), me.at_z(1)
        else:
            slab, go, to = z + step, (z + step < 4) & (z > 0), me.at_z(3)
        slab = jnp.clip(slab, 0, 3)
        src = srcs[a] if step == 0 else home.at[slab]
        copy = copy_of(a, step + (0 if up else 3), src, home.at[slab], to)
        pl.when(go)(lambda: copy.start())
        ends.append(lambda: pl.when(go)(lambda: copy.wait_send()))

    def arrived(a, step, up):
        home = outs[a].at[y, x, c]
        if up:
            slab, come = z - 1 - step, z - 1 - step >= 0
        else:
            slab, come = z + 1 + step, z + 1 + step < 4
        slab = jnp.clip(slab, 0, 3)
        copy = copy_of(a, step + (0 if up else 3), home.at[slab], home.at[slab], me.at_z(1))
        pl.when(come)(lambda: copy.wait_recv())

    waits = {}

    def half(r, which, order_):
        if order_ != "S":
            return r
        n_ = r.shape[-1] // 2
        return r.at[..., 0:n_] if which == "C" else r.at[..., n_ : 2 * n_]

    def stage(a, s):
        kind, turn = kinds[a]
        src, out = srcs[a], outs[a]
        if kind in ("za", "zg"):
            own = src.at[z] if kind == "za" else src
            keep = pltpu.make_async_copy(own, out.at[z], local.at[a])
            keep.start()
            ends.append(keep.wait)
            for k in (1, 2, 3):
                to, fro = (z + k) % 4, (z + 4 - k) % 4
                s_ref = src.at[to] if kind == "za" else src
                ends.append(push(a, k - 1, s_ref, out.at[z], me.at_z(k), out.at[fro]))
            return
        turns = "CD" if turn == "S" else turn
        if kind != "full" and s == 0:
            own = src.at[z] if kind == "cols" else src
            keep = pltpu.make_async_copy(own, out.at[y, x, c, z] if kind == "cols" else out.at[y, x, c], local.at[a])
            keep.start()
            waits[a] = [keep.wait]
            for k in (1, 2, 3) if kind == "cols" else ():
                to, fro = (z + k) % 4, (z + 4 - k) % 4
                waits[a].append(push(a, k - 1, src.at[to], out.at[y, x, c, z], me.at_z(k), out.at[y, x, c, fro]))
        elif s == 0:
            keep = pltpu.make_async_copy(src, out.at[y, x, c, z], local.at[a])
            keep.start()
            waits[a] = [keep.wait]
            along(a, 0, True)
            along(a, 0, False)
        elif s in (1, 2):
            for up in (True, False):
                arrived(a, s - 1, up)
                along(a, s, up)
        elif s == 3:
            for up in (True, False) if kind == "full" else ():
                arrived(a, 2, up)
            for w in waits.pop(a):
                w()
            waits[a] = []
            for t in turns:
                cut = lambda r: half(r, t, turn)
                to, fro = (me.at_x, (y, 1 - x)) if t == "C" else (me.at_y, (1 - y, x))
                mine = cut(out.at[y, x, c])
                waits[a].append(push(a, 6 + (t == "D"), mine, mine, to, cut(out.at[fro[0], fro[1], c])))
        elif s == 4:
            for w in waits.pop(a):
                w()
            waits[a] = []
            for t in turns:
                cut = lambda r: half(r, t, turn)
                if t == "C":
                    mine, come, to = cut(out.at[y, :, c]), cut(out.at[1 - y, :, c]), me.at_y
                else:
                    mine, come, to = cut(out.at[:, x, c]), cut(out.at[:, 1 - x, c]), me.at_x
                waits[a].append(push(a, 8 + (t == "D"), mine, mine, to, come))
        elif s == 5:
            for w in waits.pop(a):
                w()
            mine = out.at[:, :, c]
            ends.append(push(a, 10, mine, mine, me.at_c, out.at[:, :, 1 - c]))

    for a, s in order:
        stage(a, s)
    for e in ends:
        e()


def gather(ops, kinds, order, cid):
    shapes = []
    for o, (kind, _) in zip(ops, kinds):
        s = {"full": (2, 2, 2, 4) + o.shape, "zg": (4,) + o.shape, "za": o.shape, "cols": (2, 2, 2) + o.shape, "plane": (2, 2, 2) + o.shape}[kind]
        shapes.append(jax.ShapeDtypeStruct(s, o.dtype))
    n = len(ops)
    return pl.pallas_call(
        partial(gather_kernel, kinds, order),
        out_shape=shapes,
        in_specs=[pl.BlockSpec(memory_space=pl.ANY)] * n,
        out_specs=[pl.BlockSpec(memory_space=pl.ANY)] * n,
        scratch_shapes=[
            pltpu.SemaphoreType.DMA((n, 11)),
            pltpu.SemaphoreType.DMA((n, 11)),
            pltpu.SemaphoreType.DMA((n,)),
        ],
        compiler_params=pltpu.CompilerParams(collective_id=cid, has_side_effects=True),
    )(*ops)


ROWS = 80

def middle_kernel(final_in, block_in, tokens_ref, tp_in, downs_in, outs_ref, ivec_ref, tvec_ref, pbias_ref, tbias_ref,
                  label_ref, temp_ref,
                  dy_ref, branch_ref, rows_ref, sums_ref, dcap_ref, loss_ref, dz_ref,
                  tn_ref, dn_ref, send_a, recv_a, send_l, recv_l, send_t, recv_t,
                  final_ref, block_ref, tp_ref, downs_ref, send_sem, recv_sem, fetch):
    me = Place()
    cut = 2 * final_in.shape[1]
    pairs = {
        "small": (tp_in.at[:, cut:], tp_ref.at[:, cut:]), "final": (final_in, final_ref),
        "up": (tp_in.at[:, 0:cut], tp_ref.at[:, 0:cut]), "down": (downs_in, downs_ref), "block": (block_in, block_ref),
    }
    loads = {name: pltpu.make_async_copy(*pair, fetch.at[n]) for n, (name, pair) in enumerate(pairs.items())}
    for load in loads.values():
        load.start()
    z, i = me.z, me.i
    n_dp = recv_l.shape[0]
    plane = [((i + k) % n_dp, z) for k in range(1, n_dp)]
    greet([me.at_z(1), me.at_z(2), me.at_z(3)] + plane)
    width = final_in.shape[1]
    part = width // 4
    started = []

    def exchange(n, values, rows=4):
        if not isinstance(values, list):
            values = [values] * 4
        for q in range(4):
            send_a[n, q, 0:rows] = values[q]
        recv_a[n, z] = send_a[n, z]
        copies = []
        for k in (3, 2, 1):
            to, fro = (z + k) % 4, (z + 4 - k) % 4
            make = lambda dst: pltpu.make_async_remote_copy(
                send_a.at[n, to], dst, send_sem.at[n, k], recv_sem.at[n, k], device_id=me.at_z(k), device_id_type=MESH)
            copy = make(recv_a.at[n, z])
            copy.start()
            started.append(copy)
            copies.append(make(recv_a.at[n, fro]))

        def done():
            for a in copies:
                a.wait_recv()
            return [recv_a[n, q, 0:rows] for q in range(4)]

        return done

    total = lambda blocks: (blocks[0] + blocks[1]) + (blocks[2] + blocks[3])
    by_head = lambda blocks, n=3: jnp.concatenate([blocks[q][h : h + 1] for h in range(n) for q in range(4)], 0)
    pad1 = jnp.zeros((1, width), F32)
    ivec, tvec = ivec_ref[...], tvec_ref[...]
    iv = lambda k: ivec[k:k + 1]
    tv = lambda k: tvec[k:k + 1]
    names = ["tq", "tk", "tv", "thead", "pq", "pk", "pv"]
    col = {n: 2 * width + 256 * k for k, n in enumerate(names)}
    small = lambda n: tp_ref[:, col[n]:col[n] + 256]
    p_up = lambda: tp_ref[:, 0:width]
    t_up = lambda: tp_ref[:, width:2 * width]
    t_down = lambda: downs_ref[:, 0:width]
    p_down = lambda: downs_ref[:, width:2 * width]
    t_out_w = lambda: outs_ref[0:part, 0:width]
    p_out_w = lambda: outs_ref[0:part, width:2 * width]
    lane = lax.broadcasted_iota(jnp.int32, (1, 256), 1)
    own = [((lane >= 64 * h) & (lane < 64 * h + 64)).astype(F32) for h in range(3)]

    def spread(a):
        return jnp.concatenate([a * own[h] for h in range(3)], 0)

    def fold(a):
        n = a.shape[0] // 3
        return sum(a[h * n:(h + 1) * n] * own[h] for h in range(3))

    loads["small"].wait()
    p_q = mm(iv(7).astype(BF), small("pq"))
    get_keys = exchange(0, mm_two(spread(p_q), small("pk"), 1) * 0.125, 3)
    t_x = tokens_ref[...].astype(F32)
    tn = layer_norm(t_x, tv(0), tv(1)).astype(BF)
    tn_ref[...] = tn.astype(F32)
    last_at = [3 * 64 + 16 * c + 15 for c in range(4)]
    t_last = jnp.concatenate([tn_ref[r:r + 1, :] for r in last_at], 0)
    x_last = jnp.concatenate([tokens_ref[3 * 64 + 16 * c:3 * 64 + 16 * c + 16, :].astype(F32)[15:16] for c in range(4)], 0)
    t_q = mm(t_last.astype(BF), small("tq")).astype(BF).astype(F32)
    t_keys = mm(spread(t_q).astype(BF), small("tk"), 1, 1) * 0.125
    scores = mm_two(t_keys, tn, 1)
    col_id = (lax.broadcasted_iota(jnp.int32, scores.shape, 1) // 16) % 4
    row_id = lax.broadcasted_iota(jnp.int32, scores.shape, 0) % 4
    mine = col_id == row_id
    top = jnp.max(jnp.where(mine, scores, -1e30), -1, keepdims=True)
    e = jnp.where(mine, jnp.exp(jnp.where(mine, scores - top, 0.0)), 0.0)
    t_probs = e / jnp.sum(e, -1, keepdims=True)
    t_used = mm_two(t_probs, tn)
    t_mixed = fold(mm(t_used.astype(BF), small("tv"))).astype(BF)
    get_t = exchange(1, mm(t_mixed[:, 0:part], t_out_w()), 4)
    loads["final"].wait()
    final = final_ref[...]
    p_keys = jnp.concatenate(get_keys(), 0)
    p_scores = mm_two(p_keys, final, 1)
    e = jnp.exp(p_scores - jnp.max(p_scores, -1, keepdims=True))
    p_probs = e / jnp.sum(e, -1, keepdims=True)
    used = mm_two(p_probs, final)
    get_p = exchange(2, [used[3 * q:3 * q + 3] for q in range(4)], 3)
    t_hidden = x_last + total(get_t())
    t_second = layer_norm(t_hidden, tv(2), tv(3)).astype(BF)
    loads["up"].wait()
    loads["down"].wait()
    t_value, t_slope = gelu_pair(mm(t_second, t_up()) + tbias_ref[...])
    t_active = t_value.astype(BF)
    get_t = exchange(3, mm(t_active, t_down()), 4)
    pooled = fold(mm_two(by_head(get_p()), small("pv")))
    get_p = exchange(4, mm_two(pooled[:, 0:part], p_out_w()), 4)
    t_out = t_hidden + total(get_t()) + tv(4)
    t_final = layer_norm(t_out, tv(5), tv(6)).astype(BF)
    t_piece = mm(t_final, small("thead"))
    get_t = exchange(5, jnp.concatenate([t_piece[:, 0:part], jnp.zeros((4, width - part), F32)], 1), 4)
    h_start = total(get_p())
    h_normed = layer_norm(h_start, iv(8), iv(9)).astype(BF)
    h_value, h_slope = gelu_pair(mm(h_normed, p_up()) + pbias_ref[...])
    h_active = h_value.astype(BF)
    get_p = exchange(6, mm(h_active, p_down()), 4)
    text_embed = jnp.concatenate([blk[:, 0:part] for blk in get_t()], 1)
    image_embed = h_start + (total(get_p()) + iv(10))
    send_l[...] = jnp.concatenate([image_embed, text_embed], 0)
    recv_l[i] = send_l[...]
    arrive = []
    for k in range(1, n_dp):
        copy = pltpu.make_async_remote_copy(send_l, recv_l.at[i], send_sem.at[15, k], recv_sem.at[15, k],
                                            device_id=plane[k - 1], device_id_type=MESH)
        copy.start()
        started.append(copy)
        arrive.append(pltpu.make_async_remote_copy(send_l, recv_l.at[(i + n_dp - k) % n_dp], send_sem.at[15, k], recv_sem.at[15, k],
                                                   device_id=plane[k - 1], device_id_type=MESH))
    for a in arrive:
        a.wait_recv()
    every = jnp.concatenate([recv_l[k] for k in range(n_dp)], 0)
    scale = lax.rsqrt(jnp.sum(every * every, -1, keepdims=True) + EPS)
    unit = every * scale
    cosine = mm_exact(unit, unit, 1, 1)
    temper = jnp.exp(jnp.full((1, 1), temp_ref[0], F32))
    logits = cosine * temper + temp_ref[1]
    label = label_ref[...]
    valid = label != 0.0
    signed = label * logits
    n_all = n_dp * 4
    nll = jnp.maximum(-signed, 0.0) + jnp.log(1.0 + jnp.exp(-jnp.abs(signed)))
    add_all = lambda a: jnp.sum(jnp.sum(a, -1, keepdims=True), 0, keepdims=True)
    loss = add_all(jnp.where(valid, nll, 0.0)) / n_all
    g = jnp.where(valid, -label / (1.0 + jnp.exp(signed)), 0.0) / n_all
    gt0 = temper * add_all(g * cosine)
    gt1 = add_all(g)
    at = lax.broadcasted_iota(jnp.int32, (8, 128), 1)
    loss_ref[...] = jnp.where(at == 0, loss, jnp.where(at == 1, gt0, gt1))
    dz = temper * mm_exact(g + jnp.transpose(g), unit)
    dz_ref[...] = (dz - unit * jnp.sum(unit * dz, -1, keepdims=True)) * scale
    d_both = dz_ref[pl.ds(pl.multiple_of(8 * i, 8), 8), :]
    d_image, d_text = d_both[0:4], d_both[4:8]

    dh_upper = mm_two(d_image, p_down(), 1) * h_slope
    get_p = exchange(7, mm_two(dh_upper, p_up(), 1), 4)
    d_text_my = sum(jnp.where(z == q, d_text[:, part * q:part * q + part], 0.0) for q in range(4))
    get_t = exchange(8, mm_two(d_text_my, small("thead")[:, 0:part], 1), 4)
    d_start, dv8, dv9 = norm_back_rows(h_start, iv(8), total(get_p()))
    d_start = d_image + d_start
    dv10 = jnp.sum(d_image, 0, keepdims=True)
    d_pooled = mm_two(d_start, p_out_w(), 1)
    d_pooled = jnp.concatenate([d_pooled, jnp.zeros((4, 256 - part), F32)], 1)
    p_values_my = mm_two(spread(d_pooled), small("pv"), 1)
    get_p = exchange(9, [jnp.concatenate([p_values_my[4 * h + q:4 * h + q + 1] for h in range(3)], 0) for q in range(4)], 3)
    dt_out, tv5, tv6 = norm_back_rows(t_out, tv(5), total(get_t()))
    tv4 = jnp.sum(dt_out, 0, keepdims=True)
    dt_branch = dt_out.astype(BF)
    dt_upper = (mm(dt_branch, t_down(), 1, 1) * t_slope).astype(BF)
    get_t = exchange(10, mm(dt_upper, t_up(), 1, 1), 4)
    p_values = jnp.concatenate(get_p(), 0)
    d_probs = mm_two(p_values, final, 1)
    d_scores = p_probs * (d_probs - jnp.sum(p_probs * d_probs, -1, keepdims=True))
    p_used = mm_two(d_scores, final) * 0.125
    get_p = exchange(11, [p_used[3 * q:3 * q + 3] for q in range(4)], 3)
    dt_hidden, tv2, tv3 = norm_back_rows(t_hidden, tv(2), total(get_t()))
    dt_hidden = dt_out + dt_hidden
    dt_attend = dt_hidden.astype(BF)
    dt_mixed = mm(dt_attend, t_out_w(), 1, 1).astype(BF).astype(F32)
    dt_mixed = jnp.concatenate([dt_mixed, jnp.zeros((4, 256 - part), F32)], 1)
    t_values = mm(spread(dt_mixed).astype(BF), small("tv"), 1, 1)
    dt_probs = mm_two(t_values, tn, 1)
    dt_scores = t_probs * (dt_probs - jnp.sum(t_probs * dt_probs, -1, keepdims=True))
    tk_used = mm_two(dt_scores, tn) * 0.125
    dt_q = fold(mm(tk_used.astype(BF), small("tk"))).astype(BF)
    dn = mm(dt_scores.astype(BF), t_keys.astype(BF), 0, 0) + mm(t_probs.astype(BF), t_values.astype(BF), 0, 0)
    row_at = lax.broadcasted_iota(jnp.int32, dn.shape, 0)
    dq_back = mm(dt_q, small("tq"), 1, 1)
    for c in range(4):
        dn = dn + jnp.where(row_at == last_at[c], dq_back[c:c + 1], 0.0)
    dn_ref[...] = dn.astype(BF)
    arrive = []
    for k in (1, 2, 3):
        to, fro = (z + k) % 4, (z + 4 - k) % 4
        rows_to = dn_ref.at[pl.ds(pl.multiple_of(64 * to, 64), 64), :]
        copy = pltpu.make_async_remote_copy(rows_to, recv_t.at[z], send_sem.at[14, k], recv_sem.at[14, k],
                                            device_id=me.at_z(k), device_id_type=MESH)
        copy.start()
        started.append(copy)
        arrive.append(pltpu.make_async_remote_copy(rows_to, recv_t.at[fro], send_sem.at[14, k], recv_sem.at[14, k],
                                                   device_id=me.at_z(k), device_id_type=MESH))
    s_high, s_low = split_two(d_scores)
    q_high, q_low = split_two(p_probs)
    k_high, k_low = split_two(p_keys)
    v_high, v_low = split_two(p_values)
    left = jnp.concatenate([s_high.astype(F32), q_high.astype(F32)], 0)
    right = jnp.concatenate([k_high.astype(F32), v_high.astype(F32)], 0).astype(BF)
    send_t[...] = jnp.transpose(jnp.concatenate([left, jnp.zeros((104, left.shape[1]), F32)], 0))
    right = jnp.concatenate([right, jnp.zeros((104, width), BF)], 0)
    sums_ref[...] = jnp.zeros_like(sums_ref)
    tile = 128

    def step(n, carry):
        at_rows = pl.ds(pl.multiple_of(n * tile, tile), tile)
        d_final = mm(send_t[at_rows, :].astype(BF), right)
        d_y, gain, shift = norm_back_rows(block_ref[at_rows, :], iv(5), d_final)
        dy_ref[at_rows, :] = d_y
        branch_ref[at_rows, :] = d_y.astype(BF)
        sums_ref[5:6] += gain
        sums_ref[6:7] += shift
        sums_ref[4:5] += jnp.sum(d_y, 0, keepdims=True)
        return carry

    loads["block"].wait()
    lax.fori_loop(0, final_ref.shape[0] // tile, step, 0)
    w_got = by_head(get_p())
    dq_rows = fold(mm_two(w_got, small("pk")))
    dq_my = jnp.sum(dq_rows, 0, keepdims=True)
    recv_t[z] = dn_ref[pl.ds(pl.multiple_of(64 * z, 64), 64), :]
    for a in arrive:
        a.wait_recv()
    dt_normed = sum(recv_t[q].astype(F32) for q in range(4))
    x_mine = tokens_ref[pl.ds(pl.multiple_of(64 * z, 64), 64), :].astype(F32)
    d_cap, tv0, tv1 = norm_back_rows(x_mine, tv(0), dt_normed)
    row_c = lax.broadcasted_iota(jnp.int32, d_cap.shape, 0)
    for c in range(4):
        d_cap = d_cap + jnp.where((row_c == 16 * c + 15) & (z == 3), dt_hidden[c:c + 1], 0.0)
    dcap_ref[...] = d_cap
    first = (z == 0).astype(F32)
    sums_ref[8:9] = dv8 * first
    sums_ref[9:10] = dv9 * first
    sums_ref[10:11] = dv10 * first
    sums_ref[11:12] = tv0
    sums_ref[12:13] = tv1
    sums_ref[13:14] = tv2 * first
    sums_ref[14:15] = tv3 * first
    sums_ref[15:16] = tv4 * first
    sums_ref[16:17] = tv5 * first
    sums_ref[17:18] = tv6 * first
    own_row = lambda a: sum(jnp.where(z == q, a[q:q + 1].astype(F32), 0.0) for q in range(4))
    pick = lambda a: a[:, 0:part].astype(F32)
    wide = jnp.concatenate
    pieces = [
        dh_upper, dt_upper.astype(F32), h_active.astype(F32), t_active.astype(F32),
        wide([pick(d_pooled), pick(pooled), pick(dt_q), pick(t_q)], 1),
        wide([pick(dt_mixed), pick(t_mixed), jnp.broadcast_to(pick(dq_my), (4, part)), jnp.broadcast_to(pick(p_q), (4, part))], 1),
        own_row(h_normed), own_row(d_start), own_row(t_last), own_row(t_second),
        own_row(dt_attend), own_row(dt_branch), own_row(t_final), pad1,
        used, t_used, tk_used, p_used,
    ]
    rows_ref[...] = jnp.concatenate(pieces, 0).astype(BF)
    for copy in started:
        copy.wait_send()

def middle(final, block_out, tokens, tp, downs, outs, ivec, tvec, pbias, tbias, label, temp, cid, n_dp):
    length, width = final.shape
    v, hbm = pl.BlockSpec(memory_space=pltpu.VMEM), pl.BlockSpec(memory_space=pl.ANY)
    f = lambda *s: jax.ShapeDtypeStruct(s, F32)
    return pl.pallas_call(
        middle_kernel,
        in_specs=[hbm, hbm, v, hbm, hbm] + [v] * 6 + [pl.BlockSpec(memory_space=pltpu.SMEM)],
        out_specs=[v] * 7,
        out_shape=[f(length, width), jax.ShapeDtypeStruct((length, width), BF), jax.ShapeDtypeStruct((ROWS, width), BF), f(24, width), f(64, width), f(8, 128), f(8 * n_dp, width)],
        scratch_shapes=[
            pltpu.VMEM((256, width), F32), pltpu.VMEM((256, width), BF),
            pltpu.VMEM((12, 4, 4, width), F32), pltpu.VMEM((12, 4, 4, width), F32),
            pltpu.VMEM((8, width), F32), pltpu.VMEM((n_dp, 8, width), F32),
            pltpu.VMEM((length, 128), F32), pltpu.VMEM((4, 64, width), BF),
            pltpu.VMEM((length, width), BF), pltpu.VMEM((length, width), F32), pltpu.VMEM(tp.shape, BF), pltpu.VMEM(downs.shape, BF),
            pltpu.SemaphoreType.DMA((16, 8)), pltpu.SemaphoreType.DMA((16, 8)), pltpu.SemaphoreType.DMA((5,)),
        ],
        compiler_params=pltpu.CompilerParams(collective_id=cid, has_side_effects=True, vmem_limit_bytes=50 << 20),
    )(final, block_out, tokens, tp, downs, outs, ivec, tvec, pbias, tbias, label, temp)


def plane_moves(me, out, s):
    y, x, c = me.y, me.x, me.c
    n = out.shape[-1] // 2
    left, right = (lambda r: r.at[..., 0:n]), (lambda r: r.at[..., n : 2 * n])
    if s == 3:
        own = out.at[y, x, c]
        yield 6, left(own), left(own), me.at_x, None, left(out.at[y, 1 - x, c]), None
        yield 7, right(own), right(own), me.at_y, None, right(out.at[1 - y, x, c]), None
    elif s == 4:
        own = out.at[y, :, c]
        yield 8, left(own), left(own), me.at_y, None, left(out.at[1 - y, :, c]), None
        own = out.at[:, x, c]
        yield 9, right(own), right(own), me.at_x, None, right(out.at[:, 1 - x, c]), None
    else:
        mine = out.at[:, :, c]
        yield 10, mine, mine, me.at_c, None, out.at[:, :, 1 - c], None


def turn_moves(me, src, home, split):
    z = me.z
    for k in (3, 2, 1):
        to, fro = (z + k) % 4, (z + 4 - k) % 4
        yield k - 1, src.at[to] if split else src, home.at[z], me.at_z(k), None, home.at[fro], None


def run_moves(moves, act, send, recv):
    for slot, src, dst, dev, go, come, arrives in moves:
        make = lambda a, b: pltpu.make_async_remote_copy(
            a, b, send.at[slot], recv.at[slot], device_id=dev, device_id_type=MESH
        )
        if act == "arrived":
            copy, when = make(src, come).wait_recv, arrives
        else:
            copy, when = getattr(make(src, dst), "start" if act == "start" else "wait_send"), go
        if when is None:
            copy()
        else:
            pl.when(when)(lambda: copy())


class Spread:
    stages = 6

    def __init__(self, me, src, out, send, recv, local):
        self.me, self.src, self.out, self.send, self.recv, self.local = me, src, out, send, recv, local

    def moves(self, s):
        me, out = self.me, self.out
        y, x, c, z = me.y, me.x, me.c, me.z
        if s < 3:
            home = out.at[y, x, c]
            for up in (True, False):
                step = -s if up else s
                slab, come = z + step, z + step + (-1 if up else 1)
                go = ((slab >= 0) & (z < 3)) if up else ((slab < 4) & (z > 0))
                arrives = (come >= 0) & (come < 4)
                slab, come = jnp.clip(slab, 0, 3), jnp.clip(come, 0, 3)
                src = self.src if s == 0 else home.at[slab]
                yield s + (0 if up else 3), src, home.at[slab], me.at_z(1 if up else 3), go, home.at[come], arrives
        else:
            yield from plane_moves(me, out, s)

    def each(self, s, act):
        run_moves(self.moves(s), act, self.send, self.recv)

    def keep(self):
        me = self.me
        return pltpu.make_async_copy(self.src, self.out.at[me.y, me.x, me.c, me.z], self.local)

    def begin(self, s):
        if s == 0:
            self.keep().start()
        else:
            self.each(s - 1, "arrived")
        if s == 3:
            self.keep().wait()
        self.each(s, "start")

    def finish(self):
        self.each(5, "arrived")
        for s in range(6):
            self.each(s, "sent")


class Reduce:
    def __init__(self, me, g, own, acc, from_c, from_1, from_2, from_z, send, recv, local):
        self.me, self.g, self.own, self.acc = me, g, own, acc
        self.from_c, self.from_1, self.from_2, self.from_z = from_c, from_1, from_2, from_z
        self.send, self.recv, self.local = send, recv, local
        self.size = acc.shape[-1]
        self.left, self.right = slice(0, self.size // 2), slice(self.size // 2, self.size)

    def moves(self, n, stage):
        me, acc = self.me, self.acc.at[n]
        y, x, z = me.y, me.x, me.z
        if stage == "core":
            src = self.g.at[:, :, 1 - me.c, :, :, n * self.size : (n + 1) * self.size]
            yield 0, src, self.from_c.at[n], me.at_c, None, self.from_c.at[n], None
        elif stage == "one":
            a, b = self.from_1.at[n, 0], self.from_1.at[n, 1]
            yield 1, acc.at[1 - y, :, :, :, self.left], a, me.at_y, None, a, None
            yield 2, acc.at[:, 1 - x, :, :, self.right], b, me.at_x, None, b, None
        elif stage == "two":
            a, b = self.from_2.at[n, 0], self.from_2.at[n, 1]
            yield 3, acc.at[y, 1 - x, :, :, self.left], a, me.at_x, None, a, None
            yield 4, acc.at[1 - y, x, :, :, self.right], b, me.at_y, None, b, None
        else:
            for k in (3, 2, 1):
                got = self.from_z.at[n, k - 1]
                yield 4 + k, acc.at[y, x, (z + k) % 4], got, me.at_z(k), None, got, None

    def act(self, n, stage, what):
        run_moves(self.moves(n, stage), what, self.send.at[n], self.recv.at[n])

    def keep(self, n):
        src = self.g.at[:, :, self.me.c, :, :, n * self.size : (n + 1) * self.size]
        return pltpu.make_async_copy(src, self.acc.at[n], self.local.at[n])

    def start(self, n, stage):
        if stage == "core":
            self.keep(n).start()
        self.act(n, stage, "start")

    def done(self, n, stage):
        me, acc = self.me, self.acc
        y, x = me.y, me.x
        f32 = lambda v: v.astype(F32)

        def each(count, body):
            lax.fori_loop(0, count, lambda q, carry: body(q) or carry, 0)

        if stage == "core":
            self.keep(n).wait()
        self.act(n, stage, "arrived")
        if stage == "core":

            def add(q):
                for a in range(2):
                    for b in range(2):
                        acc[n, a, b, q] = (f32(acc[n, a, b, q]) + f32(self.from_c[n, a, b, q])).astype(BF)

            each(4, add)
        elif stage == "one":

            def add(q):
                for b in range(2):
                    at = (n, y, b, q, slice(None), self.left)
                    acc[at] = (f32(acc[at]) + f32(self.from_1[n, 0, b, q])).astype(BF)
                    at = (n, b, x, q, slice(None), self.right)
                    acc[at] = (f32(acc[at]) + f32(self.from_1[n, 1, b, q])).astype(BF)

            each(4, add)
        elif stage == "two":

            def add(q):
                for half, cut in enumerate((self.left, self.right)):
                    at = (n, y, x, q, slice(None), cut)
                    acc[at] = (f32(acc[at]) + f32(self.from_2[n, half, q])).astype(BF)

            each(4, add)
        else:
            total = f32(acc[n, y, x, me.z])
            for k in range(3):
                total += f32(self.from_z[n, k])
            self.own[:, n * self.size : (n + 1) * self.size] = total

    def finish(self, n):
        for stage in ("core", "one", "two", "z"):
            self.act(n, stage, "sent")


REDUCE_STEPS = {
    0: [("start", 0, "core"), ("start", 1, "core")],
    1: [("done", 0, "core"), ("start", 0, "one")],
    2: [("done", 1, "core")],
    3: [("start", 1, "one")],
    5: [("done", 0, "one"), ("start", 0, "two")],
    7: [("done", 1, "one"), ("done", 0, "two"), ("start", 0, "z"), ("start", 1, "two")],
    9: [("done", 1, "two"), ("start", 1, "z")],
    12: [("done", 0, "z"), ("done", 1, "z")],
}
CHUNKS = 2


def attend_bwd_kernel_hosting(q_ref, k_ref, v_ref, do_ref, lse_ref, d_ref, g_ref, rows_ref, dq_ref, dk_ref, dv_ref, own_ref, all_ref,
                              acc, from_c, from_1, from_2, from_z, send, recv, local, rows_send, rows_recv, rows_local):
    h_at = pl.program_id(0)
    me = Place()
    spread = Spread(me, rows_ref, all_ref, rows_send, rows_recv, rows_local)
    reduce = Reduce(me, g_ref, own_ref, acc, from_c, from_1, from_2, from_z, send, recv, local)

    def tick(step):
        if step not in REDUCE_STEPS:
            return

        def go():
            if step == 0:
                greet([me.at_z(1), me.at_z(2), me.at_z(3), me.at_x, me.at_y, me.at_c])
            for what, n, stage in REDUCE_STEPS[step]:
                getattr(reduce, what)(n, stage)

        pl.when(h_at == step // 2)(go)

    for step in range(0, 12, 2):
        tick(step)
    for s in range(6):
        pl.when(h_at == s)(partial(spread.begin, s))
    q = q_ref[...] * 0.125
    k, v, do = k_ref[...], v_ref[...], do_ref[...]
    lane = lax.broadcasted_iota(jnp.int32, k.shape, 1)
    low = lane < 64
    for h in range(2):
        if h == 1:
            for step in range(1, 12, 2):
                tick(step)
        keep = low if h == 0 else ~low
        s = mm(jnp.where(keep, k, jnp.zeros_like(k)), q, 1, 1)
        p = jnp.exp(s - lse_ref[0, h : h + 1, :])
        dp = mm(jnp.where(keep, v, jnp.zeros_like(v)), do, 1, 1)
        ds = (p * (dp - d_ref[0, h : h + 1, :])).astype(BF)
        d_v = mm(p.astype(BF), do).astype(BF)
        d_k = mm(ds, q).astype(BF)
        d_q = (mm(ds, k, 0, 0) * 0.125).astype(BF)
        for ref, value in ((dq_ref, d_q), (dk_ref, d_k), (dv_ref, d_v)):
            ref[...] = value if h == 0 else jnp.where(low, ref[...], value)

    def last():
        for what, n, stage in REDUCE_STEPS[12]:
            getattr(reduce, what)(n, stage)
        for n in range(CHUNKS):
            reduce.finish(n)
        spread.finish()

    pl.when(h_at == pl.num_programs(0) - 1)(last)


def attend_bwd_and_reduce(proj, d_out, lse, inner, g, own_rows, cid):
    length, width = proj.shape[0], proj.shape[1] // 3
    pairs = width // 128
    rows, n = g.shape[0] // 32, g.shape[1]
    size = n // CHUNKS
    block = lambda part: pl.BlockSpec((length, 128), lambda h: (0, part * pairs + h))
    row = pl.BlockSpec((1, 2, length), lambda h: (h, 0, 0))
    hbm = pl.BlockSpec(memory_space=pl.ANY)
    result = jax.ShapeDtypeStruct((length, width), BF)
    v = lambda *s: pltpu.VMEM(s, BF)
    return pl.pallas_call(
        attend_bwd_kernel_hosting,
        grid=(pairs,),
        in_specs=[block(0), block(1), block(2), block(0), row, row, hbm, hbm],
        out_specs=[block(0)] * 3 + [pl.BlockSpec((rows, n), lambda h: (0, 0)), hbm],
        out_shape=[result] * 3
        + [jax.ShapeDtypeStruct((rows, n), F32), jax.ShapeDtypeStruct((2, 2, 2, 4) + own_rows.shape, BF)],
        scratch_shapes=[
            v(CHUNKS, 2, 2, 4, rows, size), v(CHUNKS, 2, 2, 4, rows, size), v(CHUNKS, 2, 2, 4, rows, size // 2),
            v(CHUNKS, 2, 4, rows, size // 2), v(CHUNKS, 3, rows, size),
            pltpu.SemaphoreType.DMA((CHUNKS, 8)), pltpu.SemaphoreType.DMA((CHUNKS, 8)), pltpu.SemaphoreType.DMA((CHUNKS,)),
            pltpu.SemaphoreType.DMA((11,)), pltpu.SemaphoreType.DMA((11,)), pltpu.SemaphoreType.DMA,
        ],
        compiler_params=pltpu.CompilerParams(collective_id=cid, has_side_effects=True, vmem_limit_bytes=60 << 20),
    )(proj, proj, proj, d_out, lse, inner, g.reshape(2, 2, 2, 4, rows, n), own_rows)


def attend_fwd_kernel_hosting(q_ref, k_ref, v_ref, split_ref, downs_ref, tokens_ref,
                              o_ref, lse_ref, tp_ref, down_ref, token_ref, send, recv, local):
    h_at = pl.program_id(0)
    me = Place()
    home = tp_ref.at[me.y, me.x, me.c]
    down_home = down_ref.at[me.y, me.x, me.c]
    keeps = [
        pltpu.make_async_copy(split_ref.at[me.z], home.at[me.z], local.at[0]),
        pltpu.make_async_copy(downs_ref, down_home, local.at[1]),
        pltpu.make_async_copy(tokens_ref, token_ref.at[me.z], local.at[2]),
    ]
    groups = {
        "split": (lambda: turn_moves(me, split_ref, home, True), 0),
        "tokens": (lambda: turn_moves(me, tokens_ref, token_ref, False), 2),
        "split_xy": (lambda: plane_moves(me, tp_ref, 3), 0),
        "down_one": (lambda: plane_moves(me, down_ref, 3), 1),
        "down_two": (lambda: plane_moves(me, down_ref, 4), 1),
        "down_core": (lambda: plane_moves(me, down_ref, 5), 1),
    }

    def act(name, what):
        moves, a = groups[name]
        run_moves(moves(), what, send.at[a], recv.at[a])

    def first():
        greet([me.at_z(1), me.at_z(2), me.at_z(3), me.at_x, me.at_y, me.at_c])
        for keep in keeps:
            keep.start()
        act("split", "start")
        keeps[1].wait()
        act("down_one", "start")

    def second_step():
        act("down_one", "arrived")
        act("down_two", "start")

    def middle_step():
        act("split", "arrived")
        keeps[0].wait()
        act("split_xy", "start")
        act("tokens", "start")

    def fifth_step():
        act("down_two", "arrived")
        act("down_core", "start")

    def last():
        for name in ("split_xy", "down_core", "tokens"):
            act(name, "arrived")
        keeps[2].wait()
        for name in groups:
            act(name, "sent")

    pl.when(h_at == 0)(first)
    pl.when(h_at == 2)(second_step)
    pl.when(h_at == 3)(middle_step)
    pl.when(h_at == 5)(fifth_step)
    attend_fwd_kernel(q_ref, k_ref, v_ref, o_ref, lse_ref)
    pl.when(h_at == pl.num_programs(0) - 1)(last)


def attend_fwd_and_gather(proj, split, downs, tokens, cid):
    length, width = proj.shape[0], proj.shape[1] // 3
    pairs = width // 128
    block = lambda part: pl.BlockSpec((length, 128), lambda h: (0, part * pairs + h))
    hbm = pl.BlockSpec(memory_space=pl.ANY)
    s = jax.ShapeDtypeStruct
    return pl.pallas_call(
        attend_fwd_kernel_hosting,
        grid=(pairs,),
        in_specs=[block(0), block(1), block(2), hbm, hbm, hbm],
        out_specs=[block(0), pl.BlockSpec((1, 2, length), lambda h: (h, 0, 0)), hbm, hbm, hbm],
        out_shape=[
            s((length, width), BF),
            s((pairs, 2, length), F32),
            s((2, 2, 2) + split.shape, BF),
            s((2, 2, 2) + downs.shape, BF),
            s((4,) + tokens.shape, BF),
        ],
        scratch_shapes=[pltpu.SemaphoreType.DMA((3, 11)), pltpu.SemaphoreType.DMA((3, 11)), pltpu.SemaphoreType.DMA((3,))],
        compiler_params=pltpu.CompilerParams(collective_id=cid, has_side_effects=True, vmem_limit_bytes=48 << 20),
    )(proj, proj, proj, split, downs, tokens)


def mlp_fwd_kernel(x_ref, mixed_ref, wo_ref, wu_ref, wd_ref, bias_ref, vec_ref, tp_in,
                   hidden_ref, second_ref, active_ref, slope_ref, block_ref, final_ref, tp_ref, total, send, recv):
    k = pl.program_id(0)
    me = Place()

    def act(s, what):
        run_moves(plane_moves(me, tp_ref, s), what, send, recv)

    def first():
        greet([me.at_x, me.at_y, me.at_c])
        act(4, "start")

    def then():
        act(4, "arrived")
        act(5, "start")

    pl.when(k == 0)(first)
    pl.when(k == pl.num_programs(0) - 1)(then)
    vec = vec_ref[...]

    @pl.when(k == 0)
    def _():
        hidden = x_ref[...].astype(F32) + mm(mixed_ref[...], wo_ref[...])
        hidden_ref[...] = hidden
        second_ref[...] = layer_norm(hidden, vec[2:3], vec[3:4]).astype(BF)
        total[...] = hidden + vec[4:5]

    value, slope = gelu_pair(mm(second_ref[...], wu_ref[...]) + bias_ref[0])
    active = value.astype(BF)
    active_ref[...] = active
    slope_ref[...] = slope.astype(BF)
    total[...] += mm(active, wd_ref[...])

    @pl.when(k == pl.num_programs(0) - 1)
    def _():
        block_ref[...] = total[...]
        final_ref[...] = layer_norm(total[...], vec[5:6], vec[6:7]).astype(BF)
        act(5, "arrived")
        act(4, "sent")
        act(5, "sent")


def mlp_fwd(x, mixed, main, bias, vec, fold, tp, cid):
    rows, width = mixed.shape
    whole = pl.BlockSpec((rows, width), lambda k: (0, 0))
    tile = pl.BlockSpec((rows, width), lambda k: (0, k))
    at = lambda f: pl.BlockSpec((width, width), lambda k: (0, f(k)))
    s = lambda n, t: jax.ShapeDtypeStruct((rows, n * width), t)
    hbm = pl.BlockSpec(memory_space=pl.ANY)
    return pl.pallas_call(
        mlp_fwd_kernel,
        grid=(fold,),
        in_specs=[whole, whole, at(lambda k: 0), at(lambda k: 1 + k), at(lambda k: 1 + fold + k),
                  pl.BlockSpec((1, 1, width), lambda k: (k, 0, 0)), pl.BlockSpec(vec.shape, lambda k: (0, 0)), hbm],
        out_specs=[whole, whole, tile, tile, whole, whole, hbm],
        out_shape=[s(1, F32), s(1, BF), s(fold, BF), s(fold, BF), s(1, F32), s(1, BF),
                   jax.ShapeDtypeStruct(tp.shape, BF)],
        scratch_shapes=[pltpu.VMEM((rows, width), F32), pltpu.SemaphoreType.DMA((11,)), pltpu.SemaphoreType.DMA((11,))],
        input_output_aliases={7: 6},
        compiler_params=pltpu.CompilerParams(collective_id=cid, has_side_effects=True, vmem_limit_bytes=56 << 20),
    )(x, mixed, main, main, main, bias.reshape(fold, 1, width), vec, tp)


def mlp_bwd_kernel(dy_ref, branch_ref, active_ref, slope_ref, second_ref, hidden_ref, mixed_ref,
                   wo_ref, wu_ref, wd_ref, vec_ref,
                   g_ref, gs_ref, dhid_ref, dmix_ref, inner_ref, bias_ref, dvec_ref, total, dy_in, hid_in, mix_in, slots, fetch, leave):
    k = pl.program_id(0)
    fold = pl.num_programs(0)
    pairs = ((dy_ref, dy_in), (hidden_ref, hid_in), (mixed_ref, mix_in))
    loads = [pltpu.make_async_copy(src, dst, fetch.at[n]) for n, (src, dst) in enumerate(pairs)]

    @pl.when(k == 0)
    def _():
        for load in loads:
            load.start()

    width = mixed_ref.shape[1]

    def leaves(n):
        at = pl.ds(pl.multiple_of((n + 1) * width, width), width)
        return pltpu.make_async_copy(slots.at[n % 2], gs_ref.at[:, at], leave.at[n % 2])

    pl.when(k >= 2)(lambda: leaves(k - 2).wait())
    branch = branch_ref[...]
    columns = lambda n: pl.ds(pl.multiple_of(n * width, width), width)
    slots[k % 2] = mm(active_ref[...], branch, 0, 0).astype(BF)
    leaves(k).start()
    d_upper_f = mm(branch, wd_ref[...], 1, 1) * slope_ref[...].astype(F32)
    bias_ref[0] = jnp.sum(d_upper_f, 0, keepdims=True)
    d_upper = d_upper_f.astype(BF)
    g_ref[...] = mm(second_ref[...], d_upper, 0, 0).astype(BF)
    back = mm(d_upper, wu_ref[...], 1, 1)

    @pl.when(k == 0)
    def _():
        total[...] = back

    @pl.when(k > 0)
    def _():
        total[...] += back

    @pl.when(k == fold - 1)
    def _():
        vec = vec_ref[...]
        for load in loads:
            load.wait()
        d_hidden, gain, shift = norm_back_rows(hid_in[...], vec[2:3], total[...])
        dvec_ref[0:1] = gain
        dvec_ref[1:2] = shift
        d_hidden = dy_in[...] + d_hidden
        dhid_ref[...] = d_hidden
        d_attend = d_hidden.astype(BF)
        mixed = mix_in[...]
        leaves(fold - 2).wait()
        slots[fold % 2] = mm(mixed, d_attend, 0, 0).astype(BF)
        out = pltpu.make_async_copy(slots.at[fold % 2], gs_ref.at[:, 0:width], leave.at[2])
        out.start()
        d_mixed = mm(d_attend, wo_ref[...], 1, 1).astype(BF)
        dmix_ref[...] = d_mixed
        head = lax.broadcasted_iota(jnp.int32, (16, width), 0)
        lane = lax.broadcasted_iota(jnp.int32, (16, width), 1)
        own = (lane // (width // HEADS) == head).astype(BF)
        high, low = split_two(d_mixed.astype(F32) * mixed.astype(F32))
        sums = mm(own, high, 1, 1) + mm(own, low, 1, 1)
        for h in range(HEADS // 2):
            inner_ref[h] = sums[2 * h : 2 * h + 2]
        leaves(fold - 1).wait()
        out.wait()


def mlp_bwd(dy, branch, active, slope, second, hidden, mixed, main, vec, fold):
    rows, width = mixed.shape
    whole = pl.BlockSpec((rows, width), lambda k: (0, 0))
    tile = pl.BlockSpec((rows, width), lambda k: (0, k))
    at = lambda f: pl.BlockSpec((width, width), lambda k: (0, f(k)))
    f = lambda *s: jax.ShapeDtypeStruct(s, F32)
    hbm = pl.BlockSpec(memory_space=pl.ANY)
    return pl.pallas_call(
        mlp_bwd_kernel,
        grid=(fold,),
        in_specs=[hbm, whole, tile, tile, whole, hbm, hbm,
                  at(lambda k: 0), at(lambda k: 1 + k), at(lambda k: 1 + fold + k), pl.BlockSpec(vec.shape, lambda k: (0, 0))],
        out_specs=[at(lambda k: k), hbm, whole, whole,
                   pl.BlockSpec((HEADS // 2, 2, rows), lambda k: (0, 0, 0)),
                   pl.BlockSpec((1, 1, width), lambda k: (k, 0, 0)), pl.BlockSpec((8, width), lambda k: (0, 0))],
        out_shape=[jax.ShapeDtypeStruct((width, fold * width), BF), jax.ShapeDtypeStruct((width, (1 + fold) * width), BF), f(rows, width),
                   jax.ShapeDtypeStruct((rows, width), BF), f(HEADS // 2, 2, rows), f(fold, 1, width), f(8, width)],
        scratch_shapes=[pltpu.VMEM((rows, width), F32), pltpu.VMEM((rows, width), F32), pltpu.VMEM((rows, width), F32),
                        pltpu.VMEM((rows, width), BF), pltpu.VMEM((2, width, width), BF),
                        pltpu.SemaphoreType.DMA((3,)), pltpu.SemaphoreType.DMA((3,))],
        compiler_params=pltpu.CompilerParams(vmem_limit_bytes=60 << 20),
    )(dy, branch, active, slope, second, hidden, mixed, main, main, main, vec)


def finish_kernel(dq_ref, dk_ref, dv_ref, normed_ref, w_ref, x_ref, dhid_ref, sums_ref, vec_ref, own_ref, moved_ref,
                  g, dx, from_c, acc_c, from_1, from_2, from_z, q_in, k_in, v_in, n_in, w_in, x_in, h_in,
                  send, recv, local, fetch):
    me = Place()
    pairs = ((dq_ref, q_in), (normed_ref, n_in), (dk_ref, k_in), (dv_ref, v_in), (w_ref, w_in), (x_ref, x_in), (dhid_ref, h_in))
    loads = [pltpu.make_async_copy(src, dst, fetch.at[n]) for n, (src, dst) in enumerate(pairs)]
    for load in loads:
        load.start()
    dq_ref, dk_ref, dv_ref, normed_ref, w_ref, x_ref, dhid_ref = q_in, k_in, v_in, n_in, w_in, x_in, h_in
    y, x, c, z = me.y, me.x, me.c, me.z
    width = dq_ref.shape[1]
    part = g.shape[4]
    tile = dx.shape[1]
    half = g.shape[-1] // 2
    left, right = slice(0, half), slice(half, 2 * half)
    f32 = lambda v: v.astype(F32)
    started = []
    greet([me.at_z(1), me.at_z(2), me.at_z(3), me.at_x, me.at_y, me.at_c])

    def push(slot, src, dst, dev, arriving):
        copy = pltpu.make_async_remote_copy(src, dst, send.at[slot], recv.at[slot], device_id=dev, device_id_type=MESH)
        copy.start()
        started.append(copy)
        return pltpu.make_async_remote_copy(src, arriving, send.at[slot], recv.at[slot], device_id=dev, device_id_type=MESH)

    def put(value, first):
        for p in range(32):
            i, q = p // 4, p % 4
            g[i // 4, (i // 2) % 2, i % 2, q, :, first : first + value.shape[1]] = value[part * p : part * (p + 1)].astype(BF)

    gain, shift, moves = [], [], []

    def d_x_rows(k):
        to, fro = (z + k) % 4, (z + 4 - k) % 4
        at = pl.ds(pl.multiple_of(to * tile, tile), tile)
        back = None
        for n, ref in enumerate((dq_ref, dk_ref, dv_ref)):
            term = mm(ref[at, :], w_ref[:, n * width : (n + 1) * width], 1, 1)
            back = term if back is None else back + term
        d_x, a, b = norm_back_rows(x_ref[at, :].astype(F32), vec_ref[0:1], back)
        gain.append(a)
        shift.append(b)
        dx[to] = (dhid_ref[at, :] + d_x).astype(BF)
        if k:
            moves.append(push(k, dx.at[to], moved_ref.at[z], me.at_z(k), moved_ref.at[fro]))
        else:
            keep.start()

    keep = pltpu.make_async_copy(dx.at[z], moved_ref.at[z], local)

    def add(at, value):
        acc_c[at] = (f32(acc_c[at]) + f32(value)).astype(BF)

    def core(cut, slot):
        to = from_c.at[:, :, :, :, cut]
        return push(slot, g.at[:, :, 1 - c, :, :, cut], to, me.at_c, to)

    def core_done(arrive, cut):
        arrive.wait_recv()
        for a in range(2):
            for b in range(2):
                for q in range(4):
                    at = (a, b, q, slice(None), cut)
                    acc_c[at] = (f32(g[a, b, c, q, :, cut]) + f32(from_c[at])).astype(BF)

    def one_done(arrive, n, cut):
        arrive.wait_recv()
        for b in range(2):
            for q in range(4):
                add((b, x, q, slice(None), cut) if n else (y, b, q, slice(None), cut), from_1[n, b, q])

    def two_done(arrive, n, cut):
        arrive.wait_recv()
        for q in range(4):
            add((y, x, q, slice(None), cut), from_2[n, q])

    def along(cut, slot):
        arrives = []
        for k in (3, 2, 1):
            got = from_z.at[k - 1, :, cut]
            arrives.append(push(slot + k, acc_c.at[y, x, (z + k) % 4, :, cut], got, me.at_z(k), got))
        return arrives

    part_of = lambda n, ref: put(mm(normed_ref[...], ref[...], 0, 0), n * width)
    loads[0].wait()
    loads[1].wait()
    part_of(0, dq_ref)
    loads[2].wait()
    part_of(1, dk_ref)
    for load in loads[3:]:
        load.wait()
    core_left = core(left, 0)
    d_x_rows(2)
    part_of(2, dv_ref)
    core_done(core_left, left)
    one_left = push(4, acc_c.at[1 - y, :, :, :, left], from_1.at[0], me.at_y, from_1.at[0])
    d_x_rows(3)
    d_x_rows(1)
    d_x_rows(0)
    sums = jnp.concatenate([sum(gain), sum(shift), sums_ref[2:, :]], 0)
    sums = jnp.concatenate([sums, jnp.zeros((128 - sums.shape[0], width), F32)], 0)
    put(jnp.transpose(sums), 3 * width)
    put(jnp.zeros((width, 128), F32), 3 * width + 128)
    core_right = core(right, 8)
    one_done(one_left, 0, left)
    two_left = push(6, acc_c.at[y, 1 - x, :, :, left], from_2.at[0], me.at_x, from_2.at[0])
    core_done(core_right, right)
    one_right = push(5, acc_c.at[:, 1 - x, :, :, right], from_1.at[1], me.at_x, from_1.at[1])
    two_done(two_left, 0, left)
    z_left = along(left, 8)
    one_done(one_right, 1, right)
    two_right = push(7, acc_c.at[1 - y, x, :, :, right], from_2.at[1], me.at_y, from_2.at[1])
    two_done(two_right, 1, right)
    z_right = along(right, 11)
    for arrive in z_left + z_right:
        arrive.wait_recv()
    total = f32(acc_c[y, x, z]) + f32(from_z[0]) + f32(from_z[1]) + f32(from_z[2])
    own_ref[...] = total
    keep.wait()
    for arrive in moves:
        arrive.wait_recv()
    for copy in started:
        copy.wait_send()


def finish_image(dq, dk, dv, normed, w_in, x, d_hidden, sums, vec, cid):
    rows, width = dq.shape
    part, n = width // 32, 3 * width + 256
    v, hbm = pl.BlockSpec(memory_space=pltpu.VMEM), pl.BlockSpec(memory_space=pl.ANY)
    s = lambda *shape: pltpu.VMEM(shape, BF)
    return pl.pallas_call(
        finish_kernel,
        in_specs=[hbm] * 7 + [v] * 2,
        out_specs=[v, hbm],
        out_shape=[jax.ShapeDtypeStruct((part, n), F32), jax.ShapeDtypeStruct((4, rows // 4, width), BF)],
        scratch_shapes=[
            s(2, 2, 2, 4, part, n), s(4, rows // 4, width), s(2, 2, 4, part, n), s(2, 2, 4, part, n),
            s(2, 2, 4, part, n // 2), s(2, 4, part, n // 2), s(3, part, n),
            s(rows, width), s(rows, width), s(rows, width), s(rows, width), s(width, 3 * width), s(rows, width),
            pltpu.VMEM((rows, width), F32),
            pltpu.SemaphoreType.DMA((15,)), pltpu.SemaphoreType.DMA((15,)), pltpu.SemaphoreType.DMA, pltpu.SemaphoreType.DMA((7,)),
        ],
        compiler_params=pltpu.CompilerParams(collective_id=cid, has_side_effects=True, vmem_limit_bytes=56 << 20),
    )(dq, dk, dv, normed, w_in, x, d_hidden, sums, vec)


def outer_kernel(rows_ref, dimage_ref, dtext_ref,
                 pup_ref, tup_ref, pdown_ref, tdown_ref, pout_ref, tout_ref, thead_ref,
                 tq_ref, tk_ref, tv_ref, pv_ref, pk_ref, bias_ref):
    at_dp, z = lax.axis_index("dp"), lax.axis_index("seq")
    n_dp, n_z = 8, 4
    me = at_dp * n_z + z
    width = rows_ref.shape[2]
    part, quarter = width // 32, width // n_z
    wide_part = 4 * part
    n = n_dp * n_z
    each = quarter // part

    def iota(shape, d):
        return lax.broadcasted_iota(jnp.int32, shape, d)

    def selector(count, first):
        return (iota((count, width), 1) == iota((count, width), 0) + first).astype(BF)

    def group(r):
        return jnp.concatenate([rows_ref[r + c] for c in range(4)], 0)

    cols = jnp.concatenate(
        [mm(selector(part, part * me), rows_ref[r], 1, 1) for r in range(24, 80)], 1
    ).astype(BF)
    get = lambda r, count=1: cols[:, n * (r - 24) : n * (r - 24 + count)]
    a, b = iota((4 * n, n), 0), iota((4 * n, n), 1)
    same = ((a % n) // n_z == b // n_z) & (a // n == b % n_z)
    keep = lambda which: (same & (a % n_z == which)).astype(BF)
    units = selector(wide_part, wide_part * at_dp)
    heads = selector(part, quarter + part * (me % each))
    to_mine, to_head = keep(z), keep(me // each)
    chosen = lambda sel, r, perm: mm(mm(sel, group(r), 1, 1).astype(BF), perm).astype(BF)
    pdown_ref[...] = mm(chosen(units, 8, to_mine), dimage_ref[...])
    tdown_ref[...] = mm(chosen(units, 12, to_mine), rows_ref[29])
    pout_ref[...] = mm(chosen(heads, 16, to_head), rows_ref[25])
    tout_ref[...] = mm(chosen(heads, 20, to_head), rows_ref[28])
    thead_ref[...] = mm(get(30), dtext_ref[...])
    ones = jnp.ones((n, 128), BF)
    bias_ref[0] = mm(chosen(units, 0, to_mine), ones)
    bias_ref[1] = mm(chosen(units, 4, to_mine), ones)
    a, b = iota((n, 4 * n), 0), iota((n, 4 * n), 1)
    spread = ((b % n) // n_z == a // n_z) & (b // n == a % n_z)
    spread = spread.astype(BF)
    lane_z = iota((1, 4 * n), 1) % n_z
    masks = [(lane_z == q).astype(BF) for q in range(n_z)]

    def blocks(values):
        return jnp.concatenate([v * m for v, m in zip(values, masks)], 0)

    by_image = lambda r: mm(get(r), spread).astype(BF)
    g16, g20 = group(16), group(20)

    def put(ref, value, first):
        for q in range(n_z):
            ref[q] = value[q * part : (q + 1) * part, first : first + ref.shape[2]]

    put(pup_ref, mm(blocks([by_image(24)] * 4), group(0)), 0)
    put(tup_ref, mm(blocks([by_image(27)] * 4), group(4)), 0)
    put(tq_ref, mm(blocks([by_image(26)] * 4), g16), 2 * quarter)
    lane = iota((1, width), 1)
    count = HEADS // n_z
    hw = quarter // count

    def by_head(values_of, rhs, first):
        total = None
        for h in range(count):
            own = ((lane >= first + hw * h) & (lane < first + hw * h + hw)).astype(F32)
            one = mm(blocks(values_of(h)), rhs) * own
            total = one if total is None else total + one
        return total

    put(tk_ref, by_head(lambda h: [get(56 + 4 * h, 4)] * 4, g16, 3 * quarter), 3 * quarter)
    put(tv_ref, by_head(lambda h: [get(44 + 4 * h, 4)] * 4, g20, 0), 0)
    put(pv_ref, by_head(lambda h: [by_image(32 + count * q + h) for q in range(n_z)], g16, 0), 0)
    a, b = iota((HEADS * n, 128), 0), iota((HEADS * n, 128), 1)
    pk_ref[...] = mm(get(68, HEADS), (a // n == b).astype(BF))


def outer_grads(rows, d_image, d_text):
    width = rows.shape[2]
    part, quarter = width // 32, width // 4
    v = pl.BlockSpec(memory_space=pltpu.VMEM)
    f = lambda *s: jax.ShapeDtypeStruct(s, F32)
    return pl.pallas_call(
        outer_kernel,
        in_specs=[v] * 3,
        out_specs=[v] * 13,
        out_shape=[f(4, part, width), f(4, part, width), f(4 * part, width), f(4 * part, width), f(part, width), f(part, width),
                   f(part, width), f(4, part, quarter), f(4, part, quarter), f(4, part, quarter), f(4, part, quarter),
                   f(part, 128), f(2, 4 * part, 128)],
        compiler_params=pltpu.CompilerParams(vmem_limit_bytes=48 << 20),
    )(rows, d_image, d_text)


def fast_program(
    patches, captions, pairs,
    image_attend_in, image_attend_out, image_up_weight, image_up_bias, image_down_weight,
    image_vectors, probe_query_weight, probe_pair_weight, probe_out_weight, probe_up_weight,
    probe_up_bias, probe_down_weight, text_attend_in, text_attend_out, text_up_weight,
    text_up_bias, text_down_weight, text_vectors, text_head_weight, temp_bias,
):
    n_dp, n_z = lax.axis_size("dp"), lax.axis_size("seq")
    world = n_dp * n_z
    at_dp, at_z = lax.axis_index("dp"), lax.axis_index("seq")
    me = at_dp * n_z + at_z
    width = patches.shape[-1]
    head_width = width // HEADS
    hidden_width = image_up_weight.shape[1]
    part, quarter = width // world, width // n_z
    wide_part = hidden_width // world
    fold = hidden_width // width
    length = patches.shape[1] * n_z

    small = jnp.concatenate(
        [image_vectors.reshape(-1), text_vectors.reshape(-1), image_up_bias, probe_up_bias, text_up_bias]
    )
    sizes = [image_vectors.size, text_vectors.size, image_up_bias.size, probe_up_bias.size, text_up_bias.size]
    small = jnp.pad(small, (0, 2048 - small.shape[0])).reshape(16, 128)

    def by_units(w):
        return w.reshape(part, n_dp, n_z, wide_part).transpose(2, 0, 1, 3).reshape(n_z, part, width)

    def by_heads(w):
        cut = w.reshape(part, n_z, quarter).transpose(1, 0, 2)
        return jnp.pad(cut, ((0, 0), (0, 0), (0, 256 - quarter)))

    split = [by_units(probe_up_weight), by_units(text_up_weight)]
    split += [by_heads(text_attend_in[:, k * width : (k + 1) * width]) for k in range(3)]
    split += [by_heads(text_head_weight), by_heads(probe_query_weight)]
    split += [by_heads(probe_pair_weight[:, k * width : (k + 1) * width]) for k in range(2)]
    split = jnp.concatenate(split, 2)
    downs = jnp.concatenate([text_down_weight, probe_down_weight], 1)
    w_in, small_all, x = gather(
        [image_attend_in, small, patches],
        [("full", "S"), ("full", "C"), ("za", None)],
        [(0, 0), (1, 0), (0, 1), (1, 1), (0, 2), (1, 2), (0, 3), (2, 0), (1, 3), (0, 4), (1, 4), (0, 5), (1, 5)],
        1,
    )
    w_in = w_in.reshape(width, 3 * width)
    x = x.reshape(length, width)
    main = jnp.concatenate(
        [
            image_attend_out,
            image_up_weight.reshape(part, width, fold).transpose(0, 2, 1).reshape(part, hidden_width),
            image_down_weight.reshape(part, hidden_width),
            text_attend_out,
            probe_out_weight,
        ],
        1,
    )
    main = lax.all_gather(main, ALL, axis=0, tiled=True)
    outs = lax.dynamic_slice_in_dim(main[:, width + 2 * hidden_width :], at_z * quarter, quarter, 0)

    small_all = small_all.reshape(world, -1)
    cuts = [sum(sizes[:i]) for i in range(len(sizes) + 1)]
    pieces = [small_all[:, cuts[i] : cuts[i + 1]].astype(F32) for i in range(len(sizes))]
    ivec = pieces[0].reshape(world, -1, part).transpose(1, 0, 2).reshape(-1, width)
    tvec = pieces[1].reshape(world, -1, part).transpose(1, 0, 2).reshape(-1, width)
    i_bias = pieces[2].reshape(width, fold).T.reshape(1, hidden_width)

    def own_units(p):
        p = p.reshape(n_dp, n_z, wide_part)
        return lax.dynamic_index_in_dim(p, at_z, 1, False).reshape(1, width)

    p_bias, t_bias = own_units(pieces[3]), own_units(pieces[4])

    normed = layer_norm(x.astype(F32), ivec[0], ivec[1]).astype(BF)
    proj = mm(normed, w_in).astype(BF)
    mixed, lse, tp, downs, tokens = attend_fwd_and_gather(proj, split, downs, captions, 5)
    hidden, second, active, slope, block_out, final, tp = mlp_fwd(x, mixed, main, i_bias, ivec, fold, tp, 6)
    tp, downs = tp.reshape(width, -1), downs.reshape(width, -1)

    labels = (2 * pairs - 1).astype(F32).reshape(n_dp, n_z, n_dp, n_z)
    labels = jnp.pad(labels, ((0, 0), (0, n_z), (0, 0), (n_z, 0))).reshape(2 * world, 2 * world)
    dy, d_branch, rows, sums, d_captions, loss_row, d_embeds = middle(
        final, block_out, tokens.reshape(-1, width), tp, downs, outs, ivec, tvec, p_bias, t_bias, labels, temp_bias, 2, n_dp
    )
    loss, grad_temp = loss_row[0, 0], loss_row[0, 1:3]
    grad_captions = d_captions.reshape(captions.shape)

    g_up, g_rest, d_hidden, d_mixed, inner, g_bias, dvec = mlp_bwd(
        dy, d_branch, active, slope, second, hidden, mixed, main, ivec, fold
    )
    g_rest = lax.psum_scatter(g_rest, ALL, scatter_dimension=0, tiled=True).astype(F32)
    own_out = g_rest[:, :width]
    own_down = g_rest[:, width:].reshape(wide_part, width)
    d_q, d_k, d_v, own_up, rows = attend_bwd_and_reduce(proj, d_mixed, lse, inner, g_up, rows, 4)
    own_up = own_up.reshape(part, fold, width).transpose(0, 2, 1).reshape(part, hidden_width)
    rows = rows.reshape(world, ROWS, width).transpose(1, 0, 2)
    sums = jnp.concatenate([dvec[0:2], dvec[0:2], sums[4:], g_bias.reshape(fold, width)], 0)
    own_in, moved = finish_image(d_q, d_k, d_v, normed, w_in, x, d_hidden, sums, ivec, 3)
    grad_patches = moved.astype(F32)
    own_sums = own_in[:, 3 * width : 3 * width + 128].T
    own_in = own_in[:, : 3 * width]

    d_embeds = d_embeds.reshape(n_dp, 2, n_z, width).astype(BF)
    pup, tup, own_p_down, own_t_down, own_p_out, own_t_out, own_t_head, tq, tk, tv, pv, pk, biases = outer_grads(
        rows, d_embeds[:, 0].reshape(world, width), d_embeds[:, 1].reshape(world, width)
    )

    def wide(g):
        return g.reshape(n_z, part, n_dp, wide_part).transpose(1, 2, 0, 3).reshape(part, hidden_width)

    own_p_up, own_t_up = wide(pup), wide(tup)
    own_t_in = jnp.stack([tq, tk, tv]).transpose(2, 0, 1, 3).reshape(part, 3 * width)
    row20 = rows[20].reshape(n_dp, n_z, n_z, quarter).astype(F32)
    probe_query = row20[0, :, 3].reshape(HEADS, head_width)
    own_p_k = (pk[:, :HEADS, None] * probe_query[None]).reshape(part, width)
    own_p_pair = jnp.concatenate([own_p_k, pv.transpose(1, 0, 2).reshape(part, width)], 1)
    d_query = jnp.sum(row20[:, :, 2], 0).reshape(width)
    mine = lambda v, n: lax.dynamic_slice_in_dim(v, me * n, n, -1)
    own_p_query = mine(ivec[7], part)[:, None] * d_query[None, :]
    dv7 = jnp.sum(probe_query_weight.astype(F32) * d_query[None, :], 1)
    own_ivec = jnp.concatenate([own_sums[0:7], dv7[None], own_sums[8:11]], 0)
    own_tvec = own_sums[11:18]
    own_bias = own_sums[24 : 24 + fold].T.reshape(wide_part)
    return (
        loss, grad_patches, grad_captions,
        own_in, own_out, own_up, own_bias, own_down, own_ivec,
        own_p_query, own_p_pair, own_p_out, own_p_up, biases[0, :, 0], own_p_down,
        own_t_in, own_t_out, own_t_up, biases[1, :, 0], own_t_down, own_tvec, own_t_head,
        grad_temp,
    )


def solution(mesh):
    tokens, matrix, vector, table = P("dp", "seq", None), P(ALL, None), P(ALL), P(None, ALL)
    weights = (
        (matrix, matrix, matrix, vector, matrix, table, matrix, matrix, matrix, matrix, vector, matrix)
        + (matrix, matrix, matrix, vector, matrix, table, matrix)
    )
    return jax.shard_map(
        fast_program if mesh.shape["dp"] == 8 and mesh.shape["seq"] == 4 else device_program,
        mesh=mesh,
        in_specs=(tokens, tokens, P()) + weights + (P(),),
        out_specs=(P(), tokens, tokens) + weights + (P(),),
        check_vma=False,
    )
```

```python
from functools import partial

import jax
import jax.numpy as jnp
from jax import lax
from jax.experimental import pallas as pl
from jax.experimental.pallas import tpu as pltpu
from jax.sharding import PartitionSpec as P

HEADS = 12
ALL = ("dp", "seq")
F32, BF = jnp.float32, jnp.bfloat16
HIGH = lax.Precision.HIGHEST
EPS = 1e-06


def mm(a, b, ca=1, cb=0):
    return lax.dot_general(a, b, (((ca,), (cb,)), ((), ())), preferred_element_type=F32)


def mm_exact(a, b, ca=1, cb=0):
    return lax.dot_general(a, b, (((ca,), (cb,)), ((), ())), precision=HIGH, preferred_element_type=F32)


def split_two(a):
    high = a.astype(BF)
    return high, (a - high.astype(F32)).astype(BF)


def layer_norm(x, gain, shift):
    center = x - jnp.mean(x, -1, keepdims=True)
    spread = jnp.mean(center * center, -1, keepdims=True)
    return center * lax.rsqrt(spread + EPS) * gain + shift


def norm_back(x, gain, upstream):
    center = x - jnp.mean(x, -1, keepdims=True)
    inverse = lax.rsqrt(jnp.mean(center * center, -1, keepdims=True) + EPS)
    unit = center * inverse
    scaled = upstream * gain
    d_x = inverse * (
        scaled
        - jnp.mean(scaled, -1, keepdims=True)
        - unit * jnp.mean(scaled * unit, -1, keepdims=True)
    )
    return d_x, jnp.sum(upstream * unit, 0), jnp.sum(upstream, 0)


def norm_back_rows(x, gain, upstream):
    d_x, d_gain, d_shift = norm_back(x, gain, upstream)
    return d_x, d_gain[None], d_shift[None]


def mm_two(a, b, cb=0):
    n = a.shape[0]
    high = a.astype(BF).astype(F32)
    both = mm(jnp.concatenate([high, a - high], 0).astype(BF), b, 1, cb)
    return both[0:n] + both[n : 2 * n]


def gelu_pair(u):
    c = 0.7978845608028654
    t = jnp.tanh(c * (u + 0.044715 * u * u * u))
    value = 0.5 * u * (1.0 + t)
    slope = 0.5 * (1.0 + t) + 0.5 * u * (1.0 - t * t) * c * (1.0 + 3 * 0.044715 * u * u)
    return value, slope


def attend_fwd_kernel(q_ref, k_ref, v_ref, o_ref, lse_ref):
    q = q_ref[...] * 0.125
    k = k_ref[...]
    lane = lax.broadcasted_iota(jnp.int32, k.shape, 1)
    v_turned = jnp.transpose(v_ref[...])
    outs = []
    for h in range(2):
        keep = (lane < 64) if h == 0 else (lane >= 64)
        own_k = jnp.where(keep, k, jnp.zeros_like(k))
        s = mm(own_k, q, 1, 1)
        top = jnp.max(s, 0, keepdims=True)
        p = jnp.exp(s - top)
        total = jnp.sum(p, 0, keepdims=True)
        outs.append(mm(v_turned[64 * h : 64 * h + 64], p.astype(BF)) / total)
        lse_ref[0, h : h + 1, :] = top + jnp.log(total)
    o_ref[...] = jnp.transpose(jnp.concatenate(outs, 0)).astype(BF)


def attend_fwd(proj, length):
    rows, width = proj.shape[0], proj.shape[1] // 3
    pairs = width // 128
    block = lambda part: pl.BlockSpec((length, 128), lambda b, h: (b, part * pairs + h))
    return pl.pallas_call(
        attend_fwd_kernel,
        grid=(rows // length, pairs),
        in_specs=[block(0), block(1), block(2)],
        out_specs=[block(0), pl.BlockSpec((1, 2, length), lambda b, h: (h, 0, b))],
        out_shape=[
            jax.ShapeDtypeStruct((rows, width), BF),
            jax.ShapeDtypeStruct((pairs, 2, rows), F32),
        ],
        compiler_params=pltpu.CompilerParams(vmem_limit_bytes=48 << 20),
        cost_estimate=pl.CostEstimate(
            flops=rows * length * width * 8,
            bytes_accessed=rows * width * 8,
            transcendentals=rows * length * HEADS,
        ),
    )(proj, proj, proj)


def attend_bwd_kernel(q_ref, k_ref, v_ref, do_ref, lse_ref, d_ref, dq_ref, dk_ref, dv_ref):
    q = q_ref[...] * 0.125
    k, v, do = k_ref[...], v_ref[...], do_ref[...]
    lane = lax.broadcasted_iota(jnp.int32, k.shape, 1)
    dqs, dks, dvs = [], [], []
    for h in range(2):
        keep = (lane < 64) if h == 0 else (lane >= 64)
        s = mm(jnp.where(keep, k, jnp.zeros_like(k)), q, 1, 1)
        p = jnp.exp(s - lse_ref[0, h : h + 1, :])
        dp = mm(jnp.where(keep, v, jnp.zeros_like(v)), do, 1, 1)
        ds = (p * (dp - d_ref[0, h : h + 1, :])).astype(BF)
        dvs.append(mm(p.astype(BF), do))
        dks.append(mm(ds, q))
        dqs.append(mm(ds, k, 0, 0))
    low = lane < 64
    dq_ref[...] = (jnp.where(low, dqs[0], dqs[1]) * 0.125).astype(BF)
    dk_ref[...] = jnp.where(low, dks[0], dks[1]).astype(BF)
    dv_ref[...] = jnp.where(low, dvs[0], dvs[1]).astype(BF)


def attend_bwd(proj, d_out, lse, inner, length):
    rows, width = proj.shape[0], proj.shape[1] // 3
    pairs = width // 128
    block = lambda part: pl.BlockSpec((length, 128), lambda b, h: (b, part * pairs + h))
    row = pl.BlockSpec((1, 2, length), lambda b, h: (h, 0, b))
    result = jax.ShapeDtypeStruct((rows, width), BF)
    return pl.pallas_call(
        attend_bwd_kernel,
        grid=(rows // length, pairs),
        in_specs=[block(0), block(1), block(2), block(0), row, row],
        out_specs=[block(0)] * 3,
        out_shape=[result] * 3,
        compiler_params=pltpu.CompilerParams(vmem_limit_bytes=56 << 20),
        cost_estimate=pl.CostEstimate(
            flops=rows * length * width * 20,
            bytes_accessed=rows * width * 16,
            transcendentals=rows * length * HEADS,
        ),
    )(proj, proj, proj, d_out, lse, inner)


def head_blocks(width):
    own = jnp.arange(width)[None, :] // (width // HEADS) == jnp.arange(HEADS)[:, None]
    return own.astype(F32)


def spread_heads(rows):
    n, width = rows.shape
    return (rows[:, None, :] * head_blocks(width)[None]).reshape(n * HEADS, width)


def fold_heads(rows):
    total, width = rows.shape
    return jnp.sum(rows.reshape(total // HEADS, HEADS, width) * head_blocks(width)[None], 1)


def device_program(
    patches, captions, pairs,
    image_attend_in, image_attend_out, image_up_weight, image_up_bias, image_down_weight,
    image_vectors, probe_query_weight, probe_pair_weight, probe_out_weight, probe_up_weight,
    probe_up_bias, probe_down_weight, text_attend_in, text_attend_out, text_up_weight,
    text_up_bias, text_down_weight, text_vectors, text_head_weight, temp_bias,
):
    seq = lax.axis_size("seq")
    world = seq * lax.axis_size("dp")
    me = lax.axis_index("dp") * seq + lax.axis_index("seq")
    width = patches.shape[-1]
    head_width = width // HEADS
    factor = head_width ** (-0.5)
    hidden_width = image_up_weight.shape[1]
    part = width // world
    wide_part = hidden_width // world

    def gather(*weights):
        flat = jnp.concatenate([w.reshape(-1, width) for w in weights], 0)
        full = lax.all_gather(flat, ALL, axis=0)
        out, at = [], 0
        for w in weights:
            count = w.size // width
            piece = full[:, at : at + count]
            out.append(piece.reshape(world * w.shape[0], w.shape[1]))
            at += count
        return out

    small = jnp.concatenate(
        [image_vectors.reshape(-1), text_vectors.reshape(-1), image_up_bias, probe_up_bias, text_up_bias]
    )
    small_all = lax.all_gather(small, ALL, axis=0)
    sizes = [image_vectors.size, text_vectors.size, image_up_bias.size, probe_up_bias.size, text_up_bias.size]
    cuts = [sum(sizes[:i]) for i in range(len(sizes) + 1)]
    pieces = [small_all[:, cuts[i] : cuts[i + 1]].astype(F32) for i in range(len(sizes))]
    ivec = pieces[0].reshape(world, -1, part).transpose(1, 0, 2).reshape(-1, width)
    tvec = pieces[1].reshape(world, -1, part).transpose(1, 0, 2).reshape(-1, width)
    i_bias, p_bias, t_bias = (p.reshape(-1) for p in pieces[2:])

    (w_in,) = gather(image_attend_in)
    w_out, w_up, w_down = gather(image_attend_out, image_up_weight, image_down_weight)
    tw_in, tw_out, tw_up, tw_down, tw_head, pw_query, pw_pair, pw_out, pw_up, pw_down = gather(
        text_attend_in, text_attend_out, text_up_weight, text_down_weight, text_head_weight,
        probe_query_weight, probe_pair_weight, probe_out_weight, probe_up_weight, probe_down_weight,
    )

    def to_owner(x):
        return lax.all_to_all(x, "seq", 0, 1, tiled=True)

    x = to_owner(patches)
    own, length = x.shape[0], x.shape[1]
    x = x.reshape(own * length, width).astype(F32)
    captions_own = to_owner(captions)
    text_length = captions_own.shape[1]

    normed = layer_norm(x, ivec[0], ivec[1]).astype(BF)
    proj = mm(normed, w_in).astype(BF)
    mixed, lse = attend_fwd(proj, length)
    hidden = x + mm(mixed, w_out)
    second = layer_norm(hidden, ivec[2], ivec[3]).astype(BF)
    value, slope = gelu_pair(mm(second, w_up) + i_bias)
    active, slope = value.astype(BF), slope.astype(BF)
    block_out = hidden + mm(active, w_down) + ivec[4]
    final = layer_norm(block_out, ivec[5], ivec[6]).astype(BF)

    t_x = captions_own.astype(F32)
    t_normed = layer_norm(t_x, tvec[0], tvec[1]).astype(BF)
    t_last = t_normed[:, -1]
    tw_q, tw_k, tw_v = tw_in[:, :width], tw_in[:, width : 2 * width], tw_in[:, 2 * width :]
    t_q = mm(t_last, tw_q).astype(BF)
    t_keys = mm(spread_heads(t_q.astype(F32)).astype(BF), tw_k, 1, 1) * factor
    t_keys = t_keys.reshape(own, HEADS, width)
    k_high, k_low = split_two(t_keys)
    scores = jnp.einsum("bsd,bhd->bsh", t_normed, k_high, preferred_element_type=F32)
    scores += jnp.einsum("bsd,bhd->bsh", t_normed, k_low, preferred_element_type=F32)
    t_probs = jax.nn.softmax(scores, axis=1)
    t_used = jnp.einsum("bsh,bsd->bhd", t_probs, t_normed.astype(F32), precision=HIGH)
    t_mixed = fold_heads(mm(t_used.reshape(own * HEADS, width).astype(BF), tw_v)).astype(BF)
    t_hidden = t_x[:, -1] + mm(t_mixed, tw_out)
    t_second = layer_norm(t_hidden, tvec[2], tvec[3]).astype(BF)
    t_value, t_slope = gelu_pair(mm(t_second, tw_up) + t_bias)
    t_active = t_value.astype(BF)
    t_out = t_hidden + mm(t_active, tw_down) + tvec[4]
    t_final = layer_norm(t_out, tvec[5], tvec[6]).astype(BF)
    text_embed = mm(t_final, tw_head)

    pw_k, pw_v = pw_pair[:, :width], pw_pair[:, width:]
    probe_query = mm_exact(ivec[7:8], pw_query.astype(F32))
    p_keys = mm_exact(spread_heads(probe_query), pw_k.astype(F32), 1, 1) * factor
    k_high, k_low = split_two(p_keys)
    pool_scores = mm(k_high, final, 1, 1) + mm(k_low, final, 1, 1)
    pool_scores = pool_scores.reshape(HEADS, own, length)
    pool_probs = jax.nn.softmax(pool_scores, axis=-1)
    final_own = final.reshape(own, length, width)
    p_high, p_low = split_two(pool_probs)
    used = jnp.einsum("hbt,btd->bhd", p_high, final_own, preferred_element_type=F32)
    used += jnp.einsum("hbt,btd->bhd", p_low, final_own, preferred_element_type=F32)
    pooled = fold_heads(mm_exact(used.reshape(own * HEADS, width), pw_v.astype(F32)))
    head_start = mm_exact(pooled, pw_out.astype(F32))
    head_normed = layer_norm(head_start, ivec[8], ivec[9]).astype(BF)
    h_value, h_slope = gelu_pair(mm(head_normed, pw_up) + p_bias)
    head_active = h_value.astype(BF)
    image_embed = head_start + mm(head_active, pw_down) + ivec[10]

    embeds = lax.all_gather(jnp.stack([image_embed, text_embed], 1), ALL, axis=0, tiled=True)
    every_image, every_text = embeds[:, 0], embeds[:, 1]
    labels = (2 * pairs - 1).astype(F32)
    total = every_image.shape[0]
    i_scale = lax.rsqrt(jnp.sum(every_image * every_image, -1, keepdims=True) + EPS)
    t_scale = lax.rsqrt(jnp.sum(every_text * every_text, -1, keepdims=True) + EPS)
    z_i, z_t = every_image * i_scale, every_text * t_scale
    cosine = mm_exact(z_i, z_t, 1, 1)
    temper = jnp.exp(temp_bias[0])
    logits = cosine * temper + temp_bias[1]
    loss = -jnp.sum(jax.nn.log_sigmoid(labels * logits)) / total
    g = -labels * jax.nn.sigmoid(-labels * logits) / total
    grad_temp = jnp.stack([temper * jnp.sum(g * cosine), jnp.sum(g)])
    dz_i = temper * mm_exact(g, z_t)
    dz_t = temper * mm_exact(g, z_i, 0, 0)
    all_d_image = (dz_i - z_i * jnp.sum(z_i * dz_i, -1, keepdims=True)) * i_scale
    all_d_text = (dz_t - z_t * jnp.sum(z_t * dz_t, -1, keepdims=True)) * t_scale
    d_image = lax.dynamic_slice_in_dim(all_d_image, me * own, own, 0)
    d_text = lax.dynamic_slice_in_dim(all_d_text, me * own, own, 0)

    h_upper = mm_exact(d_image, pw_down.astype(F32), 1, 1) * h_slope
    h_norm = mm_exact(h_upper, pw_up.astype(F32), 1, 1)
    d_start, dv8, dv9 = norm_back(head_start, ivec[8], h_norm)
    d_start = d_image + d_start
    dv10 = jnp.sum(d_image, 0)
    d_pooled = mm_exact(d_start, pw_out.astype(F32), 1, 1)
    p_values = mm_exact(spread_heads(d_pooled), pw_v.astype(F32), 1, 1).reshape(own, HEADS, width)
    v_high, v_low = split_two(p_values)
    d_probs = jnp.einsum("bhd,btd->hbt", v_high, final_own, preferred_element_type=F32)
    d_probs += jnp.einsum("bhd,btd->hbt", v_low, final_own, preferred_element_type=F32)
    d_scores = pool_probs * (d_probs - jnp.sum(pool_probs * d_probs, -1, keepdims=True))
    s_high, s_low = split_two(d_scores)
    p_used = jnp.einsum("hbt,btd->bhd", s_high, final_own, preferred_element_type=F32)
    p_used += jnp.einsum("hbt,btd->bhd", s_low, final_own, preferred_element_type=F32)
    d_query = jnp.sum(fold_heads(mm_exact(p_used.reshape(own * HEADS, width), pw_k.astype(F32))), 0) * factor
    d_final = jnp.einsum(
        "hbt,bhd->btd",
        jnp.concatenate([s_high, p_high], 0),
        jnp.concatenate([jnp.broadcast_to(k_high[None], (own, HEADS, width)), v_high], 1),
        preferred_element_type=F32,
    ).reshape(own * length, width)
    dy, dv5, dv6 = norm_back(block_out, ivec[5], d_final)

    d_branch = dy.astype(BF)
    g_down = mm(active, d_branch, 0, 0)
    dv4 = jnp.sum(dy, 0)
    d_upper_f = mm(d_branch, w_down, 1, 1) * slope.astype(F32)
    d_upper = d_upper_f.astype(BF)
    g_bias = jnp.sum(d_upper_f, 0)
    g_up = mm(second, d_upper, 0, 0)
    d_hidden, dv2, dv3 = norm_back(hidden, ivec[2], mm(d_upper, w_up, 1, 1))
    d_hidden = dy + d_hidden
    d_attend = d_hidden.astype(BF)
    g_out = mm(mixed, d_attend, 0, 0)
    d_mixed = mm(d_attend, w_out, 1, 1).astype(BF)

    def scatter(*grads):
        flat = jnp.concatenate([g.astype(BF).reshape(world, -1, width) for g in grads], 1)
        mine = lax.psum_scatter(flat, ALL, scatter_dimension=0, tiled=False).astype(F32)
        out, at = [], 0
        for g in grads:
            count = g.size // world // width
            out.append(mine[at : at + count].reshape(g.shape[0] // world, g.shape[1]))
            at += count
        return out

    own_up, own_down, own_out = scatter(g_up, g_down, g_out)
    inner_rows = jnp.sum(
        (d_mixed.astype(F32) * mixed.astype(F32)).reshape(own * length, HEADS, head_width), -1
    ).T.reshape(HEADS // 2, 2, own * length)
    d_q, d_k, d_v = attend_bwd(proj, d_mixed, lse, inner_rows, length)
    g_in = jnp.concatenate([mm(normed, d, 0, 0) for d in (d_q, d_k, d_v)], 1)
    (own_in,) = scatter(g_in)
    d_normed = (
        mm(d_q, w_in[:, :width], 1, 1)
        + mm(d_k, w_in[:, width : 2 * width], 1, 1)
        + mm(d_v, w_in[:, 2 * width :], 1, 1)
    )
    d_x, dv0, dv1 = norm_back(x, ivec[0], d_normed)
    d_x = (d_hidden + d_x).reshape(own, length, width)

    def to_tokens(v):
        return lax.all_to_all(v.astype(BF), "seq", 1, 0, tiled=True).astype(F32)

    grad_patches = to_tokens(d_x)

    dt_final = mm_exact(d_text, tw_head.astype(F32), 1, 1)
    dt_out, tv5, tv6 = norm_back(t_out, tvec[5], dt_final)
    dt_branch = dt_out.astype(BF)
    tv4 = jnp.sum(dt_out, 0)
    dt_upper = (mm(dt_branch, tw_down, 1, 1) * t_slope).astype(BF)
    dt_hidden, tv2, tv3 = norm_back(t_hidden, tvec[2], mm(dt_upper, tw_up, 1, 1))
    dt_hidden = dt_out + dt_hidden
    dt_attend = dt_hidden.astype(BF)
    dt_mixed = mm(dt_attend, tw_out, 1, 1).astype(BF)
    t_values = mm(spread_heads(dt_mixed.astype(F32)).astype(BF), tw_v, 1, 1).reshape(own, HEADS, width)
    tv_high, tv_low = split_two(t_values)
    dt_probs = jnp.einsum("bsd,bhd->bsh", t_normed, tv_high, preferred_element_type=F32)
    dt_probs += jnp.einsum("bsd,bhd->bsh", t_normed, tv_low, preferred_element_type=F32)
    dt_scores = t_probs * (dt_probs - jnp.sum(t_probs * dt_probs, 1, keepdims=True))
    tk_used = jnp.einsum("bsh,bsd->bhd", dt_scores, t_normed.astype(F32), precision=HIGH)
    dt_q = fold_heads(mm(tk_used.reshape(own * HEADS, width).astype(BF), tw_k)) * factor
    dt_q = dt_q.astype(BF)
    dt_normed = jnp.einsum("bsh,bhd->bsd", dt_scores, t_keys, precision=HIGH)
    dt_normed += jnp.einsum("bsh,bhd->bsd", t_probs, t_values, precision=HIGH)
    dt_normed = dt_normed.at[:, -1].add(mm(dt_q, tw_q, 1, 1))
    flat_x = t_x.reshape(own * text_length, width)
    dt_x, tv0, tv1 = norm_back(flat_x, tvec[0], dt_normed.reshape(own * text_length, width))
    dt_x = dt_x.reshape(own, text_length, width).at[:, -1].add(dt_hidden)
    grad_captions = to_tokens(dt_x)

    whole = jnp.concatenate(
        [v.astype(F32) for v in (h_upper, d_start, d_pooled, dt_branch, dt_upper, dt_attend, dt_q, t_q, dt_mixed)], 1
    )
    whole = lax.all_gather(whole, ALL, axis=0, tiled=True)
    at = [0]

    def take(count):
        at[0] += count
        return whole[:, at[0] - count : at[0]]

    a_h_upper, a_start, a_pooled, a_branch, a_upper, a_attend, a_q, a_query, a_mixed = (
        take(c) for c in (hidden_width, width, width, width, hidden_width, width, width, width, width)
    )
    columns = [pooled, head_normed, t_last, t_mixed, t_second, t_final]
    columns += [used, t_used, tk_used * factor]
    columns += [head_active, t_active]
    columns = jnp.concatenate(
        [v.astype(F32).reshape(own, -1, width) for v in columns], 1
    )
    wide = 2 * (hidden_width // width)
    narrow = columns.shape[1] - wide
    cut = jnp.concatenate(
        [
            columns[:, :narrow].reshape(own, narrow, world, part).transpose(2, 0, 1, 3).reshape(world, own, -1),
            columns[:, narrow:].reshape(own, 2, world, wide_part).transpose(2, 0, 1, 3).reshape(world, own, -1),
        ],
        2,
    )
    cut = lax.all_to_all(cut, ALL, 0, 0, tiled=True).reshape(total, -1)
    slim = cut[:, : narrow * part].reshape(total, narrow, part)
    broad = cut[:, narrow * part :].reshape(total, 2, wide_part)

    def outer(rows, cols):
        return mm_exact(rows, cols, 0, 0)

    def outer_heads(rows, cols):
        cols = cols.reshape(total, HEADS, head_width)
        return jnp.einsum("chm,che->mhe", rows, cols, precision=HIGH).reshape(part, width)

    c_pooled, c_head, c_last, c_mixed, c_second, c_final = (slim[:, i] for i in range(6))
    c_used, ct_used, ctk_used = (slim[:, 6 + i * HEADS : 6 + (i + 1) * HEADS] for i in range(3))
    own_t_in = jnp.concatenate(
        [outer(c_last, a_q), outer_heads(ctk_used, a_query), outer_heads(ct_used, a_mixed)], 1
    )
    own_t_out = outer(c_mixed, a_attend)
    own_t_up = outer(c_second, a_upper)
    own_t_down = outer(broad[:, 1], a_branch)
    own_t_head = outer(c_final, all_d_text)
    own_p_out = outer(c_pooled, a_start)
    own_p_up = outer(c_head, a_h_upper)
    own_p_down = outer(broad[:, 0], all_d_image)
    own_p_values = outer_heads(c_used, a_pooled)

    summed = jnp.concatenate(
        [
            jnp.stack([dv0, dv1, dv2, dv3, dv4, dv5, dv6, dv8, dv9, dv10]),
            jnp.stack([tv0, tv1, tv2, tv3, tv4, tv5, tv6]),
            d_query[None],
            jnp.sum(p_used, 0),
            g_bias.reshape(-1, width),
        ],
        0,
    )
    summed = lax.psum(summed, ALL)
    total_query = summed[17]
    mine = lambda v, n: lax.dynamic_slice_in_dim(v, me * n, n, -1)
    own_probe = mine(ivec[7], part)
    own_p_query = own_probe[:, None] * total_query[None, :]
    dv7 = jnp.sum(probe_query_weight.astype(F32) * total_query[None, :], 1)
    pk_used = mine(summed[18 : 18 + HEADS], part)
    own_p_keys = jnp.einsum(
        "hm,he->mhe", pk_used, probe_query.reshape(HEADS, head_width) * factor
    ).reshape(part, width)
    own_p_pair = jnp.concatenate([own_p_keys, own_p_values], 1)
    ten = mine(summed[:10], part)
    own_ivec = jnp.concatenate([ten[:7], dv7[None], ten[7:]], 0)
    own_tvec = mine(summed[10:17], part)
    own_bias = mine(summed[18 + HEADS :].reshape(-1), wide_part)
    own_p_bias = mine(jnp.sum(a_h_upper, 0), wide_part)
    own_t_bias = mine(jnp.sum(a_upper, 0), wide_part)
    return (
        loss, grad_patches, grad_captions,
        own_in, own_out, own_up, own_bias, own_down, own_ivec,
        own_p_query, own_p_pair, own_p_out, own_p_up, own_p_bias, own_p_down,
        own_t_in, own_t_out, own_t_up, own_t_bias, own_t_down, own_tvec, own_t_head,
        grad_temp,
    )


MESH = pl.DeviceIdType.MESH

class Place:
    def __init__(self):
        i = lax.axis_index("dp")
        self.i, self.z = i, lax.axis_index("seq")
        self.y, self.x, self.c = i // 4, (i // 2) % 2, i % 2
        self.at_y = (i + 4 - 8 * self.y, self.z)
        self.at_x = (i + 2 - 4 * self.x, self.z)
        self.at_c = (i + 1 - 2 * self.c, self.z)

    def at_z(self, k):
        return (self.i, (self.z + k) % 4)

def greet(peers):
    barrier = pltpu.get_barrier_semaphore()
    for p in peers:
        pl.semaphore_signal(barrier, inc=1, device_id=p, device_id_type=MESH)
    pl.semaphore_wait(barrier, len(peers))

def gather_kernel(kinds, order, *refs):
    n = len(kinds)
    srcs, outs = refs[:n], refs[n : 2 * n]
    send, recv, local = refs[2 * n :]
    me = Place()
    y, x, c, z = me.y, me.x, me.c, me.z
    greet([me.at_z(1), me.at_z(2), me.at_z(3), me.at_x, me.at_y, me.at_c])
    ends = []

    def copy_of(a, slot, src, dst, dev):
        return pltpu.make_async_remote_copy(
            src, dst, send.at[a, slot], recv.at[a, slot], device_id=dev, device_id_type=MESH
        )

    def push(a, slot, src, dst, dev, arriving):
        copy = copy_of(a, slot, src, dst, dev)
        copy.start()
        ends.append(copy.wait_send)
        return copy_of(a, slot, src, arriving, dev).wait_recv

    def along(a, step, up):
        home = outs[a].at[y, x, c]
        if up:
            slab, go, to = z - step, (z - step >= 0) & (z < 3), me.at_z(1)
        else:
            slab, go, to = z + step, (z + step < 4) & (z > 0), me.at_z(3)
        slab = jnp.clip(slab, 0, 3)
        src = srcs[a] if step == 0 else home.at[slab]
        copy = copy_of(a, step + (0 if up else 3), src, home.at[slab], to)
        pl.when(go)(lambda: copy.start())
        ends.append(lambda: pl.when(go)(lambda: copy.wait_send()))

    def arrived(a, step, up):
        home = outs[a].at[y, x, c]
        if up:
            slab, come = z - 1 - step, z - 1 - step >= 0
        else:
            slab, come = z + 1 + step, z + 1 + step < 4
        slab = jnp.clip(slab, 0, 3)
        copy = copy_of(a, step + (0 if up else 3), home.at[slab], home.at[slab], me.at_z(1))
        pl.when(come)(lambda: copy.wait_recv())

    waits = {}

    def half(r, which, order_):
        if order_ != "S":
            return r
        n_ = r.shape[-1] // 2
        return r.at[..., 0:n_] if which == "C" else r.at[..., n_ : 2 * n_]

    def stage(a, s):
        kind, turn = kinds[a]
        src, out = srcs[a], outs[a]
        if kind in ("za", "zg"):
            own = src.at[z] if kind == "za" else src
            keep = pltpu.make_async_copy(own, out.at[z], local.at[a])
            keep.start()
            ends.append(keep.wait)
            for k in (1, 2, 3):
                to, fro = (z + k) % 4, (z + 4 - k) % 4
                s_ref = src.at[to] if kind == "za" else src
                ends.append(push(a, k - 1, s_ref, out.at[z], me.at_z(k), out.at[fro]))
            return
        turns = "CD" if turn == "S" else turn
        if kind != "full" and s == 0:
            own = src.at[z] if kind == "cols" else src
            keep = pltpu.make_async_copy(own, out.at[y, x, c, z] if kind == "cols" else out.at[y, x, c], local.at[a])
            keep.start()
            waits[a] = [keep.wait]
            for k in (1, 2, 3) if kind == "cols" else ():
                to, fro = (z + k) % 4, (z + 4 - k) % 4
                waits[a].append(push(a, k - 1, src.at[to], out.at[y, x, c, z], me.at_z(k), out.at[y, x, c, fro]))
        elif s == 0:
            keep = pltpu.make_async_copy(src, out.at[y, x, c, z], local.at[a])
            keep.start()
            waits[a] = [keep.wait]
            along(a, 0, True)
            along(a, 0, False)
        elif s in (1, 2):
            for up in (True, False):
                arrived(a, s - 1, up)
                along(a, s, up)
        elif s == 3:
            for up in (True, False) if kind == "full" else ():
                arrived(a, 2, up)
            for w in waits.pop(a):
                w()
            waits[a] = []
            for t in turns:
                cut = lambda r: half(r, t, turn)
                to, fro = (me.at_x, (y, 1 - x)) if t == "C" else (me.at_y, (1 - y, x))
                mine = cut(out.at[y, x, c])
                waits[a].append(push(a, 6 + (t == "D"), mine, mine, to, cut(out.at[fro[0], fro[1], c])))
        elif s == 4:
            for w in waits.pop(a):
                w()
            waits[a] = []
            for t in turns:
                cut = lambda r: half(r, t, turn)
                if t == "C":
                    mine, come, to = cut(out.at[y, :, c]), cut(out.at[1 - y, :, c]), me.at_y
                else:
                    mine, come, to = cut(out.at[:, x, c]), cut(out.at[:, 1 - x, c]), me.at_x
                waits[a].append(push(a, 8 + (t == "D"), mine, mine, to, come))
        elif s == 5:
            for w in waits.pop(a):
                w()
            mine = out.at[:, :, c]
            ends.append(push(a, 10, mine, mine, me.at_c, out.at[:, :, 1 - c]))

    for a, s in order:
        stage(a, s)
    for e in ends:
        e()


def gather(ops, kinds, order, cid):
    shapes = []
    for o, (kind, _) in zip(ops, kinds):
        s = {"full": (2, 2, 2, 4) + o.shape, "zg": (4,) + o.shape, "za": o.shape, "cols": (2, 2, 2) + o.shape, "plane": (2, 2, 2) + o.shape}[kind]
        shapes.append(jax.ShapeDtypeStruct(s, o.dtype))
    n = len(ops)
    return pl.pallas_call(
        partial(gather_kernel, kinds, order),
        out_shape=shapes,
        in_specs=[pl.BlockSpec(memory_space=pl.ANY)] * n,
        out_specs=[pl.BlockSpec(memory_space=pl.ANY)] * n,
        scratch_shapes=[
            pltpu.SemaphoreType.DMA((n, 11)),
            pltpu.SemaphoreType.DMA((n, 11)),
            pltpu.SemaphoreType.DMA((n,)),
        ],
        compiler_params=pltpu.CompilerParams(collective_id=cid, has_side_effects=True),
    )(*ops)


ROWS = 80

def middle_kernel(final_in, block_in, tokens_ref, tp_in, downs_in, outs_ref, ivec_ref, tvec_ref, pbias_ref, tbias_ref,
                  label_ref, temp_ref,
                  dy_ref, branch_ref, rows_ref, sums_ref, dcap_ref, loss_ref, dz_ref,
                  tn_ref, dn_ref, send_a, recv_a, send_l, recv_l, send_t, recv_t,
                  final_ref, block_ref, tp_ref, downs_ref, send_sem, recv_sem, fetch):
    me = Place()
    cut = 2 * final_in.shape[1]
    pairs = {
        "small": (tp_in.at[:, cut:], tp_ref.at[:, cut:]), "final": (final_in, final_ref),
        "up": (tp_in.at[:, 0:cut], tp_ref.at[:, 0:cut]), "down": (downs_in, downs_ref), "block": (block_in, block_ref),
    }
    loads = {name: pltpu.make_async_copy(*pair, fetch.at[n]) for n, (name, pair) in enumerate(pairs.items())}
    for load in loads.values():
        load.start()
    z, i = me.z, me.i
    n_dp = recv_l.shape[0]
    plane = [((i + k) % n_dp, z) for k in range(1, n_dp)]
    greet([me.at_z(1), me.at_z(2), me.at_z(3)] + plane)
    width = final_in.shape[1]
    part = width // 4
    started = []

    def exchange(n, values, rows=4):
        if not isinstance(values, list):
            values = [values] * 4
        for q in range(4):
            send_a[n, q, 0:rows] = values[q]
        recv_a[n, z] = send_a[n, z]
        copies = []
        for k in (3, 2, 1):
            to, fro = (z + k) % 4, (z + 4 - k) % 4
            make = lambda dst: pltpu.make_async_remote_copy(
                send_a.at[n, to], dst, send_sem.at[n, k], recv_sem.at[n, k], device_id=me.at_z(k), device_id_type=MESH)
            copy = make(recv_a.at[n, z])
            copy.start()
            started.append(copy)
            copies.append(make(recv_a.at[n, fro]))

        def done():
            for a in copies:
                a.wait_recv()
            return [recv_a[n, q, 0:rows] for q in range(4)]

        return done

    total = lambda blocks: (blocks[0] + blocks[1]) + (blocks[2] + blocks[3])
    by_head = lambda blocks, n=3: jnp.concatenate([blocks[q][h : h + 1] for h in range(n) for q in range(4)], 0)
    pad1 = jnp.zeros((1, width), F32)
    ivec, tvec = ivec_ref[...], tvec_ref[...]
    iv = lambda k: ivec[k:k + 1]
    tv = lambda k: tvec[k:k + 1]
    names = ["tq", "tk", "tv", "thead", "pq", "pk", "pv"]
    col = {n: 2 * width + 256 * k for k, n in enumerate(names)}
    small = lambda n: tp_ref[:, col[n]:col[n] + 256]
    p_up = lambda: tp_ref[:, 0:width]
    t_up = lambda: tp_ref[:, width:2 * width]
    t_down = lambda: downs_ref[:, 0:width]
    p_down = lambda: downs_ref[:, width:2 * width]
    t_out_w = lambda: outs_ref[0:part, 0:width]
    p_out_w = lambda: outs_ref[0:part, width:2 * width]
    lane = lax.broadcasted_iota(jnp.int32, (1, 256), 1)
    own = [((lane >= 64 * h) & (lane < 64 * h + 64)).astype(F32) for h in range(3)]

    def spread(a):
        return jnp.concatenate([a * own[h] for h in range(3)], 0)

    def fold(a):
        n = a.shape[0] // 3
        return sum(a[h * n:(h + 1) * n] * own[h] for h in range(3))

    loads["small"].wait()
    p_q = mm(iv(7).astype(BF), small("pq"))
    get_keys = exchange(0, mm_two(spread(p_q), small("pk"), 1) * 0.125, 3)
    t_x = tokens_ref[...].astype(F32)
    tn = layer_norm(t_x, tv(0), tv(1)).astype(BF)
    tn_ref[...] = tn.astype(F32)
    last_at = [3 * 64 + 16 * c + 15 for c in range(4)]
    t_last = jnp.concatenate([tn_ref[r:r + 1, :] for r in last_at], 0)
    x_last = jnp.concatenate([tokens_ref[3 * 64 + 16 * c:3 * 64 + 16 * c + 16, :].astype(F32)[15:16] for c in range(4)], 0)
    t_q = mm(t_last.astype(BF), small("tq")).astype(BF).astype(F32)
    t_keys = mm(spread(t_q).astype(BF), small("tk"), 1, 1) * 0.125
    scores = mm_two(t_keys, tn, 1)
    col_id = (lax.broadcasted_iota(jnp.int32, scores.shape, 1) // 16) % 4
    row_id = lax.broadcasted_iota(jnp.int32, scores.shape, 0) % 4
    mine = col_id == row_id
    top = jnp.max(jnp.where(mine, scores, -1e30), -1, keepdims=True)
    e = jnp.where(mine, jnp.exp(jnp.where(mine, scores - top, 0.0)), 0.0)
    t_probs = e / jnp.sum(e, -1, keepdims=True)
    t_used = mm_two(t_probs, tn)
    t_mixed = fold(mm(t_used.astype(BF), small("tv"))).astype(BF)
    get_t = exchange(1, mm(t_mixed[:, 0:part], t_out_w()), 4)
    loads["final"].wait()
    final = final_ref[...]
    p_keys = jnp.concatenate(get_keys(), 0)
    p_scores = mm_two(p_keys, final, 1)
    e = jnp.exp(p_scores - jnp.max(p_scores, -1, keepdims=True))
    p_probs = e / jnp.sum(e, -1, keepdims=True)
    used = mm_two(p_probs, final)
    get_p = exchange(2, [used[3 * q:3 * q + 3] for q in range(4)], 3)
    t_hidden = x_last + total(get_t())
    t_second = layer_norm(t_hidden, tv(2), tv(3)).astype(BF)
    loads["up"].wait()
    loads["down"].wait()
    t_value, t_slope = gelu_pair(mm(t_second, t_up()) + tbias_ref[...])
    t_active = t_value.astype(BF)
    get_t = exchange(3, mm(t_active, t_down()), 4)
    pooled = fold(mm_two(by_head(get_p()), small("pv")))
    get_p = exchange(4, mm_two(pooled[:, 0:part], p_out_w()), 4)
    t_out = t_hidden + total(get_t()) + tv(4)
    t_final = layer_norm(t_out, tv(5), tv(6)).astype(BF)
    t_piece = mm(t_final, small("thead"))
    get_t = exchange(5, jnp.concatenate([t_piece[:, 0:part], jnp.zeros((4, width - part), F32)], 1), 4)
    h_start = total(get_p())
    h_normed = layer_norm(h_start, iv(8), iv(9)).astype(BF)
    h_value, h_slope = gelu_pair(mm(h_normed, p_up()) + pbias_ref[...])
    h_active = h_value.astype(BF)
    get_p = exchange(6, mm(h_active, p_down()), 4)
    text_embed = jnp.concatenate([blk[:, 0:part] for blk in get_t()], 1)
    image_embed = h_start + (total(get_p()) + iv(10))
    send_l[...] = jnp.concatenate([image_embed, text_embed], 0)
    recv_l[i] = send_l[...]
    arrive = []
    for k in range(1, n_dp):
        copy = pltpu.make_async_remote_copy(send_l, recv_l.at[i], send_sem.at[15, k], recv_sem.at[15, k],
                                            device_id=plane[k - 1], device_id_type=MESH)
        copy.start()
        started.append(copy)
        arrive.append(pltpu.make_async_remote_copy(send_l, recv_l.at[(i + n_dp - k) % n_dp], send_sem.at[15, k], recv_sem.at[15, k],
                                                   device_id=plane[k - 1], device_id_type=MESH))
    for a in arrive:
        a.wait_recv()
    every = jnp.concatenate([recv_l[k] for k in range(n_dp)], 0)
    scale = lax.rsqrt(jnp.sum(every * every, -1, keepdims=True) + EPS)
    unit = every * scale
    cosine = mm_exact(unit, unit, 1, 1)
    temper = jnp.exp(jnp.full((1, 1), temp_ref[0], F32))
    logits = cosine * temper + temp_ref[1]
    label = label_ref[...]
    valid = label != 0.0
    signed = label * logits
    n_all = n_dp * 4
    nll = jnp.maximum(-signed, 0.0) + jnp.log(1.0 + jnp.exp(-jnp.abs(signed)))
    add_all = lambda a: jnp.sum(jnp.sum(a, -1, keepdims=True), 0, keepdims=True)
    loss = add_all(jnp.where(valid, nll, 0.0)) / n_all
    g = jnp.where(valid, -label / (1.0 + jnp.exp(signed)), 0.0) / n_all
    gt0 = temper * add_all(g * cosine)
    gt1 = add_all(g)
    at = lax.broadcasted_iota(jnp.int32, (8, 128), 1)
    loss_ref[...] = jnp.where(at == 0, loss, jnp.where(at == 1, gt0, gt1))
    dz = temper * mm_exact(g + jnp.transpose(g), unit)
    dz_ref[...] = (dz - unit * jnp.sum(unit * dz, -1, keepdims=True)) * scale
    d_both = dz_ref[pl.ds(pl.multiple_of(8 * i, 8), 8), :]
    d_image, d_text = d_both[0:4], d_both[4:8]

    dh_upper = mm_two(d_image, p_down(), 1) * h_slope
    get_p = exchange(7, mm_two(dh_upper, p_up(), 1), 4)
    d_text_my = sum(jnp.where(z == q, d_text[:, part * q:part * q + part], 0.0) for q in range(4))
    get_t = exchange(8, mm_two(d_text_my, small("thead")[:, 0:part], 1), 4)
    d_start, dv8, dv9 = norm_back_rows(h_start, iv(8), total(get_p()))
    d_start = d_image + d_start
    dv10 = jnp.sum(d_image, 0, keepdims=True)
    d_pooled = mm_two(d_start, p_out_w(), 1)
    d_pooled = jnp.concatenate([d_pooled, jnp.zeros((4, 256 - part), F32)], 1)
    p_values_my = mm_two(spread(d_pooled), small("pv"), 1)
    get_p = exchange(9, [jnp.concatenate([p_values_my[4 * h + q:4 * h + q + 1] for h in range(3)], 0) for q in range(4)], 3)
    dt_out, tv5, tv6 = norm_back_rows(t_out, tv(5), total(get_t()))
    tv4 = jnp.sum(dt_out, 0, keepdims=True)
    dt_branch = dt_out.astype(BF)
    dt_upper = (mm(dt_branch, t_down(), 1, 1) * t_slope).astype(BF)
    get_t = exchange(10, mm(dt_upper, t_up(), 1, 1), 4)
    p_values = jnp.concatenate(get_p(), 0)
    d_probs = mm_two(p_values, final, 1)
    d_scores = p_probs * (d_probs - jnp.sum(p_probs * d_probs, -1, keepdims=True))
    p_used = mm_two(d_scores, final) * 0.125
    get_p = exchange(11, [p_used[3 * q:3 * q + 3] for q in range(4)], 3)
    dt_hidden, tv2, tv3 = norm_back_rows(t_hidden, tv(2), total(get_t()))
    dt_hidden = dt_out + dt_hidden
    dt_attend = dt_hidden.astype(BF)
    dt_mixed = mm(dt_attend, t_out_w(), 1, 1).astype(BF).astype(F32)
    dt_mixed = jnp.concatenate([dt_mixed, jnp.zeros((4, 256 - part), F32)], 1)
    t_values = mm(spread(dt_mixed).astype(BF), small("tv"), 1, 1)
    dt_probs = mm_two(t_values, tn, 1)
    dt_scores = t_probs * (dt_probs - jnp.sum(t_probs * dt_probs, -1, keepdims=True))
    tk_used = mm_two(dt_scores, tn) * 0.125
    dt_q = fold(mm(tk_used.astype(BF), small("tk"))).astype(BF)
    dn = mm(dt_scores.astype(BF), t_keys.astype(BF), 0, 0) + mm(t_probs.astype(BF), t_values.astype(BF), 0, 0)
    row_at = lax.broadcasted_iota(jnp.int32, dn.shape, 0)
    dq_back = mm(dt_q, small("tq"), 1, 1)
    for c in range(4):
        dn = dn + jnp.where(row_at == last_at[c], dq_back[c:c + 1], 0.0)
    dn_ref[...] = dn.astype(BF)
    arrive = []
    for k in (1, 2, 3):
        to, fro = (z + k) % 4, (z + 4 - k) % 4
        rows_to = dn_ref.at[pl.ds(pl.multiple_of(64 * to, 64), 64), :]
        copy = pltpu.make_async_remote_copy(rows_to, recv_t.at[z], send_sem.at[14, k], recv_sem.at[14, k],
                                            device_id=me.at_z(k), device_id_type=MESH)
        copy.start()
        started.append(copy)
        arrive.append(pltpu.make_async_remote_copy(rows_to, recv_t.at[fro], send_sem.at[14, k], recv_sem.at[14, k],
                                                   device_id=me.at_z(k), device_id_type=MESH))
    s_high, s_low = split_two(d_scores)
    q_high, q_low = split_two(p_probs)
    k_high, k_low = split_two(p_keys)
    v_high, v_low = split_two(p_values)
    left = jnp.concatenate([s_high.astype(F32), q_high.astype(F32)], 0)
    right = jnp.concatenate([k_high.astype(F32), v_high.astype(F32)], 0).astype(BF)
    send_t[...] = jnp.transpose(jnp.concatenate([left, jnp.zeros((104, left.shape[1]), F32)], 0))
    right = jnp.concatenate([right, jnp.zeros((104, width), BF)], 0)
    sums_ref[...] = jnp.zeros_like(sums_ref)
    tile = 128

    def step(n, carry):
        at_rows = pl.ds(pl.multiple_of(n * tile, tile), tile)
        d_final = mm(send_t[at_rows, :].astype(BF), right)
        d_y, gain, shift = norm_back_rows(block_ref[at_rows, :], iv(5), d_final)
        dy_ref[at_rows, :] = d_y
        branch_ref[at_rows, :] = d_y.astype(BF)
        sums_ref[5:6] += gain
        sums_ref[6:7] += shift
        sums_ref[4:5] += jnp.sum(d_y, 0, keepdims=True)
        return carry

    loads["block"].wait()
    lax.fori_loop(0, final_ref.shape[0] // tile, step, 0)
    w_got = by_head(get_p())
    dq_rows = fold(mm_two(w_got, small("pk")))
    dq_my = jnp.sum(dq_rows, 0, keepdims=True)
    recv_t[z] = dn_ref[pl.ds(pl.multiple_of(64 * z, 64), 64), :]
    for a in arrive:
        a.wait_recv()
    dt_normed = sum(recv_t[q].astype(F32) for q in range(4))
    x_mine = tokens_ref[pl.ds(pl.multiple_of(64 * z, 64), 64), :].astype(F32)
    d_cap, tv0, tv1 = norm_back_rows(x_mine, tv(0), dt_normed)
    row_c = lax.broadcasted_iota(jnp.int32, d_cap.shape, 0)
    for c in range(4):
        d_cap = d_cap + jnp.where((row_c == 16 * c + 15) & (z == 3), dt_hidden[c:c + 1], 0.0)
    dcap_ref[...] = d_cap
    first = (z == 0).astype(F32)
    sums_ref[8:9] = dv8 * first
    sums_ref[9:10] = dv9 * first
    sums_ref[10:11] = dv10 * first
    sums_ref[11:12] = tv0
    sums_ref[12:13] = tv1
    sums_ref[13:14] = tv2 * first
    sums_ref[14:15] = tv3 * first
    sums_ref[15:16] = tv4 * first
    sums_ref[16:17] = tv5 * first
    sums_ref[17:18] = tv6 * first
    own_row = lambda a: sum(jnp.where(z == q, a[q:q + 1].astype(F32), 0.0) for q in range(4))
    pick = lambda a: a[:, 0:part].astype(F32)
    wide = jnp.concatenate
    pieces = [
        dh_upper, dt_upper.astype(F32), h_active.astype(F32), t_active.astype(F32),
        wide([pick(d_pooled), pick(pooled), pick(dt_q), pick(t_q)], 1),
        wide([pick(dt_mixed), pick(t_mixed), jnp.broadcast_to(pick(dq_my), (4, part)), jnp.broadcast_to(pick(p_q), (4, part))], 1),
        own_row(h_normed), own_row(d_start), own_row(t_last), own_row(t_second),
        own_row(dt_attend), own_row(dt_branch), own_row(t_final), pad1,
        used, t_used, tk_used, p_used,
    ]
    rows_ref[...] = jnp.concatenate(pieces, 0).astype(BF)
    for copy in started:
        copy.wait_send()

def middle(final, block_out, tokens, tp, downs, outs, ivec, tvec, pbias, tbias, label, temp, cid, n_dp):
    length, width = final.shape
    v, hbm = pl.BlockSpec(memory_space=pltpu.VMEM), pl.BlockSpec(memory_space=pl.ANY)
    f = lambda *s: jax.ShapeDtypeStruct(s, F32)
    return pl.pallas_call(
        middle_kernel,
        in_specs=[hbm, hbm, v, hbm, hbm] + [v] * 6 + [pl.BlockSpec(memory_space=pltpu.SMEM)],
        out_specs=[v] * 7,
        out_shape=[f(length, width), jax.ShapeDtypeStruct((length, width), BF), jax.ShapeDtypeStruct((ROWS, width), BF), f(24, width), f(64, width), f(8, 128), f(8 * n_dp, width)],
        scratch_shapes=[
            pltpu.VMEM((256, width), F32), pltpu.VMEM((256, width), BF),
            pltpu.VMEM((12, 4, 4, width), F32), pltpu.VMEM((12, 4, 4, width), F32),
            pltpu.VMEM((8, width), F32), pltpu.VMEM((n_dp, 8, width), F32),
            pltpu.VMEM((length, 128), F32), pltpu.VMEM((4, 64, width), BF),
            pltpu.VMEM((length, width), BF), pltpu.VMEM((length, width), F32), pltpu.VMEM(tp.shape, BF), pltpu.VMEM(downs.shape, BF),
            pltpu.SemaphoreType.DMA((16, 8)), pltpu.SemaphoreType.DMA((16, 8)), pltpu.SemaphoreType.DMA((5,)),
        ],
        compiler_params=pltpu.CompilerParams(collective_id=cid, has_side_effects=True, vmem_limit_bytes=50 << 20),
    )(final, block_out, tokens, tp, downs, outs, ivec, tvec, pbias, tbias, label, temp)


def plane_moves(me, out, s):
    y, x, c = me.y, me.x, me.c
    n = out.shape[-1] // 2
    left, right = (lambda r: r.at[..., 0:n]), (lambda r: r.at[..., n : 2 * n])
    if s == 3:
        own = out.at[y, x, c]
        yield 6, left(own), left(own), me.at_x, None, left(out.at[y, 1 - x, c]), None
        yield 7, right(own), right(own), me.at_y, None, right(out.at[1 - y, x, c]), None
    elif s == 4:
        own = out.at[y, :, c]
        yield 8, left(own), left(own), me.at_y, None, left(out.at[1 - y, :, c]), None
        own = out.at[:, x, c]
        yield 9, right(own), right(own), me.at_x, None, right(out.at[:, 1 - x, c]), None
    else:
        mine = out.at[:, :, c]
        yield 10, mine, mine, me.at_c, None, out.at[:, :, 1 - c], None


def turn_moves(me, src, home, split):
    z = me.z
    for k in (3, 2, 1):
        to, fro = (z + k) % 4, (z + 4 - k) % 4
        yield k - 1, src.at[to] if split else src, home.at[z], me.at_z(k), None, home.at[fro], None


def run_moves(moves, act, send, recv):
    for slot, src, dst, dev, go, come, arrives in moves:
        make = lambda a, b: pltpu.make_async_remote_copy(
            a, b, send.at[slot], recv.at[slot], device_id=dev, device_id_type=MESH
        )
        if act == "arrived":
            copy, when = make(src, come).wait_recv, arrives
        else:
            copy, when = getattr(make(src, dst), "start" if act == "start" else "wait_send"), go
        if when is None:
            copy()
        else:
            pl.when(when)(lambda: copy())


class Spread:
    stages = 6

    def __init__(self, me, src, out, send, recv, local):
        self.me, self.src, self.out, self.send, self.recv, self.local = me, src, out, send, recv, local

    def moves(self, s):
        me, out = self.me, self.out
        y, x, c, z = me.y, me.x, me.c, me.z
        if s < 3:
            home = out.at[y, x, c]
            for up in (True, False):
                step = -s if up else s
                slab, come = z + step, z + step + (-1 if up else 1)
                go = ((slab >= 0) & (z < 3)) if up else ((slab < 4) & (z > 0))
                arrives = (come >= 0) & (come < 4)
                slab, come = jnp.clip(slab, 0, 3), jnp.clip(come, 0, 3)
                src = self.src if s == 0 else home.at[slab]
                yield s + (0 if up else 3), src, home.at[slab], me.at_z(1 if up else 3), go, home.at[come], arrives
        else:
            yield from plane_moves(me, out, s)

    def each(self, s, act):
        run_moves(self.moves(s), act, self.send, self.recv)

    def keep(self):
        me = self.me
        return pltpu.make_async_copy(self.src, self.out.at[me.y, me.x, me.c, me.z], self.local)

    def begin(self, s):
        if s == 0:
            self.keep().start()
        else:
            self.each(s - 1, "arrived")
        if s == 3:
            self.keep().wait()
        self.each(s, "start")

    def finish(self):
        self.each(5, "arrived")
        for s in range(6):
            self.each(s, "sent")


class Reduce:
    def __init__(self, me, g, own, acc, from_c, from_1, from_2, from_z, send, recv, local):
        self.me, self.g, self.own, self.acc = me, g, own, acc
        self.from_c, self.from_1, self.from_2, self.from_z = from_c, from_1, from_2, from_z
        self.send, self.recv, self.local = send, recv, local
        self.size = acc.shape[-1]
        self.left, self.right = slice(0, self.size // 2), slice(self.size // 2, self.size)

    def moves(self, n, stage):
        me, acc = self.me, self.acc.at[n]
        y, x, z = me.y, me.x, me.z
        if stage == "core":
            src = self.g.at[:, :, 1 - me.c, :, :, n * self.size : (n + 1) * self.size]
            yield 0, src, self.from_c.at[n], me.at_c, None, self.from_c.at[n], None
        elif stage == "one":
            a, b = self.from_1.at[n, 0], self.from_1.at[n, 1]
            yield 1, acc.at[1 - y, :, :, :, self.left], a, me.at_y, None, a, None
            yield 2, acc.at[:, 1 - x, :, :, self.right], b, me.at_x, None, b, None
        elif stage == "two":
            a, b = self.from_2.at[n, 0], self.from_2.at[n, 1]
            yield 3, acc.at[y, 1 - x, :, :, self.left], a, me.at_x, None, a, None
            yield 4, acc.at[1 - y, x, :, :, self.right], b, me.at_y, None, b, None
        else:
            for k in (3, 2, 1):
                got = self.from_z.at[n, k - 1]
                yield 4 + k, acc.at[y, x, (z + k) % 4], got, me.at_z(k), None, got, None

    def act(self, n, stage, what):
        run_moves(self.moves(n, stage), what, self.send.at[n], self.recv.at[n])

    def keep(self, n):
        src = self.g.at[:, :, self.me.c, :, :, n * self.size : (n + 1) * self.size]
        return pltpu.make_async_copy(src, self.acc.at[n], self.local.at[n])

    def start(self, n, stage):
        if stage == "core":
            self.keep(n).start()
        self.act(n, stage, "start")

    def done(self, n, stage):
        me, acc = self.me, self.acc
        y, x = me.y, me.x
        f32 = lambda v: v.astype(F32)

        def each(count, body):
            lax.fori_loop(0, count, lambda q, carry: body(q) or carry, 0)

        if stage == "core":
            self.keep(n).wait()
        self.act(n, stage, "arrived")
        if stage == "core":

            def add(q):
                for a in range(2):
                    for b in range(2):
                        acc[n, a, b, q] = (f32(acc[n, a, b, q]) + f32(self.from_c[n, a, b, q])).astype(BF)

            each(4, add)
        elif stage == "one":

            def add(q):
                for b in range(2):
                    at = (n, y, b, q, slice(None), self.left)
                    acc[at] = (f32(acc[at]) + f32(self.from_1[n, 0, b, q])).astype(BF)
                    at = (n, b, x, q, slice(None), self.right)
                    acc[at] = (f32(acc[at]) + f32(self.from_1[n, 1, b, q])).astype(BF)

            each(4, add)
        elif stage == "two":

            def add(q):
                for half, cut in enumerate((self.left, self.right)):
                    at = (n, y, x, q, slice(None), cut)
                    acc[at] = (f32(acc[at]) + f32(self.from_2[n, half, q])).astype(BF)

            each(4, add)
        else:
            total = f32(acc[n, y, x, me.z])
            for k in range(3):
                total += f32(self.from_z[n, k])
            self.own[:, n * self.size : (n + 1) * self.size] = total

    def finish(self, n):
        for stage in ("core", "one", "two", "z"):
            self.act(n, stage, "sent")


REDUCE_STEPS = {
    0: [("start", 0, "core"), ("start", 1, "core")],
    1: [("done", 0, "core"), ("start", 0, "one")],
    2: [("done", 1, "core")],
    3: [("start", 1, "one")],
    5: [("done", 0, "one"), ("start", 0, "two")],
    7: [("done", 1, "one"), ("done", 0, "two"), ("start", 0, "z"), ("start", 1, "two")],
    9: [("done", 1, "two"), ("start", 1, "z")],
    12: [("done", 0, "z"), ("done", 1, "z")],
}
CHUNKS = 2


def attend_bwd_kernel_hosting(q_ref, k_ref, v_ref, do_ref, lse_ref, d_ref, g_ref, rows_ref, dq_ref, dk_ref, dv_ref, own_ref, all_ref,
                              acc, from_c, from_1, from_2, from_z, send, recv, local, rows_send, rows_recv, rows_local):
    h_at = pl.program_id(0)
    me = Place()
    spread = Spread(me, rows_ref, all_ref, rows_send, rows_recv, rows_local)
    reduce = Reduce(me, g_ref, own_ref, acc, from_c, from_1, from_2, from_z, send, recv, local)

    def tick(step):
        if step not in REDUCE_STEPS:
            return

        def go():
            if step == 0:
                greet([me.at_z(1), me.at_z(2), me.at_z(3), me.at_x, me.at_y, me.at_c])
            for what, n, stage in REDUCE_STEPS[step]:
                getattr(reduce, what)(n, stage)

        pl.when(h_at == step // 2)(go)

    for step in range(0, 12, 2):
        tick(step)
    for s in range(6):
        pl.when(h_at == s)(partial(spread.begin, s))
    q = q_ref[...] * 0.125
    k, v, do = k_ref[...], v_ref[...], do_ref[...]
    lane = lax.broadcasted_iota(jnp.int32, k.shape, 1)
    low = lane < 64
    for h in range(2):
        if h == 1:
            for step in range(1, 12, 2):
                tick(step)
        keep = low if h == 0 else ~low
        s = mm(jnp.where(keep, k, jnp.zeros_like(k)), q, 1, 1)
        p = jnp.exp(s - lse_ref[0, h : h + 1, :])
        dp = mm(jnp.where(keep, v, jnp.zeros_like(v)), do, 1, 1)
        ds = (p * (dp - d_ref[0, h : h + 1, :])).astype(BF)
        d_v = mm(p.astype(BF), do).astype(BF)
        d_k = mm(ds, q).astype(BF)
        d_q = (mm(ds, k, 0, 0) * 0.125).astype(BF)
        for ref, value in ((dq_ref, d_q), (dk_ref, d_k), (dv_ref, d_v)):
            ref[...] = value if h == 0 else jnp.where(low, ref[...], value)

    def last():
        for what, n, stage in REDUCE_STEPS[12]:
            getattr(reduce, what)(n, stage)
        for n in range(CHUNKS):
            reduce.finish(n)
        spread.finish()

    pl.when(h_at == pl.num_programs(0) - 1)(last)


def attend_bwd_and_reduce(proj, d_out, lse, inner, g, own_rows, cid):
    length, width = proj.shape[0], proj.shape[1] // 3
    pairs = width // 128
    rows, n = g.shape[0] // 32, g.shape[1]
    size = n // CHUNKS
    block = lambda part: pl.BlockSpec((length, 128), lambda h: (0, part * pairs + h))
    row = pl.BlockSpec((1, 2, length), lambda h: (h, 0, 0))
    hbm = pl.BlockSpec(memory_space=pl.ANY)
    result = jax.ShapeDtypeStruct((length, width), BF)
    v = lambda *s: pltpu.VMEM(s, BF)
    return pl.pallas_call(
        attend_bwd_kernel_hosting,
        grid=(pairs,),
        in_specs=[block(0), block(1), block(2), block(0), row, row, hbm, hbm],
        out_specs=[block(0)] * 3 + [pl.BlockSpec((rows, n), lambda h: (0, 0)), hbm],
        out_shape=[result] * 3
        + [jax.ShapeDtypeStruct((rows, n), F32), jax.ShapeDtypeStruct((2, 2, 2, 4) + own_rows.shape, BF)],
        scratch_shapes=[
            v(CHUNKS, 2, 2, 4, rows, size), v(CHUNKS, 2, 2, 4, rows, size), v(CHUNKS, 2, 2, 4, rows, size // 2),
            v(CHUNKS, 2, 4, rows, size // 2), v(CHUNKS, 3, rows, size),
            pltpu.SemaphoreType.DMA((CHUNKS, 8)), pltpu.SemaphoreType.DMA((CHUNKS, 8)), pltpu.SemaphoreType.DMA((CHUNKS,)),
            pltpu.SemaphoreType.DMA((11,)), pltpu.SemaphoreType.DMA((11,)), pltpu.SemaphoreType.DMA,
        ],
        compiler_params=pltpu.CompilerParams(collective_id=cid, has_side_effects=True, vmem_limit_bytes=60 << 20),
    )(proj, proj, proj, d_out, lse, inner, g.reshape(2, 2, 2, 4, rows, n), own_rows)


def attend_fwd_kernel_hosting(q_ref, k_ref, v_ref, split_ref, downs_ref, tokens_ref,
                              o_ref, lse_ref, tp_ref, down_ref, token_ref, send, recv, local):
    h_at = pl.program_id(0)
    me = Place()
    home = tp_ref.at[me.y, me.x, me.c]
    down_home = down_ref.at[me.y, me.x, me.c]
    keeps = [
        pltpu.make_async_copy(split_ref.at[me.z], home.at[me.z], local.at[0]),
        pltpu.make_async_copy(downs_ref, down_home, local.at[1]),
        pltpu.make_async_copy(tokens_ref, token_ref.at[me.z], local.at[2]),
    ]
    groups = {
        "split": (lambda: turn_moves(me, split_ref, home, True), 0),
        "tokens": (lambda: turn_moves(me, tokens_ref, token_ref, False), 2),
        "split_xy": (lambda: plane_moves(me, tp_ref, 3), 0),
        "down_one": (lambda: plane_moves(me, down_ref, 3), 1),
        "down_two": (lambda: plane_moves(me, down_ref, 4), 1),
        "down_core": (lambda: plane_moves(me, down_ref, 5), 1),
    }

    def act(name, what):
        moves, a = groups[name]
        run_moves(moves(), what, send.at[a], recv.at[a])

    def first():
        greet([me.at_z(1), me.at_z(2), me.at_z(3), me.at_x, me.at_y, me.at_c])
        for keep in keeps:
            keep.start()
        act("split", "start")
        keeps[1].wait()
        act("down_one", "start")

    def second_step():
        act("down_one", "arrived")
        act("down_two", "start")

    def middle_step():
        act("split", "arrived")
        keeps[0].wait()
        act("split_xy", "start")
        act("tokens", "start")

    def fifth_step():
        act("down_two", "arrived")
        act("down_core", "start")

    def last():
        for name in ("split_xy", "down_core", "tokens"):
            act(name, "arrived")
        keeps[2].wait()
        for name in groups:
            act(name, "sent")

    pl.when(h_at == 0)(first)
    pl.when(h_at == 2)(second_step)
    pl.when(h_at == 3)(middle_step)
    pl.when(h_at == 5)(fifth_step)
    attend_fwd_kernel(q_ref, k_ref, v_ref, o_ref, lse_ref)
    pl.when(h_at == pl.num_programs(0) - 1)(last)


def attend_fwd_and_gather(proj, split, downs, tokens, cid):
    length, width = proj.shape[0], proj.shape[1] // 3
    pairs = width // 128
    block = lambda part: pl.BlockSpec((length, 128), lambda h: (0, part * pairs + h))
    hbm = pl.BlockSpec(memory_space=pl.ANY)
    s = jax.ShapeDtypeStruct
    return pl.pallas_call(
        attend_fwd_kernel_hosting,
        grid=(pairs,),
        in_specs=[block(0), block(1), block(2), hbm, hbm, hbm],
        out_specs=[block(0), pl.BlockSpec((1, 2, length), lambda h: (h, 0, 0)), hbm, hbm, hbm],
        out_shape=[
            s((length, width), BF),
            s((pairs, 2, length), F32),
            s((2, 2, 2) + split.shape, BF),
            s((2, 2, 2) + downs.shape, BF),
            s((4,) + tokens.shape, BF),
        ],
        scratch_shapes=[pltpu.SemaphoreType.DMA((3, 11)), pltpu.SemaphoreType.DMA((3, 11)), pltpu.SemaphoreType.DMA((3,))],
        compiler_params=pltpu.CompilerParams(collective_id=cid, has_side_effects=True, vmem_limit_bytes=48 << 20),
    )(proj, proj, proj, split, downs, tokens)


def mlp_fwd_kernel(x_ref, mixed_ref, wo_ref, wu_ref, wd_ref, bias_ref, vec_ref, tp_in,
                   hidden_ref, second_ref, active_ref, slope_ref, block_ref, final_ref, tp_ref, total, send, recv):
    k = pl.program_id(0)
    me = Place()

    def act(s, what):
        run_moves(plane_moves(me, tp_ref, s), what, send, recv)

    def first():
        greet([me.at_x, me.at_y, me.at_c])
        act(4, "start")

    def then():
        act(4, "arrived")
        act(5, "start")

    pl.when(k == 0)(first)
    pl.when(k == pl.num_programs(0) - 1)(then)
    vec = vec_ref[...]

    @pl.when(k == 0)
    def _():
        hidden = x_ref[...].astype(F32) + mm(mixed_ref[...], wo_ref[...])
        hidden_ref[...] = hidden
        second_ref[...] = layer_norm(hidden, vec[2:3], vec[3:4]).astype(BF)
        total[...] = hidden + vec[4:5]

    value, slope = gelu_pair(mm(second_ref[...], wu_ref[...]) + bias_ref[0])
    active = value.astype(BF)
    active_ref[...] = active
    slope_ref[...] = slope.astype(BF)
    total[...] += mm(active, wd_ref[...])

    @pl.when(k == pl.num_programs(0) - 1)
    def _():
        block_ref[...] = total[...]
        final_ref[...] = layer_norm(total[...], vec[5:6], vec[6:7]).astype(BF)
        act(5, "arrived")
        act(4, "sent")
        act(5, "sent")


def mlp_fwd(x, mixed, main, bias, vec, fold, tp, cid):
    rows, width = mixed.shape
    whole = pl.BlockSpec((rows, width), lambda k: (0, 0))
    tile = pl.BlockSpec((rows, width), lambda k: (0, k))
    at = lambda f: pl.BlockSpec((width, width), lambda k: (0, f(k)))
    s = lambda n, t: jax.ShapeDtypeStruct((rows, n * width), t)
    hbm = pl.BlockSpec(memory_space=pl.ANY)
    return pl.pallas_call(
        mlp_fwd_kernel,
        grid=(fold,),
        in_specs=[whole, whole, at(lambda k: 0), at(lambda k: 1 + k), at(lambda k: 1 + fold + k),
                  pl.BlockSpec((1, 1, width), lambda k: (k, 0, 0)), pl.BlockSpec(vec.shape, lambda k: (0, 0)), hbm],
        out_specs=[whole, whole, tile, tile, whole, whole, hbm],
        out_shape=[s(1, F32), s(1, BF), s(fold, BF), s(fold, BF), s(1, F32), s(1, BF),
                   jax.ShapeDtypeStruct(tp.shape, BF)],
        scratch_shapes=[pltpu.VMEM((rows, width), F32), pltpu.SemaphoreType.DMA((11,)), pltpu.SemaphoreType.DMA((11,))],
        input_output_aliases={7: 6},
        compiler_params=pltpu.CompilerParams(collective_id=cid, has_side_effects=True, vmem_limit_bytes=56 << 20),
    )(x, mixed, main, main, main, bias.reshape(fold, 1, width), vec, tp)


def mlp_bwd_kernel(dy_ref, branch_ref, active_ref, slope_ref, second_ref, hidden_ref, mixed_ref,
                   wo_ref, wu_ref, wd_ref, vec_ref,
                   g_ref, gs_ref, dhid_ref, dmix_ref, inner_ref, bias_ref, dvec_ref, total, dy_in, hid_in, mix_in, slots, fetch, leave):
    k = pl.program_id(0)
    fold = pl.num_programs(0)
    pairs = ((dy_ref, dy_in), (hidden_ref, hid_in), (mixed_ref, mix_in))
    loads = [pltpu.make_async_copy(src, dst, fetch.at[n]) for n, (src, dst) in enumerate(pairs)]

    @pl.when(k == 0)
    def _():
        for load in loads:
            load.start()

    width = mixed_ref.shape[1]

    def leaves(n):
        at = pl.ds(pl.multiple_of((n + 1) * width, width), width)
        return pltpu.make_async_copy(slots.at[n % 2], gs_ref.at[:, at], leave.at[n % 2])

    pl.when(k >= 2)(lambda: leaves(k - 2).wait())
    branch = branch_ref[...]
    columns = lambda n: pl.ds(pl.multiple_of(n * width, width), width)
    slots[k % 2] = mm(active_ref[...], branch, 0, 0).astype(BF)
    leaves(k).start()
    d_upper_f = mm(branch, wd_ref[...], 1, 1) * slope_ref[...].astype(F32)
    bias_ref[0] = jnp.sum(d_upper_f, 0, keepdims=True)
    d_upper = d_upper_f.astype(BF)
    g_ref[...] = mm(second_ref[...], d_upper, 0, 0).astype(BF)
    back = mm(d_upper, wu_ref[...], 1, 1)

    @pl.when(k == 0)
    def _():
        total[...] = back

    @pl.when(k > 0)
    def _():
        total[...] += back

    @pl.when(k == fold - 1)
    def _():
        vec = vec_ref[...]
        for load in loads:
            load.wait()
        d_hidden, gain, shift = norm_back_rows(hid_in[...], vec[2:3], total[...])
        dvec_ref[0:1] = gain
        dvec_ref[1:2] = shift
        d_hidden = dy_in[...] + d_hidden
        dhid_ref[...] = d_hidden
        d_attend = d_hidden.astype(BF)
        mixed = mix_in[...]
        leaves(fold - 2).wait()
        slots[fold % 2] = mm(mixed, d_attend, 0, 0).astype(BF)
        out = pltpu.make_async_copy(slots.at[fold % 2], gs_ref.at[:, 0:width], leave.at[2])
        out.start()
        d_mixed = mm(d_attend, wo_ref[...], 1, 1).astype(BF)
        dmix_ref[...] = d_mixed
        head = lax.broadcasted_iota(jnp.int32, (16, width), 0)
        lane = lax.broadcasted_iota(jnp.int32, (16, width), 1)
        own = (lane // (width // HEADS) == head).astype(BF)
        high, low = split_two(d_mixed.astype(F32) * mixed.astype(F32))
        sums = mm(own, high, 1, 1) + mm(own, low, 1, 1)
        for h in range(HEADS // 2):
            inner_ref[h] = sums[2 * h : 2 * h + 2]
        leaves(fold - 1).wait()
        out.wait()


def mlp_bwd(dy, branch, active, slope, second, hidden, mixed, main, vec, fold):
    rows, width = mixed.shape
    whole = pl.BlockSpec((rows, width), lambda k: (0, 0))
    tile = pl.BlockSpec((rows, width), lambda k: (0, k))
    at = lambda f: pl.BlockSpec((width, width), lambda k: (0, f(k)))
    f = lambda *s: jax.ShapeDtypeStruct(s, F32)
    hbm = pl.BlockSpec(memory_space=pl.ANY)
    return pl.pallas_call(
        mlp_bwd_kernel,
        grid=(fold,),
        in_specs=[hbm, whole, tile, tile, whole, hbm, hbm,
                  at(lambda k: 0), at(lambda k: 1 + k), at(lambda k: 1 + fold + k), pl.BlockSpec(vec.shape, lambda k: (0, 0))],
        out_specs=[at(lambda k: k), hbm, whole, whole,
                   pl.BlockSpec((HEADS // 2, 2, rows), lambda k: (0, 0, 0)),
                   pl.BlockSpec((1, 1, width), lambda k: (k, 0, 0)), pl.BlockSpec((8, width), lambda k: (0, 0))],
        out_shape=[jax.ShapeDtypeStruct((width, fold * width), BF), jax.ShapeDtypeStruct((width, (1 + fold) * width), BF), f(rows, width),
                   jax.ShapeDtypeStruct((rows, width), BF), f(HEADS // 2, 2, rows), f(fold, 1, width), f(8, width)],
        scratch_shapes=[pltpu.VMEM((rows, width), F32), pltpu.VMEM((rows, width), F32), pltpu.VMEM((rows, width), F32),
                        pltpu.VMEM((rows, width), BF), pltpu.VMEM((2, width, width), BF),
                        pltpu.SemaphoreType.DMA((3,)), pltpu.SemaphoreType.DMA((3,))],
        compiler_params=pltpu.CompilerParams(vmem_limit_bytes=60 << 20),
    )(dy, branch, active, slope, second, hidden, mixed, main, main, main, vec)


def finish_kernel(dq_ref, dk_ref, dv_ref, normed_ref, w_ref, x_ref, dhid_ref, rows_ref, sums_ref, vec_ref, dimage_ref, dtext_ref, own_ref, moved_ref, *rest):
    outer_refs, rest = rest[:13], rest[13:]
    (g, dx, from_c, acc_c, from_1, from_2, from_z, q_in, k_in, v_in, n_in, w_in, x_in, h_in, r_in, turned,
     send, recv, local, fetch) = rest
    me = Place()
    pairs = ((dq_ref, q_in), (normed_ref, n_in), (dk_ref, k_in), (dv_ref, v_in), (w_ref, w_in), (x_ref, x_in), (dhid_ref, h_in), (rows_ref, r_in))
    loads = [pltpu.make_async_copy(src, dst, fetch.at[n]) for n, (src, dst) in enumerate(pairs)]
    for load in loads:
        load.start()
    dq_ref, dk_ref, dv_ref, normed_ref, w_ref, x_ref, dhid_ref = q_in, k_in, v_in, n_in, w_in, x_in, h_in
    y, x, c, z = me.y, me.x, me.c, me.z
    width = dq_ref.shape[1]
    part = g.shape[4]
    tile = dx.shape[1]
    half = g.shape[-1] // 2
    left, right = slice(0, half), slice(half, 2 * half)
    f32 = lambda v: v.astype(F32)
    started = []
    greet([me.at_z(1), me.at_z(2), me.at_z(3), me.at_x, me.at_y, me.at_c])

    def push(slot, src, dst, dev, arriving):
        copy = pltpu.make_async_remote_copy(src, dst, send.at[slot], recv.at[slot], device_id=dev, device_id_type=MESH)
        copy.start()
        started.append(copy)
        return pltpu.make_async_remote_copy(src, arriving, send.at[slot], recv.at[slot], device_id=dev, device_id_type=MESH)

    def put(value, first):
        for p in range(32):
            i, q = p // 4, p % 4
            g[i // 4, (i // 2) % 2, i % 2, q, :, first : first + value.shape[1]] = value[part * p : part * (p + 1)].astype(BF)

    gain, shift, moves = [], [], []

    def d_x_rows(k):
        to, fro = (z + k) % 4, (z + 4 - k) % 4
        at = pl.ds(pl.multiple_of(to * tile, tile), tile)
        back = None
        for n, ref in enumerate((dq_ref, dk_ref, dv_ref)):
            term = mm(ref[at, :], w_ref[:, n * width : (n + 1) * width], 1, 1)
            back = term if back is None else back + term
        d_x, a, b = norm_back_rows(x_ref[at, :].astype(F32), vec_ref[0:1], back)
        gain.append(a)
        shift.append(b)
        dx[to] = (dhid_ref[at, :] + d_x).astype(BF)
        if k:
            moves.append(push(k, dx.at[to], moved_ref.at[z], me.at_z(k), moved_ref.at[fro]))
        else:
            keep.start()

    keep = pltpu.make_async_copy(dx.at[z], moved_ref.at[z], local)

    def add(at, value):
        acc_c[at] = (f32(acc_c[at]) + f32(value)).astype(BF)

    def core(cut, slot):
        to = from_c.at[:, :, :, :, cut]
        return push(slot, g.at[:, :, 1 - c, :, :, cut], to, me.at_c, to)

    def core_done(arrive, cut):
        arrive.wait_recv()
        for a in range(2):
            for b in range(2):
                for q in range(4):
                    at = (a, b, q, slice(None), cut)
                    acc_c[at] = (f32(g[a, b, c, q, :, cut]) + f32(from_c[at])).astype(BF)

    def one_done(arrive, n, cut):
        arrive.wait_recv()
        for b in range(2):
            for q in range(4):
                add((b, x, q, slice(None), cut) if n else (y, b, q, slice(None), cut), from_1[n, b, q])

    def two_done(arrive, n, cut):
        arrive.wait_recv()
        for q in range(4):
            add((y, x, q, slice(None), cut), from_2[n, q])

    def along(cut, slot):
        arrives = []
        for k in (3, 2, 1):
            got = from_z.at[k - 1, :, cut]
            arrives.append(push(slot + k, acc_c.at[y, x, (z + k) % 4, :, cut], got, me.at_z(k), got))
        return arrives

    part_of = lambda n, ref: put(mm(normed_ref[...], ref[...], 0, 0), n * width)
    loads[0].wait()
    loads[1].wait()
    part_of(0, dq_ref)
    loads[2].wait()
    part_of(1, dk_ref)
    for load in loads[3:7]:
        load.wait()
    core_left = core(left, 0)
    d_x_rows(2)
    part_of(2, dv_ref)
    core_done(core_left, left)
    one_left = push(4, acc_c.at[1 - y, :, :, :, left], from_1.at[0], me.at_y, from_1.at[0])
    d_x_rows(3)
    d_x_rows(1)
    d_x_rows(0)
    sums = jnp.concatenate([sum(gain), sum(shift), sums_ref[2:, :]], 0)
    sums = jnp.concatenate([sums, jnp.zeros((128 - sums.shape[0], width), F32)], 0)
    put(jnp.transpose(sums), 3 * width)
    put(jnp.zeros((width, 128), F32), 3 * width + 128)
    core_right = core(right, 8)
    one_done(one_left, 0, left)
    two_left = push(6, acc_c.at[y, 1 - x, :, :, left], from_2.at[0], me.at_x, from_2.at[0])
    core_done(core_right, right)
    one_right = push(5, acc_c.at[:, 1 - x, :, :, right], from_1.at[1], me.at_x, from_1.at[1])
    loads[7].wait()
    group = 16
    count = 32 * group
    to, fro = lax.broadcasted_iota(jnp.int32, (count, count), 0), lax.broadcasted_iota(jnp.int32, (count, count), 1)
    turn = ((to % 32 == fro // group) & (to // 32 == fro % group)).astype(BF)
    for n in range(r_in.shape[1] // group):
        value = mm(turn, r_in[:, n * group : (n + 1) * group, :].reshape(count, width)).astype(BF)
        turned[n * group : (n + 1) * group] = value.reshape(group, 32, width)
    two_done(two_left, 0, left)
    z_left = along(left, 8)
    one_done(one_right, 1, right)
    two_right = push(7, acc_c.at[1 - y, x, :, :, right], from_2.at[1], me.at_y, from_2.at[1])
    outer_kernel(turned, dimage_ref, dtext_ref, *outer_refs)
    two_done(two_right, 1, right)
    z_right = along(right, 11)
    for arrive in z_left + z_right:
        arrive.wait_recv()
    total = f32(acc_c[y, x, z]) + f32(from_z[0]) + f32(from_z[1]) + f32(from_z[2])
    own_ref[...] = total
    keep.wait()
    for arrive in moves:
        arrive.wait_recv()
    for copy in started:
        copy.wait_send()


def finish_image(dq, dk, dv, normed, w_in, x, d_hidden, own_rows, sums, vec, d_image, d_text, cid):
    rows, width = dq.shape
    part, n, quarter = width // 32, 3 * width + 256, width // 4
    f = lambda *s: jax.ShapeDtypeStruct(s, F32)
    v, hbm = pl.BlockSpec(memory_space=pltpu.VMEM), pl.BlockSpec(memory_space=pl.ANY)
    s = lambda *shape: pltpu.VMEM(shape, BF)
    return pl.pallas_call(
        finish_kernel,
        in_specs=[hbm] * 8 + [v] * 4,
        out_specs=[v, hbm] + [v] * 13,
        out_shape=[jax.ShapeDtypeStruct((part, n), F32), jax.ShapeDtypeStruct((4, rows // 4, width), BF),
                   f(4, part, width), f(4, part, width), f(4 * part, width), f(4 * part, width), f(part, width), f(part, width),
                   f(part, width), f(4, part, quarter), f(4, part, quarter), f(4, part, quarter), f(4, part, quarter),
                   f(part, 128), f(2, 4 * part, 128)],
        scratch_shapes=[
            s(2, 2, 2, 4, part, n), s(4, rows // 4, width), s(2, 2, 4, part, n), s(2, 2, 4, part, n),
            s(2, 2, 4, part, n // 2), s(2, 4, part, n // 2), s(3, part, n),
            s(rows, width), s(rows, width), s(rows, width), s(rows, width), s(width, 3 * width), s(rows, width),
            pltpu.VMEM((rows, width), F32), s(32, ROWS, width), s(ROWS, 32, width),
            pltpu.SemaphoreType.DMA((15,)), pltpu.SemaphoreType.DMA((15,)), pltpu.SemaphoreType.DMA, pltpu.SemaphoreType.DMA((8,)),
        ],
        compiler_params=pltpu.CompilerParams(collective_id=cid, has_side_effects=True, vmem_limit_bytes=60 << 20),
    )(dq, dk, dv, normed, w_in, x, d_hidden, own_rows, sums, vec, d_image, d_text)


def outer_kernel(rows_ref, dimage_ref, dtext_ref,
                 pup_ref, tup_ref, pdown_ref, tdown_ref, pout_ref, tout_ref, thead_ref,
                 tq_ref, tk_ref, tv_ref, pv_ref, pk_ref, bias_ref):
    at_dp, z = lax.axis_index("dp"), lax.axis_index("seq")
    n_dp, n_z = 8, 4
    me = at_dp * n_z + z
    width = rows_ref.shape[2]
    part, quarter = width // 32, width // n_z
    wide_part = 4 * part
    n = n_dp * n_z
    each = quarter // part

    def iota(shape, d):
        return lax.broadcasted_iota(jnp.int32, shape, d)

    def selector(count, first):
        return (iota((count, width), 1) == iota((count, width), 0) + first).astype(BF)

    def group(r):
        return jnp.concatenate([rows_ref[r + c] for c in range(4)], 0)

    cols = jnp.concatenate(
        [mm(selector(part, part * me), rows_ref[r], 1, 1) for r in range(24, 80)], 1
    ).astype(BF)
    get = lambda r, count=1: cols[:, n * (r - 24) : n * (r - 24 + count)]
    a, b = iota((4 * n, n), 0), iota((4 * n, n), 1)
    same = ((a % n) // n_z == b // n_z) & (a // n == b % n_z)
    keep = lambda which: (same & (a % n_z == which)).astype(BF)
    units = selector(wide_part, wide_part * at_dp)
    heads = selector(part, quarter + part * (me % each))
    to_mine, to_head = keep(z), keep(me // each)
    chosen = lambda sel, r, perm: mm(mm(sel, group(r), 1, 1).astype(BF), perm).astype(BF)
    pdown_ref[...] = mm(chosen(units, 8, to_mine), dimage_ref[...])
    tdown_ref[...] = mm(chosen(units, 12, to_mine), rows_ref[29])
    pout_ref[...] = mm(chosen(heads, 16, to_head), rows_ref[25])
    tout_ref[...] = mm(chosen(heads, 20, to_head), rows_ref[28])
    thead_ref[...] = mm(get(30), dtext_ref[...])
    ones = jnp.ones((n, 128), BF)
    bias_ref[0] = mm(chosen(units, 0, to_mine), ones)
    bias_ref[1] = mm(chosen(units, 4, to_mine), ones)
    a, b = iota((n, 4 * n), 0), iota((n, 4 * n), 1)
    spread = ((b % n) // n_z == a // n_z) & (b // n == a % n_z)
    spread = spread.astype(BF)
    lane_z = iota((1, 4 * n), 1) % n_z
    masks = [(lane_z == q).astype(BF) for q in range(n_z)]

    def blocks(values):
        return jnp.concatenate([v * m for v, m in zip(values, masks)], 0)

    by_image = lambda r: mm(get(r), spread).astype(BF)
    g16, g20 = group(16), group(20)

    def put(ref, value, first):
        for q in range(n_z):
            ref[q] = value[q * part : (q + 1) * part, first : first + ref.shape[2]]

    put(pup_ref, mm(blocks([by_image(24)] * 4), group(0)), 0)
    put(tup_ref, mm(blocks([by_image(27)] * 4), group(4)), 0)
    put(tq_ref, mm(blocks([by_image(26)] * 4), g16), 2 * quarter)
    lane = iota((1, width), 1)
    count = HEADS // n_z
    hw = quarter // count

    def by_head(values_of, rhs, first):
        total = None
        for h in range(count):
            own = ((lane >= first + hw * h) & (lane < first + hw * h + hw)).astype(F32)
            one = mm(blocks(values_of(h)), rhs) * own
            total = one if total is None else total + one
        return total

    put(tk_ref, by_head(lambda h: [get(56 + 4 * h, 4)] * 4, g16, 3 * quarter), 3 * quarter)
    put(tv_ref, by_head(lambda h: [get(44 + 4 * h, 4)] * 4, g20, 0), 0)
    put(pv_ref, by_head(lambda h: [by_image(32 + count * q + h) for q in range(n_z)], g16, 0), 0)
    a, b = iota((HEADS * n, 128), 0), iota((HEADS * n, 128), 1)
    pk_ref[...] = mm(get(68, HEADS), (a // n == b).astype(BF))


def fast_program(
    patches, captions, pairs,
    image_attend_in, image_attend_out, image_up_weight, image_up_bias, image_down_weight,
    image_vectors, probe_query_weight, probe_pair_weight, probe_out_weight, probe_up_weight,
    probe_up_bias, probe_down_weight, text_attend_in, text_attend_out, text_up_weight,
    text_up_bias, text_down_weight, text_vectors, text_head_weight, temp_bias,
):
    n_dp, n_z = lax.axis_size("dp"), lax.axis_size("seq")
    world = n_dp * n_z
    at_dp, at_z = lax.axis_index("dp"), lax.axis_index("seq")
    me = at_dp * n_z + at_z
    width = patches.shape[-1]
    head_width = width // HEADS
    hidden_width = image_up_weight.shape[1]
    part, quarter = width // world, width // n_z
    wide_part = hidden_width // world
    fold = hidden_width // width
    length = patches.shape[1] * n_z

    small = jnp.concatenate(
        [image_vectors.reshape(-1), text_vectors.reshape(-1), image_up_bias, probe_up_bias, text_up_bias]
    )
    sizes = [image_vectors.size, text_vectors.size, image_up_bias.size, probe_up_bias.size, text_up_bias.size]
    small = jnp.pad(small, (0, 2048 - small.shape[0])).reshape(16, 128)

    def by_units(w):
        return w.reshape(part, n_dp, n_z, wide_part).transpose(2, 0, 1, 3).reshape(n_z, part, width)

    def by_heads(w):
        cut = w.reshape(part, n_z, quarter).transpose(1, 0, 2)
        return jnp.pad(cut, ((0, 0), (0, 0), (0, 256 - quarter)))

    split = [by_units(probe_up_weight), by_units(text_up_weight)]
    split += [by_heads(text_attend_in[:, k * width : (k + 1) * width]) for k in range(3)]
    split += [by_heads(text_head_weight), by_heads(probe_query_weight)]
    split += [by_heads(probe_pair_weight[:, k * width : (k + 1) * width]) for k in range(2)]
    split = jnp.concatenate(split, 2)
    downs = jnp.concatenate([text_down_weight, probe_down_weight], 1)
    w_in, small_all, x = gather(
        [image_attend_in, small, patches],
        [("full", "S"), ("full", "C"), ("za", None)],
        [(0, 0), (1, 0), (0, 1), (1, 1), (0, 2), (1, 2), (0, 3), (2, 0), (1, 3), (0, 4), (1, 4), (0, 5), (1, 5)],
        1,
    )
    w_in = w_in.reshape(width, 3 * width)
    x = x.reshape(length, width)
    main = jnp.concatenate(
        [
            image_attend_out,
            image_up_weight.reshape(part, width, fold).transpose(0, 2, 1).reshape(part, hidden_width),
            image_down_weight.reshape(part, hidden_width),
            text_attend_out,
            probe_out_weight,
        ],
        1,
    )
    main = lax.all_gather(main, ALL, axis=0, tiled=True)
    outs = lax.dynamic_slice_in_dim(main[:, width + 2 * hidden_width :], at_z * quarter, quarter, 0)

    small_all = small_all.reshape(world, -1)
    cuts = [sum(sizes[:i]) for i in range(len(sizes) + 1)]
    pieces = [small_all[:, cuts[i] : cuts[i + 1]].astype(F32) for i in range(len(sizes))]
    ivec = pieces[0].reshape(world, -1, part).transpose(1, 0, 2).reshape(-1, width)
    tvec = pieces[1].reshape(world, -1, part).transpose(1, 0, 2).reshape(-1, width)
    i_bias = pieces[2].reshape(width, fold).T.reshape(1, hidden_width)

    def own_units(p):
        p = p.reshape(n_dp, n_z, wide_part)
        return lax.dynamic_index_in_dim(p, at_z, 1, False).reshape(1, width)

    p_bias, t_bias = own_units(pieces[3]), own_units(pieces[4])

    normed = layer_norm(x.astype(F32), ivec[0], ivec[1]).astype(BF)
    proj = mm(normed, w_in).astype(BF)
    mixed, lse, tp, downs, tokens = attend_fwd_and_gather(proj, split, downs, captions, 5)
    hidden, second, active, slope, block_out, final, tp = mlp_fwd(x, mixed, main, i_bias, ivec, fold, tp, 6)
    tp, downs = tp.reshape(width, -1), downs.reshape(width, -1)

    labels = (2 * pairs - 1).astype(F32).reshape(n_dp, n_z, n_dp, n_z)
    labels = jnp.pad(labels, ((0, 0), (0, n_z), (0, 0), (n_z, 0))).reshape(2 * world, 2 * world)
    dy, d_branch, rows, sums, d_captions, loss_row, d_embeds = middle(
        final, block_out, tokens.reshape(-1, width), tp, downs, outs, ivec, tvec, p_bias, t_bias, labels, temp_bias, 2, n_dp
    )
    loss, grad_temp = loss_row[0, 0], loss_row[0, 1:3]
    grad_captions = d_captions.reshape(captions.shape)

    g_up, g_rest, d_hidden, d_mixed, inner, g_bias, dvec = mlp_bwd(
        dy, d_branch, active, slope, second, hidden, mixed, main, ivec, fold
    )
    g_rest = lax.psum_scatter(g_rest, ALL, scatter_dimension=0, tiled=True).astype(F32)
    own_out = g_rest[:, :width]
    own_down = g_rest[:, width:].reshape(wide_part, width)
    d_q, d_k, d_v, own_up, rows = attend_bwd_and_reduce(proj, d_mixed, lse, inner, g_up, rows, 4)
    own_up = own_up.reshape(part, fold, width).transpose(0, 2, 1).reshape(part, hidden_width)
    rows = rows.reshape(world, ROWS, width)
    sums = jnp.concatenate([dvec[0:2], dvec[0:2], sums[4:], g_bias.reshape(fold, width)], 0)
    d_embeds = d_embeds.reshape(n_dp, 2, n_z, width).astype(BF)
    own_in, moved, *outer = finish_image(
        d_q, d_k, d_v, normed, w_in, x, d_hidden, rows, sums, ivec,
        d_embeds[:, 0].reshape(world, width), d_embeds[:, 1].reshape(world, width), 3
    )
    pup, tup, own_p_down, own_t_down, own_p_out, own_t_out, own_t_head, tq, tk, tv, pv, pk, biases = outer
    grad_patches = moved.astype(F32)
    own_sums = own_in[:, 3 * width : 3 * width + 128].T
    own_in = own_in[:, : 3 * width]

    def wide(g):
        return g.reshape(n_z, part, n_dp, wide_part).transpose(1, 2, 0, 3).reshape(part, hidden_width)

    own_p_up, own_t_up = wide(pup), wide(tup)
    own_t_in = jnp.stack([tq, tk, tv]).transpose(2, 0, 1, 3).reshape(part, 3 * width)
    row20 = rows[:, 20].reshape(n_dp, n_z, n_z, quarter).astype(F32)
    probe_query = row20[0, :, 3].reshape(HEADS, head_width)
    own_p_k = (pk[:, :HEADS, None] * probe_query[None]).reshape(part, width)
    own_p_pair = jnp.concatenate([own_p_k, pv.transpose(1, 0, 2).reshape(part, width)], 1)
    d_query = jnp.sum(row20[:, :, 2], 0).reshape(width)
    mine = lambda v, n: lax.dynamic_slice_in_dim(v, me * n, n, -1)
    own_p_query = mine(ivec[7], part)[:, None] * d_query[None, :]
    dv7 = jnp.sum(probe_query_weight.astype(F32) * d_query[None, :], 1)
    own_ivec = jnp.concatenate([own_sums[0:7], dv7[None], own_sums[8:11]], 0)
    own_tvec = own_sums[11:18]
    own_bias = own_sums[24 : 24 + fold].T.reshape(wide_part)
    return (
        loss, grad_patches, grad_captions,
        own_in, own_out, own_up, own_bias, own_down, own_ivec,
        own_p_query, own_p_pair, own_p_out, own_p_up, biases[0, :, 0], own_p_down,
        own_t_in, own_t_out, own_t_up, biases[1, :, 0], own_t_down, own_tvec, own_t_head,
        grad_temp,
    )


def solution(mesh):
    tokens, matrix, vector, table = P("dp", "seq", None), P(ALL, None), P(ALL), P(None, ALL)
    weights = (
        (matrix, matrix, matrix, vector, matrix, table, matrix, matrix, matrix, matrix, vector, matrix)
        + (matrix, matrix, matrix, vector, matrix, table, matrix)
    )
    return jax.shard_map(
        fast_program if mesh.shape["dp"] == 8 and mesh.shape["seq"] == 4 else device_program,
        mesh=mesh,
        in_specs=(tokens, tokens, P()) + weights + (P(),),
        out_specs=(P(), tokens, tokens) + weights + (P(),),
        check_vma=False,
    )
```

```python
from functools import partial

import jax
import jax.numpy as jnp
from jax import lax
from jax.experimental import pallas as pl
from jax.experimental.pallas import tpu as pltpu
from jax.sharding import PartitionSpec as P

HEADS = 12
ALL = ("dp", "seq")
F32, BF = jnp.float32, jnp.bfloat16
HIGH = lax.Precision.HIGHEST
EPS = 1e-06


def mm(a, b, ca=1, cb=0):
    return lax.dot_general(a, b, (((ca,), (cb,)), ((), ())), preferred_element_type=F32)


def mm_exact(a, b, ca=1, cb=0):
    return lax.dot_general(a, b, (((ca,), (cb,)), ((), ())), precision=HIGH, preferred_element_type=F32)


def split_two(a):
    high = a.astype(BF)
    return high, (a - high.astype(F32)).astype(BF)


def layer_norm(x, gain, shift):
    center = x - jnp.mean(x, -1, keepdims=True)
    spread = jnp.mean(center * center, -1, keepdims=True)
    return center * lax.rsqrt(spread + EPS) * gain + shift


def norm_back(x, gain, upstream):
    center = x - jnp.mean(x, -1, keepdims=True)
    inverse = lax.rsqrt(jnp.mean(center * center, -1, keepdims=True) + EPS)
    unit = center * inverse
    scaled = upstream * gain
    d_x = inverse * (
        scaled
        - jnp.mean(scaled, -1, keepdims=True)
        - unit * jnp.mean(scaled * unit, -1, keepdims=True)
    )
    return d_x, jnp.sum(upstream * unit, 0), jnp.sum(upstream, 0)


def norm_back_rows(x, gain, upstream):
    d_x, d_gain, d_shift = norm_back(x, gain, upstream)
    return d_x, d_gain[None], d_shift[None]


def mm_two(a, b, cb=0):
    n = a.shape[0]
    high = a.astype(BF).astype(F32)
    both = mm(jnp.concatenate([high, a - high], 0).astype(BF), b, 1, cb)
    return both[0:n] + both[n : 2 * n]


def gelu_pair(u):
    c = 0.7978845608028654
    t = jnp.tanh(c * (u + 0.044715 * u * u * u))
    value = 0.5 * u * (1.0 + t)
    slope = 0.5 * (1.0 + t) + 0.5 * u * (1.0 - t * t) * c * (1.0 + 3 * 0.044715 * u * u)
    return value, slope


def attend_fwd_kernel(q_ref, k_ref, v_ref, o_ref, lse_ref):
    q = q_ref[...] * 0.125
    k = k_ref[...]
    lane = lax.broadcasted_iota(jnp.int32, k.shape, 1)
    v_turned = jnp.transpose(v_ref[...])
    outs = []
    for h in range(2):
        keep = (lane < 64) if h == 0 else (lane >= 64)
        own_k = jnp.where(keep, k, jnp.zeros_like(k))
        s = mm(own_k, q, 1, 1)
        top = jnp.max(s, 0, keepdims=True)
        p = jnp.exp(s - top)
        total = jnp.sum(p, 0, keepdims=True)
        outs.append(mm(v_turned[64 * h : 64 * h + 64], p.astype(BF)) / total)
        lse_ref[0, h : h + 1, :] = top + jnp.log(total)
    o_ref[...] = jnp.transpose(jnp.concatenate(outs, 0)).astype(BF)


def attend_fwd(proj, length):
    rows, width = proj.shape[0], proj.shape[1] // 3
    pairs = width // 128
    block = lambda part: pl.BlockSpec((length, 128), lambda b, h: (b, part * pairs + h))
    return pl.pallas_call(
        attend_fwd_kernel,
        grid=(rows // length, pairs),
        in_specs=[block(0), block(1), block(2)],
        out_specs=[block(0), pl.BlockSpec((1, 2, length), lambda b, h: (h, 0, b))],
        out_shape=[
            jax.ShapeDtypeStruct((rows, width), BF),
            jax.ShapeDtypeStruct((pairs, 2, rows), F32),
        ],
        compiler_params=pltpu.CompilerParams(vmem_limit_bytes=48 << 20),
        cost_estimate=pl.CostEstimate(
            flops=rows * length * width * 8,
            bytes_accessed=rows * width * 8,
            transcendentals=rows * length * HEADS,
        ),
    )(proj, proj, proj)


def attend_bwd_kernel(q_ref, k_ref, v_ref, do_ref, lse_ref, d_ref, dq_ref, dk_ref, dv_ref):
    q = q_ref[...] * 0.125
    k, v, do = k_ref[...], v_ref[...], do_ref[...]
    lane = lax.broadcasted_iota(jnp.int32, k.shape, 1)
    dqs, dks, dvs = [], [], []
    for h in range(2):
        keep = (lane < 64) if h == 0 else (lane >= 64)
        s = mm(jnp.where(keep, k, jnp.zeros_like(k)), q, 1, 1)
        p = jnp.exp(s - lse_ref[0, h : h + 1, :])
        dp = mm(jnp.where(keep, v, jnp.zeros_like(v)), do, 1, 1)
        ds = (p * (dp - d_ref[0, h : h + 1, :])).astype(BF)
        dvs.append(mm(p.astype(BF), do))
        dks.append(mm(ds, q))
        dqs.append(mm(ds, k, 0, 0))
    low = lane < 64
    dq_ref[...] = (jnp.where(low, dqs[0], dqs[1]) * 0.125).astype(BF)
    dk_ref[...] = jnp.where(low, dks[0], dks[1]).astype(BF)
    dv_ref[...] = jnp.where(low, dvs[0], dvs[1]).astype(BF)


def attend_bwd(proj, d_out, lse, inner, length):
    rows, width = proj.shape[0], proj.shape[1] // 3
    pairs = width // 128
    block = lambda part: pl.BlockSpec((length, 128), lambda b, h: (b, part * pairs + h))
    row = pl.BlockSpec((1, 2, length), lambda b, h: (h, 0, b))
    result = jax.ShapeDtypeStruct((rows, width), BF)
    return pl.pallas_call(
        attend_bwd_kernel,
        grid=(rows // length, pairs),
        in_specs=[block(0), block(1), block(2), block(0), row, row],
        out_specs=[block(0)] * 3,
        out_shape=[result] * 3,
        compiler_params=pltpu.CompilerParams(vmem_limit_bytes=56 << 20),
        cost_estimate=pl.CostEstimate(
            flops=rows * length * width * 20,
            bytes_accessed=rows * width * 16,
            transcendentals=rows * length * HEADS,
        ),
    )(proj, proj, proj, d_out, lse, inner)


def head_blocks(width):
    own = jnp.arange(width)[None, :] // (width // HEADS) == jnp.arange(HEADS)[:, None]
    return own.astype(F32)


def spread_heads(rows):
    n, width = rows.shape
    return (rows[:, None, :] * head_blocks(width)[None]).reshape(n * HEADS, width)


def fold_heads(rows):
    total, width = rows.shape
    return jnp.sum(rows.reshape(total // HEADS, HEADS, width) * head_blocks(width)[None], 1)


def device_program(
    patches, captions, pairs,
    image_attend_in, image_attend_out, image_up_weight, image_up_bias, image_down_weight,
    image_vectors, probe_query_weight, probe_pair_weight, probe_out_weight, probe_up_weight,
    probe_up_bias, probe_down_weight, text_attend_in, text_attend_out, text_up_weight,
    text_up_bias, text_down_weight, text_vectors, text_head_weight, temp_bias,
):
    seq = lax.axis_size("seq")
    world = seq * lax.axis_size("dp")
    me = lax.axis_index("dp") * seq + lax.axis_index("seq")
    width = patches.shape[-1]
    head_width = width // HEADS
    factor = head_width ** (-0.5)
    hidden_width = image_up_weight.shape[1]
    part = width // world
    wide_part = hidden_width // world

    def gather(*weights):
        flat = jnp.concatenate([w.reshape(-1, width) for w in weights], 0)
        full = lax.all_gather(flat, ALL, axis=0)
        out, at = [], 0
        for w in weights:
            count = w.size // width
            piece = full[:, at : at + count]
            out.append(piece.reshape(world * w.shape[0], w.shape[1]))
            at += count
        return out

    small = jnp.concatenate(
        [image_vectors.reshape(-1), text_vectors.reshape(-1), image_up_bias, probe_up_bias, text_up_bias]
    )
    small_all = lax.all_gather(small, ALL, axis=0)
    sizes = [image_vectors.size, text_vectors.size, image_up_bias.size, probe_up_bias.size, text_up_bias.size]
    cuts = [sum(sizes[:i]) for i in range(len(sizes) + 1)]
    pieces = [small_all[:, cuts[i] : cuts[i + 1]].astype(F32) for i in range(len(sizes))]
    ivec = pieces[0].reshape(world, -1, part).transpose(1, 0, 2).reshape(-1, width)
    tvec = pieces[1].reshape(world, -1, part).transpose(1, 0, 2).reshape(-1, width)
    i_bias, p_bias, t_bias = (p.reshape(-1) for p in pieces[2:])

    (w_in,) = gather(image_attend_in)
    w_out, w_up, w_down = gather(image_attend_out, image_up_weight, image_down_weight)
    tw_in, tw_out, tw_up, tw_down, tw_head, pw_query, pw_pair, pw_out, pw_up, pw_down = gather(
        text_attend_in, text_attend_out, text_up_weight, text_down_weight, text_head_weight,
        probe_query_weight, probe_pair_weight, probe_out_weight, probe_up_weight, probe_down_weight,
    )

    def to_owner(x):
        return lax.all_to_all(x, "seq", 0, 1, tiled=True)

    x = to_owner(patches)
    own, length = x.shape[0], x.shape[1]
    x = x.reshape(own * length, width).astype(F32)
    captions_own = to_owner(captions)
    text_length = captions_own.shape[1]

    normed = layer_norm(x, ivec[0], ivec[1]).astype(BF)
    proj = mm(normed, w_in).astype(BF)
    mixed, lse = attend_fwd(proj, length)
    hidden = x + mm(mixed, w_out)
    second = layer_norm(hidden, ivec[2], ivec[3]).astype(BF)
    value, slope = gelu_pair(mm(second, w_up) + i_bias)
    active, slope = value.astype(BF), slope.astype(BF)
    block_out = hidden + mm(active, w_down) + ivec[4]
    final = layer_norm(block_out, ivec[5], ivec[6]).astype(BF)

    t_x = captions_own.astype(F32)
    t_normed = layer_norm(t_x, tvec[0], tvec[1]).astype(BF)
    t_last = t_normed[:, -1]
    tw_q, tw_k, tw_v = tw_in[:, :width], tw_in[:, width : 2 * width], tw_in[:, 2 * width :]
    t_q = mm(t_last, tw_q).astype(BF)
    t_keys = mm(spread_heads(t_q.astype(F32)).astype(BF), tw_k, 1, 1) * factor
    t_keys = t_keys.reshape(own, HEADS, width)
    k_high, k_low = split_two(t_keys)
    scores = jnp.einsum("bsd,bhd->bsh", t_normed, k_high, preferred_element_type=F32)
    scores += jnp.einsum("bsd,bhd->bsh", t_normed, k_low, preferred_element_type=F32)
    t_probs = jax.nn.softmax(scores, axis=1)
    t_used = jnp.einsum("bsh,bsd->bhd", t_probs, t_normed.astype(F32), precision=HIGH)
    t_mixed = fold_heads(mm(t_used.reshape(own * HEADS, width).astype(BF), tw_v)).astype(BF)
    t_hidden = t_x[:, -1] + mm(t_mixed, tw_out)
    t_second = layer_norm(t_hidden, tvec[2], tvec[3]).astype(BF)
    t_value, t_slope = gelu_pair(mm(t_second, tw_up) + t_bias)
    t_active = t_value.astype(BF)
    t_out = t_hidden + mm(t_active, tw_down) + tvec[4]
    t_final = layer_norm(t_out, tvec[5], tvec[6]).astype(BF)
    text_embed = mm(t_final, tw_head)

    pw_k, pw_v = pw_pair[:, :width], pw_pair[:, width:]
    probe_query = mm_exact(ivec[7:8], pw_query.astype(F32))
    p_keys = mm_exact(spread_heads(probe_query), pw_k.astype(F32), 1, 1) * factor
    k_high, k_low = split_two(p_keys)
    pool_scores = mm(k_high, final, 1, 1) + mm(k_low, final, 1, 1)
    pool_scores = pool_scores.reshape(HEADS, own, length)
    pool_probs = jax.nn.softmax(pool_scores, axis=-1)
    final_own = final.reshape(own, length, width)
    p_high, p_low = split_two(pool_probs)
    used = jnp.einsum("hbt,btd->bhd", p_high, final_own, preferred_element_type=F32)
    used += jnp.einsum("hbt,btd->bhd", p_low, final_own, preferred_element_type=F32)
    pooled = fold_heads(mm_exact(used.reshape(own * HEADS, width), pw_v.astype(F32)))
    head_start = mm_exact(pooled, pw_out.astype(F32))
    head_normed = layer_norm(head_start, ivec[8], ivec[9]).astype(BF)
    h_value, h_slope = gelu_pair(mm(head_normed, pw_up) + p_bias)
    head_active = h_value.astype(BF)
    image_embed = head_start + mm(head_active, pw_down) + ivec[10]

    embeds = lax.all_gather(jnp.stack([image_embed, text_embed], 1), ALL, axis=0, tiled=True)
    every_image, every_text = embeds[:, 0], embeds[:, 1]
    labels = (2 * pairs - 1).astype(F32)
    total = every_image.shape[0]
    i_scale = lax.rsqrt(jnp.sum(every_image * every_image, -1, keepdims=True) + EPS)
    t_scale = lax.rsqrt(jnp.sum(every_text * every_text, -1, keepdims=True) + EPS)
    z_i, z_t = every_image * i_scale, every_text * t_scale
    cosine = mm_exact(z_i, z_t, 1, 1)
    temper = jnp.exp(temp_bias[0])
    logits = cosine * temper + temp_bias[1]
    loss = -jnp.sum(jax.nn.log_sigmoid(labels * logits)) / total
    g = -labels * jax.nn.sigmoid(-labels * logits) / total
    grad_temp = jnp.stack([temper * jnp.sum(g * cosine), jnp.sum(g)])
    dz_i = temper * mm_exact(g, z_t)
    dz_t = temper * mm_exact(g, z_i, 0, 0)
    all_d_image = (dz_i - z_i * jnp.sum(z_i * dz_i, -1, keepdims=True)) * i_scale
    all_d_text = (dz_t - z_t * jnp.sum(z_t * dz_t, -1, keepdims=True)) * t_scale
    d_image = lax.dynamic_slice_in_dim(all_d_image, me * own, own, 0)
    d_text = lax.dynamic_slice_in_dim(all_d_text, me * own, own, 0)

    h_upper = mm_exact(d_image, pw_down.astype(F32), 1, 1) * h_slope
    h_norm = mm_exact(h_upper, pw_up.astype(F32), 1, 1)
    d_start, dv8, dv9 = norm_back(head_start, ivec[8], h_norm)
    d_start = d_image + d_start
    dv10 = jnp.sum(d_image, 0)
    d_pooled = mm_exact(d_start, pw_out.astype(F32), 1, 1)
    p_values = mm_exact(spread_heads(d_pooled), pw_v.astype(F32), 1, 1).reshape(own, HEADS, width)
    v_high, v_low = split_two(p_values)
    d_probs = jnp.einsum("bhd,btd->hbt", v_high, final_own, preferred_element_type=F32)
    d_probs += jnp.einsum("bhd,btd->hbt", v_low, final_own, preferred_element_type=F32)
    d_scores = pool_probs * (d_probs - jnp.sum(pool_probs * d_probs, -1, keepdims=True))
    s_high, s_low = split_two(d_scores)
    p_used = jnp.einsum("hbt,btd->bhd", s_high, final_own, preferred_element_type=F32)
    p_used += jnp.einsum("hbt,btd->bhd", s_low, final_own, preferred_element_type=F32)
    d_query = jnp.sum(fold_heads(mm_exact(p_used.reshape(own * HEADS, width), pw_k.astype(F32))), 0) * factor
    d_final = jnp.einsum(
        "hbt,bhd->btd",
        jnp.concatenate([s_high, p_high], 0),
        jnp.concatenate([jnp.broadcast_to(k_high[None], (own, HEADS, width)), v_high], 1),
        preferred_element_type=F32,
    ).reshape(own * length, width)
    dy, dv5, dv6 = norm_back(block_out, ivec[5], d_final)

    d_branch = dy.astype(BF)
    g_down = mm(active, d_branch, 0, 0)
    dv4 = jnp.sum(dy, 0)
    d_upper_f = mm(d_branch, w_down, 1, 1) * slope.astype(F32)
    d_upper = d_upper_f.astype(BF)
    g_bias = jnp.sum(d_upper_f, 0)
    g_up = mm(second, d_upper, 0, 0)
    d_hidden, dv2, dv3 = norm_back(hidden, ivec[2], mm(d_upper, w_up, 1, 1))
    d_hidden = dy + d_hidden
    d_attend = d_hidden.astype(BF)
    g_out = mm(mixed, d_attend, 0, 0)
    d_mixed = mm(d_attend, w_out, 1, 1).astype(BF)

    def scatter(*grads):
        flat = jnp.concatenate([g.astype(BF).reshape(world, -1, width) for g in grads], 1)
        mine = lax.psum_scatter(flat, ALL, scatter_dimension=0, tiled=False).astype(F32)
        out, at = [], 0
        for g in grads:
            count = g.size // world // width
            out.append(mine[at : at + count].reshape(g.shape[0] // world, g.shape[1]))
            at += count
        return out

    own_up, own_down, own_out = scatter(g_up, g_down, g_out)
    inner_rows = jnp.sum(
        (d_mixed.astype(F32) * mixed.astype(F32)).reshape(own * length, HEADS, head_width), -1
    ).T.reshape(HEADS // 2, 2, own * length)
    d_q, d_k, d_v = attend_bwd(proj, d_mixed, lse, inner_rows, length)
    g_in = jnp.concatenate([mm(normed, d, 0, 0) for d in (d_q, d_k, d_v)], 1)
    (own_in,) = scatter(g_in)
    d_normed = (
        mm(d_q, w_in[:, :width], 1, 1)
        + mm(d_k, w_in[:, width : 2 * width], 1, 1)
        + mm(d_v, w_in[:, 2 * width :], 1, 1)
    )
    d_x, dv0, dv1 = norm_back(x, ivec[0], d_normed)
    d_x = (d_hidden + d_x).reshape(own, length, width)

    def to_tokens(v):
        return lax.all_to_all(v.astype(BF), "seq", 1, 0, tiled=True).astype(F32)

    grad_patches = to_tokens(d_x)

    dt_final = mm_exact(d_text, tw_head.astype(F32), 1, 1)
    dt_out, tv5, tv6 = norm_back(t_out, tvec[5], dt_final)
    dt_branch = dt_out.astype(BF)
    tv4 = jnp.sum(dt_out, 0)
    dt_upper = (mm(dt_branch, tw_down, 1, 1) * t_slope).astype(BF)
    dt_hidden, tv2, tv3 = norm_back(t_hidden, tvec[2], mm(dt_upper, tw_up, 1, 1))
    dt_hidden = dt_out + dt_hidden
    dt_attend = dt_hidden.astype(BF)
    dt_mixed = mm(dt_attend, tw_out, 1, 1).astype(BF)
    t_values = mm(spread_heads(dt_mixed.astype(F32)).astype(BF), tw_v, 1, 1).reshape(own, HEADS, width)
    tv_high, tv_low = split_two(t_values)
    dt_probs = jnp.einsum("bsd,bhd->bsh", t_normed, tv_high, preferred_element_type=F32)
    dt_probs += jnp.einsum("bsd,bhd->bsh", t_normed, tv_low, preferred_element_type=F32)
    dt_scores = t_probs * (dt_probs - jnp.sum(t_probs * dt_probs, 1, keepdims=True))
    tk_used = jnp.einsum("bsh,bsd->bhd", dt_scores, t_normed.astype(F32), precision=HIGH)
    dt_q = fold_heads(mm(tk_used.reshape(own * HEADS, width).astype(BF), tw_k)) * factor
    dt_q = dt_q.astype(BF)
    dt_normed = jnp.einsum("bsh,bhd->bsd", dt_scores, t_keys, precision=HIGH)
    dt_normed += jnp.einsum("bsh,bhd->bsd", t_probs, t_values, precision=HIGH)
    dt_normed = dt_normed.at[:, -1].add(mm(dt_q, tw_q, 1, 1))
    flat_x = t_x.reshape(own * text_length, width)
    dt_x, tv0, tv1 = norm_back(flat_x, tvec[0], dt_normed.reshape(own * text_length, width))
    dt_x = dt_x.reshape(own, text_length, width).at[:, -1].add(dt_hidden)
    grad_captions = to_tokens(dt_x)

    whole = jnp.concatenate(
        [v.astype(F32) for v in (h_upper, d_start, d_pooled, dt_branch, dt_upper, dt_attend, dt_q, t_q, dt_mixed)], 1
    )
    whole = lax.all_gather(whole, ALL, axis=0, tiled=True)
    at = [0]

    def take(count):
        at[0] += count
        return whole[:, at[0] - count : at[0]]

    a_h_upper, a_start, a_pooled, a_branch, a_upper, a_attend, a_q, a_query, a_mixed = (
        take(c) for c in (hidden_width, width, width, width, hidden_width, width, width, width, width)
    )
    columns = [pooled, head_normed, t_last, t_mixed, t_second, t_final]
    columns += [used, t_used, tk_used * factor]
    columns += [head_active, t_active]
    columns = jnp.concatenate(
        [v.astype(F32).reshape(own, -1, width) for v in columns], 1
    )
    wide = 2 * (hidden_width // width)
    narrow = columns.shape[1] - wide
    cut = jnp.concatenate(
        [
            columns[:, :narrow].reshape(own, narrow, world, part).transpose(2, 0, 1, 3).reshape(world, own, -1),
            columns[:, narrow:].reshape(own, 2, world, wide_part).transpose(2, 0, 1, 3).reshape(world, own, -1),
        ],
        2,
    )
    cut = lax.all_to_all(cut, ALL, 0, 0, tiled=True).reshape(total, -1)
    slim = cut[:, : narrow * part].reshape(total, narrow, part)
    broad = cut[:, narrow * part :].reshape(total, 2, wide_part)

    def outer(rows, cols):
        return mm_exact(rows, cols, 0, 0)

    def outer_heads(rows, cols):
        cols = cols.reshape(total, HEADS, head_width)
        return jnp.einsum("chm,che->mhe", rows, cols, precision=HIGH).reshape(part, width)

    c_pooled, c_head, c_last, c_mixed, c_second, c_final = (slim[:, i] for i in range(6))
    c_used, ct_used, ctk_used = (slim[:, 6 + i * HEADS : 6 + (i + 1) * HEADS] for i in range(3))
    own_t_in = jnp.concatenate(
        [outer(c_last, a_q), outer_heads(ctk_used, a_query), outer_heads(ct_used, a_mixed)], 1
    )
    own_t_out = outer(c_mixed, a_attend)
    own_t_up = outer(c_second, a_upper)
    own_t_down = outer(broad[:, 1], a_branch)
    own_t_head = outer(c_final, all_d_text)
    own_p_out = outer(c_pooled, a_start)
    own_p_up = outer(c_head, a_h_upper)
    own_p_down = outer(broad[:, 0], all_d_image)
    own_p_values = outer_heads(c_used, a_pooled)

    summed = jnp.concatenate(
        [
            jnp.stack([dv0, dv1, dv2, dv3, dv4, dv5, dv6, dv8, dv9, dv10]),
            jnp.stack([tv0, tv1, tv2, tv3, tv4, tv5, tv6]),
            d_query[None],
            jnp.sum(p_used, 0),
            g_bias.reshape(-1, width),
        ],
        0,
    )
    summed = lax.psum(summed, ALL)
    total_query = summed[17]
    mine = lambda v, n: lax.dynamic_slice_in_dim(v, me * n, n, -1)
    own_probe = mine(ivec[7], part)
    own_p_query = own_probe[:, None] * total_query[None, :]
    dv7 = jnp.sum(probe_query_weight.astype(F32) * total_query[None, :], 1)
    pk_used = mine(summed[18 : 18 + HEADS], part)
    own_p_keys = jnp.einsum(
        "hm,he->mhe", pk_used, probe_query.reshape(HEADS, head_width) * factor
    ).reshape(part, width)
    own_p_pair = jnp.concatenate([own_p_keys, own_p_values], 1)
    ten = mine(summed[:10], part)
    own_ivec = jnp.concatenate([ten[:7], dv7[None], ten[7:]], 0)
    own_tvec = mine(summed[10:17], part)
    own_bias = mine(summed[18 + HEADS :].reshape(-1), wide_part)
    own_p_bias = mine(jnp.sum(a_h_upper, 0), wide_part)
    own_t_bias = mine(jnp.sum(a_upper, 0), wide_part)
    return (
        loss, grad_patches, grad_captions,
        own_in, own_out, own_up, own_bias, own_down, own_ivec,
        own_p_query, own_p_pair, own_p_out, own_p_up, own_p_bias, own_p_down,
        own_t_in, own_t_out, own_t_up, own_t_bias, own_t_down, own_tvec, own_t_head,
        grad_temp,
    )


MESH = pl.DeviceIdType.MESH

class Place:
    def __init__(self):
        i = lax.axis_index("dp")
        self.i, self.z = i, lax.axis_index("seq")
        self.y, self.x, self.c = i // 4, (i // 2) % 2, i % 2
        self.at_y = (i + 4 - 8 * self.y, self.z)
        self.at_x = (i + 2 - 4 * self.x, self.z)
        self.at_c = (i + 1 - 2 * self.c, self.z)

    def at_z(self, k):
        return (self.i, (self.z + k) % 4)

def greet(peers):
    barrier = pltpu.get_barrier_semaphore()
    for p in peers:
        pl.semaphore_signal(barrier, inc=1, device_id=p, device_id_type=MESH)
    pl.semaphore_wait(barrier, len(peers))

def gather_kernel(kinds, order, *refs):
    n = len(kinds)
    srcs, outs = refs[:n], refs[n : 2 * n]
    send, recv, local = refs[2 * n :]
    me = Place()
    y, x, c, z = me.y, me.x, me.c, me.z
    greet([me.at_z(1), me.at_z(2), me.at_z(3), me.at_x, me.at_y, me.at_c])
    ends = []

    def copy_of(a, slot, src, dst, dev):
        return pltpu.make_async_remote_copy(
            src, dst, send.at[a, slot], recv.at[a, slot], device_id=dev, device_id_type=MESH
        )

    def push(a, slot, src, dst, dev, arriving):
        copy = copy_of(a, slot, src, dst, dev)
        copy.start()
        ends.append(copy.wait_send)
        return copy_of(a, slot, src, arriving, dev).wait_recv

    def along(a, step, up):
        home = outs[a].at[y, x, c]
        if up:
            slab, go, to = z - step, (z - step >= 0) & (z < 3), me.at_z(1)
        else:
            slab, go, to = z + step, (z + step < 4) & (z > 0), me.at_z(3)
        slab = jnp.clip(slab, 0, 3)
        src = srcs[a] if step == 0 else home.at[slab]
        copy = copy_of(a, step + (0 if up else 3), src, home.at[slab], to)
        pl.when(go)(lambda: copy.start())
        ends.append(lambda: pl.when(go)(lambda: copy.wait_send()))

    def arrived(a, step, up):
        home = outs[a].at[y, x, c]
        if up:
            slab, come = z - 1 - step, z - 1 - step >= 0
        else:
            slab, come = z + 1 + step, z + 1 + step < 4
        slab = jnp.clip(slab, 0, 3)
        copy = copy_of(a, step + (0 if up else 3), home.at[slab], home.at[slab], me.at_z(1))
        pl.when(come)(lambda: copy.wait_recv())

    waits = {}

    def half(r, which, order_):
        if order_ != "S":
            return r
        n_ = r.shape[-1] // 2
        return r.at[..., 0:n_] if which == "C" else r.at[..., n_ : 2 * n_]

    def stage(a, s):
        kind, turn = kinds[a]
        src, out = srcs[a], outs[a]
        if kind in ("za", "zg"):
            own = src.at[z] if kind == "za" else src
            keep = pltpu.make_async_copy(own, out.at[z], local.at[a])
            keep.start()
            ends.append(keep.wait)
            for k in (1, 2, 3):
                to, fro = (z + k) % 4, (z + 4 - k) % 4
                s_ref = src.at[to] if kind == "za" else src
                ends.append(push(a, k - 1, s_ref, out.at[z], me.at_z(k), out.at[fro]))
            return
        turns = "CD" if turn == "S" else turn
        if kind != "full" and s == 0:
            own = src.at[z] if kind == "cols" else src
            keep = pltpu.make_async_copy(own, out.at[y, x, c, z] if kind == "cols" else out.at[y, x, c], local.at[a])
            keep.start()
            waits[a] = [keep.wait]
            for k in (1, 2, 3) if kind == "cols" else ():
                to, fro = (z + k) % 4, (z + 4 - k) % 4
                waits[a].append(push(a, k - 1, src.at[to], out.at[y, x, c, z], me.at_z(k), out.at[y, x, c, fro]))
        elif s == 0:
            keep = pltpu.make_async_copy(src, out.at[y, x, c, z], local.at[a])
            keep.start()
            waits[a] = [keep.wait]
            along(a, 0, True)
            along(a, 0, False)
        elif s in (1, 2):
            for up in (True, False):
                arrived(a, s - 1, up)
                along(a, s, up)
        elif s == 3:
            for up in (True, False) if kind == "full" else ():
                arrived(a, 2, up)
            for w in waits.pop(a):
                w()
            waits[a] = []
            for t in turns:
                cut = lambda r: half(r, t, turn)
                to, fro = (me.at_x, (y, 1 - x)) if t == "C" else (me.at_y, (1 - y, x))
                mine = cut(out.at[y, x, c])
                waits[a].append(push(a, 6 + (t == "D"), mine, mine, to, cut(out.at[fro[0], fro[1], c])))
        elif s == 4:
            for w in waits.pop(a):
                w()
            waits[a] = []
            for t in turns:
                cut = lambda r: half(r, t, turn)
                if t == "C":
                    mine, come, to = cut(out.at[y, :, c]), cut(out.at[1 - y, :, c]), me.at_y
                else:
                    mine, come, to = cut(out.at[:, x, c]), cut(out.at[:, 1 - x, c]), me.at_x
                waits[a].append(push(a, 8 + (t == "D"), mine, mine, to, come))
        elif s == 5:
            for w in waits.pop(a):
                w()
            mine = out.at[:, :, c]
            ends.append(push(a, 10, mine, mine, me.at_c, out.at[:, :, 1 - c]))

    for a, s in order:
        stage(a, s)
    for e in ends:
        e()


def gather(ops, kinds, order, cid):
    shapes = []
    for o, (kind, _) in zip(ops, kinds):
        s = {"full": (2, 2, 2, 4) + o.shape, "zg": (4,) + o.shape, "za": o.shape, "cols": (2, 2, 2) + o.shape, "plane": (2, 2, 2) + o.shape}[kind]
        shapes.append(jax.ShapeDtypeStruct(s, o.dtype))
    n = len(ops)
    return pl.pallas_call(
        partial(gather_kernel, kinds, order),
        out_shape=shapes,
        in_specs=[pl.BlockSpec(memory_space=pl.ANY)] * n,
        out_specs=[pl.BlockSpec(memory_space=pl.ANY)] * n,
        scratch_shapes=[
            pltpu.SemaphoreType.DMA((n, 11)),
            pltpu.SemaphoreType.DMA((n, 11)),
            pltpu.SemaphoreType.DMA((n,)),
        ],
        compiler_params=pltpu.CompilerParams(collective_id=cid, has_side_effects=True),
    )(*ops)


ROWS = 80

def middle_kernel(final_in, block_in, tokens_ref, tp_in, downs_in, outs_ref, ivec_ref, tvec_ref, pbias_ref, tbias_ref,
                  label_ref, temp_ref,
                  dy_ref, branch_ref, rows_ref, sums_ref, dcap_ref, loss_ref, dz_ref,
                  tn_ref, dn_ref, send_a, recv_a, send_l, recv_l, send_t, recv_t,
                  final_ref, block_ref, tp_ref, downs_ref, send_sem, recv_sem, fetch):
    me = Place()
    cut = 2 * final_in.shape[1]
    pairs = {
        "small": (tp_in.at[:, cut:], tp_ref.at[:, cut:]), "final": (final_in, final_ref),
        "up": (tp_in.at[:, 0:cut], tp_ref.at[:, 0:cut]), "down": (downs_in, downs_ref), "block": (block_in, block_ref),
    }
    loads = {name: pltpu.make_async_copy(*pair, fetch.at[n]) for n, (name, pair) in enumerate(pairs.items())}
    for load in loads.values():
        load.start()
    z, i = me.z, me.i
    n_dp = recv_l.shape[0]
    plane = [((i + k) % n_dp, z) for k in range(1, n_dp)]
    greet([me.at_z(1), me.at_z(2), me.at_z(3)] + plane)
    width = final_in.shape[1]
    part = width // 4
    started = []

    def exchange(n, values, rows=4):
        if not isinstance(values, list):
            values = [values] * 4
        for q in range(4):
            send_a[n, q, 0:rows] = values[q]
        recv_a[n, z] = send_a[n, z]
        copies = []
        for k in (3, 2, 1):
            to, fro = (z + k) % 4, (z + 4 - k) % 4
            make = lambda dst: pltpu.make_async_remote_copy(
                send_a.at[n, to], dst, send_sem.at[n, k], recv_sem.at[n, k], device_id=me.at_z(k), device_id_type=MESH)
            copy = make(recv_a.at[n, z])
            copy.start()
            started.append(copy)
            copies.append(make(recv_a.at[n, fro]))

        def done():
            for a in copies:
                a.wait_recv()
            return [recv_a[n, q, 0:rows] for q in range(4)]

        return done

    total = lambda blocks: (blocks[0] + blocks[1]) + (blocks[2] + blocks[3])
    by_head = lambda blocks, n=3: jnp.concatenate([blocks[q][h : h + 1] for h in range(n) for q in range(4)], 0)
    pad1 = jnp.zeros((1, width), F32)
    ivec, tvec = ivec_ref[...], tvec_ref[...]
    iv = lambda k: ivec[k:k + 1]
    tv = lambda k: tvec[k:k + 1]
    names = ["tq", "tk", "tv", "thead", "pq", "pk", "pv"]
    col = {n: 2 * width + 256 * k for k, n in enumerate(names)}
    small = lambda n: tp_ref[:, col[n]:col[n] + 256]
    p_up = lambda: tp_ref[:, 0:width]
    t_up = lambda: tp_ref[:, width:2 * width]
    t_down = lambda: downs_ref[:, 0:width]
    p_down = lambda: downs_ref[:, width:2 * width]
    t_out_w = lambda: outs_ref[0:part, 0:width]
    p_out_w = lambda: outs_ref[0:part, width:2 * width]
    lane = lax.broadcasted_iota(jnp.int32, (1, 256), 1)
    own = [((lane >= 64 * h) & (lane < 64 * h + 64)).astype(F32) for h in range(3)]

    def spread(a):
        return jnp.concatenate([a * own[h] for h in range(3)], 0)

    def fold(a):
        n = a.shape[0] // 3
        return sum(a[h * n:(h + 1) * n] * own[h] for h in range(3))

    loads["small"].wait()
    p_q = mm(iv(7).astype(BF), small("pq"))
    get_keys = exchange(0, mm_two(spread(p_q), small("pk"), 1) * 0.125, 3)
    t_x = tokens_ref[...].astype(F32)
    tn = layer_norm(t_x, tv(0), tv(1)).astype(BF)
    tn_ref[...] = tn.astype(F32)
    last_at = [3 * 64 + 16 * c + 15 for c in range(4)]
    t_last = jnp.concatenate([tn_ref[r:r + 1, :] for r in last_at], 0)
    x_last = jnp.concatenate([tokens_ref[3 * 64 + 16 * c:3 * 64 + 16 * c + 16, :].astype(F32)[15:16] for c in range(4)], 0)
    t_q = mm(t_last.astype(BF), small("tq")).astype(BF).astype(F32)
    t_keys = mm(spread(t_q).astype(BF), small("tk"), 1, 1) * 0.125
    scores = mm_two(t_keys, tn, 1)
    col_id = (lax.broadcasted_iota(jnp.int32, scores.shape, 1) // 16) % 4
    row_id = lax.broadcasted_iota(jnp.int32, scores.shape, 0) % 4
    mine = col_id == row_id
    top = jnp.max(jnp.where(mine, scores, -1e30), -1, keepdims=True)
    e = jnp.where(mine, jnp.exp(jnp.where(mine, scores - top, 0.0)), 0.0)
    t_probs = e / jnp.sum(e, -1, keepdims=True)
    t_used = mm_two(t_probs, tn)
    t_mixed = fold(mm(t_used.astype(BF), small("tv"))).astype(BF)
    get_t = exchange(1, mm(t_mixed[:, 0:part], t_out_w()), 4)
    loads["final"].wait()
    final = final_ref[...]
    p_keys = jnp.concatenate(get_keys(), 0)
    p_scores = mm_two(p_keys, final, 1)
    e = jnp.exp(p_scores - jnp.max(p_scores, -1, keepdims=True))
    p_probs = e / jnp.sum(e, -1, keepdims=True)
    used = mm_two(p_probs, final)
    get_p = exchange(2, [used[3 * q:3 * q + 3] for q in range(4)], 3)
    t_hidden = x_last + total(get_t())
    t_second = layer_norm(t_hidden, tv(2), tv(3)).astype(BF)
    loads["up"].wait()
    loads["down"].wait()
    t_value, t_slope = gelu_pair(mm(t_second, t_up()) + tbias_ref[...])
    t_active = t_value.astype(BF)
    get_t = exchange(3, mm(t_active, t_down()), 4)
    pooled = fold(mm_two(by_head(get_p()), small("pv")))
    get_p = exchange(4, mm_two(pooled[:, 0:part], p_out_w()), 4)
    t_out = t_hidden + total(get_t()) + tv(4)
    t_final = layer_norm(t_out, tv(5), tv(6)).astype(BF)
    t_piece = mm(t_final, small("thead"))
    get_t = exchange(5, jnp.concatenate([t_piece[:, 0:part], jnp.zeros((4, width - part), F32)], 1), 4)
    h_start = total(get_p())
    h_normed = layer_norm(h_start, iv(8), iv(9)).astype(BF)
    h_value, h_slope = gelu_pair(mm(h_normed, p_up()) + pbias_ref[...])
    h_active = h_value.astype(BF)
    get_p = exchange(6, mm(h_active, p_down()), 4)
    text_embed = jnp.concatenate([blk[:, 0:part] for blk in get_t()], 1)
    image_embed = h_start + (total(get_p()) + iv(10))
    send_l[...] = jnp.concatenate([image_embed, text_embed], 0)
    recv_l[i] = send_l[...]
    arrive = []
    for k in range(1, n_dp):
        copy = pltpu.make_async_remote_copy(send_l, recv_l.at[i], send_sem.at[15, k], recv_sem.at[15, k],
                                            device_id=plane[k - 1], device_id_type=MESH)
        copy.start()
        started.append(copy)
        arrive.append(pltpu.make_async_remote_copy(send_l, recv_l.at[(i + n_dp - k) % n_dp], send_sem.at[15, k], recv_sem.at[15, k],
                                                   device_id=plane[k - 1], device_id_type=MESH))
    for a in arrive:
        a.wait_recv()
    every = jnp.concatenate([recv_l[k] for k in range(n_dp)], 0)
    scale = lax.rsqrt(jnp.sum(every * every, -1, keepdims=True) + EPS)
    unit = every * scale
    cosine = mm_exact(unit, unit, 1, 1)
    temper = jnp.exp(jnp.full((1, 1), temp_ref[0], F32))
    logits = cosine * temper + temp_ref[1]
    label = label_ref[...]
    valid = label != 0.0
    signed = label * logits
    n_all = n_dp * 4
    nll = jnp.maximum(-signed, 0.0) + jnp.log(1.0 + jnp.exp(-jnp.abs(signed)))
    add_all = lambda a: jnp.sum(jnp.sum(a, -1, keepdims=True), 0, keepdims=True)
    loss = add_all(jnp.where(valid, nll, 0.0)) / n_all
    g = jnp.where(valid, -label / (1.0 + jnp.exp(signed)), 0.0) / n_all
    gt0 = temper * add_all(g * cosine)
    gt1 = add_all(g)
    at = lax.broadcasted_iota(jnp.int32, (8, 128), 1)
    loss_ref[...] = jnp.where(at == 0, loss, jnp.where(at == 1, gt0, gt1))
    dz = temper * mm_exact(g + jnp.transpose(g), unit)
    dz_ref[...] = (dz - unit * jnp.sum(unit * dz, -1, keepdims=True)) * scale
    d_both = dz_ref[pl.ds(pl.multiple_of(8 * i, 8), 8), :]
    d_image, d_text = d_both[0:4], d_both[4:8]

    dh_upper = mm_two(d_image, p_down(), 1) * h_slope
    get_p = exchange(7, mm_two(dh_upper, p_up(), 1), 4)
    d_text_my = sum(jnp.where(z == q, d_text[:, part * q:part * q + part], 0.0) for q in range(4))
    get_t = exchange(8, mm_two(d_text_my, small("thead")[:, 0:part], 1), 4)
    d_start, dv8, dv9 = norm_back_rows(h_start, iv(8), total(get_p()))
    d_start = d_image + d_start
    dv10 = jnp.sum(d_image, 0, keepdims=True)
    d_pooled = mm_two(d_start, p_out_w(), 1)
    d_pooled = jnp.concatenate([d_pooled, jnp.zeros((4, 256 - part), F32)], 1)
    p_values_my = mm_two(spread(d_pooled), small("pv"), 1)
    get_p = exchange(9, [jnp.concatenate([p_values_my[4 * h + q:4 * h + q + 1] for h in range(3)], 0) for q in range(4)], 3)
    dt_out, tv5, tv6 = norm_back_rows(t_out, tv(5), total(get_t()))
    tv4 = jnp.sum(dt_out, 0, keepdims=True)
    dt_branch = dt_out.astype(BF)
    dt_upper = (mm(dt_branch, t_down(), 1, 1) * t_slope).astype(BF)
    get_t = exchange(10, mm(dt_upper, t_up(), 1, 1), 4)
    p_values = jnp.concatenate(get_p(), 0)
    d_probs = mm_two(p_values, final, 1)
    d_scores = p_probs * (d_probs - jnp.sum(p_probs * d_probs, -1, keepdims=True))
    p_used = mm_two(d_scores, final) * 0.125
    get_p = exchange(11, [p_used[3 * q:3 * q + 3] for q in range(4)], 3)
    dt_hidden, tv2, tv3 = norm_back_rows(t_hidden, tv(2), total(get_t()))
    dt_hidden = dt_out + dt_hidden
    dt_attend = dt_hidden.astype(BF)
    dt_mixed = mm(dt_attend, t_out_w(), 1, 1).astype(BF).astype(F32)
    dt_mixed = jnp.concatenate([dt_mixed, jnp.zeros((4, 256 - part), F32)], 1)
    t_values = mm(spread(dt_mixed).astype(BF), small("tv"), 1, 1)
    dt_probs = mm_two(t_values, tn, 1)
    dt_scores = t_probs * (dt_probs - jnp.sum(t_probs * dt_probs, -1, keepdims=True))
    tk_used = mm_two(dt_scores, tn) * 0.125
    dt_q = fold(mm(tk_used.astype(BF), small("tk"))).astype(BF)
    dn = mm(dt_scores.astype(BF), t_keys.astype(BF), 0, 0) + mm(t_probs.astype(BF), t_values.astype(BF), 0, 0)
    row_at = lax.broadcasted_iota(jnp.int32, dn.shape, 0)
    dq_back = mm(dt_q, small("tq"), 1, 1)
    for c in range(4):
        dn = dn + jnp.where(row_at == last_at[c], dq_back[c:c + 1], 0.0)
    dn_ref[...] = dn.astype(BF)
    arrive = []
    for k in (1, 2, 3):
        to, fro = (z + k) % 4, (z + 4 - k) % 4
        rows_to = dn_ref.at[pl.ds(pl.multiple_of(64 * to, 64), 64), :]
        copy = pltpu.make_async_remote_copy(rows_to, recv_t.at[z], send_sem.at[14, k], recv_sem.at[14, k],
                                            device_id=me.at_z(k), device_id_type=MESH)
        copy.start()
        started.append(copy)
        arrive.append(pltpu.make_async_remote_copy(rows_to, recv_t.at[fro], send_sem.at[14, k], recv_sem.at[14, k],
                                                   device_id=me.at_z(k), device_id_type=MESH))
    s_high, s_low = split_two(d_scores)
    q_high, q_low = split_two(p_probs)
    k_high, k_low = split_two(p_keys)
    v_high, v_low = split_two(p_values)
    left = jnp.concatenate([s_high.astype(F32), q_high.astype(F32)], 0)
    right = jnp.concatenate([k_high.astype(F32), v_high.astype(F32)], 0).astype(BF)
    send_t[...] = jnp.transpose(jnp.concatenate([left, jnp.zeros((104, left.shape[1]), F32)], 0))
    right = jnp.concatenate([right, jnp.zeros((104, width), BF)], 0)
    sums_ref[...] = jnp.zeros_like(sums_ref)
    tile = 128

    def step(n, carry):
        at_rows = pl.ds(pl.multiple_of(n * tile, tile), tile)
        d_final = mm(send_t[at_rows, :].astype(BF), right)
        d_y, gain, shift = norm_back_rows(block_ref[at_rows, :], iv(5), d_final)
        dy_ref[at_rows, :] = d_y
        branch_ref[at_rows, :] = d_y.astype(BF)
        sums_ref[5:6] += gain
        sums_ref[6:7] += shift
        sums_ref[4:5] += jnp.sum(d_y, 0, keepdims=True)
        return carry

    loads["block"].wait()
    lax.fori_loop(0, final_ref.shape[0] // tile, step, 0)
    w_got = by_head(get_p())
    dq_rows = fold(mm_two(w_got, small("pk")))
    dq_my = jnp.sum(dq_rows, 0, keepdims=True)
    recv_t[z] = dn_ref[pl.ds(pl.multiple_of(64 * z, 64), 64), :]
    for a in arrive:
        a.wait_recv()
    dt_normed = sum(recv_t[q].astype(F32) for q in range(4))
    x_mine = tokens_ref[pl.ds(pl.multiple_of(64 * z, 64), 64), :].astype(F32)
    d_cap, tv0, tv1 = norm_back_rows(x_mine, tv(0), dt_normed)
    row_c = lax.broadcasted_iota(jnp.int32, d_cap.shape, 0)
    for c in range(4):
        d_cap = d_cap + jnp.where((row_c == 16 * c + 15) & (z == 3), dt_hidden[c:c + 1], 0.0)
    dcap_ref[...] = d_cap
    first = (z == 0).astype(F32)
    sums_ref[8:9] = dv8 * first
    sums_ref[9:10] = dv9 * first
    sums_ref[10:11] = dv10 * first
    sums_ref[11:12] = tv0
    sums_ref[12:13] = tv1
    sums_ref[13:14] = tv2 * first
    sums_ref[14:15] = tv3 * first
    sums_ref[15:16] = tv4 * first
    sums_ref[16:17] = tv5 * first
    sums_ref[17:18] = tv6 * first
    own_row = lambda a: sum(jnp.where(z == q, a[q:q + 1].astype(F32), 0.0) for q in range(4))
    pick = lambda a: a[:, 0:part].astype(F32)
    wide = jnp.concatenate
    pieces = [
        dh_upper, dt_upper.astype(F32), h_active.astype(F32), t_active.astype(F32),
        wide([pick(d_pooled), pick(pooled), pick(dt_q), pick(t_q)], 1),
        wide([pick(dt_mixed), pick(t_mixed), jnp.broadcast_to(pick(dq_my), (4, part)), jnp.broadcast_to(pick(p_q), (4, part))], 1),
        own_row(h_normed), own_row(d_start), own_row(t_last), own_row(t_second),
        own_row(dt_attend), own_row(dt_branch), own_row(t_final), pad1,
        used, t_used, tk_used, p_used,
    ]
    rows_ref[...] = jnp.concatenate(pieces, 0).astype(BF)
    for copy in started:
        copy.wait_send()

def middle(final, block_out, tokens, tp, downs, outs, ivec, tvec, pbias, tbias, label, temp, cid, n_dp):
    length, width = final.shape
    v, hbm = pl.BlockSpec(memory_space=pltpu.VMEM), pl.BlockSpec(memory_space=pl.ANY)
    f = lambda *s: jax.ShapeDtypeStruct(s, F32)
    return pl.pallas_call(
        middle_kernel,
        in_specs=[hbm, hbm, v, hbm, hbm] + [v] * 6 + [pl.BlockSpec(memory_space=pltpu.SMEM)],
        out_specs=[v] * 7,
        out_shape=[f(length, width), jax.ShapeDtypeStruct((length, width), BF), jax.ShapeDtypeStruct((ROWS, width), BF), f(24, width), f(64, width), f(8, 128), f(8 * n_dp, width)],
        scratch_shapes=[
            pltpu.VMEM((256, width), F32), pltpu.VMEM((256, width), BF),
            pltpu.VMEM((12, 4, 4, width), F32), pltpu.VMEM((12, 4, 4, width), F32),
            pltpu.VMEM((8, width), F32), pltpu.VMEM((n_dp, 8, width), F32),
            pltpu.VMEM((length, 128), F32), pltpu.VMEM((4, 64, width), BF),
            pltpu.VMEM((length, width), BF), pltpu.VMEM((length, width), F32), pltpu.VMEM(tp.shape, BF), pltpu.VMEM(downs.shape, BF),
            pltpu.SemaphoreType.DMA((16, 8)), pltpu.SemaphoreType.DMA((16, 8)), pltpu.SemaphoreType.DMA((5,)),
        ],
        compiler_params=pltpu.CompilerParams(collective_id=cid, has_side_effects=True, vmem_limit_bytes=50 << 20),
    )(final, block_out, tokens, tp, downs, outs, ivec, tvec, pbias, tbias, label, temp)


def plane_moves(me, out, s):
    y, x, c = me.y, me.x, me.c
    n = out.shape[-1] // 2
    left, right = (lambda r: r.at[..., 0:n]), (lambda r: r.at[..., n : 2 * n])
    if s == 3:
        own = out.at[y, x, c]
        yield 6, left(own), left(own), me.at_x, None, left(out.at[y, 1 - x, c]), None
        yield 7, right(own), right(own), me.at_y, None, right(out.at[1 - y, x, c]), None
    elif s == 4:
        own = out.at[y, :, c]
        yield 8, left(own), left(own), me.at_y, None, left(out.at[1 - y, :, c]), None
        own = out.at[:, x, c]
        yield 9, right(own), right(own), me.at_x, None, right(out.at[:, 1 - x, c]), None
    else:
        mine = out.at[:, :, c]
        yield 10, mine, mine, me.at_c, None, out.at[:, :, 1 - c], None


def turn_moves(me, src, home, split):
    z = me.z
    for k in (3, 2, 1):
        to, fro = (z + k) % 4, (z + 4 - k) % 4
        yield k - 1, src.at[to] if split else src, home.at[z], me.at_z(k), None, home.at[fro], None


def run_moves(moves, act, send, recv):
    for slot, src, dst, dev, go, come, arrives in moves:
        make = lambda a, b: pltpu.make_async_remote_copy(
            a, b, send.at[slot], recv.at[slot], device_id=dev, device_id_type=MESH
        )
        if act == "arrived":
            copy, when = make(src, come).wait_recv, arrives
        else:
            copy, when = getattr(make(src, dst), "start" if act == "start" else "wait_send"), go
        if when is None:
            copy()
        else:
            pl.when(when)(lambda: copy())


class Spread:
    stages = 6

    def __init__(self, me, src, out, send, recv, local):
        self.me, self.src, self.out, self.send, self.recv, self.local = me, src, out, send, recv, local

    def moves(self, s):
        me, out = self.me, self.out
        y, x, c, z = me.y, me.x, me.c, me.z
        if s < 3:
            home = out.at[y, x, c]
            for up in (True, False):
                step = -s if up else s
                slab, come = z + step, z + step + (-1 if up else 1)
                go = ((slab >= 0) & (z < 3)) if up else ((slab < 4) & (z > 0))
                arrives = (come >= 0) & (come < 4)
                slab, come = jnp.clip(slab, 0, 3), jnp.clip(come, 0, 3)
                src = self.src if s == 0 else home.at[slab]
                yield s + (0 if up else 3), src, home.at[slab], me.at_z(1 if up else 3), go, home.at[come], arrives
        else:
            yield from plane_moves(me, out, s)

    def each(self, s, act):
        run_moves(self.moves(s), act, self.send, self.recv)

    def keep(self):
        me = self.me
        return pltpu.make_async_copy(self.src, self.out.at[me.y, me.x, me.c, me.z], self.local)

    def begin(self, s):
        if s == 0:
            self.keep().start()
        else:
            self.each(s - 1, "arrived")
        if s == 3:
            self.keep().wait()
        self.each(s, "start")

    def finish(self):
        self.each(5, "arrived")
        for s in range(6):
            self.each(s, "sent")


class Reduce:
    def __init__(self, me, g, own, acc, from_c, from_1, from_2, from_z, send, recv, local):
        self.me, self.g, self.own, self.acc = me, g, own, acc
        self.from_c, self.from_1, self.from_2, self.from_z = from_c, from_1, from_2, from_z
        self.send, self.recv, self.local = send, recv, local
        self.size = acc.shape[-1]
        self.left, self.right = slice(0, self.size // 2), slice(self.size // 2, self.size)

    def moves(self, n, stage):
        me, acc = self.me, self.acc.at[n]
        y, x, z = me.y, me.x, me.z
        if stage == "core":
            src = self.g.at[:, :, 1 - me.c, :, :, n * self.size : (n + 1) * self.size]
            yield 0, src, self.from_c.at[n], me.at_c, None, self.from_c.at[n], None
        elif stage == "one":
            a, b = self.from_1.at[n, 0], self.from_1.at[n, 1]
            yield 1, acc.at[1 - y, :, :, :, self.left], a, me.at_y, None, a, None
            yield 2, acc.at[:, 1 - x, :, :, self.right], b, me.at_x, None, b, None
        elif stage == "two":
            a, b = self.from_2.at[n, 0], self.from_2.at[n, 1]
            yield 3, acc.at[y, 1 - x, :, :, self.left], a, me.at_x, None, a, None
            yield 4, acc.at[1 - y, x, :, :, self.right], b, me.at_y, None, b, None
        else:
            for k in (3, 2, 1):
                got = self.from_z.at[n, k - 1]
                yield 4 + k, acc.at[y, x, (z + k) % 4], got, me.at_z(k), None, got, None

    def act(self, n, stage, what):
        run_moves(self.moves(n, stage), what, self.send.at[n], self.recv.at[n])

    def keep(self, n):
        src = self.g.at[:, :, self.me.c, :, :, n * self.size : (n + 1) * self.size]
        return pltpu.make_async_copy(src, self.acc.at[n], self.local.at[n])

    def start(self, n, stage):
        if stage == "core":
            self.keep(n).start()
        self.act(n, stage, "start")

    def done(self, n, stage):
        me, acc = self.me, self.acc
        y, x = me.y, me.x
        f32 = lambda v: v.astype(F32)

        def each(count, body):
            lax.fori_loop(0, count, lambda q, carry: body(q) or carry, 0)

        if stage == "core":
            self.keep(n).wait()
        self.act(n, stage, "arrived")
        if stage == "core":

            def add(q):
                for a in range(2):
                    for b in range(2):
                        acc[n, a, b, q] = (f32(acc[n, a, b, q]) + f32(self.from_c[n, a, b, q])).astype(BF)

            each(4, add)
        elif stage == "one":

            def add(q):
                for b in range(2):
                    at = (n, y, b, q, slice(None), self.left)
                    acc[at] = (f32(acc[at]) + f32(self.from_1[n, 0, b, q])).astype(BF)
                    at = (n, b, x, q, slice(None), self.right)
                    acc[at] = (f32(acc[at]) + f32(self.from_1[n, 1, b, q])).astype(BF)

            each(4, add)
        elif stage == "two":

            def add(q):
                for half, cut in enumerate((self.left, self.right)):
                    at = (n, y, x, q, slice(None), cut)
                    acc[at] = (f32(acc[at]) + f32(self.from_2[n, half, q])).astype(BF)

            each(4, add)
        else:
            total = f32(acc[n, y, x, me.z])
            for k in range(3):
                total += f32(self.from_z[n, k])
            self.own[:, n * self.size : (n + 1) * self.size] = total

    def finish(self, n):
        for stage in ("core", "one", "two", "z"):
            self.act(n, stage, "sent")


REDUCE_STEPS = {
    0: [("start", 0, "core"), ("start", 1, "core")],
    1: [("done", 0, "core"), ("start", 0, "one")],
    2: [("done", 1, "core")],
    3: [("start", 1, "one")],
    5: [("done", 0, "one"), ("start", 0, "two")],
    7: [("done", 1, "one"), ("done", 0, "two"), ("start", 0, "z"), ("start", 1, "two")],
    9: [("done", 1, "two"), ("start", 1, "z")],
    12: [("done", 0, "z"), ("done", 1, "z")],
}
CHUNKS = 2


def attend_bwd_kernel_hosting(q_ref, k_ref, v_ref, do_ref, lse_ref, d_ref, g_ref, rows_ref, dq_ref, dk_ref, dv_ref, own_ref, all_ref,
                              acc, from_c, from_1, from_2, from_z, send, recv, local, rows_send, rows_recv, rows_local):
    h_at = pl.program_id(0)
    me = Place()
    spread = Spread(me, rows_ref, all_ref, rows_send, rows_recv, rows_local)
    reduce = Reduce(me, g_ref, own_ref, acc, from_c, from_1, from_2, from_z, send, recv, local)

    def tick(step):
        if step not in REDUCE_STEPS:
            return

        def go():
            if step == 0:
                greet([me.at_z(1), me.at_z(2), me.at_z(3), me.at_x, me.at_y, me.at_c])
            for what, n, stage in REDUCE_STEPS[step]:
                getattr(reduce, what)(n, stage)

        pl.when(h_at == step // 2)(go)

    for step in range(0, 12, 2):
        tick(step)
    for s in range(6):
        pl.when(h_at == s)(partial(spread.begin, s))
    q = q_ref[...] * 0.125
    k, v, do = k_ref[...], v_ref[...], do_ref[...]
    lane = lax.broadcasted_iota(jnp.int32, k.shape, 1)
    low = lane < 64
    for h in range(2):
        if h == 1:
            for step in range(1, 12, 2):
                tick(step)
        keep = low if h == 0 else ~low
        s = mm(jnp.where(keep, k, jnp.zeros_like(k)), q, 1, 1)
        p = jnp.exp(s - lse_ref[0, h : h + 1, :])
        dp = mm(jnp.where(keep, v, jnp.zeros_like(v)), do, 1, 1)
        ds = (p * (dp - d_ref[0, h : h + 1, :])).astype(BF)
        d_v = mm(p.astype(BF), do).astype(BF)
        d_k = mm(ds, q).astype(BF)
        d_q = (mm(ds, k, 0, 0) * 0.125).astype(BF)
        for ref, value in ((dq_ref, d_q), (dk_ref, d_k), (dv_ref, d_v)):
            ref[...] = value if h == 0 else jnp.where(low, ref[...], value)

    def last():
        for what, n, stage in REDUCE_STEPS[12]:
            getattr(reduce, what)(n, stage)
        for n in range(CHUNKS):
            reduce.finish(n)
        spread.finish()

    pl.when(h_at == pl.num_programs(0) - 1)(last)


def attend_bwd_and_reduce(proj, d_out, lse, inner, g, own_rows, cid):
    length, width = proj.shape[0], proj.shape[1] // 3
    pairs = width // 128
    rows, n = g.shape[0] // 32, g.shape[1]
    size = n // CHUNKS
    block = lambda part: pl.BlockSpec((length, 128), lambda h: (0, part * pairs + h))
    row = pl.BlockSpec((1, 2, length), lambda h: (h, 0, 0))
    hbm = pl.BlockSpec(memory_space=pl.ANY)
    result = jax.ShapeDtypeStruct((length, width), BF)
    v = lambda *s: pltpu.VMEM(s, BF)
    return pl.pallas_call(
        attend_bwd_kernel_hosting,
        grid=(pairs,),
        in_specs=[block(0), block(1), block(2), block(0), row, row, hbm, hbm],
        out_specs=[block(0)] * 3 + [pl.BlockSpec((rows, n), lambda h: (0, 0)), hbm],
        out_shape=[result] * 3
        + [jax.ShapeDtypeStruct((rows, n), F32), jax.ShapeDtypeStruct((2, 2, 2, 4) + own_rows.shape, BF)],
        scratch_shapes=[
            v(CHUNKS, 2, 2, 4, rows, size), v(CHUNKS, 2, 2, 4, rows, size), v(CHUNKS, 2, 2, 4, rows, size // 2),
            v(CHUNKS, 2, 4, rows, size // 2), v(CHUNKS, 3, rows, size),
            pltpu.SemaphoreType.DMA((CHUNKS, 8)), pltpu.SemaphoreType.DMA((CHUNKS, 8)), pltpu.SemaphoreType.DMA((CHUNKS,)),
            pltpu.SemaphoreType.DMA((11,)), pltpu.SemaphoreType.DMA((11,)), pltpu.SemaphoreType.DMA,
        ],
        compiler_params=pltpu.CompilerParams(collective_id=cid, has_side_effects=True, vmem_limit_bytes=60 << 20),
    )(proj, proj, proj, d_out, lse, inner, g.reshape(2, 2, 2, 4, rows, n), own_rows)


def attend_fwd_kernel_hosting(q_ref, k_ref, v_ref, split_ref, downs_ref, tokens_ref,
                              o_ref, lse_ref, tp_ref, down_ref, token_ref, send, recv, local):
    h_at = pl.program_id(0)
    me = Place()
    home = tp_ref.at[me.y, me.x, me.c]
    down_home = down_ref.at[me.y, me.x, me.c]
    keeps = [
        pltpu.make_async_copy(split_ref.at[me.z], home.at[me.z], local.at[0]),
        pltpu.make_async_copy(downs_ref, down_home, local.at[1]),
        pltpu.make_async_copy(tokens_ref, token_ref.at[me.z], local.at[2]),
    ]
    groups = {
        "split": (lambda: turn_moves(me, split_ref, home, True), 0),
        "tokens": (lambda: turn_moves(me, tokens_ref, token_ref, False), 2),
        "split_xy": (lambda: plane_moves(me, tp_ref, 3), 0),
        "down_one": (lambda: plane_moves(me, down_ref, 3), 1),
        "down_two": (lambda: plane_moves(me, down_ref, 4), 1),
        "down_core": (lambda: plane_moves(me, down_ref, 5), 1),
    }

    def act(name, what):
        moves, a = groups[name]
        run_moves(moves(), what, send.at[a], recv.at[a])

    def first():
        greet([me.at_z(1), me.at_z(2), me.at_z(3), me.at_x, me.at_y, me.at_c])
        for keep in keeps:
            keep.start()
        act("split", "start")
        keeps[1].wait()
        act("down_one", "start")

    def second_step():
        act("down_one", "arrived")
        act("down_two", "start")

    def middle_step():
        act("split", "arrived")
        keeps[0].wait()
        act("split_xy", "start")
        act("tokens", "start")

    def fifth_step():
        act("down_two", "arrived")
        act("down_core", "start")

    def last():
        for name in ("split_xy", "down_core", "tokens"):
            act(name, "arrived")
        keeps[2].wait()
        for name in groups:
            act(name, "sent")

    pl.when(h_at == 0)(first)
    pl.when(h_at == 2)(second_step)
    pl.when(h_at == 3)(middle_step)
    pl.when(h_at == 5)(fifth_step)
    attend_fwd_kernel(q_ref, k_ref, v_ref, o_ref, lse_ref)
    pl.when(h_at == pl.num_programs(0) - 1)(last)


def attend_fwd_and_gather(proj, split, downs, tokens, cid):
    length, width = proj.shape[0], proj.shape[1] // 3
    pairs = width // 128
    block = lambda part: pl.BlockSpec((length, 128), lambda h: (0, part * pairs + h))
    hbm = pl.BlockSpec(memory_space=pl.ANY)
    s = jax.ShapeDtypeStruct
    return pl.pallas_call(
        attend_fwd_kernel_hosting,
        grid=(pairs,),
        in_specs=[block(0), block(1), block(2), hbm, hbm, hbm],
        out_specs=[block(0), pl.BlockSpec((1, 2, length), lambda h: (h, 0, 0)), hbm, hbm, hbm],
        out_shape=[
            s((length, width), BF),
            s((pairs, 2, length), F32),
            s((2, 2, 2) + split.shape, BF),
            s((2, 2, 2) + downs.shape, BF),
            s((4,) + tokens.shape, BF),
        ],
        scratch_shapes=[pltpu.SemaphoreType.DMA((3, 11)), pltpu.SemaphoreType.DMA((3, 11)), pltpu.SemaphoreType.DMA((3,))],
        compiler_params=pltpu.CompilerParams(collective_id=cid, has_side_effects=True, vmem_limit_bytes=48 << 20),
    )(proj, proj, proj, split, downs, tokens)


def mlp_fwd_kernel(x_ref, mixed_ref, wo_ref, wu_ref, wd_ref, bias_ref, vec_ref, tp_in,
                   hidden_ref, second_ref, active_ref, slope_ref, block_ref, final_ref, tp_ref, total, send, recv):
    k = pl.program_id(0)
    me = Place()

    def act(s, what):
        run_moves(plane_moves(me, tp_ref, s), what, send, recv)

    def first():
        greet([me.at_x, me.at_y, me.at_c])
        act(4, "start")

    def then():
        act(4, "arrived")
        act(5, "start")

    pl.when(k == 0)(first)
    pl.when(k == pl.num_programs(0) - 1)(then)
    vec = vec_ref[...]

    @pl.when(k == 0)
    def _():
        hidden = x_ref[...].astype(F32) + mm(mixed_ref[...], wo_ref[...])
        hidden_ref[...] = hidden
        second_ref[...] = layer_norm(hidden, vec[2:3], vec[3:4]).astype(BF)
        total[...] = hidden + vec[4:5]

    value, slope = gelu_pair(mm(second_ref[...], wu_ref[...]) + bias_ref[0])
    active = value.astype(BF)
    active_ref[...] = active
    slope_ref[...] = slope.astype(BF)
    total[...] += mm(active, wd_ref[...])

    @pl.when(k == pl.num_programs(0) - 1)
    def _():
        block_ref[...] = total[...]
        final_ref[...] = layer_norm(total[...], vec[5:6], vec[6:7]).astype(BF)
        act(5, "arrived")
        act(4, "sent")
        act(5, "sent")


def mlp_fwd(x, mixed, w_outs, main, bias, vec, fold, tp, cid):
    rows, width = mixed.shape
    whole = pl.BlockSpec((rows, width), lambda k: (0, 0))
    tile = pl.BlockSpec((rows, width), lambda k: (0, k))
    at = lambda f: pl.BlockSpec((width, width), lambda k: (0, f(k)))
    s = lambda n, t: jax.ShapeDtypeStruct((rows, n * width), t)
    hbm = pl.BlockSpec(memory_space=pl.ANY)
    return pl.pallas_call(
        mlp_fwd_kernel,
        grid=(fold,),
        in_specs=[whole, whole, at(lambda k: 0), at(lambda k: k), at(lambda k: fold + k),
                  pl.BlockSpec((1, 1, width), lambda k: (k, 0, 0)), pl.BlockSpec(vec.shape, lambda k: (0, 0)), hbm],
        out_specs=[whole, whole, tile, tile, whole, whole, hbm],
        out_shape=[s(1, F32), s(1, BF), s(fold, BF), s(fold, BF), s(1, F32), s(1, BF),
                   jax.ShapeDtypeStruct(tp.shape, BF)],
        scratch_shapes=[pltpu.VMEM((rows, width), F32), pltpu.SemaphoreType.DMA((11,)), pltpu.SemaphoreType.DMA((11,))],
        input_output_aliases={7: 6},
        compiler_params=pltpu.CompilerParams(collective_id=cid, has_side_effects=True, vmem_limit_bytes=56 << 20),
    )(x, mixed, w_outs, main, main, bias.reshape(fold, 1, width), vec, tp)


def mlp_bwd_kernel(dy_ref, branch_ref, active_ref, slope_ref, second_ref, hidden_ref, mixed_ref,
                   wo_ref, wu_ref, wd_ref, vec_ref,
                   g_ref, gs_ref, dhid_ref, dmix_ref, inner_ref, bias_ref, dvec_ref, total, dy_in, hid_in, mix_in, slots, fetch, leave):
    k = pl.program_id(0)
    fold = pl.num_programs(0)
    pairs = ((dy_ref, dy_in), (hidden_ref, hid_in), (mixed_ref, mix_in))
    loads = [pltpu.make_async_copy(src, dst, fetch.at[n]) for n, (src, dst) in enumerate(pairs)]

    @pl.when(k == 0)
    def _():
        for load in loads:
            load.start()

    width = mixed_ref.shape[1]

    def leaves(n):
        at = pl.ds(pl.multiple_of((n + 1) * width, width), width)
        return pltpu.make_async_copy(slots.at[n % 2], gs_ref.at[:, at], leave.at[n % 2])

    pl.when(k >= 2)(lambda: leaves(k - 2).wait())
    branch = branch_ref[...]
    columns = lambda n: pl.ds(pl.multiple_of(n * width, width), width)
    slots[k % 2] = mm(active_ref[...], branch, 0, 0).astype(BF)
    leaves(k).start()
    d_upper_f = mm(branch, wd_ref[...], 1, 1) * slope_ref[...].astype(F32)
    bias_ref[0] = jnp.sum(d_upper_f, 0, keepdims=True)
    d_upper = d_upper_f.astype(BF)
    g_ref[...] = mm(second_ref[...], d_upper, 0, 0).astype(BF)
    back = mm(d_upper, wu_ref[...], 1, 1)

    @pl.when(k == 0)
    def _():
        total[...] = back

    @pl.when(k > 0)
    def _():
        total[...] += back

    @pl.when(k == fold - 1)
    def _():
        vec = vec_ref[...]
        for load in loads:
            load.wait()
        d_hidden, gain, shift = norm_back_rows(hid_in[...], vec[2:3], total[...])
        dvec_ref[0:1] = gain
        dvec_ref[1:2] = shift
        d_hidden = dy_in[...] + d_hidden
        dhid_ref[...] = d_hidden
        d_attend = d_hidden.astype(BF)
        mixed = mix_in[...]
        leaves(fold - 2).wait()
        slots[fold % 2] = mm(mixed, d_attend, 0, 0).astype(BF)
        out = pltpu.make_async_copy(slots.at[fold % 2], gs_ref.at[:, 0:width], leave.at[2])
        out.start()
        d_mixed = mm(d_attend, wo_ref[...], 1, 1).astype(BF)
        dmix_ref[...] = d_mixed
        head = lax.broadcasted_iota(jnp.int32, (16, width), 0)
        lane = lax.broadcasted_iota(jnp.int32, (16, width), 1)
        own = (lane // (width // HEADS) == head).astype(BF)
        high, low = split_two(d_mixed.astype(F32) * mixed.astype(F32))
        sums = mm(own, high, 1, 1) + mm(own, low, 1, 1)
        for h in range(HEADS // 2):
            inner_ref[h] = sums[2 * h : 2 * h + 2]
        leaves(fold - 1).wait()
        out.wait()


def mlp_bwd(dy, branch, active, slope, second, hidden, mixed, w_outs, main, vec, fold):
    rows, width = mixed.shape
    whole = pl.BlockSpec((rows, width), lambda k: (0, 0))
    tile = pl.BlockSpec((rows, width), lambda k: (0, k))
    at = lambda f: pl.BlockSpec((width, width), lambda k: (0, f(k)))
    f = lambda *s: jax.ShapeDtypeStruct(s, F32)
    hbm = pl.BlockSpec(memory_space=pl.ANY)
    return pl.pallas_call(
        mlp_bwd_kernel,
        grid=(fold,),
        in_specs=[hbm, whole, tile, tile, whole, hbm, hbm,
                  at(lambda k: 0), at(lambda k: k), at(lambda k: fold + k), pl.BlockSpec(vec.shape, lambda k: (0, 0))],
        out_specs=[at(lambda k: k), hbm, whole, whole,
                   pl.BlockSpec((HEADS // 2, 2, rows), lambda k: (0, 0, 0)),
                   pl.BlockSpec((1, 1, width), lambda k: (k, 0, 0)), pl.BlockSpec((8, width), lambda k: (0, 0))],
        out_shape=[jax.ShapeDtypeStruct((width, fold * width), BF), jax.ShapeDtypeStruct((width, (1 + fold) * width), BF), f(rows, width),
                   jax.ShapeDtypeStruct((rows, width), BF), f(HEADS // 2, 2, rows), f(fold, 1, width), f(8, width)],
        scratch_shapes=[pltpu.VMEM((rows, width), F32), pltpu.VMEM((rows, width), F32), pltpu.VMEM((rows, width), F32),
                        pltpu.VMEM((rows, width), BF), pltpu.VMEM((2, width, width), BF),
                        pltpu.SemaphoreType.DMA((3,)), pltpu.SemaphoreType.DMA((3,))],
        compiler_params=pltpu.CompilerParams(vmem_limit_bytes=60 << 20),
    )(dy, branch, active, slope, second, hidden, mixed, w_outs, main, main, vec)


def finish_kernel(dq_ref, dk_ref, dv_ref, normed_ref, w_ref, x_ref, dhid_ref, rows_ref, sums_ref, vec_ref, dimage_ref, dtext_ref, own_ref, moved_ref, *rest):
    outer_refs, rest = rest[:13], rest[13:]
    (g, dx, from_c, acc_c, from_1, from_2, from_z, q_in, k_in, v_in, n_in, w_in, x_in, h_in, r_in, turned,
     send, recv, local, fetch) = rest
    me = Place()
    pairs = ((dq_ref, q_in), (normed_ref, n_in), (dk_ref, k_in), (dv_ref, v_in), (w_ref, w_in), (x_ref, x_in), (dhid_ref, h_in), (rows_ref, r_in))
    loads = [pltpu.make_async_copy(src, dst, fetch.at[n]) for n, (src, dst) in enumerate(pairs)]
    for load in loads:
        load.start()
    dq_ref, dk_ref, dv_ref, normed_ref, w_ref, x_ref, dhid_ref = q_in, k_in, v_in, n_in, w_in, x_in, h_in
    y, x, c, z = me.y, me.x, me.c, me.z
    width = dq_ref.shape[1]
    part = g.shape[4]
    tile = dx.shape[1]
    half = g.shape[-1] // 2
    left, right = slice(0, half), slice(half, 2 * half)
    f32 = lambda v: v.astype(F32)
    started = []
    greet([me.at_z(1), me.at_z(2), me.at_z(3), me.at_x, me.at_y, me.at_c])

    def push(slot, src, dst, dev, arriving):
        copy = pltpu.make_async_remote_copy(src, dst, send.at[slot], recv.at[slot], device_id=dev, device_id_type=MESH)
        copy.start()
        started.append(copy)
        return pltpu.make_async_remote_copy(src, arriving, send.at[slot], recv.at[slot], device_id=dev, device_id_type=MESH)

    def put(value, first):
        for p in range(32):
            i, q = p // 4, p % 4
            g[i // 4, (i // 2) % 2, i % 2, q, :, first : first + value.shape[1]] = value[part * p : part * (p + 1)].astype(BF)

    gain, shift, moves = [], [], []

    def d_x_rows(k):
        to, fro = (z + k) % 4, (z + 4 - k) % 4
        at = pl.ds(pl.multiple_of(to * tile, tile), tile)
        back = None
        for n, ref in enumerate((dq_ref, dk_ref, dv_ref)):
            term = mm(ref[at, :], w_ref[:, n * width : (n + 1) * width], 1, 1)
            back = term if back is None else back + term
        d_x, a, b = norm_back_rows(x_ref[at, :].astype(F32), vec_ref[0:1], back)
        gain.append(a)
        shift.append(b)
        dx[to] = (dhid_ref[at, :] + d_x).astype(BF)
        if k:
            moves.append(push(k, dx.at[to], moved_ref.at[z], me.at_z(k), moved_ref.at[fro]))
        else:
            keep.start()

    keep = pltpu.make_async_copy(dx.at[z], moved_ref.at[z], local)

    def add(at, value):
        acc_c[at] = (f32(acc_c[at]) + f32(value)).astype(BF)

    def core(cut, slot):
        to = from_c.at[:, :, :, :, cut]
        return push(slot, g.at[:, :, 1 - c, :, :, cut], to, me.at_c, to)

    def core_done(arrive, cut):
        arrive.wait_recv()
        for a in range(2):
            for b in range(2):
                for q in range(4):
                    at = (a, b, q, slice(None), cut)
                    acc_c[at] = (f32(g[a, b, c, q, :, cut]) + f32(from_c[at])).astype(BF)

    def one_done(arrive, n, cut):
        arrive.wait_recv()
        for b in range(2):
            for q in range(4):
                add((b, x, q, slice(None), cut) if n else (y, b, q, slice(None), cut), from_1[n, b, q])

    def two_done(arrive, n, cut):
        arrive.wait_recv()
        for q in range(4):
            add((y, x, q, slice(None), cut), from_2[n, q])

    def along(cut, slot):
        arrives = []
        for k in (3, 2, 1):
            got = from_z.at[k - 1, :, cut]
            arrives.append(push(slot + k, acc_c.at[y, x, (z + k) % 4, :, cut], got, me.at_z(k), got))
        return arrives

    part_of = lambda n, ref: put(mm(normed_ref[...], ref[...], 0, 0), n * width)
    loads[0].wait()
    loads[1].wait()
    part_of(0, dq_ref)
    loads[2].wait()
    part_of(1, dk_ref)
    for load in loads[3:7]:
        load.wait()
    core_left = core(left, 0)
    d_x_rows(2)
    part_of(2, dv_ref)
    core_done(core_left, left)
    one_left = push(4, acc_c.at[1 - y, :, :, :, left], from_1.at[0], me.at_y, from_1.at[0])
    d_x_rows(3)
    d_x_rows(1)
    d_x_rows(0)
    sums = jnp.concatenate([sum(gain), sum(shift), sums_ref[2:, :]], 0)
    sums = jnp.concatenate([sums, jnp.zeros((128 - sums.shape[0], width), F32)], 0)
    put(jnp.transpose(sums), 3 * width)
    put(jnp.zeros((width, 128), F32), 3 * width + 128)
    core_right = core(right, 8)
    one_done(one_left, 0, left)
    two_left = push(6, acc_c.at[y, 1 - x, :, :, left], from_2.at[0], me.at_x, from_2.at[0])
    core_done(core_right, right)
    one_right = push(5, acc_c.at[:, 1 - x, :, :, right], from_1.at[1], me.at_x, from_1.at[1])
    loads[7].wait()
    group = 16
    count = 32 * group
    to, fro = lax.broadcasted_iota(jnp.int32, (count, count), 0), lax.broadcasted_iota(jnp.int32, (count, count), 1)
    turn = ((to % 32 == fro // group) & (to // 32 == fro % group)).astype(BF)
    for n in range(r_in.shape[1] // group):
        value = mm(turn, r_in[:, n * group : (n + 1) * group, :].reshape(count, width)).astype(BF)
        turned[n * group : (n + 1) * group] = value.reshape(group, 32, width)
    two_done(two_left, 0, left)
    z_left = along(left, 8)
    one_done(one_right, 1, right)
    two_right = push(7, acc_c.at[1 - y, x, :, :, right], from_2.at[1], me.at_y, from_2.at[1])
    outer_kernel(turned, dimage_ref, dtext_ref, *outer_refs)
    two_done(two_right, 1, right)
    z_right = along(right, 11)
    for arrive in z_left + z_right:
        arrive.wait_recv()
    total = f32(acc_c[y, x, z]) + f32(from_z[0]) + f32(from_z[1]) + f32(from_z[2])
    own_ref[...] = total
    keep.wait()
    for arrive in moves:
        arrive.wait_recv()
    for copy in started:
        copy.wait_send()


def finish_image(dq, dk, dv, normed, w_in, x, d_hidden, own_rows, sums, vec, d_image, d_text, cid):
    rows, width = dq.shape
    part, n, quarter = width // 32, 3 * width + 256, width // 4
    f = lambda *s: jax.ShapeDtypeStruct(s, F32)
    v, hbm = pl.BlockSpec(memory_space=pltpu.VMEM), pl.BlockSpec(memory_space=pl.ANY)
    s = lambda *shape: pltpu.VMEM(shape, BF)
    return pl.pallas_call(
        finish_kernel,
        in_specs=[hbm] * 8 + [v] * 4,
        out_specs=[v, hbm] + [v] * 13,
        out_shape=[jax.ShapeDtypeStruct((part, n), F32), jax.ShapeDtypeStruct((4, rows // 4, width), BF),
                   f(4, part, width), f(4, part, width), f(4 * part, width), f(4 * part, width), f(part, width), f(part, width),
                   f(part, width), f(4, part, quarter), f(4, part, quarter), f(4, part, quarter), f(4, part, quarter),
                   f(part, 128), f(2, 4 * part, 128)],
        scratch_shapes=[
            s(2, 2, 2, 4, part, n), s(4, rows // 4, width), s(2, 2, 4, part, n), s(2, 2, 4, part, n),
            s(2, 2, 4, part, n // 2), s(2, 4, part, n // 2), s(3, part, n),
            s(rows, width), s(rows, width), s(rows, width), s(rows, width), s(width, 3 * width), s(rows, width),
            pltpu.VMEM((rows, width), F32), s(32, ROWS, width), s(ROWS, 32, width),
            pltpu.SemaphoreType.DMA((15,)), pltpu.SemaphoreType.DMA((15,)), pltpu.SemaphoreType.DMA, pltpu.SemaphoreType.DMA((8,)),
        ],
        compiler_params=pltpu.CompilerParams(collective_id=cid, has_side_effects=True, vmem_limit_bytes=60 << 20),
    )(dq, dk, dv, normed, w_in, x, d_hidden, own_rows, sums, vec, d_image, d_text)


def outer_kernel(rows_ref, dimage_ref, dtext_ref,
                 pup_ref, tup_ref, pdown_ref, tdown_ref, pout_ref, tout_ref, thead_ref,
                 tq_ref, tk_ref, tv_ref, pv_ref, pk_ref, bias_ref):
    at_dp, z = lax.axis_index("dp"), lax.axis_index("seq")
    n_dp, n_z = 8, 4
    me = at_dp * n_z + z
    width = rows_ref.shape[2]
    part, quarter = width // 32, width // n_z
    wide_part = 4 * part
    n = n_dp * n_z
    each = quarter // part

    def iota(shape, d):
        return lax.broadcasted_iota(jnp.int32, shape, d)

    def selector(count, first):
        return (iota((count, width), 1) == iota((count, width), 0) + first).astype(BF)

    def group(r):
        return jnp.concatenate([rows_ref[r + c] for c in range(4)], 0)

    cols = jnp.concatenate(
        [mm(selector(part, part * me), rows_ref[r], 1, 1) for r in range(24, 80)], 1
    ).astype(BF)
    get = lambda r, count=1: cols[:, n * (r - 24) : n * (r - 24 + count)]
    a, b = iota((4 * n, n), 0), iota((4 * n, n), 1)
    same = ((a % n) // n_z == b // n_z) & (a // n == b % n_z)
    keep = lambda which: (same & (a % n_z == which)).astype(BF)
    units = selector(wide_part, wide_part * at_dp)
    heads = selector(part, quarter + part * (me % each))
    to_mine, to_head = keep(z), keep(me // each)
    chosen = lambda sel, r, perm: mm(mm(sel, group(r), 1, 1).astype(BF), perm).astype(BF)
    pdown_ref[...] = mm(chosen(units, 8, to_mine), dimage_ref[...])
    tdown_ref[...] = mm(chosen(units, 12, to_mine), rows_ref[29])
    pout_ref[...] = mm(chosen(heads, 16, to_head), rows_ref[25])
    tout_ref[...] = mm(chosen(heads, 20, to_head), rows_ref[28])
    thead_ref[...] = mm(get(30), dtext_ref[...])
    ones = jnp.ones((n, 128), BF)
    bias_ref[0] = mm(chosen(units, 0, to_mine), ones)
    bias_ref[1] = mm(chosen(units, 4, to_mine), ones)
    a, b = iota((n, 4 * n), 0), iota((n, 4 * n), 1)
    spread = ((b % n) // n_z == a // n_z) & (b // n == a % n_z)
    spread = spread.astype(BF)
    lane_z = iota((1, 4 * n), 1) % n_z
    masks = [(lane_z == q).astype(BF) for q in range(n_z)]

    def blocks(values):
        return jnp.concatenate([v * m for v, m in zip(values, masks)], 0)

    by_image = lambda r: mm(get(r), spread).astype(BF)
    g16, g20 = group(16), group(20)

    def put(ref, value, first):
        for q in range(n_z):
            ref[q] = value[q * part : (q + 1) * part, first : first + ref.shape[2]]

    put(pup_ref, mm(blocks([by_image(24)] * 4), group(0)), 0)
    put(tup_ref, mm(blocks([by_image(27)] * 4), group(4)), 0)
    put(tq_ref, mm(blocks([by_image(26)] * 4), g16), 2 * quarter)
    lane = iota((1, width), 1)
    count = HEADS // n_z
    hw = quarter // count

    def by_head(values_of, rhs, first):
        total = None
        for h in range(count):
            own = ((lane >= first + hw * h) & (lane < first + hw * h + hw)).astype(F32)
            one = mm(blocks(values_of(h)), rhs) * own
            total = one if total is None else total + one
        return total

    put(tk_ref, by_head(lambda h: [get(56 + 4 * h, 4)] * 4, g16, 3 * quarter), 3 * quarter)
    put(tv_ref, by_head(lambda h: [get(44 + 4 * h, 4)] * 4, g20, 0), 0)
    put(pv_ref, by_head(lambda h: [by_image(32 + count * q + h) for q in range(n_z)], g16, 0), 0)
    a, b = iota((HEADS * n, 128), 0), iota((HEADS * n, 128), 1)
    pk_ref[...] = mm(get(68, HEADS), (a // n == b).astype(BF))


def fast_program(
    patches, captions, pairs,
    image_attend_in, image_attend_out, image_up_weight, image_up_bias, image_down_weight,
    image_vectors, probe_query_weight, probe_pair_weight, probe_out_weight, probe_up_weight,
    probe_up_bias, probe_down_weight, text_attend_in, text_attend_out, text_up_weight,
    text_up_bias, text_down_weight, text_vectors, text_head_weight, temp_bias,
):
    n_dp, n_z = lax.axis_size("dp"), lax.axis_size("seq")
    world = n_dp * n_z
    at_dp, at_z = lax.axis_index("dp"), lax.axis_index("seq")
    me = at_dp * n_z + at_z
    width = patches.shape[-1]
    head_width = width // HEADS
    hidden_width = image_up_weight.shape[1]
    part, quarter = width // world, width // n_z
    wide_part = hidden_width // world
    fold = hidden_width // width
    length = patches.shape[1] * n_z

    small = jnp.concatenate(
        [image_vectors.reshape(-1), text_vectors.reshape(-1), image_up_bias, probe_up_bias, text_up_bias]
    )
    sizes = [image_vectors.size, text_vectors.size, image_up_bias.size, probe_up_bias.size, text_up_bias.size]
    small = jnp.pad(small, (0, 2048 - small.shape[0])).reshape(16, 128)

    def by_units(w):
        return w.reshape(part, n_dp, n_z, wide_part).transpose(2, 0, 1, 3).reshape(n_z, part, width)

    def by_heads(w):
        cut = w.reshape(part, n_z, quarter).transpose(1, 0, 2)
        return jnp.pad(cut, ((0, 0), (0, 0), (0, 256 - quarter)))

    split = [by_units(probe_up_weight), by_units(text_up_weight)]
    split += [by_heads(text_attend_in[:, k * width : (k + 1) * width]) for k in range(3)]
    split += [by_heads(text_head_weight), by_heads(probe_query_weight)]
    split += [by_heads(probe_pair_weight[:, k * width : (k + 1) * width]) for k in range(2)]
    split = jnp.concatenate(split, 2)
    downs = jnp.concatenate([text_down_weight, probe_down_weight], 1)
    w_in, small_all, w_outs, x = gather(
        [image_attend_in, small, jnp.concatenate([image_attend_out, text_attend_out, probe_out_weight], 1), patches],
        [("full", "S"), ("full", "C"), ("full", "S"), ("za", None)],
        [(0, 0), (1, 0), (0, 1), (1, 1), (0, 2), (1, 2), (2, 0), (0, 3), (2, 1), (1, 3), (2, 2), (3, 0)]
        + [(0, 4), (1, 4), (2, 3), (0, 5), (1, 5), (2, 4), (2, 5)],
        1,
    )
    w_outs = w_outs.reshape(width, 3 * width)
    outs = lax.dynamic_slice_in_dim(w_outs[:, width:], at_z * quarter, quarter, 0)
    w_in = w_in.reshape(width, 3 * width)
    x = x.reshape(length, width)
    main = jnp.concatenate(
        [
            image_up_weight.reshape(part, width, fold).transpose(0, 2, 1).reshape(part, hidden_width),
            image_down_weight.reshape(part, hidden_width),
        ],
        1,
    )
    main = lax.all_gather(main, ALL, axis=0, tiled=True)

    small_all = small_all.reshape(world, -1)
    cuts = [sum(sizes[:i]) for i in range(len(sizes) + 1)]
    pieces = [small_all[:, cuts[i] : cuts[i + 1]].astype(F32) for i in range(len(sizes))]
    ivec = pieces[0].reshape(world, -1, part).transpose(1, 0, 2).reshape(-1, width)
    tvec = pieces[1].reshape(world, -1, part).transpose(1, 0, 2).reshape(-1, width)
    i_bias = pieces[2].reshape(width, fold).T.reshape(1, hidden_width)

    def own_units(p):
        p = p.reshape(n_dp, n_z, wide_part)
        return lax.dynamic_index_in_dim(p, at_z, 1, False).reshape(1, width)

    p_bias, t_bias = own_units(pieces[3]), own_units(pieces[4])

    normed = layer_norm(x.astype(F32), ivec[0], ivec[1]).astype(BF)
    proj = mm(normed, w_in).astype(BF)
    mixed, lse, tp, downs, tokens = attend_fwd_and_gather(proj, split, downs, captions, 5)
    hidden, second, active, slope, block_out, final, tp = mlp_fwd(x, mixed, w_outs, main, i_bias, ivec, fold, tp, 6)
    tp, downs = tp.reshape(width, -1), downs.reshape(width, -1)

    labels = (2 * pairs - 1).astype(F32).reshape(n_dp, n_z, n_dp, n_z)
    labels = jnp.pad(labels, ((0, 0), (0, n_z), (0, 0), (n_z, 0))).reshape(2 * world, 2 * world)
    dy, d_branch, rows, sums, d_captions, loss_row, d_embeds = middle(
        final, block_out, tokens.reshape(-1, width), tp, downs, outs, ivec, tvec, p_bias, t_bias, labels, temp_bias, 2, n_dp
    )
    loss, grad_temp = loss_row[0, 0], loss_row[0, 1:3]
    grad_captions = d_captions.reshape(captions.shape)

    g_up, g_rest, d_hidden, d_mixed, inner, g_bias, dvec = mlp_bwd(
        dy, d_branch, active, slope, second, hidden, mixed, w_outs, main, ivec, fold
    )
    g_rest = lax.psum_scatter(g_rest, ALL, scatter_dimension=0, tiled=True).astype(F32)
    own_out = g_rest[:, :width]
    own_down = g_rest[:, width:].reshape(wide_part, width)
    d_q, d_k, d_v, own_up, rows = attend_bwd_and_reduce(proj, d_mixed, lse, inner, g_up, rows, 4)
    own_up = own_up.reshape(part, fold, width).transpose(0, 2, 1).reshape(part, hidden_width)
    rows = rows.reshape(world, ROWS, width)
    sums = jnp.concatenate([dvec[0:2], dvec[0:2], sums[4:], g_bias.reshape(fold, width)], 0)
    d_embeds = d_embeds.reshape(n_dp, 2, n_z, width).astype(BF)
    own_in, moved, *outer = finish_image(
        d_q, d_k, d_v, normed, w_in, x, d_hidden, rows, sums, ivec,
        d_embeds[:, 0].reshape(world, width), d_embeds[:, 1].reshape(world, width), 3
    )
    pup, tup, own_p_down, own_t_down, own_p_out, own_t_out, own_t_head, tq, tk, tv, pv, pk, biases = outer
    grad_patches = moved.astype(F32)
    own_sums = own_in[:, 3 * width : 3 * width + 128].T
    own_in = own_in[:, : 3 * width]

    def wide(g):
        return g.reshape(n_z, part, n_dp, wide_part).transpose(1, 2, 0, 3).reshape(part, hidden_width)

    own_p_up, own_t_up = wide(pup), wide(tup)
    own_t_in = jnp.stack([tq, tk, tv]).transpose(2, 0, 1, 3).reshape(part, 3 * width)
    row20 = rows[:, 20].reshape(n_dp, n_z, n_z, quarter).astype(F32)
    probe_query = row20[0, :, 3].reshape(HEADS, head_width)
    own_p_k = (pk[:, :HEADS, None] * probe_query[None]).reshape(part, width)
    own_p_pair = jnp.concatenate([own_p_k, pv.transpose(1, 0, 2).reshape(part, width)], 1)
    d_query = jnp.sum(row20[:, :, 2], 0).reshape(width)
    mine = lambda v, n: lax.dynamic_slice_in_dim(v, me * n, n, -1)
    own_p_query = mine(ivec[7], part)[:, None] * d_query[None, :]
    dv7 = jnp.sum(probe_query_weight.astype(F32) * d_query[None, :], 1)
    own_ivec = jnp.concatenate([own_sums[0:7], dv7[None], own_sums[8:11]], 0)
    own_tvec = own_sums[11:18]
    own_bias = own_sums[24 : 24 + fold].T.reshape(wide_part)
    return (
        loss, grad_patches, grad_captions,
        own_in, own_out, own_up, own_bias, own_down, own_ivec,
        own_p_query, own_p_pair, own_p_out, own_p_up, biases[0, :, 0], own_p_down,
        own_t_in, own_t_out, own_t_up, biases[1, :, 0], own_t_down, own_tvec, own_t_head,
        grad_temp,
    )


def solution(mesh):
    tokens, matrix, vector, table = P("dp", "seq", None), P(ALL, None), P(ALL), P(None, ALL)
    weights = (
        (matrix, matrix, matrix, vector, matrix, table, matrix, matrix, matrix, matrix, vector, matrix)
        + (matrix, matrix, matrix, vector, matrix, table, matrix)
    )
    return jax.shard_map(
        fast_program if mesh.shape["dp"] == 8 and mesh.shape["seq"] == 4 else device_program,
        mesh=mesh,
        in_specs=(tokens, tokens, P()) + weights + (P(),),
        out_specs=(P(), tokens, tokens) + weights + (P(),),
        check_vma=False,
    )
```
